32 devices in a mesh: section: 4 (over x, core), dp: 8 (over z, y).
Axes of the slice: x: 2, y: 2, z: 4, core: 2. Of those that a mesh axis runs over, the one named last changes fastest.
Arguments:
- token_ids: int32 [2, 8, 128], P(None, 'dp'), may hold values from 0 to 14591
- segment_ids: int32 [2, 8, 128], P(None, 'dp'), may hold values from 0 to 3, never falling along the last dimension, each value on 1 to 64 neighbouring positions
- masked_rows: int32 [2, 8, 40], P(None, 'dp'), may hold values from 0 to 127, as said below
- embedding: bfloat16 [14592, 768], P('section'), may hold values from -0.59765625 to 0.59765625
- pos_table: bfloat16 [128, 768], replicated, may hold values from -6 to 6
- w_in: bfloat16 [4, 768, 3072], P('section')
- w_out: bfloat16 [4, 3072, 768], P('section'), may hold values from -0.109375 to 0.109375
- b_in: bfloat16 [4, 3072], P('section'), may hold values from -1.796875 to 1.796875
- b_out: bfloat16 [4, 768], P('section'), may hold values from -1.796875 to 1.796875
- norm_gain: bfloat16 [4, 768], P('section'), may hold values from 0.5 to 1.5
- norm_shift: bfloat16 [4, 768], P('section'), may hold values from -1.796875 to 1.796875
- logit_grad: bfloat16 [2, 8, 40, 14592], P(None, 'dp', None, 'section'), may hold values from -0.5 to 0.5
Outputs:
- logits: float32 [2, 8, 40, 14592], P(None, 'dp', None, 'section')
- table_grad: float32 [14592, 768], P(('section', 'dp'))
- pos_grad: float32 [128, 768], P('dp')
- w_in_grad: float32 [4, 768, 3072], P('section', 'dp')
- w_out_grad: float32 [4, 3072, 768], P('section', 'dp')
- b_in_grad: float32 [4, 3072], P('section', 'dp')
- b_out_grad: float32 [4, 768], P('section', 'dp')
- gain_grad: float32 [4, 768], P('section', 'dp')
- shift_grad: float32 [4, 768], P('section', 'dp')
The draws below stay inside these ranges and needn't reach their ends.
Inputs may be any that keep to these rules, and one draw needn't show every extreme that they name: `masked_rows`: the 40 positions of one row are different from one another. `segment_ids`: document numbers never fall along a row.
All inputs are finite; a program needn't handle non-finite values.
Results may differ from the reference program's by a relative error of at most 0.025.
Values may be sent and summed in bfloat16 or wider, within the bound.
A program may use at most 256 MiB of HBM per device.

```python
import math
import jax
import jax.numpy as jnp
import numpy as np
from jax import lax

D = 768
HEADS = 12
FF = 3072
V = 14592
LEN = 128
MB = 2
MASKS = 40
DOCS = 4
ROWS = 8
N_SECTION = 4


def draw_masked_rows(key, part):
    key = jax.random.fold_in(key, 3)
    row_keys = jax.random.split(key, MB * ROWS)
    orders = jax.vmap(lambda row_key: jax.random.permutation(row_key, LEN))(row_keys)
    return orders[:, :MASKS].reshape(MB, ROWS, MASKS).astype(jnp.int32)


def draw_w_in(key, part):
    key = jax.random.fold_in(key, 5)
    base = jnp.clip(jax.random.normal(key, (N_SECTION, D, FF), jnp.float32), -6.0, 6.0)
    column = jnp.arange(FF)
    section_index = jnp.arange(N_SECTION)
    boost = jnp.where((section_index[:, None] % 2 == 0) & (column[None, :] >= 3 * D), 5.0, 1.0)
    weights = base * boost[:, None, :] * D ** (-0.5)
    return weights.astype(jnp.bfloat16)


def set_ends(entries, stream_key, smallest, largest):
    index_at = [jax.random.randint(jax.random.fold_in(stream_key, axis), (), 0, length) for axis, length in enumerate(entries.shape)]
    widest = entries.shape.index(max(entries.shape))
    next_to = index_at[:widest] + [(index_at[widest] + 1) % entries.shape[widest]] + index_at[widest + 1:]
    return entries.at[tuple(index_at)].set(smallest).at[tuple(next_to)].set(largest)


def block_scale(own_key, shape, cuts, least, top_value):
    def one(axis_at, blocks):
        steps = jax.random.uniform(jax.random.fold_in(jax.random.fold_in(own_key, 6), axis_at), (blocks,), jnp.float32, least / len(cuts), top_value / len(cuts))
        return jnp.repeat(jnp.exp(steps), shape[axis_at] // blocks).reshape((-1,) + (1,) * (len(shape) - axis_at - 1))

    factor_of = one(*cuts[0])
    for cut in cuts[1:]:
        factor_of = factor_of * one(*cut)
    return factor_of


def rank_table(count, skew):
    weights = [(1 << 20) // math.isqrt(rank ** skew) + 1 for rank in range(1, count + 1)]
    scale = 1 + sum(weights) // (1 << 30)
    return np.cumsum(np.array([max(1, weight // scale) for weight in weights]))


def ranked(rng, extent, amount, skew):
    table = rank_table(amount, skew)
    lot = jax.random.randint(jax.random.fold_in(rng, 1), extent, 0, int(table[amount - 1]))
    rank = jnp.searchsorted(jnp.asarray(table, jnp.int32), lot, side="right")
    return jax.random.permutation(jax.random.fold_in(rng, 2), amount)[rank].astype(jnp.int32)


def length_profile(number_of, total, bound, skew):
    loads = [(1 << 20) // math.isqrt(rank ** skew) + 1 for rank in range(2, number_of + 1)]
    rest, holding = total - bound - (number_of - 1), [1] * (number_of - 1)
    while rest > 0:
        movable = [i for i in range(number_of - 1) if holding[i] < bound]
        mass, left = sum([loads[i] for i in movable]), rest
        for i in movable:
            addition = min(bound - holding[i], max(1, left * loads[i] // mass), rest)
            holding[i] = holding[i] + addition
            rest = rest - addition
    return np.array([bound] + holding)


def uneven(rng, count, total, limit, lean):
    if count == 2:
        one = jax.random.randint(rng, (), max(1, total - limit), min(limit, total - 1) + 1)
        return jnp.stack([one, total - one])
    lengths = jnp.asarray(length_profile(count, total, limit, lean), jnp.int32)
    couples = (count - 1) // 2
    giver, receiver = lengths[1:1 + 2 * couples:2], lengths[2:2 + 2 * couples:2]
    margin = jnp.minimum(giver - 1, limit - receiver)
    moved = jax.random.randint(jax.random.fold_in(rng, 1), (couples,), 0, 1 << 20) % (margin + 1)
    lengths = lengths.at[1:1 + 2 * couples:2].set(giver - moved).at[2:2 + 2 * couples:2].set(receiver + moved)
    return lengths[jax.random.permutation(jax.random.fold_in(rng, 2), count)]


def gaussian(own_key, dims, scale, bound, cuts=(), dtype=jnp.bfloat16):
    array = scale * jax.random.normal(own_key, dims, jnp.float32)
    if cuts:
        array = array * block_scale(own_key, dims, cuts, -0.22, 0.18)
    return jnp.clip(array, -bound, bound).astype(dtype)


def setup_inputs(seed: int = 0) -> dict:
    keys = jax.random.split(jax.random.key(seed), 13)
    return {
        "token_ids": set_ends(ranked(keys[0], (MB, ROWS, LEN), V, 2), jax.random.fold_in(keys[0], 3), 0, V - 1).astype(jnp.int32),
        "segment_ids": jax.vmap(lambda own: jnp.searchsorted(jnp.cumsum(uneven(own, DOCS, LEN, LEN // 2, 0)), jnp.arange(LEN), side="right"))(jax.random.split(keys[1], MB * ROWS)).reshape((MB, ROWS, LEN)).astype(jnp.int32),
        "masked_rows": draw_masked_rows(jax.random.fold_in(keys[12], 71), 0),
        "embedding": gaussian(keys[3], (V, D), 0.1, 0.59765625, ((0, 4),)),
        "pos_table": gaussian(keys[4], (LEN, D), 1.0, 6.0),
        "w_in": draw_w_in(jax.random.fold_in(keys[12], 71), 0),
        "w_out": gaussian(keys[6], (N_SECTION, FF, D), FF ** -0.5, 0.109375, ((0, 4),)),
        "b_in": gaussian(keys[7], (N_SECTION, FF), 0.3, 1.796875, ((0, 4),)),
        "b_out": gaussian(keys[8], (N_SECTION, D), 0.3, 1.796875, ((0, 4),)),
        "norm_gain": jnp.clip(1.0 + 0.1 * jax.random.normal(keys[9], (N_SECTION, D), jnp.float32), 0.5, 1.5).astype(jnp.bfloat16),
        "norm_shift": gaussian(keys[10], (N_SECTION, D), 0.3, 1.796875, ((0, 4),)),
        "logit_grad": gaussian(keys[11], (MB, ROWS, MASKS, V), 0.08, 0.5, ((1, 8), (3, 4))),
    }


EPSILON = 1e-12
FINE = lax.Precision.HIGHEST

@jax.custom_vjp
def low(v):
    return lax.optimization_barrier(v.astype(jnp.bfloat16)).astype(jnp.float32)

@jax.custom_vjp
def low_back(v):
    return v

def low_keep(v):
    return (low(v), None)

def low_pass(kept, grad):
    return (grad,)

def back_keep(v):
    return (v, None)

def back_low(kept, grad):
    return (low(grad),)
low.defvjp(low_keep, low_pass)
low_back.defvjp(back_keep, back_low)

def product(left, right):
    return jnp.dot(left, right, precision=FINE)

def layer_norm(resid, gain_row, shift_row):
    centre = lax.optimization_barrier(jnp.mean(resid, -1, keepdims=True))
    centred = resid - centre
    variance = lax.optimization_barrier(jnp.mean(centred * centred, -1, keepdims=True))
    return centred * lax.rsqrt(variance + EPSILON) * gain_row + shift_row

def to_heads(values):
    return values.reshape(values.shape[0], HEADS, values.shape[1] // HEADS)

def attention_block(inputs, segment, weights, bias_first, bias_second, gain_row, shift_row):
    width = inputs.shape[-1]
    factor = (width // HEADS) ** (-0.5)
    query = low_back(low(product(inputs, weights[:, :width]) + bias_first[:width]))
    keyed = low_back(low(product(inputs, weights[:, width:2 * width])))
    value = low_back(low(product(inputs, weights[:, 2 * width:3 * width]) + bias_first[2 * width:3 * width]))
    scores = jnp.einsum('qhd,khd->hqk', to_heads(query), to_heads(keyed), precision=FINE) * factor
    scores = low_back(scores)
    allowed = segment[:, None] == segment[None, :]
    scores = jnp.where(allowed[None], scores, -1000000000.0)
    row_peak = lax.optimization_barrier(jnp.max(scores, -1, keepdims=True))
    exponent = jnp.exp(scores - row_peak)
    chance = low(exponent / lax.optimization_barrier(jnp.sum(exponent, -1, keepdims=True)))
    context = jnp.einsum('hqk,khd->qhd', chance, to_heads(value), precision=FINE).reshape(-1, width)
    context = low_back(low(context))
    branch = low_back(product(context, weights[:, 3 * width:]) + bias_second)
    return layer_norm(inputs + branch, gain_row, shift_row)

def feed_block(inputs, w_first, w_second, bias_first, bias_second, gain_row, shift_row):
    hidden = low_back(product(inputs, w_first) + bias_first)
    active = low(jax.nn.gelu(hidden, approximate=False))
    branch = low_back(product(active, w_second) + bias_second)
    return layer_norm(inputs + branch, gain_row, shift_row)

def row_forward(params, tokens, segment, picks):
    table, positions, w_in, w_out, b_in, b_out, norm_gain, norm_shift = params
    state = low_back(low(jnp.take(table, tokens, axis=0) + positions))
    for section_index in range(N_SECTION):
        if section_index % 2 == 0:
            state = attention_block(state, segment, w_in[section_index], b_in[section_index], b_out[section_index], norm_gain[section_index], norm_shift[section_index])
        else:
            state = feed_block(state, w_in[section_index], w_out[section_index], b_in[section_index], b_out[section_index], norm_gain[section_index], norm_shift[section_index])
        state = low(state)
        if section_index + 1 < N_SECTION:
            state = low_back(state)
    chosen = jnp.take(state, picks, axis=0)
    return product(chosen, table.T)

def reference(token_ids, segment_ids, masked_rows, embedding, pos_table, w_in, w_out, b_in, b_out, norm_gain, norm_shift, logit_grad):
    params = tuple((item.astype(jnp.float32) for item in (embedding, pos_table, w_in, w_out, b_in, b_out, norm_gain, norm_shift)))
    tokens = token_ids.reshape(-1, LEN)
    segments = segment_ids.reshape(-1, LEN)
    picks = masked_rows.reshape(-1, MASKS)

    def forward(weights):

        def one_row(row_data):
            return row_forward(weights, row_data[0], row_data[1], row_data[2])
        return lax.map(jax.checkpoint(one_row), (tokens, segments, picks))
    flat_logits, pullback = jax.vjp(forward, params)
    cotangent = logit_grad.astype(jnp.float32).reshape(flat_logits.shape)
    gradients, = pullback(cotangent)
    table_grad, pos_grad, w_in_grad, w_out_grad, b_in_grad, b_out_grad, gain_grad, shift_grad = gradients
    logits = flat_logits.reshape(MB, ROWS, MASKS, V)
    return (logits, table_grad, pos_grad, w_in_grad, w_out_grad, b_in_grad, b_out_grad, gain_grad, shift_grad)
```

```python
import functools
import types

import jax
import jax.numpy as jnp
from jax import lax
from jax.experimental import pallas as pl
from jax.experimental.pallas import tpu as pltpu
from jax.sharding import PartitionSpec as P

HEADS = 12


EPSILON = 1e-12


def for_sending(array):
    return jax.tree.map(lambda a: a.astype(jnp.bfloat16) if a.dtype == jnp.float32 else a, array)


def passed_along(block, axis, distance):
    devices = range(lax.axis_size(axis))
    route = [(i - distance, i) for i in devices if i - distance in devices]
    return lax.ppermute(block, axis, route)


def broadcast(value, axis, source):
    kept = jnp.where(lax.axis_index(axis) == source, value, 0).astype(value.dtype)
    return lax.psum(kept, axis)


def norm_forward(resid, gain_row, shift_row):
    centre = jnp.mean(resid, -1, keepdims=True)
    centred = resid - centre
    inverse = lax.rsqrt(jnp.mean(centred * centred, -1, keepdims=True) + EPSILON)
    normed = centred * inverse
    return (normed * gain_row + shift_row, normed, inverse)


def norm_backward(upstream, normed, inverse, gain_row):
    gain_part = jnp.sum(upstream * normed, 0)
    shift_part = jnp.sum(upstream, 0)
    scaled = upstream * gain_row
    first_mean = jnp.mean(scaled, -1, keepdims=True)
    second_mean = jnp.mean(scaled * normed, -1, keepdims=True)
    return (inverse * (scaled - first_mean - normed * second_mean), gain_part, shift_part)


def to_heads(values):
    return values.reshape(values.shape[0], HEADS, values.shape[1] // HEADS)


def row_scores(query, keyed, segment):
    factor = (query.shape[1] // HEADS) ** (-0.5)
    scores = (
        jnp.einsum(
            "qhd,khd->hqk", to_heads(query), to_heads(keyed), preferred_element_type=jnp.float32
        )
        * factor
    )
    allowed = segment[:, None] == segment[None, :]
    return jnp.where(allowed[None], scores, -1000000000.0)


def attend_row(packed, segment):
    width = packed.shape[1] // 3
    scores = row_scores(packed[:, :width], packed[:, width : 2 * width], segment)
    row_peak = jnp.max(scores, -1, keepdims=True)
    exponent = jnp.exp(scores - row_peak)
    row_total = jnp.sum(exponent, -1, keepdims=True)
    chance = (exponent / row_total).astype(jnp.bfloat16)
    context = jnp.einsum(
        "hqk,khd->qhd", chance, to_heads(packed[:, 2 * width :]), preferred_element_type=jnp.float32
    )
    summary = (row_peak + jnp.log(row_total))[..., 0]
    return (context.reshape(packed.shape[0], width).astype(jnp.bfloat16), summary)


def attend_back(packed, segment, summary, upstream):
    length = packed.shape[0]
    width = packed.shape[1] // 3
    factor = (width // HEADS) ** (-0.5)
    scores = row_scores(packed[:, :width], packed[:, width : 2 * width], segment)
    chance = jnp.exp(scores - summary[..., None])
    grad_heads = to_heads(upstream)
    grad_chance = jnp.einsum(
        "qhd,khd->hqk",
        grad_heads,
        to_heads(packed[:, 2 * width :]),
        preferred_element_type=jnp.float32,
    )
    grad_value = jnp.einsum(
        "hqk,qhd->khd", chance.astype(jnp.bfloat16), grad_heads, preferred_element_type=jnp.float32
    )
    grad_score = chance * (grad_chance - jnp.sum(chance * grad_chance, -1, keepdims=True))
    grad_score = grad_score.astype(jnp.bfloat16)
    grad_query = (
        jnp.einsum(
            "hqk,khd->qhd",
            grad_score,
            to_heads(packed[:, width : 2 * width]),
            preferred_element_type=jnp.float32,
        )
        * factor
    )
    grad_key = (
        jnp.einsum(
            "hqk,qhd->khd",
            grad_score,
            to_heads(packed[:, :width]),
            preferred_element_type=jnp.float32,
        )
        * factor
    )
    joined = jnp.concatenate(
        [
            grad_query.reshape(length, width),
            grad_key.reshape(length, width),
            grad_value.reshape(length, width),
        ],
        1,
    )
    return joined.astype(jnp.bfloat16)


def attention_forward(inputs, segment, params):
    w_first, w_second, bias_first, bias_second, gain_row, shift_row = params
    rows_here, length, width = inputs.shape
    flat = inputs.reshape(rows_here * length, width)
    offset = jnp.concatenate(
        [bias_first[:width], jnp.zeros((width,), jnp.float32), bias_first[2 * width : 3 * width]]
    )
    packed = jnp.dot(flat, w_first[:, : 3 * width], preferred_element_type=jnp.float32) + offset
    packed = packed.astype(jnp.bfloat16).reshape(rows_here, length, 3 * width)
    context, summary = lax.map(lambda item: attend_row(item[0], item[1]), (packed, segment))
    branch = (
        jnp.dot(
            context.reshape(-1, width), w_first[:, 3 * width :], preferred_element_type=jnp.float32
        )
        + bias_second
    )
    result, normed, inverse = norm_forward(flat.astype(jnp.float32) + branch, gain_row, shift_row)
    return (result.reshape(rows_here, length, width), (packed, context, summary, normed, inverse))


def attention_backward(inputs, segment, upstream, params, totals):
    w_first, w_second, bias_first, bias_second, gain_row, shift_row = params
    rows_here, length, width = inputs.shape
    result, saved = attention_forward(inputs, segment, params)
    packed, context, summary, normed, inverse = saved
    flat = inputs.reshape(-1, width)
    grad_resid, gain_part, shift_part = norm_backward(
        upstream.reshape(-1, width), normed, inverse, gain_row
    )
    grad_branch = grad_resid.astype(jnp.bfloat16)
    grad_out_proj = jnp.einsum(
        "nd,ne->de", context.reshape(-1, width), grad_branch, preferred_element_type=jnp.float32
    )
    bias_second_part = jnp.sum(grad_branch.astype(jnp.float32), 0)
    grad_context = jnp.einsum(
        "ne,de->nd", grad_branch, w_first[:, 3 * width :], preferred_element_type=jnp.float32
    )
    grad_context = grad_context.astype(jnp.bfloat16).reshape(rows_here, length, width)
    grad_packed = lax.map(
        lambda item: attend_back(item[0], item[1], item[2], item[3]),
        (packed, segment, summary, grad_context),
    )
    flat_packed = grad_packed.reshape(-1, 3 * width)
    grad_proj = jnp.einsum("nd,nc->dc", flat, flat_packed, preferred_element_type=jnp.float32)
    bias_sums = jnp.sum(flat_packed.astype(jnp.float32), 0)
    grad_input = grad_resid + jnp.einsum(
        "nc,dc->nd", flat_packed, w_first[:, : 3 * width], preferred_element_type=jnp.float32
    )
    first_total, second_total, bias_first_total, bias_second_total, gain_total, shift_total = totals
    first_total = (
        first_total.at[:, : 3 * width].add(grad_proj).at[:, 3 * width :].add(grad_out_proj)
    )
    bias_first_total = (
        bias_first_total.at[:width]
        .add(bias_sums[:width])
        .at[2 * width : 3 * width]
        .add(bias_sums[2 * width :])
    )
    updated = (
        first_total,
        second_total,
        bias_first_total,
        bias_second_total + bias_second_part,
        gain_total + gain_part,
        shift_total + shift_part,
    )
    return (grad_input.reshape(rows_here, length, width).astype(jnp.bfloat16), updated)


def feed_forward(inputs, params):
    w_first, w_second, bias_first, bias_second, gain_row, shift_row = params
    rows_here, length, width = inputs.shape
    flat = inputs.reshape(-1, width)
    hidden = jnp.dot(flat, w_first, preferred_element_type=jnp.float32) + bias_first
    active = jax.nn.gelu(hidden, approximate=False).astype(jnp.bfloat16)
    branch = jnp.dot(active, w_second, preferred_element_type=jnp.float32) + bias_second
    result, normed, inverse = norm_forward(flat.astype(jnp.float32) + branch, gain_row, shift_row)
    return (result.reshape(rows_here, length, width), (hidden, active, normed, inverse))


def feed_backward(inputs, upstream, params, totals):
    w_first, w_second, bias_first, bias_second, gain_row, shift_row = params
    rows_here, length, width = inputs.shape
    result, saved = feed_forward(inputs, params)
    hidden, active, normed, inverse = saved
    flat = inputs.reshape(-1, width)
    grad_resid, gain_part, shift_part = norm_backward(
        upstream.reshape(-1, width), normed, inverse, gain_row
    )
    grad_branch = grad_resid.astype(jnp.bfloat16)
    grad_second = jnp.einsum("nf,nd->fd", active, grad_branch, preferred_element_type=jnp.float32)
    bias_second_part = jnp.sum(grad_branch.astype(jnp.float32), 0)
    grad_active = jnp.einsum("nd,fd->nf", grad_branch, w_second, preferred_element_type=jnp.float32)
    through = jax.vjp(lambda inner: jax.nn.gelu(inner, approximate=False), hidden)[1](grad_active)[
        0
    ]
    grad_hidden = through.astype(jnp.bfloat16)
    grad_first = jnp.einsum("nd,nf->df", flat, grad_hidden, preferred_element_type=jnp.float32)
    bias_first_part = jnp.sum(grad_hidden.astype(jnp.float32), 0)
    grad_input = grad_resid + jnp.einsum(
        "nf,df->nd", grad_hidden, w_first, preferred_element_type=jnp.float32
    )
    terms = (grad_first, grad_second, bias_first_part, bias_second_part, gain_part, shift_part)
    updated = tuple((total + term for total, term in zip(totals, terms)))
    return (grad_input.reshape(rows_here, length, width).astype(jnp.bfloat16), updated)


def local(
    token_ids,
    segment_ids,
    masked_rows,
    embedding,
    pos_table,
    w_in,
    w_out,
    b_in,
    b_out,
    norm_gain,
    norm_shift,
    logit_grad,
):
    sections = lax.axis_size("section")
    section_index = lax.axis_index("section")
    quarter, width = embedding.shape
    batches, rows_here, length = token_ids.shape
    params = (
        w_in[0],
        w_out[0],
        b_in[0].astype(jnp.float32),
        b_out[0].astype(jnp.float32),
        norm_gain[0].astype(jnp.float32),
        norm_shift[0].astype(jnp.float32),
    )
    local_ids = token_ids - section_index * quarter
    inside = (local_ids >= 0) & (local_ids < quarter)
    picked = jnp.take(embedding, jnp.clip(local_ids, 0, quarter - 1), axis=0)
    partial_rows = jnp.where(inside[..., None], picked.astype(jnp.float32), 0.0)
    looked = lax.psum(partial_rows.astype(jnp.bfloat16), "section").astype(jnp.float32)
    entry = (looked + pos_table.astype(jnp.float32)).astype(jnp.bfloat16)

    def spare_forward(inputs, segment):
        return jnp.zeros(inputs.shape, jnp.bfloat16)

    def attend_forward(inputs, segment):
        return attention_forward(inputs, segment, params)[0].astype(jnp.bfloat16)

    def feed_only(inputs, segment):
        return feed_forward(inputs, params)[0].astype(jnp.bfloat16)

    def spare_backward(inputs, segment, upstream, totals):
        return (jnp.zeros(inputs.shape, jnp.bfloat16), totals)

    def attend_backward(inputs, segment, upstream, totals):
        return attention_backward(inputs, segment, upstream, params, totals)

    def feed_back_only(inputs, segment, upstream, totals):
        return feed_backward(inputs, upstream, params, totals)

    ticks = batches + sections - 1
    kept = jnp.zeros_like(entry)
    outputs = jnp.zeros_like(entry)
    incoming = jnp.zeros_like(entry[0])
    for moment in range(ticks):
        micro_index = moment - section_index
        is_live = (micro_index >= 0) & (micro_index < batches)
        micro_slot = jnp.clip(micro_index, 0, batches - 1)
        current = jnp.where(section_index == 0, entry[micro_slot], incoming)
        kept = kept.at[micro_slot].set(jnp.where(is_live, current, kept[micro_slot]))
        branch_index = jnp.where(is_live, 1 + section_index % 2, 0)
        result = lax.switch(
            branch_index,
            [spare_forward, attend_forward, feed_only],
            current,
            segment_ids[micro_slot],
        )
        outputs = outputs.at[micro_slot].set(jnp.where(is_live, result, outputs[micro_slot]))
        if moment + 1 < ticks:
            incoming = jax.tree.map(
                lambda part, own: part.astype(own.dtype),
                passed_along(for_sending(result), "section", 1),
                result,
            )
    final_rows = jnp.take_along_axis(outputs, masked_rows[..., None], axis=2)
    head_rows = broadcast(final_rows, "section", sections - 1)
    logits = jnp.einsum("mrkd,vd->mrkv", head_rows, embedding, preferred_element_type=jnp.float32)
    partial_grad = jnp.einsum(
        "mrkv,vd->mrkd", logit_grad, embedding, preferred_element_type=jnp.float32
    )
    grad_rows = lax.psum(partial_grad.astype(jnp.bfloat16), "section").astype(jnp.float32)
    table_head = jnp.einsum(
        "mrkv,mrkd->vd", logit_grad, head_rows, preferred_element_type=jnp.float32
    )
    places = (masked_rows[..., None] == jnp.arange(length)[None, None, None, :]).astype(jnp.float32)
    top_grad = jnp.einsum("mrkl,mrkd->mrld", places, grad_rows, precision=lax.Precision.HIGHEST)
    gradients = (
        jnp.zeros(w_in.shape[1:], jnp.float32),
        jnp.zeros(w_out.shape[1:], jnp.float32),
        jnp.zeros(b_in.shape[1:], jnp.float32),
        jnp.zeros((width,), jnp.float32),
        jnp.zeros((width,), jnp.float32),
        jnp.zeros((width,), jnp.float32),
    )
    grad_entry = jnp.zeros_like(entry)
    back_in = jnp.zeros_like(entry[0])
    for moment in range(ticks):
        micro_index = moment - (sections - 1 - section_index)
        is_live = (micro_index >= 0) & (micro_index < batches)
        micro_slot = jnp.clip(micro_index, 0, batches - 1)
        upstream = jnp.where(
            section_index == sections - 1, top_grad[micro_slot], back_in.astype(jnp.float32)
        )
        branch_index = jnp.where(is_live, 1 + section_index % 2, 0)
        grad_input, gradients = lax.switch(
            branch_index,
            [spare_backward, attend_backward, feed_back_only],
            kept[micro_slot],
            segment_ids[micro_slot],
            upstream,
            gradients,
        )
        grad_entry = grad_entry.at[micro_slot].set(
            jnp.where(is_live, grad_input, grad_entry[micro_slot])
        )
        if moment + 1 < ticks:
            back_in = jax.tree.map(
                lambda part, own: part.astype(own.dtype),
                passed_along(for_sending(grad_input), "section", -1),
                grad_input,
            )
    input_grad = broadcast(grad_entry, "section", 0)
    input_wide = input_grad.astype(jnp.float32)
    pos_grad = jnp.sum(input_wide, (0, 1))
    targets = jnp.where(inside, local_ids, quarter).reshape(-1)
    table_input = jax.ops.segment_sum(
        input_wide.reshape(-1, width), targets, num_segments=quarter + 1
    )[:quarter]
    w_in_part, w_out_part, b_in_part, b_out_part, gain_part, shift_part = gradients
    reduced = (
        lax.psum_scatter(w_in_part, "dp", scatter_dimension=0, tiled=True),
        lax.psum_scatter(w_out_part, "dp", scatter_dimension=0, tiled=True),
        lax.psum_scatter(b_in_part, "dp", scatter_dimension=0, tiled=True),
        lax.psum_scatter(b_out_part, "dp", scatter_dimension=0, tiled=True),
        lax.psum_scatter(gain_part, "dp", scatter_dimension=0, tiled=True),
        lax.psum_scatter(shift_part, "dp", scatter_dimension=0, tiled=True),
        lax.psum_scatter(pos_grad, "dp", scatter_dimension=0, tiled=True),
        lax.psum_scatter(table_input + table_head, "dp", scatter_dimension=0, tiled=True),
    )
    table_grad = reduced[7]
    return (
        logits,
        table_grad,
        reduced[6],
        reduced[0][None],
        reduced[1][None],
        reduced[2][None],
        reduced[3][None],
        reduced[4][None],
        reduced[5][None],
    )


SENDS = 140
RECVS = 150
VMEM_LIMIT = 64 * 2**20
BF = jnp.bfloat16
F32 = jnp.float32
MESH = pl.DeviceIdType.MESH


def mm(a, b):
    return jnp.dot(a, b, preferred_element_type=F32)


def mm_nt(a, b):
    return lax.dot_general(a, b, (((1,), (1,)), ((), ())), preferred_element_type=F32)


def mm_tn(a, b):
    return lax.dot_general(a, b, (((0,), (0,)), ((), ())), preferred_element_type=F32)


def iota(shape, dim):
    return lax.broadcasted_iota(jnp.int32, shape, dim)


def column(row):
    return jnp.broadcast_to(row.astype(F32), (128, 128)).T


class Plan:
    def __init__(self, n_dp, length, width, ff, quarter, masks):
        self.n_dp, self.length, self.width, self.ff = n_dp, length, width, ff
        self.quarter, self.masks = quarter, masks
        self.nz = n_dp // 2
        self.share = quarter // n_dp
        self.in_rows = width // n_dp
        self.out_rows = ff // n_dp
        self.mask_pad = -(-masks // 16) * 16
        self.share_pad = -(-self.share // 128) * 128
        self.share_rows = -(-self.share // 16) * 16
        self.chunks = []
        at = 0
        while at < quarter:
            size = min(1024, quarter - at)
            self.chunks.append((at, size))
            at += size


class Counter:
    def __init__(self):
        self.n = 0

    def take(self, k=1):
        first = self.n
        self.n += k
        return first


def scratch_list(p):
    w, ff, ln = p.width, p.ff, p.length
    mp = p.mask_pad
    return dict(
        emb=((p.quarter, w), BF),
        wa=((w, ff), BF),
        w1=((w, ff), BF),
        w2=((ff, w), BF),
        par_a=((8, ff), F32),
        par_f=((8, ff), F32),
        acc=((2 * ln, w), F32),
        psend=((ln, w), BF),
        psum=((ln, w), BF),
        prow=((2, ln, w), BF),
        lgp=((2 * mp, p.quarter), BF),
        lgs=((p.n_dp, 2, mp, p.share_pad), BF),
        lgr=((2, p.n_dp, mp, p.share_pad), BF),
        g=((2 * mp, w), F32),
        grow=((2, p.masks, w), F32),
        gwide=((ln, w), F32),
        mrow=((8, ln), jnp.int32),
        ids_own=((8, ln), jnp.int32),
        ids_all=((p.n_dp, 8, ln), jnp.int32),
        x_a=((ln, w), BF),
        x_f=((ln, w), BF),
        y_f=((ln, w), BF),
        pk=((ln, 3 * w), BF),
        ctx=((ln, w), BF),
        probs=((w // 128, ln, 256), F32),
        n_a=((ln, w), F32),
        n_f=((ln, w), F32),
        inv_a=((ln, 1), F32),
        inv_f=((ln, 1), F32),
        hid=((ln, ff), F32),
        phi=((ln, ff), F32),
        act=((ln, ff), BF),
        xt_a=((p.nz, 2, p.in_rows, ln), BF),
        ct_a=((p.nz, 2, p.in_rows, ln), BF),
        xt_f=((p.nz, 2, p.in_rows, ln), BF),
        at_f=((p.nz, 2, p.out_rows, ln), BF),
        dyin=((ln, w), BF),
        dyf=((ln, w), F32),
        dres=((ln, w), F32),
        dbr_a=((ln, w), BF),
        dbr_f=((ln, w), BF),
        dh=((ln, ff), BF),
        dpk=((ln, 3 * w), BF),
        dctx=((ln, w), BF),
        dx=((ln, w), BF),
        bsum=((1, ff), F32),
        sm_a=((8, w), F32),
        sm_f=((8, w), F32),
        b_act=((p.nz, p.out_rows, 4 * ln), BF),
        b_x=((p.nz, p.in_rows, 4 * ln), BF),
        b_dbr=((4 * ln, w), BF),
        b_dh=((4 * ln, ff), BF),
        b_sm=((4, 8, w), F32),
        sm_tot=((8, w), F32),
        sm_all=((8, w), F32),
        r_sm=((p.nz, 8, w), F32),
        r_in=((p.nz, p.in_rows, ff), BF),
        r_out=((p.nz, p.out_rows, w), BF),
        ch_all=((2, p.n_dp, mp, w), BF),
        de_all=((2, p.n_dp, ln, w), BF),
    )


def fused(p, names, *refs):
    (tok, seg, picks, lg, pos, b_in, b_out, gain, shift, emb_h, w_in_h, w_out_h) = refs[:12]
    (o_log, o_tab, o_pos, o_win, o_wout, o_bin, o_bout, o_gain, o_shift) = refs[12:21]
    r = types.SimpleNamespace(**dict(zip(names, refs[21:])))
    ss, rs, ls = refs[21 + len(names) :]
    w, ff, ln, mp, nz, n_dp = p.width, p.ff, p.length, p.mask_pad, p.nz, p.n_dp
    heads = w // 64
    pairs = heads // 2

    s = lax.axis_index("section")
    dp = lax.axis_index("dp")
    x, c = s // 2, lax.rem(s, 2)
    z, y = dp // 2, lax.rem(dp, 2)
    core = s + 1 - 2 * c
    across = s + 2 - 4 * x
    ydp = dp + 1 - 2 * y
    other = 1 - c
    at_x0, at_x1 = x == 0, x == 1
    is_att, is_ff = c == 0, c == 1
    sends, recvs = Counter(), Counter()
    pending = []

    def send(cond, src, dst, dev, recv):
        slot = sends.take()

        def make():
            return pltpu.make_async_remote_copy(
                src_ref=src,
                dst_ref=dst,
                send_sem=ss.at[slot],
                recv_sem=rs.at[recv],
                device_id=dev,
                device_id_type=MESH,
            )

        if cond is None:
            make().start()
        else:

            @pl.when(cond)
            def _():
                make().start()

        pending.append((cond, make))

    def arrived(dst, recv):
        pltpu.make_async_remote_copy(
            src_ref=dst,
            dst_ref=dst,
            send_sem=ss.at[0],
            recv_sem=rs.at[recv],
            device_id=(core, dp),
            device_id_type=MESH,
        ).wait_recv()

    for i, (at, size) in enumerate(p.chunks):
        pltpu.make_async_copy(emb_h.at[pl.ds(at, size)], r.emb.at[pl.ds(at, size)], ls.at[i]).start()
    l_w = len(p.chunks)

    @pl.when(is_att)
    def _():
        pltpu.make_async_copy(w_in_h.at[0], r.wa, ls.at[l_w]).start()

    @pl.when(is_ff)
    def _():
        pltpu.make_async_copy(w_in_h.at[0], r.w1, ls.at[l_w]).start()
        pltpu.make_async_copy(w_out_h.at[0], r.w2, ls.at[l_w + 1]).start()

    def fill(par):
        par[0:1, :] = b_in[...].astype(F32)
        par[1:2, 0:w] = b_out[...].astype(F32)
        par[2:3, 0:w] = gain[...].astype(F32)
        par[3:4, 0:w] = shift[...].astype(F32)

    pl.when(is_att)(lambda: fill(r.par_a))
    pl.when(is_ff)(lambda: fill(r.par_f))

    barrier = pltpu.get_barrier_semaphore()
    peers = [(s, lax.rem(dp + k, n_dp)) for k in range(1, n_dp)]
    peers += [(core, dp), (across, dp), (core, ydp)]
    for peer in peers:
        pl.semaphore_signal(barrier, inc=1, device_id=peer, device_id_type=MESH)
    pl.semaphore_wait(barrier, len(peers))

    k_wa, k_w1, k_w2, k_pa, k_pf = (recvs.take() for _ in range(5))

    def weights(cond_att, cond_ff):
        send(cond_att, r.par_a, r.par_a, (core, dp), k_pa)
        send(cond_att, w_in_h.at[0], r.wa, (core, dp), k_wa)
        if cond_ff is not None:
            send(cond_ff, r.par_f, r.par_f, (core, dp), k_pf)
            send(cond_ff, w_in_h.at[0], r.w1, (core, dp), k_w1)
            send(cond_ff, w_out_h.at[0], r.w2, (core, dp), k_w2)

    weights(is_att & at_x0, None)

    cols = [column(tok[m]) for m in range(2)]
    first = s * p.quarter
    for i, (at, size) in enumerate(p.chunks):
        pltpu.make_async_copy(emb_h.at[pl.ds(at, size)], r.emb.at[pl.ds(at, size)], ls.at[i]).wait()
        lane = (iota((ln, size), 1) + (first + at)).astype(F32)
        hot = []
        for m in range(2):
            wide = jnp.concatenate([cols[m]] * (-(-size // 128)), 1)[:, :size]
            hot.append(jnp.where(wide == lane, 1.0, 0.0).astype(BF))
        part = mm(jnp.concatenate(hot, 0), r.emb[at : at + size, :])
        if i == 0:
            r.acc[...] = part
        else:
            r.acc[...] += part
    k_p = recvs.take(2)
    r.psend[...] = r.acc[pl.ds(pl.multiple_of(ln * other, ln), ln), :].astype(BF)
    send(None, r.psend, r.prow.at[0], (core, dp), k_p)
    weights(is_att & at_x1, is_ff)

    r.lgp[...] = jnp.zeros(r.lgp.shape, BF)
    r.lgp[0 : p.masks] = lg[0, 0]
    r.lgp[mp : mp + p.masks] = lg[1, 0]
    arrived(r.prow.at[0], k_p)
    own_rows = r.acc[pl.ds(pl.multiple_of(ln * c, ln), ln), :]
    r.acc[0:ln, :] = own_rows + r.prow[0].astype(F32)

    r.psum[...] = r.acc[0:ln, :].astype(BF)
    send(at_x1, r.psum, r.prow.at[1], (across, dp), k_p + 1)

    for i, (at, size) in enumerate(p.chunks):
        part = mm(r.lgp[:, at : at + size], r.emb[at : at + size, :])
        if i == 0:
            r.g[...] = part
        else:
            r.g[...] += part
    k_g = recvs.take(2)
    send(None, r.g.at[pl.ds(pl.multiple_of(mp * other, mp), p.masks)], r.grow.at[0], (core, dp), k_g)

    r.lgs[...] = jnp.zeros(r.lgs.shape, BF)
    for j in range(n_dp):
        for m in range(2):
            r.lgs[j, m, :, 0 : p.share] = r.lgp[mp * m : mp * m + mp, p.share * j : p.share * (j + 1)]
    r.ids_own[...] = jnp.zeros(r.ids_own.shape, jnp.int32)
    for m in range(2):
        r.ids_own[m : m + 1, :] = tok[m]
    r.ids_all[dp] = r.ids_own[...]
    k_lg, k_id = recvs.take(n_dp), recvs.take(n_dp)
    r.lgr[:, dp] = r.lgs[dp]
    for k in range(1, n_dp):
        to = lax.rem(dp + k, n_dp)
        send(None, r.lgs.at[to], r.lgr.at[:, dp], (s, to), k_lg + dp)
        send(None, r.ids_own, r.ids_all.at[dp], (s, to), k_id + dp)

    arrived(r.grow.at[0], k_g)
    own_g = r.g[pl.ds(pl.multiple_of(mp * c, mp), p.masks), :] + r.grow[0]
    r.gwide[...] = jnp.zeros(r.gwide.shape, F32)
    r.gwide[0 : p.masks, :] = own_g
    send(at_x0, r.gwide.at[0 : p.masks], r.grow.at[1], (across, dp), k_g + 1)

    k_x = recvs.take()

    @pl.when(at_x0)
    def _():
        arrived(r.prow.at[1], k_p + 1)
        whole = r.acc[0:ln, :] + r.prow[1].astype(F32)
        r.x_a[...] = (whole + pos[...].astype(F32)).astype(BF)

    @pl.when(is_att)
    def _():
        pltpu.make_async_copy(w_in_h.at[0], r.wa, ls.at[l_w]).wait()
        arrived(r.par_f, k_pf)

    @pl.when(is_ff)
    def _():
        arrived(r.par_a, k_pa)
        arrived(r.wa, k_wa)

    @pl.when(at_x1)
    def _():
        arrived(r.x_a, k_x)

    low = jnp.where(iota((ln, 128), 1) < 64, 1.0, 0.0).astype(BF)
    high = jnp.where(iota((ln, 128), 1) < 64, 0.0, 1.0).astype(BF)

    def split(block):
        return jnp.concatenate([block * low, block * high], 0)

    def stack(block):
        return jnp.concatenate([block[:, 0:128], block[:, 128:256]], 0)

    def norm_forward(resid, par, n_ref, inv_ref):
        centred = resid - jnp.mean(resid, -1, keepdims=True)
        inverse = lax.rsqrt(jnp.mean(centred * centred, -1, keepdims=True) + EPSILON)
        normed = centred * inverse
        n_ref[...] = normed
        inv_ref[...] = inverse
        return (normed * par[2:3, 0:w] + par[3:4, 0:w]).astype(BF)

    rows_x = r.x_a[...]
    for j in range(3):
        part = mm(rows_x, r.wa[:, j * w : (j + 1) * w])
        if j != 1:
            part = part + r.par_a[0:1, j * w : (j + 1) * w]
        r.pk[:, j * w : (j + 1) * w] = part.astype(BF)
    seg_row = seg[c].astype(F32)
    seg_col = column(seg[c])
    seg_row = jnp.broadcast_to(jnp.concatenate([seg_row, seg_row], 1), (ln, 256))
    seg_col = jnp.concatenate([seg_col, seg_col], 1)
    for h in range(pairs):
        at = 128 * h
        query = r.pk[:, at : at + 128]
        keyed = split(r.pk[:, w + at : w + at + 128])
        value = split(r.pk[:, 2 * w + at : 2 * w + at + 128])
        scores = jnp.where(seg_row == seg_col, mm_nt(query, keyed) * 0.125, -1e9)
        chance = []
        for half in (scores[:, 0:128], scores[:, 128:256]):
            power = jnp.exp(half - jnp.max(half, -1, keepdims=True))
            chance.append(power / jnp.sum(power, -1, keepdims=True))
        chance = jnp.concatenate(chance, 1)
        r.probs[h] = chance
        r.ctx[:, at : at + 128] = mm(chance.astype(BF), value).astype(BF)
    resid = rows_x.astype(F32) + mm(r.ctx[...], r.wa[:, 3 * w : 4 * w]) + r.par_a[1:2, 0:w]
    r.x_f[...] = norm_forward(resid, r.par_a, r.n_a, r.inv_a)

    @pl.when(is_ff)
    def _():
        pltpu.make_async_copy(w_in_h.at[0], r.w1, ls.at[l_w]).wait()
        pltpu.make_async_copy(w_out_h.at[0], r.w2, ls.at[l_w + 1]).wait()

    @pl.when(is_att)
    def _():
        arrived(r.w1, k_w1)
        arrived(r.w2, k_w2)

    rows_x = r.x_f[...]
    total = rows_x.astype(F32) + r.par_f[1:2, 0:w]
    for j in range(ff // w):
        cut = slice(j * w, (j + 1) * w)
        hidden = mm(rows_x, r.w1[:, cut]) + r.par_f[0:1, cut]
        below = 0.5 + 0.5 * lax.erf(hidden * (0.5**0.5))
        active = (hidden * below).astype(BF)
        r.hid[:, cut] = hidden
        r.phi[:, cut] = below
        r.act[:, cut] = active
        total = total + mm(active, r.w2[cut, :])
    r.y_f[...] = norm_forward(total, r.par_f, r.n_f, r.inv_f)
    send(at_x0, r.y_f, r.x_a, (across, dp), k_x)

    def line(buf, base):
        own = buf(dp)
        send(None, own, own, (s, ydp), base + dp)
        send(z < nz - 1, own, own, (s, dp + 2), base + dp)
        send(z > 0, own, own, (s, dp - 2), base + dp)

    def line_step(buf, base, t):
        for sign in (-1, 1):
            from_z = z + sign * t
            here = (from_z >= 0) & (from_z < nz)
            from_dp = jnp.clip(from_z, 0, nz - 1) * 2 + y
            piece = buf(from_dp)
            pl.when(here)(lambda piece=piece, from_dp=from_dp: arrived(piece, base + from_dp))
            to_z = z - sign
            on = here & (to_z >= 0) & (to_z < nz)
            if t < nz - 1:
                send(on, piece, piece, (s, dp - 2 * sign), base + from_dp)
            send(here, piece, piece, (s, ydp), base + from_dp)

    def line_end(buf, base):
        for zz in range(nz):
            from_dp = 2 * zz + 1 - y
            arrived(buf(from_dp), base + from_dp)

    k_ch, k_chx, k_de, k_dex = recvs.take(n_dp), recvs.take(), recvs.take(n_dp), recvs.take()

    def ch(i):
        return r.ch_all.at[c, i]

    def de(i):
        return r.de_all.at[c, i]

    @pl.when(at_x1)
    def _():
        r.mrow[...] = jnp.full(r.mrow.shape, -1, jnp.int32)
        r.mrow[0:1, 0 : p.masks] = picks[c]
        places = jnp.where(iota((ln, ln), 0) == r.mrow[0:1, :], 1.0, 0.0).astype(BF)
        r.ch_all[c, dp] = mm_tn(places, r.y_f[...])[0:mp].astype(BF)
        arrived(r.grow.at[1], k_g + 1)
        r.gwide[0 : p.masks, :] += r.grow[1]
        coarse = r.gwide[...].astype(BF)
        fine = (r.gwide[...] - coarse.astype(F32)).astype(BF)
        r.dyf[...] = mm(places, coarse) + mm(places, fine)

    send(at_x1, ch(dp), ch(dp), (across, dp), k_ch + dp)

    def push(owner, kind, src, dst):
        home = c == owner
        slot_y = 2 + jnp.where(home, 0, 1)
        own_dst, near_dst, far_dst = dst(0), dst(1), dst(slot_y)

        @pl.when(home)
        def _():
            pltpu.make_async_copy(src(y), own_dst, rs.at[kind]).start()

        send(jnp.logical_not(home), src(y), near_dst, (core, dp), kind + 1)
        far_s = jnp.where(home, s, core)
        send(None, src(1 - y), far_dst, (far_s, ydp), kind + slot_y)

    def gathered(kind, dst):
        pltpu.make_async_copy(dst(0), dst(0), rs.at[kind]).wait()
        for slot in range(1, 4):
            arrived(dst(slot), kind + slot)

    def lanes(slot):
        return pl.ds(slot * ln if isinstance(slot, int) else pl.multiple_of(slot * ln, ln), ln)

    tiles = ff // w
    k_dh = [recvs.take(4) for _ in range(tiles)]
    k_act, k_xt, k_db, k_sm = (recvs.take(4) for _ in range(4))
    to_x = lambda slot: r.b_x.at[:, :, lanes(slot)]
    to_act = lambda slot: r.b_act.at[:, :, lanes(slot)]
    to_ctx = lambda slot: r.b_act.at[:, 0 : p.in_rows, lanes(slot)]
    to_dbr = lambda slot: r.b_dbr.at[lanes(slot), :]
    to_sm = lambda slot: r.b_sm.at[slot]

    def to_dh(j):
        return lambda slot: r.b_dh.at[lanes(slot), j * w : (j + 1) * w]

    def blocks(dst, value, rows):
        turned = value.T
        for b in range(n_dp):
            dst[b // 2, b % 2] = turned[b * rows : (b + 1) * rows]

    def prepare():
        blocks(r.xt_a, r.x_a[...], p.in_rows)
        blocks(r.ct_a, r.ctx[...], p.in_rows)
        blocks(r.xt_f, r.x_f[...], p.in_rows)
        blocks(r.at_f, r.act[...], p.out_rows)

    prepare()
    push(0, k_xt, lambda i: r.xt_a.at[:, i], to_x)
    push(0, k_act, lambda i: r.ct_a.at[:, i], to_ctx)
    push(1, k_xt, lambda i: r.xt_f.at[:, i], to_x)
    push(1, k_act, lambda i: r.at_f.at[:, i], to_act)

    @pl.when(at_x0)
    def _():
        arrived(ch(dp), k_ch + dp)

    line(ch, k_ch)
    k_dy = recvs.take()

    @pl.when(at_x0)
    def _():
        arrived(r.dyin, k_dy)
        r.dyf[...] = r.dyin[...].astype(F32)

    def norm_backward(par, n_ref, inv_ref):
        up, normed = r.dyf[...], n_ref[...]
        gain_part = jnp.sum(up * normed, 0, keepdims=True)
        shift_part = jnp.sum(up, 0, keepdims=True)
        scaled = up * par[2:3, 0:w]
        first_mean = jnp.mean(scaled, -1, keepdims=True)
        second_mean = jnp.mean(scaled * normed, -1, keepdims=True)
        return inv_ref[...] * (scaled - first_mean - normed * second_mean), gain_part, shift_part

    def small(dst, out_part, gain_part, shift_part):
        dst[...] = jnp.zeros(dst.shape, F32)
        n_b, n_w = ff // n_dp, w // n_dp
        for k in range(n_dp):
            dst[k : k + 1, 0:n_b] = r.bsum[:, k * n_b : (k + 1) * n_b]
            dst[k : k + 1, n_b : n_b + n_w] = out_part[:, k * n_w : (k + 1) * n_w]
            dst[k : k + 1, n_b + 128 : n_b + 128 + n_w] = gain_part[:, k * n_w : (k + 1) * n_w]
            dst[k : k + 1, n_b + 256 : n_b + 256 + n_w] = shift_part[:, k * n_w : (k + 1) * n_w]

    dres, gain_part, shift_part = norm_backward(r.par_f, r.n_f, r.inv_f)
    r.dres[...] = dres
    r.dbr_f[...] = dres.astype(BF)
    push(1, k_db, lambda i: r.dbr_f, to_dbr)
    branch = r.dbr_f[...]
    total = r.dres[...]
    for j in range(tiles):
        cut = slice(j * w, (j + 1) * w)
        hidden = r.hid[:, cut]
        slope = r.phi[:, cut] + hidden * (0.3989422804014327 * jnp.exp(-0.5 * hidden * hidden))
        dhidden = (mm_nt(branch, r.w2[cut, :]) * slope).astype(BF)
        r.dh[:, cut] = dhidden
        push(1, k_dh[j], lambda i, cut=cut: r.dh.at[:, cut], to_dh(j))
        r.bsum[:, cut] = jnp.sum(dhidden.astype(F32), 0, keepdims=True)
        total = total + mm_nt(dhidden, r.w1[:, cut])
    r.dyf[...] = total.astype(BF).astype(F32)
    small(r.sm_f, jnp.sum(branch.astype(F32), 0, keepdims=True), gain_part, shift_part)
    push(1, k_sm, lambda i: r.sm_f, to_sm)

    dres, gain_part, shift_part = norm_backward(r.par_a, r.n_a, r.inv_a)
    r.dres[...] = dres
    r.dbr_a[...] = dres.astype(BF)
    push(0, k_db, lambda i: r.dbr_a, to_dbr)
    branch = r.dbr_a[...]
    r.dctx[...] = mm_nt(branch, r.wa[:, 3 * w : 4 * w]).astype(BF)
    for h in range(pairs):
        at = 128 * h
        query = r.pk[:, at : at + 128]
        keyed = split(r.pk[:, w + at : w + at + 128])
        value = split(r.pk[:, 2 * w + at : 2 * w + at + 128])
        upper = r.dctx[:, at : at + 128]
        chance = r.probs[h]
        dchance = mm_nt(upper, value)
        mixed = chance * dchance
        dscores = []
        for cut in (slice(0, 128), slice(128, 256)):
            dscores.append(mixed[:, cut] - chance[:, cut] * jnp.sum(mixed[:, cut], -1, keepdims=True))
        dscores = jnp.concatenate(dscores, 1).astype(BF)
        r.dpk[:, at : at + 128] = (mm(dscores, keyed) * 0.125).astype(BF)
        r.dpk[:, w + at : w + at + 128] = (mm_tn(stack(dscores), split(query)) * 0.125).astype(BF)
        r.dpk[:, 2 * w + at : 2 * w + at + 128] = mm_tn(stack(chance.astype(BF)), split(upper)).astype(BF)
    total = r.dres[...]
    r.bsum[...] = jnp.zeros(r.bsum.shape, F32)
    for j in range(3):
        cut = slice(j * w, (j + 1) * w)
        push(0, k_dh[j], lambda i, cut=cut: r.dpk.at[:, cut], to_dh(j))
        dpart = r.dpk[:, cut]
        if j != 1:
            r.bsum[:, cut] = jnp.sum(dpart.astype(F32), 0, keepdims=True)
        total = total + mm_nt(dpart, r.wa[:, cut])
    r.dx[...] = total.astype(BF)
    send(at_x1, r.dx, r.dyin, (across, dp), k_dy)

    @pl.when(at_x0)
    def _():
        r.de_all[c, dp] = r.dx[...]

    send(at_x0, r.dx, de(dp), (across, dp), k_de + dp)
    small(r.sm_a, jnp.sum(branch.astype(F32), 0, keepdims=True), gain_part, shift_part)
    push(0, k_sm, lambda i: r.sm_a, to_sm)

    k_in = [recvs.take(nz) for _ in range(tiles)]
    k_out, k_smz = recvs.take(nz), recvs.take(nz)
    half = nz * p.in_rows

    def spread(cond, src, dst, base):
        for k in range(1, nz):
            zz = lax.rem(z + k, nz)
            send(cond, src(zz), dst, (s, 2 * zz + y), base + z)

    @pl.when(is_ff)
    def _():
        gathered(k_act, to_act)
        gathered(k_db, to_dbr)
        for zz in range(nz):
            grad = mm(r.b_act[zz], r.b_dbr[...])
            r.w2[zz * p.out_rows : (zz + 1) * p.out_rows, :] = grad.astype(BF)
        r.r_out[z] = r.w2[pl.ds(pl.multiple_of(z * p.out_rows, p.out_rows), p.out_rows), :]

    def out_part(zz):
        return r.w2.at[pl.ds(pl.multiple_of(zz * p.out_rows, p.out_rows), p.out_rows)]

    spread(is_ff, out_part, r.r_out.at[z], k_out)

    @pl.when(is_ff)
    def _():
        gathered(k_xt, to_x)

    @pl.when(is_att)
    def _():
        gathered(k_xt, to_x)
        gathered(k_act, to_ctx)
        gathered(k_db, to_dbr)

    for j in (3, 0, 1, 2):
        cut = slice(j * w, (j + 1) * w)

        def keep(grad, cut=cut):
            r.wa[0:half, cut] = grad.astype(BF)
            r.r_in[z, :, cut] = r.wa[pl.ds(pl.multiple_of(z * p.in_rows, p.in_rows), p.in_rows), cut]

        @pl.when(is_ff)
        def _():
            gathered(k_dh[j], to_dh(j))
            keep(mm(r.b_x[...].reshape(half, 4 * ln), r.b_dh[:, cut]))

        @pl.when(is_att)
        def _():
            if j == 3:
                keep(mm(r.b_act[:, 0 : p.in_rows].reshape(half, 4 * ln), r.b_dbr[...]))
            else:
                gathered(k_dh[j], to_dh(j))
                keep(mm(r.b_x[...].reshape(half, 4 * ln), r.b_dh[:, cut]))

        def in_part(zz, cut=cut):
            return r.wa.at[pl.ds(pl.multiple_of(zz * p.in_rows, p.in_rows), p.in_rows), cut]

        spread(None, in_part, r.r_in.at[z, :, cut], k_in[j])

    gathered(k_sm, to_sm)
    r.sm_tot[...] = r.b_sm[0] + r.b_sm[1] + r.b_sm[2] + r.b_sm[3]
    r.r_sm[z] = r.sm_tot[...]
    spread(None, lambda zz: r.sm_tot, r.r_sm.at[z], k_smz)

    @pl.when(at_x1)
    def _():
        arrived(de(dp), k_de + dp)

    line(de, k_de)
    for t in range(1, nz):
        line_step(ch, k_ch, t)
        line_step(de, k_de, t)
    line_end(ch, k_ch)
    send(None, r.ch_all.at[c], r.ch_all.at[c], (core, dp), k_chx)
    line_end(de, k_de)
    send(None, r.de_all.at[c], r.de_all.at[c], (core, dp), k_dex)

    arrived(r.ch_all.at[other], k_chx)
    chosen = jnp.concatenate([r.ch_all[0, dp], r.ch_all[1, dp]], 0)
    for at, size in p.chunks:
        part = mm_nt(chosen, r.emb[at : at + size, :])
        for m in range(2):
            o_log[m, 0, :, at : at + size] = part[mp * m : mp * m + p.masks]
    for k in range(1, n_dp):
        src = lax.rem(dp + k, n_dp)
        arrived(r.lgr.at[:, src], k_lg + src)
        arrived(r.ids_all.at[src], k_id + src)
    lines = 2 * n_dp * mp
    grad = mm_tn(r.lgr[...].reshape(lines, p.share_pad), r.ch_all[...].reshape(lines, w))
    o_tab[...] = grad[0 : p.share]

    arrived(r.de_all.at[other], k_dex)
    entry = iota((p.share_rows, ln), 0) + (s * p.quarter + dp * p.share)

    def scatter(i, carry):
        hot = []
        for m in range(2):
            hot.append(jnp.where(entry == r.ids_all[i, m : m + 1, :], 1.0, 0.0).astype(BF))
        rows = jnp.concatenate([r.de_all[0, i], r.de_all[1, i]], 0)
        o_tab[...] += mm(jnp.concatenate(hot, 1), rows)[0 : p.share]
        return carry

    lax.fori_loop(0, n_dp, scatter, 0)
    n_pos = ln // n_dp
    here = pl.ds(pl.multiple_of(dp * n_pos, n_pos), n_pos)
    total = jnp.zeros((n_pos, w), F32)
    for m in range(2):
        for i in range(n_dp):
            total = total + r.de_all[m, i, here, :].astype(F32)
    o_pos[...] = total

    for j in range(tiles):
        for k in range(1, nz):
            src = lax.rem(z + k, nz)
            arrived(r.r_in.at[src, :, j * w : (j + 1) * w], k_in[j] + src)
    total = r.r_in[0].astype(F32)
    for zz in range(1, nz):
        total = total + r.r_in[zz].astype(F32)
    o_win[0] = total

    @pl.when(is_ff)
    def _():
        for k in range(1, nz):
            src = lax.rem(z + k, nz)
            arrived(r.r_out.at[src], k_out + src)
        total = r.r_out[0].astype(F32)
        for zz in range(1, nz):
            total = total + r.r_out[zz].astype(F32)
        o_wout[0] = total

    @pl.when(is_att)
    def _():
        o_wout[...] = jnp.zeros(o_wout.shape, F32)

    for k in range(1, nz):
        src = lax.rem(z + k, nz)
        arrived(r.r_sm.at[src], k_smz + src)
    r.sm_all[...] = r.r_sm[0] + r.r_sm[1] + r.r_sm[2] + r.r_sm[3]
    mine = r.sm_all[pl.ds(dp, 1), :]
    n_b, n_w = ff // n_dp, w // n_dp
    o_bin[...] = mine[:, 0:n_b]
    o_bout[...] = mine[:, n_b : n_b + n_w]
    o_gain[...] = mine[:, n_b + 128 : n_b + 128 + n_w]
    o_shift[...] = mine[:, n_b + 256 : n_b + 256 + n_w]

    for cond, make in pending:
        if cond is None:
            make().wait_send()
        else:
            pl.when(cond)(lambda make=make: make().wait_send())
    assert sends.n <= SENDS and recvs.n <= RECVS, (sends.n, recvs.n)


def whole(
    n_dp,
    token_ids,
    segment_ids,
    masked_rows,
    embedding,
    pos_table,
    w_in,
    w_out,
    b_in,
    b_out,
    norm_gain,
    norm_shift,
    logit_grad,
):
    quarter, width = embedding.shape
    batches, _, length = token_ids.shape
    masks = masked_rows.shape[-1]
    ff = w_in.shape[-1]
    p = Plan(n_dp, length, width, ff, quarter, masks)
    scratch = scratch_list(p)
    shapes = [
        (batches, 1, masks, quarter),
        (p.share, width),
        (length // n_dp, width),
        (1, p.in_rows, ff),
        (1, p.out_rows, width),
        (1, ff // n_dp),
        (1, p.in_rows),
        (1, p.in_rows),
        (1, p.in_rows),
    ]
    vmem = pl.BlockSpec(memory_space=pltpu.VMEM)
    far = pl.BlockSpec(memory_space=pl.ANY)
    return pl.pallas_call(
        functools.partial(fused, p, list(scratch)),
        out_shape=[jax.ShapeDtypeStruct(shape, F32) for shape in shapes],
        in_specs=[vmem] * 9 + [far] * 3,
        out_specs=[vmem] * 9,
        scratch_shapes=[pltpu.VMEM(*one) for one in scratch.values()]
        + [
            pltpu.SemaphoreType.DMA((SENDS,)),
            pltpu.SemaphoreType.DMA((RECVS,)),
            pltpu.SemaphoreType.DMA((len(p.chunks) + 2,)),
        ],
        compiler_params=pltpu.CompilerParams(
            collective_id=0, has_side_effects=True, vmem_limit_bytes=VMEM_LIMIT
        ),
    )(
        token_ids,
        segment_ids,
        masked_rows,
        logit_grad,
        pos_table,
        b_in,
        b_out,
        norm_gain,
        norm_shift,
        embedding,
        w_in,
        w_out,
    )


def solution(mesh):
    n_section, n_dp = mesh.shape["section"], mesh.shape["dp"]

    def chosen_form(*args):
        token_ids, embedding, w_in = args[0], args[3], args[5]
        fits = (
            n_section == 4
            and n_dp == 8
            and token_ids.shape[0] == 2
            and token_ids.shape[1:] == (1, 128)
            and w_in.shape[1] % (16 * n_dp) == 0
            and w_in.shape[2] == 4 * w_in.shape[1]
            and embedding.shape[0] % (8 * n_dp) == 0
        )
        return whole(n_dp, *args) if fits else local(*args)

    placed = (
        P(None, "dp", None),
        P(None, "dp", None),
        P(None, "dp", None),
        P("section", None),
        P(),
        P("section", None, None),
        P("section", None, None),
        P("section", None),
        P("section", None),
        P("section", None),
        P("section", None),
        P(None, "dp", None, "section"),
    )
    return jax.shard_map(
        chosen_form,
        mesh=mesh,
        in_specs=placed,
        out_specs=(
            P(None, "dp", None, "section"),
            P(("section", "dp"), None),
            P("dp", None),
            P("section", "dp", None),
            P("section", "dp", None),
            P("section", "dp"),
            P("section", "dp"),
            P("section", "dp"),
            P("section", "dp"),
        ),
        check_vma=False,
    )
```

```python
import functools
import types

import jax
import jax.numpy as jnp
from jax import lax
from jax.experimental import pallas as pl
from jax.experimental.pallas import tpu as pltpu
from jax.sharding import PartitionSpec as P

HEADS = 12


EPSILON = 1e-12


def for_sending(array):
    return jax.tree.map(lambda a: a.astype(jnp.bfloat16) if a.dtype == jnp.float32 else a, array)


def passed_along(block, axis, distance):
    devices = range(lax.axis_size(axis))
    route = [(i - distance, i) for i in devices if i - distance in devices]
    return lax.ppermute(block, axis, route)


def broadcast(value, axis, source):
    kept = jnp.where(lax.axis_index(axis) == source, value, 0).astype(value.dtype)
    return lax.psum(kept, axis)


def norm_forward(resid, gain_row, shift_row):
    centre = jnp.mean(resid, -1, keepdims=True)
    centred = resid - centre
    inverse = lax.rsqrt(jnp.mean(centred * centred, -1, keepdims=True) + EPSILON)
    normed = centred * inverse
    return (normed * gain_row + shift_row, normed, inverse)


def norm_backward(upstream, normed, inverse, gain_row):
    gain_part = jnp.sum(upstream * normed, 0)
    shift_part = jnp.sum(upstream, 0)
    scaled = upstream * gain_row
    first_mean = jnp.mean(scaled, -1, keepdims=True)
    second_mean = jnp.mean(scaled * normed, -1, keepdims=True)
    return (inverse * (scaled - first_mean - normed * second_mean), gain_part, shift_part)


def to_heads(values):
    return values.reshape(values.shape[0], HEADS, values.shape[1] // HEADS)


def row_scores(query, keyed, segment):
    factor = (query.shape[1] // HEADS) ** (-0.5)
    scores = (
        jnp.einsum(
            "qhd,khd->hqk", to_heads(query), to_heads(keyed), preferred_element_type=jnp.float32
        )
        * factor
    )
    allowed = segment[:, None] == segment[None, :]
    return jnp.where(allowed[None], scores, -1000000000.0)


def attend_row(packed, segment):
    width = packed.shape[1] // 3
    scores = row_scores(packed[:, :width], packed[:, width : 2 * width], segment)
    row_peak = jnp.max(scores, -1, keepdims=True)
    exponent = jnp.exp(scores - row_peak)
    row_total = jnp.sum(exponent, -1, keepdims=True)
    chance = (exponent / row_total).astype(jnp.bfloat16)
    context = jnp.einsum(
        "hqk,khd->qhd", chance, to_heads(packed[:, 2 * width :]), preferred_element_type=jnp.float32
    )
    summary = (row_peak + jnp.log(row_total))[..., 0]
    return (context.reshape(packed.shape[0], width).astype(jnp.bfloat16), summary)


def attend_back(packed, segment, summary, upstream):
    length = packed.shape[0]
    width = packed.shape[1] // 3
    factor = (width // HEADS) ** (-0.5)
    scores = row_scores(packed[:, :width], packed[:, width : 2 * width], segment)
    chance = jnp.exp(scores - summary[..., None])
    grad_heads = to_heads(upstream)
    grad_chance = jnp.einsum(
        "qhd,khd->hqk",
        grad_heads,
        to_heads(packed[:, 2 * width :]),
        preferred_element_type=jnp.float32,
    )
    grad_value = jnp.einsum(
        "hqk,qhd->khd", chance.astype(jnp.bfloat16), grad_heads, preferred_element_type=jnp.float32
    )
    grad_score = chance * (grad_chance - jnp.sum(chance * grad_chance, -1, keepdims=True))
    grad_score = grad_score.astype(jnp.bfloat16)
    grad_query = (
        jnp.einsum(
            "hqk,khd->qhd",
            grad_score,
            to_heads(packed[:, width : 2 * width]),
            preferred_element_type=jnp.float32,
        )
        * factor
    )
    grad_key = (
        jnp.einsum(
            "hqk,qhd->khd",
            grad_score,
            to_heads(packed[:, :width]),
            preferred_element_type=jnp.float32,
        )
        * factor
    )
    joined = jnp.concatenate(
        [
            grad_query.reshape(length, width),
            grad_key.reshape(length, width),
            grad_value.reshape(length, width),
        ],
        1,
    )
    return joined.astype(jnp.bfloat16)


def attention_forward(inputs, segment, params):
    w_first, w_second, bias_first, bias_second, gain_row, shift_row = params
    rows_here, length, width = inputs.shape
    flat = inputs.reshape(rows_here * length, width)
    offset = jnp.concatenate(
        [bias_first[:width], jnp.zeros((width,), jnp.float32), bias_first[2 * width : 3 * width]]
    )
    packed = jnp.dot(flat, w_first[:, : 3 * width], preferred_element_type=jnp.float32) + offset
    packed = packed.astype(jnp.bfloat16).reshape(rows_here, length, 3 * width)
    context, summary = lax.map(lambda item: attend_row(item[0], item[1]), (packed, segment))
    branch = (
        jnp.dot(
            context.reshape(-1, width), w_first[:, 3 * width :], preferred_element_type=jnp.float32
        )
        + bias_second
    )
    result, normed, inverse = norm_forward(flat.astype(jnp.float32) + branch, gain_row, shift_row)
    return (result.reshape(rows_here, length, width), (packed, context, summary, normed, inverse))


def attention_backward(inputs, segment, upstream, params, totals):
    w_first, w_second, bias_first, bias_second, gain_row, shift_row = params
    rows_here, length, width = inputs.shape
    result, saved = attention_forward(inputs, segment, params)
    packed, context, summary, normed, inverse = saved
    flat = inputs.reshape(-1, width)
    grad_resid, gain_part, shift_part = norm_backward(
        upstream.reshape(-1, width), normed, inverse, gain_row
    )
    grad_branch = grad_resid.astype(jnp.bfloat16)
    grad_out_proj = jnp.einsum(
        "nd,ne->de", context.reshape(-1, width), grad_branch, preferred_element_type=jnp.float32
    )
    bias_second_part = jnp.sum(grad_branch.astype(jnp.float32), 0)
    grad_context = jnp.einsum(
        "ne,de->nd", grad_branch, w_first[:, 3 * width :], preferred_element_type=jnp.float32
    )
    grad_context = grad_context.astype(jnp.bfloat16).reshape(rows_here, length, width)
    grad_packed = lax.map(
        lambda item: attend_back(item[0], item[1], item[2], item[3]),
        (packed, segment, summary, grad_context),
    )
    flat_packed = grad_packed.reshape(-1, 3 * width)
    grad_proj = jnp.einsum("nd,nc->dc", flat, flat_packed, preferred_element_type=jnp.float32)
    bias_sums = jnp.sum(flat_packed.astype(jnp.float32), 0)
    grad_input = grad_resid + jnp.einsum(
        "nc,dc->nd", flat_packed, w_first[:, : 3 * width], preferred_element_type=jnp.float32
    )
    first_total, second_total, bias_first_total, bias_second_total, gain_total, shift_total = totals
    first_total = (
        first_total.at[:, : 3 * width].add(grad_proj).at[:, 3 * width :].add(grad_out_proj)
    )
    bias_first_total = (
        bias_first_total.at[:width]
        .add(bias_sums[:width])
        .at[2 * width : 3 * width]
        .add(bias_sums[2 * width :])
    )
    updated = (
        first_total,
        second_total,
        bias_first_total,
        bias_second_total + bias_second_part,
        gain_total + gain_part,
        shift_total + shift_part,
    )
    return (grad_input.reshape(rows_here, length, width).astype(jnp.bfloat16), updated)


def feed_forward(inputs, params):
    w_first, w_second, bias_first, bias_second, gain_row, shift_row = params
    rows_here, length, width = inputs.shape
    flat = inputs.reshape(-1, width)
    hidden = jnp.dot(flat, w_first, preferred_element_type=jnp.float32) + bias_first
    active = jax.nn.gelu(hidden, approximate=False).astype(jnp.bfloat16)
    branch = jnp.dot(active, w_second, preferred_element_type=jnp.float32) + bias_second
    result, normed, inverse = norm_forward(flat.astype(jnp.float32) + branch, gain_row, shift_row)
    return (result.reshape(rows_here, length, width), (hidden, active, normed, inverse))


def feed_backward(inputs, upstream, params, totals):
    w_first, w_second, bias_first, bias_second, gain_row, shift_row = params
    rows_here, length, width = inputs.shape
    result, saved = feed_forward(inputs, params)
    hidden, active, normed, inverse = saved
    flat = inputs.reshape(-1, width)
    grad_resid, gain_part, shift_part = norm_backward(
        upstream.reshape(-1, width), normed, inverse, gain_row
    )
    grad_branch = grad_resid.astype(jnp.bfloat16)
    grad_second = jnp.einsum("nf,nd->fd", active, grad_branch, preferred_element_type=jnp.float32)
    bias_second_part = jnp.sum(grad_branch.astype(jnp.float32), 0)
    grad_active = jnp.einsum("nd,fd->nf", grad_branch, w_second, preferred_element_type=jnp.float32)
    through = jax.vjp(lambda inner: jax.nn.gelu(inner, approximate=False), hidden)[1](grad_active)[
        0
    ]
    grad_hidden = through.astype(jnp.bfloat16)
    grad_first = jnp.einsum("nd,nf->df", flat, grad_hidden, preferred_element_type=jnp.float32)
    bias_first_part = jnp.sum(grad_hidden.astype(jnp.float32), 0)
    grad_input = grad_resid + jnp.einsum(
        "nf,df->nd", grad_hidden, w_first, preferred_element_type=jnp.float32
    )
    terms = (grad_first, grad_second, bias_first_part, bias_second_part, gain_part, shift_part)
    updated = tuple((total + term for total, term in zip(totals, terms)))
    return (grad_input.reshape(rows_here, length, width).astype(jnp.bfloat16), updated)


def local(
    token_ids,
    segment_ids,
    masked_rows,
    embedding,
    pos_table,
    w_in,
    w_out,
    b_in,
    b_out,
    norm_gain,
    norm_shift,
    logit_grad,
):
    sections = lax.axis_size("section")
    section_index = lax.axis_index("section")
    quarter, width = embedding.shape
    batches, rows_here, length = token_ids.shape
    params = (
        w_in[0],
        w_out[0],
        b_in[0].astype(jnp.float32),
        b_out[0].astype(jnp.float32),
        norm_gain[0].astype(jnp.float32),
        norm_shift[0].astype(jnp.float32),
    )
    local_ids = token_ids - section_index * quarter
    inside = (local_ids >= 0) & (local_ids < quarter)
    picked = jnp.take(embedding, jnp.clip(local_ids, 0, quarter - 1), axis=0)
    partial_rows = jnp.where(inside[..., None], picked.astype(jnp.float32), 0.0)
    looked = lax.psum(partial_rows.astype(jnp.bfloat16), "section").astype(jnp.float32)
    entry = (looked + pos_table.astype(jnp.float32)).astype(jnp.bfloat16)

    def spare_forward(inputs, segment):
        return jnp.zeros(inputs.shape, jnp.bfloat16)

    def attend_forward(inputs, segment):
        return attention_forward(inputs, segment, params)[0].astype(jnp.bfloat16)

    def feed_only(inputs, segment):
        return feed_forward(inputs, params)[0].astype(jnp.bfloat16)

    def spare_backward(inputs, segment, upstream, totals):
        return (jnp.zeros(inputs.shape, jnp.bfloat16), totals)

    def attend_backward(inputs, segment, upstream, totals):
        return attention_backward(inputs, segment, upstream, params, totals)

    def feed_back_only(inputs, segment, upstream, totals):
        return feed_backward(inputs, upstream, params, totals)

    ticks = batches + sections - 1
    kept = jnp.zeros_like(entry)
    outputs = jnp.zeros_like(entry)
    incoming = jnp.zeros_like(entry[0])
    for moment in range(ticks):
        micro_index = moment - section_index
        is_live = (micro_index >= 0) & (micro_index < batches)
        micro_slot = jnp.clip(micro_index, 0, batches - 1)
        current = jnp.where(section_index == 0, entry[micro_slot], incoming)
        kept = kept.at[micro_slot].set(jnp.where(is_live, current, kept[micro_slot]))
        branch_index = jnp.where(is_live, 1 + section_index % 2, 0)
        result = lax.switch(
            branch_index,
            [spare_forward, attend_forward, feed_only],
            current,
            segment_ids[micro_slot],
        )
        outputs = outputs.at[micro_slot].set(jnp.where(is_live, result, outputs[micro_slot]))
        if moment + 1 < ticks:
            incoming = jax.tree.map(
                lambda part, own: part.astype(own.dtype),
                passed_along(for_sending(result), "section", 1),
                result,
            )
    final_rows = jnp.take_along_axis(outputs, masked_rows[..., None], axis=2)
    head_rows = broadcast(final_rows, "section", sections - 1)
    logits = jnp.einsum("mrkd,vd->mrkv", head_rows, embedding, preferred_element_type=jnp.float32)
    partial_grad = jnp.einsum(
        "mrkv,vd->mrkd", logit_grad, embedding, preferred_element_type=jnp.float32
    )
    grad_rows = lax.psum(partial_grad.astype(jnp.bfloat16), "section").astype(jnp.float32)
    table_head = jnp.einsum(
        "mrkv,mrkd->vd", logit_grad, head_rows, preferred_element_type=jnp.float32
    )
    places = (masked_rows[..., None] == jnp.arange(length)[None, None, None, :]).astype(jnp.float32)
    top_grad = jnp.einsum("mrkl,mrkd->mrld", places, grad_rows, precision=lax.Precision.HIGHEST)
    gradients = (
        jnp.zeros(w_in.shape[1:], jnp.float32),
        jnp.zeros(w_out.shape[1:], jnp.float32),
        jnp.zeros(b_in.shape[1:], jnp.float32),
        jnp.zeros((width,), jnp.float32),
        jnp.zeros((width,), jnp.float32),
        jnp.zeros((width,), jnp.float32),
    )
    grad_entry = jnp.zeros_like(entry)
    back_in = jnp.zeros_like(entry[0])
    for moment in range(ticks):
        micro_index = moment - (sections - 1 - section_index)
        is_live = (micro_index >= 0) & (micro_index < batches)
        micro_slot = jnp.clip(micro_index, 0, batches - 1)
        upstream = jnp.where(
            section_index == sections - 1, top_grad[micro_slot], back_in.astype(jnp.float32)
        )
        branch_index = jnp.where(is_live, 1 + section_index % 2, 0)
        grad_input, gradients = lax.switch(
            branch_index,
            [spare_backward, attend_backward, feed_back_only],
            kept[micro_slot],
            segment_ids[micro_slot],
            upstream,
            gradients,
        )
        grad_entry = grad_entry.at[micro_slot].set(
            jnp.where(is_live, grad_input, grad_entry[micro_slot])
        )
        if moment + 1 < ticks:
            back_in = jax.tree.map(
                lambda part, own: part.astype(own.dtype),
                passed_along(for_sending(grad_input), "section", -1),
                grad_input,
            )
    input_grad = broadcast(grad_entry, "section", 0)
    input_wide = input_grad.astype(jnp.float32)
    pos_grad = jnp.sum(input_wide, (0, 1))
    targets = jnp.where(inside, local_ids, quarter).reshape(-1)
    table_input = jax.ops.segment_sum(
        input_wide.reshape(-1, width), targets, num_segments=quarter + 1
    )[:quarter]
    w_in_part, w_out_part, b_in_part, b_out_part, gain_part, shift_part = gradients
    reduced = (
        lax.psum_scatter(w_in_part, "dp", scatter_dimension=0, tiled=True),
        lax.psum_scatter(w_out_part, "dp", scatter_dimension=0, tiled=True),
        lax.psum_scatter(b_in_part, "dp", scatter_dimension=0, tiled=True),
        lax.psum_scatter(b_out_part, "dp", scatter_dimension=0, tiled=True),
        lax.psum_scatter(gain_part, "dp", scatter_dimension=0, tiled=True),
        lax.psum_scatter(shift_part, "dp", scatter_dimension=0, tiled=True),
        lax.psum_scatter(pos_grad, "dp", scatter_dimension=0, tiled=True),
        lax.psum_scatter(table_input + table_head, "dp", scatter_dimension=0, tiled=True),
    )
    table_grad = reduced[7]
    return (
        logits,
        table_grad,
        reduced[6],
        reduced[0][None],
        reduced[1][None],
        reduced[2][None],
        reduced[3][None],
        reduced[4][None],
        reduced[5][None],
    )


SENDS = 230
RECVS = 160
VMEM_LIMIT = 64 * 2**20
BF = jnp.bfloat16
F32 = jnp.float32
MESH = pl.DeviceIdType.MESH


def mm(a, b):
    return jnp.dot(a, b, preferred_element_type=F32)


def mm_nt(a, b):
    return lax.dot_general(a, b, (((1,), (1,)), ((), ())), preferred_element_type=F32)


def mm_tn(a, b):
    return lax.dot_general(a, b, (((0,), (0,)), ((), ())), preferred_element_type=F32)


def iota(shape, dim):
    return lax.broadcasted_iota(jnp.int32, shape, dim)


def column(row):
    return jnp.broadcast_to(row.astype(F32), (128, 128)).T


class Plan:
    def __init__(self, n_dp, length, width, ff, quarter, masks):
        self.n_dp, self.length, self.width, self.ff = n_dp, length, width, ff
        self.quarter, self.masks = quarter, masks
        self.nz = n_dp // 2
        self.share = quarter // n_dp
        self.in_rows = width // n_dp
        self.out_rows = ff // n_dp
        self.mask_pad = -(-masks // 16) * 16
        self.share_pad = -(-self.share // 128) * 128
        self.share_rows = -(-self.share // 16) * 16
        self.chunks = []
        at = 0
        while at < quarter:
            size = min(1024, quarter - at)
            self.chunks.append((at, size))
            at += size


class Counter:
    def __init__(self):
        self.n = 0

    def take(self, k=1):
        first = self.n
        self.n += k
        return first


def scratch_list(p):
    w, ff, ln = p.width, p.ff, p.length
    mp = p.mask_pad
    return dict(
        emb=((p.quarter, w), BF),
        wa=((w, ff), BF),
        w1=((w, ff), BF),
        w2=((ff, w), BF),
        par_a=((8, ff), F32),
        par_f=((8, ff), F32),
        acc=((2 * ln, w), F32),
        psend=((ln, w), BF),
        psum=((ln, w), BF),
        prow=((2, ln, w), BF),
        lgp=((2 * mp, p.quarter), BF),
        lgs=((p.n_dp, 2 * p.masks, p.share_pad), BF),
        lgr=((p.n_dp, 2 * p.masks, p.share_pad), BF),
        ch_pack=((p.n_dp, 2 * p.masks, w), BF),
        g=((2 * mp, w), F32),
        grow=((2, p.masks, w), F32),
        gwide=((ln, w), F32),
        mrow=((8, ln), jnp.int32),
        ids_own=((8, ln), jnp.int32),
        ids_all=((p.n_dp, 8, ln), jnp.int32),
        x_a=((ln, w), BF),
        x_f=((ln, w), BF),
        y_f=((ln, w), BF),
        y_o=((ln, w), BF),
        pk=((ln, 3 * w), BF),
        ctx=((ln, w), BF),
        probs=((w // 128, ln, 256), F32),
        n_a=((ln, w), F32),
        n_f=((ln, w), F32),
        inv_a=((ln, 1), F32),
        inv_f=((ln, 1), F32),
        slope=((ln, ff), BF),
        xt_a=((p.nz, 2, p.in_rows, ln), BF),
        ct_a=((p.nz, 2, p.in_rows, ln), BF),
        dyin=((ln, w), BF),
        dyf=((ln, w), F32),
        dres=((ln, w), F32),
        dbr_a=((ln, w), BF),
        dpk=((ln, 3 * w), BF),
        dctx=((ln, w), BF),
        dx=((ln, w), BF),
        bsum=((1, ff), F32),
        sm_a=((8, w), F32),
        sm_f=((8, w), F32),
        b_ctx=((p.nz, p.in_rows, 4 * ln), BF),
        b_x=((p.nz, p.in_rows, 4 * ln), BF),
        b_dbr=((4 * ln, w), BF),
        b_dh=((4 * ln, 3 * w), BF),
        b_sm=((4, 8, w), F32),
        sm_tot=((8, w), F32),
        sm_all=((8, w), F32),
        r_sm=((p.nz, 8, w), F32),
        r_in=((4, p.in_rows, ff), BF),
        x_all=((2, p.nz, 2, ln, w), BF),
        db_all=((2, p.nz, 2, ln, w), BF),
        w_col=((w, p.out_rows), F32),
        w_send=((p.n_dp, p.in_rows, p.out_rows), BF),
        r_col=((p.n_dp, p.in_rows, p.out_rows), BF),
        ch_own=((mp, w), BF),
        ch_two=((mp, w), BF),
        ch_all=((2, p.n_dp, mp, w), BF),
        de_all=((2, p.n_dp, ln, w), BF),
    )


def fused(p, names, *refs):
    (tok, seg, picks, lg, pos, b_in, b_out, gain, shift, emb_h, w_in_h, w_out_h) = refs[:12]
    (o_log, o_tab, o_pos, o_win, o_wout, o_bin, o_bout, o_gain, o_shift) = refs[12:21]
    r = types.SimpleNamespace(**dict(zip(names, refs[21:])))
    ss, rs, ls = refs[21 + len(names) :]
    w, ff, ln, mp, nz, n_dp = p.width, p.ff, p.length, p.mask_pad, p.nz, p.n_dp
    heads = w // 64
    pairs = heads // 2

    s = lax.axis_index("section")
    dp = lax.axis_index("dp")
    x, c = s // 2, lax.rem(s, 2)
    z, y = dp // 2, lax.rem(dp, 2)
    core = s + 1 - 2 * c
    across = s + 2 - 4 * x
    ydp = dp + 1 - 2 * y
    other = 1 - c
    at_x0, at_x1 = x == 0, x == 1
    is_att, is_ff = c == 0, c == 1
    sends, recvs = Counter(), Counter()
    pending = []

    def send(cond, src, dst, dev, recv):
        slot = sends.take()

        def make():
            return pltpu.make_async_remote_copy(
                src_ref=src,
                dst_ref=dst,
                send_sem=ss.at[slot],
                recv_sem=rs.at[recv],
                device_id=dev,
                device_id_type=MESH,
            )

        if cond is None:
            make().start()
        else:

            @pl.when(cond)
            def _():
                make().start()

        pending.append((cond, make))

    def arrived(dst, recv):
        pltpu.make_async_remote_copy(
            src_ref=dst,
            dst_ref=dst,
            send_sem=ss.at[0],
            recv_sem=rs.at[recv],
            device_id=(core, dp),
            device_id_type=MESH,
        ).wait_recv()

    for i, (at, size) in enumerate(p.chunks):
        pltpu.make_async_copy(emb_h.at[pl.ds(at, size)], r.emb.at[pl.ds(at, size)], ls.at[i]).start()
    l_w = len(p.chunks)

    @pl.when(is_att)
    def _():
        pltpu.make_async_copy(w_in_h.at[0], r.wa, ls.at[l_w]).start()

    @pl.when(is_ff)
    def _():
        pltpu.make_async_copy(w_in_h.at[0], r.w1, ls.at[l_w]).start()
        pltpu.make_async_copy(w_out_h.at[0], r.w2, ls.at[l_w + 1]).start()

    def fill(par):
        par[0:1, :] = b_in[...].astype(F32)
        par[1:2, 0:w] = b_out[...].astype(F32)
        par[2:3, 0:w] = gain[...].astype(F32)
        par[3:4, 0:w] = shift[...].astype(F32)

    pl.when(is_att)(lambda: fill(r.par_a))
    pl.when(is_ff)(lambda: fill(r.par_f))

    barrier = pltpu.get_barrier_semaphore()
    peers = [(s, lax.rem(dp + k, n_dp)) for k in range(1, n_dp)]
    peers += [(core, dp), (across, dp), (3 - s, dp), (core, ydp)]
    for peer in peers:
        pl.semaphore_signal(barrier, inc=1, device_id=peer, device_id_type=MESH)

    cols = [column(tok[m]) for m in range(2)]
    first = s * p.quarter
    for i, (at, size) in enumerate(p.chunks):
        pltpu.make_async_copy(emb_h.at[pl.ds(at, size)], r.emb.at[pl.ds(at, size)], ls.at[i]).wait()
        lane = (iota((ln, size), 1) + (first + at)).astype(F32)
        hot = []
        for m in range(2):
            wide = jnp.concatenate([cols[m]] * (-(-size // 128)), 1)[:, :size]
            hot.append(jnp.where(wide == lane, 1.0, 0.0).astype(BF))
        part = mm(jnp.concatenate(hot, 0), r.emb[at : at + size, :])
        if i == 0:
            r.acc[...] = part
        else:
            r.acc[...] += part
    r.psend[...] = r.acc[pl.ds(pl.multiple_of(ln * other, ln), ln), :].astype(BF)

    tiles = ff // w
    k_p, k_g = recvs.take(2), recvs.take(2)
    k_pa, k_pf, k_wa, k_w1, k_w2 = recvs.take(), recvs.take(), recvs.take(tiles), recvs.take(tiles), recvs.take(tiles)
    pl.semaphore_wait(barrier, len(peers))
    send(None, r.psend, r.prow.at[0], (core, dp), k_p)


    r.lgp[...] = jnp.zeros(r.lgp.shape, BF)
    r.lgp[0 : p.masks] = lg[0, 0]
    r.lgp[mp : mp + p.masks] = lg[1, 0]

    k_lg, k_id = recvs.take(n_dp), recvs.take(n_dp)
    for j in range(n_dp):
        r.lgs[j, :, p.share :] = jnp.zeros((2 * p.masks, p.share_pad - p.share), BF)
        for m in range(2):
            r.lgs[j, p.masks * m : p.masks * (m + 1), 0 : p.share] = lg[m, 0, :, p.share * j : p.share * (j + 1)]
    r.ids_own[...] = jnp.zeros(r.ids_own.shape, jnp.int32)
    for m in range(2):
        r.ids_own[m : m + 1, :] = tok[m]
    r.ids_all[dp] = r.ids_own[...]
    r.lgr[dp] = r.lgs[dp]
    for k in range(1, n_dp):
        to = lax.rem(dp + k, n_dp)
        send(None, r.lgs.at[to], r.lgr.at[dp], (s, to), k_lg + dp)
        send(None, r.ids_own, r.ids_all.at[dp], (s, to), k_id + dp)
    arrived(r.prow.at[0], k_p)
    own_rows = r.acc[pl.ds(pl.multiple_of(ln * c, ln), ln), :]
    r.acc[0:ln, :] = own_rows + r.prow[0].astype(F32)
    r.psum[...] = r.acc[0:ln, :].astype(BF)
    send(at_x1, r.psum, r.prow.at[1], (across, dp), k_p + 1)

    send(is_att, r.par_a, r.par_a, (core, dp), k_pa)
    send(is_ff, r.par_f, r.par_f, (core, dp), k_pf)
    for j in range(tiles):
        cut = slice(j * w, (j + 1) * w)
        send(is_att, w_in_h.at[0, :, cut], r.wa.at[:, cut], (core, dp), k_wa + j)
        send(is_ff, w_in_h.at[0, :, cut], r.w1.at[:, cut], (core, dp), k_w1 + j)
        send(is_ff, w_out_h.at[0, cut, :], r.w2.at[cut, :], (core, dp), k_w2 + j)


    for i, (at, size) in enumerate(p.chunks):
        part = mm(r.lgp[:, at : at + size], r.emb[at : at + size, :])
        if i == 0:
            r.g[...] = part
        else:
            r.g[...] += part
    send(None, r.g.at[pl.ds(pl.multiple_of(mp * other, mp), p.masks)], r.grow.at[0], (core, dp), k_g)

    def masked_gradient():
        arrived(r.grow.at[0], k_g)
        r.gwide[...] = jnp.zeros(r.gwide.shape, F32)
        r.gwide[0 : p.masks, :] = r.g[pl.ds(pl.multiple_of(mp * c, mp), p.masks), :] + r.grow[0]

    pl.when(at_x1)(masked_gradient)

    k_x = recvs.take()

    @pl.when(at_x0)
    def _():
        arrived(r.prow.at[1], k_p + 1)
        whole = r.acc[0:ln, :] + r.prow[1].astype(F32)
        r.x_a[...] = (whole + pos[...].astype(F32)).astype(BF)

    @pl.when(is_att)
    def _():
        pltpu.make_async_copy(w_in_h.at[0], r.wa, ls.at[l_w]).wait()
        arrived(r.par_f, k_pf)

    @pl.when(is_ff)
    def _():
        pltpu.make_async_copy(w_in_h.at[0], r.w1, ls.at[l_w]).wait()
        pltpu.make_async_copy(w_out_h.at[0], r.w2, ls.at[l_w + 1]).wait()
        arrived(r.par_a, k_pa)

    @pl.when(at_x1)
    def _():
        arrived(r.x_a, k_x)

    low = jnp.where(iota((ln, 128), 1) < 64, 1.0, 0.0).astype(BF)
    high = jnp.where(iota((ln, 128), 1) < 64, 0.0, 1.0).astype(BF)

    def split(block):
        return jnp.concatenate([block * low, block * high], 0)

    def stack(block):
        return jnp.concatenate([block[:, 0:128], block[:, 128:256]], 0)

    def norm_forward(resid, par):
        centred = resid - jnp.mean(resid, -1, keepdims=True)
        inverse = lax.rsqrt(jnp.mean(centred * centred, -1, keepdims=True) + EPSILON)
        normed = centred * inverse
        return (normed * par[2:3, 0:w] + par[3:4, 0:w]).astype(BF), normed, inverse

    rows_x = r.x_a[...]

    def wa_tile(j):
        pl.when(is_ff)(lambda: arrived(r.wa.at[:, j * w : (j + 1) * w], k_wa + j))

    for j in range(3):
        wa_tile(j)
        part = mm(rows_x, r.wa[:, j * w : (j + 1) * w])
        if j != 1:
            part = part + r.par_a[0:1, j * w : (j + 1) * w]
        r.pk[:, j * w : (j + 1) * w] = part.astype(BF)
    seg_row = seg[c].astype(F32)
    seg_col = column(seg[c])
    seg_row = jnp.broadcast_to(jnp.concatenate([seg_row, seg_row], 1), (ln, 256))
    seg_col = jnp.concatenate([seg_col, seg_col], 1)
    for h in range(pairs):
        at = 128 * h
        query = r.pk[:, at : at + 128]
        keyed = split(r.pk[:, w + at : w + at + 128])
        value = split(r.pk[:, 2 * w + at : 2 * w + at + 128])
        scores = jnp.where(seg_row == seg_col, mm_nt(query, keyed) * 0.125, -1e9)
        chance = []
        for half in (scores[:, 0:128], scores[:, 128:256]):
            power = jnp.exp(half - jnp.max(half, -1, keepdims=True))
            chance.append(power / jnp.sum(power, -1, keepdims=True))
        chance = jnp.concatenate(chance, 1)
        r.probs[h] = chance
        r.ctx[:, at : at + 128] = mm(chance.astype(BF), value).astype(BF)
    wa_tile(3)
    resid = rows_x.astype(F32) + mm(r.ctx[...], r.wa[:, 3 * w : 4 * w]) + r.par_a[1:2, 0:w]
    r.x_f[...], r.n_a[...], r.inv_a[...] = norm_forward(resid, r.par_a)

    def line(buf, base, cond=True, owner=None):
        own = buf(dp)
        send(cond & (z < nz - 1), own, own, (s, dp + 2), base + dp)
        send(cond & (z > 0), own, own, (s, dp - 2), base + dp)
        to_y(buf, base, dp, cond, owner)

    def to_y(buf, base, i, cond, owner):
        piece = buf(i)
        if owner is None:
            send(None if cond is True else cond, piece, piece, (s, ydp), base + i)
        else:
            whose = jnp.where(is_att, core, s)
            send(None if cond is True else cond, piece, piece, (whose, ydp), jnp.where(is_att, owner, base) + i)
            send(is_att & cond, piece, piece, (core, dp), owner + i)

    def line_step(buf, base, t, cond=True, owner=None, on_x=None):
        for sign in (-1, 1):
            from_z = z + sign * t
            here = (from_z >= 0) & (from_z < nz) & cond
            from_dp = jnp.clip(from_z, 0, nz - 1) * 2 + y
            piece = buf(from_dp)
            pl.when(here)(lambda piece=piece, from_dp=from_dp: arrived(piece, base + from_dp))
            to_z = z - sign
            on = here & (to_z >= 0) & (to_z < nz)
            if t < nz - 1:
                send(on, piece, piece, (s, dp - 2 * sign), base + from_dp)
            to_y(buf, base, from_dp, here, owner)
            if on_x is not None:
                send(here, piece, piece, (across, dp), on_x + from_dp)

    def line_y(buf, base, t, cond=True, on_x=None):
        for sign in (-1, 1) if t else (1,):
            from_z = z + sign * t
            here = (from_z >= 0) & (from_z < nz) & cond
            from_dp = jnp.clip(from_z, 0, nz - 1) * 2 + 1 - y
            piece = buf(from_dp)
            pl.when(here)(lambda piece=piece, from_dp=from_dp: arrived(piece, base + from_dp))
            if on_x is not None:
                send(here, piece, piece, (across, dp), on_x + from_dp)

    def ch(i):
        return r.ch_all.at[c, i]

    def de(i):
        return r.de_all.at[c, i]

    def xs(i):
        return r.x_all.at[c, i // 2, lax.rem(i, 2)]

    def db(i):
        return r.db_all.at[c, i // 2, lax.rem(i, 2)]

    k_ch, k_de, k_xs, k_db = (recvs.take(n_dp) for _ in range(4))
    k_cho, k_chc, k_cha, k_chx, k_dex = (recvs.take() for _ in range(5))
    k_xsc, k_dbc = recvs.take(n_dp), recvs.take(n_dp)

    r.x_all[c, z, y] = r.x_f[...]
    line(xs, k_xs, True, k_xsc)

    def feed(rows_x, keep=True):
        total = rows_x.astype(F32) + r.par_f[1:2, 0:w]
        for j in range(tiles):
            cut = slice(j * w, (j + 1) * w)

            @pl.when(is_att)
            def _():
                arrived(r.w1.at[:, cut], k_w1 + j)
                arrived(r.w2.at[cut, :], k_w2 + j)

            hidden = mm(rows_x, r.w1[:, cut]) + r.par_f[0:1, cut]
            below = 0.5 + 0.5 * lax.erf(hidden * (0.5**0.5))
            total = total + mm((hidden * below).astype(BF), r.w2[cut, :])
            if keep:
                slope = below + hidden * (0.3989422804014327 * jnp.exp(-0.5 * hidden * hidden))
                r.slope[:, cut] = slope.astype(BF)
        result, normed, inverse = norm_forward(total, r.par_f)
        if keep:
            r.y_f[...], r.n_f[...], r.inv_f[...] = result, normed, inverse
        else:
            r.y_o[...] = result

    pl.when(is_ff | at_x1)(lambda: feed(r.x_f[...]))
    send(at_x0 & is_ff, r.y_f, r.x_a, (across, dp), k_x)

    @pl.when(at_x0 & is_ff)
    def _():
        arrived(r.x_all.at[0, z, y], k_xsc + dp)
        feed(r.x_all[0, z, y], False)

    send(at_x0 & is_ff, r.y_o, r.x_a, (3 - s, dp), k_x)

    @pl.when(at_x1)
    def _():
        r.mrow[...] = jnp.full(r.mrow.shape, -1, jnp.int32)
        r.mrow[0:1, 0 : p.masks] = picks[c]
        places = jnp.where(iota((ln, ln), 0) == r.mrow[0:1, :], 1.0, 0.0).astype(BF)
        r.ch_own[...] = mm_tn(places, r.y_f[...])[0:mp].astype(BF)
        arrived(r.grow.at[1], k_g + 1)
        r.gwide[0 : p.masks, :] += r.grow[1]
        coarse = r.gwide[...].astype(BF)
        fine = (r.gwide[...] - coarse.astype(F32)).astype(BF)
        r.dyf[...] = mm(places, coarse) + mm(places, fine)

    send(at_x1, r.ch_own, r.ch_own, (across, dp), k_cho)
    send(at_x1, r.ch_own, r.ch_two, (core, dp), k_chc)

    def push(owner, kind, src, dst, cond=None):
        home = c == owner
        slot_y = 2 + jnp.where(home, 0, 1)
        own_dst, near_dst, far_dst = dst(0), dst(1), dst(slot_y)

        away = jnp.logical_not(home)

        @pl.when(home if cond is None else home & cond)
        def _():
            pltpu.make_async_copy(src(y), own_dst, rs.at[kind]).start()

        send(away if cond is None else away & cond, src(y), near_dst, (core, dp), kind + 1)
        far_s = jnp.where(home, s, core)
        send(cond, src(1 - y), far_dst, (far_s, ydp), kind + slot_y)

    def gathered(kind, dst):
        pltpu.make_async_copy(dst(0), dst(0), rs.at[kind]).wait()
        for slot in range(1, 4):
            arrived(dst(slot), kind + slot)

    def lanes(slot):
        return pl.ds(slot * ln if isinstance(slot, int) else pl.multiple_of(slot * ln, ln), ln)

    k_dh = [recvs.take(4) for _ in range(3)]
    k_ctx, k_xt, k_dba, k_sm = (recvs.take(4) for _ in range(4))
    to_x = lambda slot: r.b_x.at[:, :, lanes(slot)]
    to_ctx = lambda slot: r.b_ctx.at[:, :, lanes(slot)]
    to_dbr = lambda slot: r.b_dbr.at[lanes(slot), :]
    to_sm = lambda slot: r.b_sm.at[slot]

    def to_dh(j):
        return lambda slot: r.b_dh.at[lanes(slot), j * w : (j + 1) * w]

    def push_dh(j):
        push(0, k_dh[j], lambda i: r.dpk.at[:, j * w : (j + 1) * w], to_dh(j))

    def push_rows(cond):
        push(0, k_xt, lambda i: r.xt_a.at[:, i], to_x, cond)
        push(0, k_ctx, lambda i: r.ct_a.at[:, i], to_ctx, cond)

    def turn():
        for dst, src in ((r.xt_a, r.x_a), (r.ct_a, r.ctx)):
            turned = src[...].T
            for b in range(n_dp):
                dst[b // 2, b % 2] = turned[b * p.in_rows : (b + 1) * p.in_rows]

    @pl.when(at_x0)
    def _():
        masked_gradient()
        turn()

    send(at_x0, r.gwide.at[0 : p.masks], r.grow.at[1], (across, dp), k_g + 1)
    push_rows(at_x0)

    @pl.when(at_x0 & is_att)
    def _():
        feed(r.x_f[...])

    line_step(xs, k_xs, 1, at_x0, k_xsc)
    line_step(xs, k_xs, 2, at_x0, k_xsc)

    @pl.when(at_x0)
    def _():
        arrived(r.ch_own, k_cho)
        r.ch_all[c, dp] = r.ch_own[...]

    send(at_x0, r.ch_own, r.ch_two, (core, dp), k_chc)
    for k in range(1, n_dp):
        send(at_x0, r.ch_own, ch(dp), (s, lax.rem(dp + k, n_dp)), k_ch + dp)

    def logits():
        arrived(r.ch_two, k_chc)
        chosen = jnp.concatenate([r.ch_own[...], r.ch_two[...]], 0)
        for at, size in p.chunks:
            part = mm_nt(chosen, r.emb[at : at + size, :])
            o_log[c, 0, :, at : at + size] = part[0 : p.masks]
            o_log[other, 0, :, at : at + size] = part[mp : mp + p.masks]

    pl.when(at_x0)(logits)
    line_step(xs, k_xs, 3, at_x0, k_xsc)

    k_dy = recvs.take()

    @pl.when(at_x0)
    def _():
        arrived(r.dyin, k_dy)
        r.dyf[...] = r.dyin[...].astype(F32)

    def norm_backward(par, n_ref, inv_ref):
        up, normed = r.dyf[...], n_ref[...]
        gain_part = jnp.sum(up * normed, 0, keepdims=True)
        shift_part = jnp.sum(up, 0, keepdims=True)
        scaled = up * par[2:3, 0:w]
        first_mean = jnp.mean(scaled, -1, keepdims=True)
        second_mean = jnp.mean(scaled * normed, -1, keepdims=True)
        return inv_ref[...] * (scaled - first_mean - normed * second_mean), gain_part, shift_part

    def small(dst, out_part, gain_part, shift_part):
        dst[...] = jnp.zeros(dst.shape, F32)
        n_b, n_w = ff // n_dp, w // n_dp
        for k in range(n_dp):
            dst[k : k + 1, 0:n_b] = r.bsum[:, k * n_b : (k + 1) * n_b]
            dst[k : k + 1, n_b : n_b + n_w] = out_part[:, k * n_w : (k + 1) * n_w]
            dst[k : k + 1, n_b + 128 : n_b + 128 + n_w] = gain_part[:, k * n_w : (k + 1) * n_w]
            dst[k : k + 1, n_b + 256 : n_b + 256 + n_w] = shift_part[:, k * n_w : (k + 1) * n_w]

    dres, gain_part, shift_part = norm_backward(r.par_f, r.n_f, r.inv_f)
    r.dres[...] = dres
    r.db_all[c, z, y] = dres.astype(BF)
    line(db, k_db, True, k_dbc)
    branch = r.db_all[c, z, y]
    total = r.dres[...]
    for j in range(tiles):
        cut = slice(j * w, (j + 1) * w)
        dhidden = (mm_nt(branch, r.w2[cut, :]) * r.slope[:, cut].astype(F32)).astype(BF)
        r.bsum[:, cut] = jnp.sum(dhidden.astype(F32), 0, keepdims=True)
        total = total + mm_nt(dhidden, r.w1[:, cut])
    r.dyf[...] = total.astype(BF).astype(F32)
    small(r.sm_f, jnp.sum(branch.astype(F32), 0, keepdims=True), gain_part, shift_part)
    line_step(xs, k_xs, 1, at_x1, k_xsc)

    dres, gain_part, shift_part = norm_backward(r.par_a, r.n_a, r.inv_a)
    r.dres[...] = dres
    r.dbr_a[...] = dres.astype(BF)
    branch = r.dbr_a[...]
    r.dctx[...] = mm_nt(branch, r.wa[:, 3 * w : 4 * w]).astype(BF)
    for h in range(pairs):
        at = 128 * h
        query = r.pk[:, at : at + 128]
        keyed = split(r.pk[:, w + at : w + at + 128])
        value = split(r.pk[:, 2 * w + at : 2 * w + at + 128])
        upper = r.dctx[:, at : at + 128]
        chance = r.probs[h]
        dchance = mm_nt(upper, value)
        mixed = chance * dchance
        dscores = []
        for cut in (slice(0, 128), slice(128, 256)):
            dscores.append(mixed[:, cut] - chance[:, cut] * jnp.sum(mixed[:, cut], -1, keepdims=True))
        dscores = jnp.concatenate(dscores, 1).astype(BF)
        r.dpk[:, at : at + 128] = (mm(dscores, keyed) * 0.125).astype(BF)
        r.dpk[:, w + at : w + at + 128] = (mm_tn(stack(dscores), split(query)) * 0.125).astype(BF)
        r.dpk[:, 2 * w + at : 2 * w + at + 128] = mm_tn(stack(chance.astype(BF)), split(upper)).astype(BF)
    total = r.dres[...]
    for j in range(3):
        cut = slice(j * w, (j + 1) * w)
        total = total + mm_nt(r.dpk[:, cut], r.wa[:, cut])
    r.dx[...] = total.astype(BF)
    send(at_x1, r.dx, r.dyin, (across, dp), k_dy)

    gathers = c == 1 - x

    @pl.when(at_x0)
    def _():
        r.de_all[c, dp] = r.dx[...]

    send(at_x0, de(dp), de(dp), (across, dp), k_de + dp)
    line(de, k_de, at_x0 & is_ff)

    line_step(xs, k_xs, 2, at_x1, k_xsc)
    line_step(db, k_db, 1, True, k_dbc)
    pl.when(at_x1)(turn)
    push_rows(at_x1)
    push(0, k_dba, lambda i: r.dbr_a, to_dbr)
    push_dh(0)
    push(1, k_sm, lambda i: r.sm_f, to_sm)

    @pl.when(at_x0)
    def _():
        for k in range(1, n_dp):
            arrived(ch(lax.rem(dp + k, n_dp)), k_ch + lax.rem(dp + k, n_dp))

    send(at_x0, r.ch_all.at[c], r.ch_all.at[c], (across, dp), k_cha)
    send(at_x0, r.ch_all.at[c], r.ch_all.at[c], (core, dp), k_chx)
    r.bsum[...] = jnp.zeros(r.bsum.shape, F32)
    for j in (0, 2):
        cut = slice(j * w, (j + 1) * w)
        r.bsum[:, cut] = jnp.sum(r.dpk[:, cut].astype(F32), 0, keepdims=True)
    small(r.sm_a, jnp.sum(branch.astype(F32), 0, keepdims=True), gain_part, shift_part)
    push(0, k_sm, lambda i: r.sm_a, to_sm)
    line_step(xs, k_xs, 3, at_x1, k_xsc)
    line_step(db, k_db, 2, True, k_dbc)
    push_dh(1)
    line_step(de, k_de, 1, at_x0 & is_ff, None, k_de)
    line_step(db, k_db, 3, True, k_dbc)
    push_dh(2)
    line_step(de, k_de, 2, at_x0 & is_ff, None, k_de)
    line_step(de, k_de, 3, at_x0 & is_ff, None, k_de)

    def head_part():
        arrived(r.ch_all.at[other], k_chx)
        for k in range(1, n_dp):
            src = lax.rem(dp + k, n_dp)
            arrived(r.lgr.at[src], k_lg + src)
            arrived(r.ids_all.at[src], k_id + src)
        for i in range(n_dp):
            for m in range(2):
                r.ch_pack[i, p.masks * m : p.masks * (m + 1)] = r.ch_all[m, i, 0 : p.masks]
        lines = 2 * n_dp * p.masks
        grad = mm_tn(r.lgr[...].reshape(lines, p.share_pad), r.ch_pack[...].reshape(lines, w))
        o_tab[...] = grad[0 : p.share]

    @pl.when(at_x1 & is_att)
    def _():
        arrived(de(dp), k_de + dp)

    line(de, k_de, at_x1 & is_att)
    pl.when(at_x1)(logits)

    k_in = [recvs.take(4) for _ in range(tiles)]
    half = nz * p.in_rows
    outer = (z == 0) | (z == nz - 1)
    mate = z + 1 - 2 * lax.rem(z, 2)
    far_base = 2 - 2 * (z // 2)

    def shard(zz, cut):
        return r.wa.at[pl.ds(pl.multiple_of(zz * p.in_rows, p.in_rows), p.in_rows), cut]

    def tile_cut(j):
        return slice(j * w, (j + 1) * w)

    def attention_tile(j):
        cut = tile_cut(j)

        @pl.when(is_att)
        def _():
            if j == 3:
                gathered(k_ctx, to_ctx)
                gathered(k_dba, to_dbr)
                grad = mm(r.b_ctx[...].reshape(half, 4 * ln), r.b_dbr[...])
            else:
                if j == 0:
                    gathered(k_xt, to_x)
                gathered(k_dh[j], to_dh(j))
                grad = mm(r.b_x[...].reshape(half, 4 * ln), r.b_dh[:, cut])
            r.wa[0:half, cut] = grad.astype(BF)

        to_mate = (s, 2 * mate + y)
        for k in range(2):
            send(is_att & outer, shard(far_base + k, cut), r.r_in.at[2 + k, :, cut], to_mate, k_in[j] + 2 + k)
        send(is_att, shard(mate, cut), r.r_in.at[0, :, cut], to_mate, k_in[j])

    def attention_sum(j):
        cut = tile_cut(j)
        inner = is_att & jnp.logical_not(outer)
        for k in range(2):

            @pl.when(inner)
            def _():
                arrived(r.r_in.at[2 + k, :, cut], k_in[j] + 2 + k)
                rows = pl.ds(pl.multiple_of((far_base + k) * p.in_rows, p.in_rows), p.in_rows)
                r.wa[rows, cut] = (r.wa[rows, cut].astype(F32) + r.r_in[2 + k, :, cut].astype(F32)).astype(BF)

            send(inner, shard(far_base + k, cut), r.r_in.at[1, :, cut], (s, 2 * (far_base + k) + y), k_in[j] + 1)

    attention_tile(3)
    line_step(de, k_de, 1, at_x1 & is_att, None, k_de)
    attention_tile(0)
    attention_sum(3)
    line_step(de, k_de, 2, at_x1 & is_att, None, k_de)

    k_col = recvs.take(n_dp)
    mine_in = pl.ds(pl.multiple_of(dp * p.out_rows, p.out_rows), p.out_rows)

    def unit_grads(yy, i):
        def four(buf):
            return jnp.concatenate([buf[m, 2 * i + k, yy] for m in range(2) for k in range(2)], 0)

        rows_x, up = four(r.x_all), four(r.db_all)
        hidden = mm(rows_x, r.w1[:, mine_in]) + r.par_f[0:1, mine_in]
        below = 0.5 + 0.5 * lax.erf(hidden * (0.5**0.5))
        slope = below + hidden * (0.3989422804014327 * jnp.exp(-0.5 * hidden * hidden))
        dhidden = (mm_nt(up, r.w2[mine_in, :]) * slope).astype(BF)
        o_wout[0] += mm_tn((hidden * below).astype(BF), up)
        r.w_col[...] += mm_tn(rows_x, dhidden)

    def units_of(yy):
        for zz in range(nz):
            i = 2 * zz + yy
            pl.when((i != dp) | at_x1)(lambda i=i: arrived(r.x_all.at[0, i // 2, lax.rem(i, 2)], k_xsc + i))
            arrived(r.db_all.at[0, i // 2, lax.rem(i, 2)], k_dbc + i)
        lax.fori_loop(0, nz // 2, lambda i, carry: (unit_grads(yy, i), carry)[1], 0)

    @pl.when(is_ff)
    def _():
        o_wout[...] = jnp.zeros(o_wout.shape, F32)
        r.w_col[...] = jnp.zeros(r.w_col.shape, F32)
        units_of(y)

    k_smz = recvs.take(nz)
    gathered(k_sm, to_sm)
    r.sm_tot[...] = r.b_sm[0] + r.b_sm[1] + r.b_sm[2] + r.b_sm[3]
    r.r_sm[z] = r.sm_tot[...]
    for k in range(1, nz):
        zz = lax.rem(z + k, nz)
        send(None, r.sm_tot, r.r_sm.at[z], (s, 2 * zz + y), k_smz + z)

    attention_tile(1)
    attention_sum(0)
    line_step(de, k_de, 3, at_x1 & is_att, None, k_de)
    line_y(de, k_de, 0, gathers, k_de)
    line_y(de, k_de, 1, gathers, k_de)
    attention_tile(2)
    attention_sum(1)

    @pl.when(is_ff)
    def _():
        for t in range(nz):
            line_y(xs, k_xs, t)
        for t in range(nz):
            line_y(db, k_db, t)
        units_of(1 - y)
        for k in range(n_dp):
            r.w_send[k] = r.w_col[k * p.in_rows : (k + 1) * p.in_rows, :].astype(BF)
        r.r_col[dp] = r.w_send[dp]

    for k in range(1, n_dp):
        to = lax.rem(dp + k, n_dp)
        send(is_ff, r.w_send.at[to], r.r_col.at[dp], (s, to), k_col + dp)
    line_y(de, k_de, 2, gathers, k_de)
    line_y(de, k_de, 3, gathers, k_de)
    attention_sum(2)

    @pl.when(at_x1)
    def _():
        arrived(r.ch_all.at[c], k_cha)

    send(at_x1, r.ch_all.at[c], r.ch_all.at[c], (core, dp), k_chx)

    head_part()

    for i in range(n_dp):
        pl.when(jnp.logical_not(gathers) & ((i != dp) | at_x1))(lambda i=i: arrived(de(i), k_de + i))
    send(None, r.de_all.at[c], r.de_all.at[c], (core, dp), k_dex)

    entry = iota((p.share_rows, ln), 0) + (s * p.quarter + dp * p.share)

    def scatter(m):
        def step(i, carry):
            hot = []
            for k in range(2):
                hot.append(jnp.where(entry == r.ids_all[2 * i + k, pl.ds(m, 1), :], 1.0, 0.0).astype(BF))
            rows = r.de_all[m, pl.ds(2 * i, 2)].reshape(2 * ln, w)
            o_tab[...] += mm(jnp.concatenate(hot, 1), rows)[0 : p.share]
            return carry

        lax.fori_loop(0, n_dp // 2, step, 0)

    scatter(c)
    arrived(r.de_all.at[other], k_dex)
    scatter(other)
    n_pos = ln // n_dp
    here = pl.ds(pl.multiple_of(dp * n_pos, n_pos), n_pos)
    total = jnp.zeros((n_pos, w), F32)
    for m in range(2):
        for i in range(n_dp):
            total = total + r.de_all[m, i, here, :].astype(F32)
    o_pos[...] = total

    @pl.when(is_att)
    def _():
        mine = pl.ds(pl.multiple_of(z * p.in_rows, p.in_rows), p.in_rows)
        for j in (3, 0, 1, 2):
            cut = tile_cut(j)
            arrived(r.r_in.at[0, :, cut], k_in[j])
            arrived(r.r_in.at[1, :, cut], k_in[j] + 1)
            near_sum = r.wa[mine, cut].astype(F32) + r.r_in[0, :, cut].astype(F32)
            o_win[0, :, cut] = near_sum + r.r_in[1, :, cut].astype(F32)
        o_wout[...] = jnp.zeros(o_wout.shape, F32)

    @pl.when(is_ff)
    def _():
        for k in range(1, n_dp):
            src = lax.rem(dp + k, n_dp)
            arrived(r.r_col.at[src], k_col + src)
        for k in range(n_dp):
            o_win[0, :, k * p.out_rows : (k + 1) * p.out_rows] = r.r_col[k].astype(F32)

    for k in range(1, nz):
        src = lax.rem(z + k, nz)
        arrived(r.r_sm.at[src], k_smz + src)
    r.sm_all[...] = r.r_sm[0] + r.r_sm[1] + r.r_sm[2] + r.r_sm[3]
    mine = r.sm_all[pl.ds(dp, 1), :]
    n_b, n_w = ff // n_dp, w // n_dp
    o_bin[...] = mine[:, 0:n_b]
    o_bout[...] = mine[:, n_b : n_b + n_w]
    o_gain[...] = mine[:, n_b + 128 : n_b + 128 + n_w]
    o_shift[...] = mine[:, n_b + 256 : n_b + 256 + n_w]

    for cond, make in pending:
        if cond is None:
            make().wait_send()
        else:
            pl.when(cond)(lambda make=make: make().wait_send())
    assert sends.n <= SENDS and recvs.n <= RECVS, (sends.n, recvs.n)


def whole(
    n_dp,
    token_ids,
    segment_ids,
    masked_rows,
    embedding,
    pos_table,
    w_in,
    w_out,
    b_in,
    b_out,
    norm_gain,
    norm_shift,
    logit_grad,
):
    quarter, width = embedding.shape
    batches, _, length = token_ids.shape
    masks = masked_rows.shape[-1]
    ff = w_in.shape[-1]
    p = Plan(n_dp, length, width, ff, quarter, masks)
    scratch = scratch_list(p)
    shapes = [
        (batches, 1, masks, quarter),
        (p.share, width),
        (length // n_dp, width),
        (1, p.in_rows, ff),
        (1, p.out_rows, width),
        (1, ff // n_dp),
        (1, p.in_rows),
        (1, p.in_rows),
        (1, p.in_rows),
    ]
    vmem = pl.BlockSpec(memory_space=pltpu.VMEM)
    far = pl.BlockSpec(memory_space=pl.ANY)
    return pl.pallas_call(
        functools.partial(fused, p, list(scratch)),
        out_shape=[jax.ShapeDtypeStruct(shape, F32) for shape in shapes],
        in_specs=[vmem] * 9 + [far] * 3,
        out_specs=[vmem] * 9,
        scratch_shapes=[pltpu.VMEM(*one) for one in scratch.values()]
        + [
            pltpu.SemaphoreType.DMA((SENDS,)),
            pltpu.SemaphoreType.DMA((RECVS,)),
            pltpu.SemaphoreType.DMA((len(p.chunks) + 2,)),
        ],
        compiler_params=pltpu.CompilerParams(
            collective_id=0, has_side_effects=True, vmem_limit_bytes=VMEM_LIMIT
        ),
    )(
        token_ids,
        segment_ids,
        masked_rows,
        logit_grad,
        pos_table,
        b_in,
        b_out,
        norm_gain,
        norm_shift,
        embedding,
        w_in,
        w_out,
    )


def solution(mesh):
    n_section, n_dp = mesh.shape["section"], mesh.shape["dp"]

    def chosen_form(*args):
        token_ids, embedding, w_in = args[0], args[3], args[5]
        fits = (
            n_section == 4
            and n_dp == 8
            and token_ids.shape[0] == 2
            and token_ids.shape[1:] == (1, 128)
            and w_in.shape[1] % (16 * n_dp) == 0
            and w_in.shape[2] == 4 * w_in.shape[1]
            and embedding.shape[0] % (8 * n_dp) == 0
        )
        return whole(n_dp, *args) if fits else local(*args)

    placed = (
        P(None, "dp", None),
        P(None, "dp", None),
        P(None, "dp", None),
        P("section", None),
        P(),
        P("section", None, None),
        P("section", None, None),
        P("section", None),
        P("section", None),
        P("section", None),
        P("section", None),
        P(None, "dp", None, "section"),
    )
    return jax.shard_map(
        chosen_form,
        mesh=mesh,
        in_specs=placed,
        out_specs=(
            P(None, "dp", None, "section"),
            P(("section", "dp"), None),
            P("dp", None),
            P("section", "dp", None),
            P("section", "dp", None),
            P("section", "dp"),
            P("section", "dp"),
            P("section", "dp"),
            P("section", "dp"),
        ),
        check_vma=False,
    )
```

```python
import functools
import types

import jax
import jax.numpy as jnp
from jax import lax
from jax.experimental import pallas as pl
from jax.experimental.pallas import tpu as pltpu
from jax.sharding import PartitionSpec as P

HEADS = 12


EPSILON = 1e-12


def for_sending(array):
    return jax.tree.map(lambda a: a.astype(jnp.bfloat16) if a.dtype == jnp.float32 else a, array)


def passed_along(block, axis, distance):
    devices = range(lax.axis_size(axis))
    route = [(i - distance, i) for i in devices if i - distance in devices]
    return lax.ppermute(block, axis, route)


def broadcast(value, axis, source):
    kept = jnp.where(lax.axis_index(axis) == source, value, 0).astype(value.dtype)
    return lax.psum(kept, axis)


def norm_forward(resid, gain_row, shift_row):
    centre = jnp.mean(resid, -1, keepdims=True)
    centred = resid - centre
    inverse = lax.rsqrt(jnp.mean(centred * centred, -1, keepdims=True) + EPSILON)
    normed = centred * inverse
    return (normed * gain_row + shift_row, normed, inverse)


def norm_backward(upstream, normed, inverse, gain_row):
    gain_part = jnp.sum(upstream * normed, 0)
    shift_part = jnp.sum(upstream, 0)
    scaled = upstream * gain_row
    first_mean = jnp.mean(scaled, -1, keepdims=True)
    second_mean = jnp.mean(scaled * normed, -1, keepdims=True)
    return (inverse * (scaled - first_mean - normed * second_mean), gain_part, shift_part)


def to_heads(values):
    return values.reshape(values.shape[0], HEADS, values.shape[1] // HEADS)


def row_scores(query, keyed, segment):
    factor = (query.shape[1] // HEADS) ** (-0.5)
    scores = (
        jnp.einsum(
            "qhd,khd->hqk", to_heads(query), to_heads(keyed), preferred_element_type=jnp.float32
        )
        * factor
    )
    allowed = segment[:, None] == segment[None, :]
    return jnp.where(allowed[None], scores, -1000000000.0)


def attend_row(packed, segment):
    width = packed.shape[1] // 3
    scores = row_scores(packed[:, :width], packed[:, width : 2 * width], segment)
    row_peak = jnp.max(scores, -1, keepdims=True)
    exponent = jnp.exp(scores - row_peak)
    row_total = jnp.sum(exponent, -1, keepdims=True)
    chance = (exponent / row_total).astype(jnp.bfloat16)
    context = jnp.einsum(
        "hqk,khd->qhd", chance, to_heads(packed[:, 2 * width :]), preferred_element_type=jnp.float32
    )
    summary = (row_peak + jnp.log(row_total))[..., 0]
    return (context.reshape(packed.shape[0], width).astype(jnp.bfloat16), summary)


def attend_back(packed, segment, summary, upstream):
    length = packed.shape[0]
    width = packed.shape[1] // 3
    factor = (width // HEADS) ** (-0.5)
    scores = row_scores(packed[:, :width], packed[:, width : 2 * width], segment)
    chance = jnp.exp(scores - summary[..., None])
    grad_heads = to_heads(upstream)
    grad_chance = jnp.einsum(
        "qhd,khd->hqk",
        grad_heads,
        to_heads(packed[:, 2 * width :]),
        preferred_element_type=jnp.float32,
    )
    grad_value = jnp.einsum(
        "hqk,qhd->khd", chance.astype(jnp.bfloat16), grad_heads, preferred_element_type=jnp.float32
    )
    grad_score = chance * (grad_chance - jnp.sum(chance * grad_chance, -1, keepdims=True))
    grad_score = grad_score.astype(jnp.bfloat16)
    grad_query = (
        jnp.einsum(
            "hqk,khd->qhd",
            grad_score,
            to_heads(packed[:, width : 2 * width]),
            preferred_element_type=jnp.float32,
        )
        * factor
    )
    grad_key = (
        jnp.einsum(
            "hqk,qhd->khd",
            grad_score,
            to_heads(packed[:, :width]),
            preferred_element_type=jnp.float32,
        )
        * factor
    )
    joined = jnp.concatenate(
        [
            grad_query.reshape(length, width),
            grad_key.reshape(length, width),
            grad_value.reshape(length, width),
        ],
        1,
    )
    return joined.astype(jnp.bfloat16)


def attention_forward(inputs, segment, params):
    w_first, w_second, bias_first, bias_second, gain_row, shift_row = params
    rows_here, length, width = inputs.shape
    flat = inputs.reshape(rows_here * length, width)
    offset = jnp.concatenate(
        [bias_first[:width], jnp.zeros((width,), jnp.float32), bias_first[2 * width : 3 * width]]
    )
    packed = jnp.dot(flat, w_first[:, : 3 * width], preferred_element_type=jnp.float32) + offset
    packed = packed.astype(jnp.bfloat16).reshape(rows_here, length, 3 * width)
    context, summary = lax.map(lambda item: attend_row(item[0], item[1]), (packed, segment))
    branch = (
        jnp.dot(
            context.reshape(-1, width), w_first[:, 3 * width :], preferred_element_type=jnp.float32
        )
        + bias_second
    )
    result, normed, inverse = norm_forward(flat.astype(jnp.float32) + branch, gain_row, shift_row)
    return (result.reshape(rows_here, length, width), (packed, context, summary, normed, inverse))


def attention_backward(inputs, segment, upstream, params, totals):
    w_first, w_second, bias_first, bias_second, gain_row, shift_row = params
    rows_here, length, width = inputs.shape
    result, saved = attention_forward(inputs, segment, params)
    packed, context, summary, normed, inverse = saved
    flat = inputs.reshape(-1, width)
    grad_resid, gain_part, shift_part = norm_backward(
        upstream.reshape(-1, width), normed, inverse, gain_row
    )
    grad_branch = grad_resid.astype(jnp.bfloat16)
    grad_out_proj = jnp.einsum(
        "nd,ne->de", context.reshape(-1, width), grad_branch, preferred_element_type=jnp.float32
    )
    bias_second_part = jnp.sum(grad_branch.astype(jnp.float32), 0)
    grad_context = jnp.einsum(
        "ne,de->nd", grad_branch, w_first[:, 3 * width :], preferred_element_type=jnp.float32
    )
    grad_context = grad_context.astype(jnp.bfloat16).reshape(rows_here, length, width)
    grad_packed = lax.map(
        lambda item: attend_back(item[0], item[1], item[2], item[3]),
        (packed, segment, summary, grad_context),
    )
    flat_packed = grad_packed.reshape(-1, 3 * width)
    grad_proj = jnp.einsum("nd,nc->dc", flat, flat_packed, preferred_element_type=jnp.float32)
    bias_sums = jnp.sum(flat_packed.astype(jnp.float32), 0)
    grad_input = grad_resid + jnp.einsum(
        "nc,dc->nd", flat_packed, w_first[:, : 3 * width], preferred_element_type=jnp.float32
    )
    first_total, second_total, bias_first_total, bias_second_total, gain_total, shift_total = totals
    first_total = (
        first_total.at[:, : 3 * width].add(grad_proj).at[:, 3 * width :].add(grad_out_proj)
    )
    bias_first_total = (
        bias_first_total.at[:width]
        .add(bias_sums[:width])
        .at[2 * width : 3 * width]
        .add(bias_sums[2 * width :])
    )
    updated = (
        first_total,
        second_total,
        bias_first_total,
        bias_second_total + bias_second_part,
        gain_total + gain_part,
        shift_total + shift_part,
    )
    return (grad_input.reshape(rows_here, length, width).astype(jnp.bfloat16), updated)


def feed_forward(inputs, params):
    w_first, w_second, bias_first, bias_second, gain_row, shift_row = params
    rows_here, length, width = inputs.shape
    flat = inputs.reshape(-1, width)
    hidden = jnp.dot(flat, w_first, preferred_element_type=jnp.float32) + bias_first
    active = jax.nn.gelu(hidden, approximate=False).astype(jnp.bfloat16)
    branch = jnp.dot(active, w_second, preferred_element_type=jnp.float32) + bias_second
    result, normed, inverse = norm_forward(flat.astype(jnp.float32) + branch, gain_row, shift_row)
    return (result.reshape(rows_here, length, width), (hidden, active, normed, inverse))


def feed_backward(inputs, upstream, params, totals):
    w_first, w_second, bias_first, bias_second, gain_row, shift_row = params
    rows_here, length, width = inputs.shape
    result, saved = feed_forward(inputs, params)
    hidden, active, normed, inverse = saved
    flat = inputs.reshape(-1, width)
    grad_resid, gain_part, shift_part = norm_backward(
        upstream.reshape(-1, width), normed, inverse, gain_row
    )
    grad_branch = grad_resid.astype(jnp.bfloat16)
    grad_second = jnp.einsum("nf,nd->fd", active, grad_branch, preferred_element_type=jnp.float32)
    bias_second_part = jnp.sum(grad_branch.astype(jnp.float32), 0)
    grad_active = jnp.einsum("nd,fd->nf", grad_branch, w_second, preferred_element_type=jnp.float32)
    through = jax.vjp(lambda inner: jax.nn.gelu(inner, approximate=False), hidden)[1](grad_active)[
        0
    ]
    grad_hidden = through.astype(jnp.bfloat16)
    grad_first = jnp.einsum("nd,nf->df", flat, grad_hidden, preferred_element_type=jnp.float32)
    bias_first_part = jnp.sum(grad_hidden.astype(jnp.float32), 0)
    grad_input = grad_resid + jnp.einsum(
        "nf,df->nd", grad_hidden, w_first, preferred_element_type=jnp.float32
    )
    terms = (grad_first, grad_second, bias_first_part, bias_second_part, gain_part, shift_part)
    updated = tuple((total + term for total, term in zip(totals, terms)))
    return (grad_input.reshape(rows_here, length, width).astype(jnp.bfloat16), updated)


def local(
    token_ids,
    segment_ids,
    masked_rows,
    embedding,
    pos_table,
    w_in,
    w_out,
    b_in,
    b_out,
    norm_gain,
    norm_shift,
    logit_grad,
):
    sections = lax.axis_size("section")
    section_index = lax.axis_index("section")
    quarter, width = embedding.shape
    batches, rows_here, length = token_ids.shape
    params = (
        w_in[0],
        w_out[0],
        b_in[0].astype(jnp.float32),
        b_out[0].astype(jnp.float32),
        norm_gain[0].astype(jnp.float32),
        norm_shift[0].astype(jnp.float32),
    )
    local_ids = token_ids - section_index * quarter
    inside = (local_ids >= 0) & (local_ids < quarter)
    picked = jnp.take(embedding, jnp.clip(local_ids, 0, quarter - 1), axis=0)
    partial_rows = jnp.where(inside[..., None], picked.astype(jnp.float32), 0.0)
    looked = lax.psum(partial_rows.astype(jnp.bfloat16), "section").astype(jnp.float32)
    entry = (looked + pos_table.astype(jnp.float32)).astype(jnp.bfloat16)

    def spare_forward(inputs, segment):
        return jnp.zeros(inputs.shape, jnp.bfloat16)

    def attend_forward(inputs, segment):
        return attention_forward(inputs, segment, params)[0].astype(jnp.bfloat16)

    def feed_only(inputs, segment):
        return feed_forward(inputs, params)[0].astype(jnp.bfloat16)

    def spare_backward(inputs, segment, upstream, totals):
        return (jnp.zeros(inputs.shape, jnp.bfloat16), totals)

    def attend_backward(inputs, segment, upstream, totals):
        return attention_backward(inputs, segment, upstream, params, totals)

    def feed_back_only(inputs, segment, upstream, totals):
        return feed_backward(inputs, upstream, params, totals)

    ticks = batches + sections - 1
    kept = jnp.zeros_like(entry)
    outputs = jnp.zeros_like(entry)
    incoming = jnp.zeros_like(entry[0])
    for moment in range(ticks):
        micro_index = moment - section_index
        is_live = (micro_index >= 0) & (micro_index < batches)
        micro_slot = jnp.clip(micro_index, 0, batches - 1)
        current = jnp.where(section_index == 0, entry[micro_slot], incoming)
        kept = kept.at[micro_slot].set(jnp.where(is_live, current, kept[micro_slot]))
        branch_index = jnp.where(is_live, 1 + section_index % 2, 0)
        result = lax.switch(
            branch_index,
            [spare_forward, attend_forward, feed_only],
            current,
            segment_ids[micro_slot],
        )
        outputs = outputs.at[micro_slot].set(jnp.where(is_live, result, outputs[micro_slot]))
        if moment + 1 < ticks:
            incoming = jax.tree.map(
                lambda part, own: part.astype(own.dtype),
                passed_along(for_sending(result), "section", 1),
                result,
            )
    final_rows = jnp.take_along_axis(outputs, masked_rows[..., None], axis=2)
    head_rows = broadcast(final_rows, "section", sections - 1)
    logits = jnp.einsum("mrkd,vd->mrkv", head_rows, embedding, preferred_element_type=jnp.float32)
    partial_grad = jnp.einsum(
        "mrkv,vd->mrkd", logit_grad, embedding, preferred_element_type=jnp.float32
    )
    grad_rows = lax.psum(partial_grad.astype(jnp.bfloat16), "section").astype(jnp.float32)
    table_head = jnp.einsum(
        "mrkv,mrkd->vd", logit_grad, head_rows, preferred_element_type=jnp.float32
    )
    places = (masked_rows[..., None] == jnp.arange(length)[None, None, None, :]).astype(jnp.float32)
    top_grad = jnp.einsum("mrkl,mrkd->mrld", places, grad_rows, precision=lax.Precision.HIGHEST)
    gradients = (
        jnp.zeros(w_in.shape[1:], jnp.float32),
        jnp.zeros(w_out.shape[1:], jnp.float32),
        jnp.zeros(b_in.shape[1:], jnp.float32),
        jnp.zeros((width,), jnp.float32),
        jnp.zeros((width,), jnp.float32),
        jnp.zeros((width,), jnp.float32),
    )
    grad_entry = jnp.zeros_like(entry)
    back_in = jnp.zeros_like(entry[0])
    for moment in range(ticks):
        micro_index = moment - (sections - 1 - section_index)
        is_live = (micro_index >= 0) & (micro_index < batches)
        micro_slot = jnp.clip(micro_index, 0, batches - 1)
        upstream = jnp.where(
            section_index == sections - 1, top_grad[micro_slot], back_in.astype(jnp.float32)
        )
        branch_index = jnp.where(is_live, 1 + section_index % 2, 0)
        grad_input, gradients = lax.switch(
            branch_index,
            [spare_backward, attend_backward, feed_back_only],
            kept[micro_slot],
            segment_ids[micro_slot],
            upstream,
            gradients,
        )
        grad_entry = grad_entry.at[micro_slot].set(
            jnp.where(is_live, grad_input, grad_entry[micro_slot])
        )
        if moment + 1 < ticks:
            back_in = jax.tree.map(
                lambda part, own: part.astype(own.dtype),
                passed_along(for_sending(grad_input), "section", -1),
                grad_input,
            )
    input_grad = broadcast(grad_entry, "section", 0)
    input_wide = input_grad.astype(jnp.float32)
    pos_grad = jnp.sum(input_wide, (0, 1))
    targets = jnp.where(inside, local_ids, quarter).reshape(-1)
    table_input = jax.ops.segment_sum(
        input_wide.reshape(-1, width), targets, num_segments=quarter + 1
    )[:quarter]
    w_in_part, w_out_part, b_in_part, b_out_part, gain_part, shift_part = gradients
    reduced = (
        lax.psum_scatter(w_in_part, "dp", scatter_dimension=0, tiled=True),
        lax.psum_scatter(w_out_part, "dp", scatter_dimension=0, tiled=True),
        lax.psum_scatter(b_in_part, "dp", scatter_dimension=0, tiled=True),
        lax.psum_scatter(b_out_part, "dp", scatter_dimension=0, tiled=True),
        lax.psum_scatter(gain_part, "dp", scatter_dimension=0, tiled=True),
        lax.psum_scatter(shift_part, "dp", scatter_dimension=0, tiled=True),
        lax.psum_scatter(pos_grad, "dp", scatter_dimension=0, tiled=True),
        lax.psum_scatter(table_input + table_head, "dp", scatter_dimension=0, tiled=True),
    )
    table_grad = reduced[7]
    return (
        logits,
        table_grad,
        reduced[6],
        reduced[0][None],
        reduced[1][None],
        reduced[2][None],
        reduced[3][None],
        reduced[4][None],
        reduced[5][None],
    )


SENDS = 260
RECVS = 160
VMEM_LIMIT = 64 * 2**20
BF = jnp.bfloat16
F32 = jnp.float32
MESH = pl.DeviceIdType.MESH


def mm(a, b):
    return jnp.dot(a, b, preferred_element_type=F32)


def mm_nt(a, b):
    return lax.dot_general(a, b, (((1,), (1,)), ((), ())), preferred_element_type=F32)


def mm_tn(a, b):
    return lax.dot_general(a, b, (((0,), (0,)), ((), ())), preferred_element_type=F32)


def iota(shape, dim):
    return lax.broadcasted_iota(jnp.int32, shape, dim)


def column(row):
    return jnp.broadcast_to(row.astype(F32), (128, 128)).T


class Plan:
    def __init__(self, n_dp, length, width, ff, quarter, masks):
        self.n_dp, self.length, self.width, self.ff = n_dp, length, width, ff
        self.quarter, self.masks = quarter, masks
        self.nz = n_dp // 2
        self.share = quarter // n_dp
        self.in_rows = width // n_dp
        self.out_rows = ff // n_dp
        self.mask_pad = -(-masks // 16) * 16
        self.share_pad = -(-self.share // 128) * 128
        self.share_rows = -(-self.share // 16) * 16
        self.chunks = []
        at = 0
        while at < quarter:
            size = min(1024, quarter - at)
            self.chunks.append((at, size))
            at += size


class Counter:
    def __init__(self):
        self.n = 0

    def take(self, k=1):
        first = self.n
        self.n += k
        return first


def scratch_list(p):
    w, ff, ln = p.width, p.ff, p.length
    mp = p.mask_pad
    return dict(
        emb=((p.quarter, w), BF),
        lg=((2, 1, p.masks, p.quarter), BF),
        pos=((ln, w), BF),
        wa=((w, ff), BF),
        w1=((w, ff), BF),
        w2=((ff, w), BF),
        par_a=((8, ff), F32),
        par_f=((8, ff), F32),
        acc=((2 * ln, w), F32),
        psend=((ln, w), BF),
        psum=((ln, w), BF),
        prow=((2, ln, w), BF),
        lgp=((2 * mp, p.quarter), BF),
        lgs=((p.n_dp, 2 * p.masks, p.share_pad), BF),
        lgr=((p.n_dp, 2 * p.masks, p.share_pad), BF),
        ch_pack=((p.n_dp, 2 * p.masks, w), BF),
        g=((2 * mp, w), F32),
        grow=((2, p.masks, w), F32),
        gwide=((ln, w), F32),
        mrow=((8, ln), jnp.int32),
        ids_own=((8, ln), jnp.int32),
        ids_all=((p.n_dp, 8, ln), jnp.int32),
        x_a=((ln, w), BF),
        x_f=((ln, w), BF),
        y_f=((ln, w), BF),
        y_o=((ln, w), BF),
        pk=((ln, 3 * w), BF),
        ctx=((ln, w), BF),
        probs=((w // 128, ln, 256), F32),
        n_a=((ln, w), F32),
        n_f=((ln, w), F32),
        inv_a=((ln, 1), F32),
        inv_f=((ln, 1), F32),
        slope=((ln, ff), BF),
        xt_a=((p.nz, 2, p.in_rows, ln), BF),
        ct_a=((p.nz, 2, p.in_rows, ln), BF),
        dyin=((ln, w), BF),
        dyf=((ln, w), F32),
        dres=((ln, w), F32),
        dbr_a=((ln, w), BF),
        dpk=((ln, 3 * w), BF),
        dctx=((ln, w), BF),
        dx=((ln, w), BF),
        bsum=((1, ff), F32),
        vecs=((8, w), F32),
        sm_a=((8, w), F32),
        sm_f=((8, w), F32),
        b_ctx=((p.nz, p.in_rows, 4 * ln), BF),
        b_x=((p.nz, p.in_rows, 4 * ln), BF),
        b_dbr=((4 * ln, w), BF),
        b_dh=((4 * ln, 3 * w), BF),
        b_sm=((4, 8, w), F32),
        sm_tot=((8, w), F32),
        sm_all=((8, w), F32),
        r_sm=((p.nz, 8, w), F32),
        r_in=((4, p.in_rows, ff), BF),
        x_all=((2, p.nz, 2, ln, w), BF),
        db_all=((2, p.nz, 2, ln, w), BF),
        w_col=((w, p.out_rows), F32),
        w_send=((p.n_dp, p.in_rows, p.out_rows), BF),
        r_col=((p.n_dp, p.in_rows, p.out_rows), BF),
        ch_own=((mp, w), BF),
        ch_two=((mp, w), BF),
        ch_all=((2, p.n_dp, mp, w), BF),
        de_all=((2, p.n_dp, ln, w), BF),
        u_out=((p.out_rows, w), F32),
        o_log=((2, 1, p.masks, p.quarter), BF),
        o_tab=((p.share, w), F32),
        o_pos=((ln // p.n_dp, w), F32),
        o_win=((1, p.in_rows, ff), BF),
        o_wout=((1, p.out_rows, w), BF),
    )


def fused(p, names, *refs):
    (tok, seg, picks, b_in, b_out, gain, shift, lg_h, pos_h, emb_h, w_in_h, w_out_h) = refs[:12]
    outs = refs[12:18]
    r = types.SimpleNamespace(**dict(zip(names, refs[18:])))
    ss, rs, ls, os = refs[18 + len(names) :]
    (o_log, o_tab, o_pos, o_win, o_wout, o_vec) = (r.o_log, r.o_tab, r.o_pos, r.o_win, r.o_wout, r.sm_all)
    w, ff, ln, mp, nz, n_dp = p.width, p.ff, p.length, p.mask_pad, p.nz, p.n_dp
    heads = w // 64
    pairs = heads // 2

    s = lax.axis_index("section")
    dp = lax.axis_index("dp")
    x, c = s // 2, lax.rem(s, 2)
    z, y = dp // 2, lax.rem(dp, 2)
    core = s + 1 - 2 * c
    across = s + 2 - 4 * x
    ydp = dp + 1 - 2 * y
    other = 1 - c
    at_x0, at_x1 = x == 0, x == 1
    is_att, is_ff = c == 0, c == 1
    sends, recvs = Counter(), Counter()
    pending = []

    def send(cond, src, dst, dev, recv):
        slot = sends.take()

        def make():
            return pltpu.make_async_remote_copy(
                src_ref=src,
                dst_ref=dst,
                send_sem=ss.at[slot],
                recv_sem=rs.at[recv],
                device_id=dev,
                device_id_type=MESH,
            )

        if cond is None:
            make().start()
        else:

            @pl.when(cond)
            def _():
                make().start()

        pending.append((cond, make))

    def arrived(dst, recv):
        pltpu.make_async_remote_copy(
            src_ref=dst,
            dst_ref=dst,
            send_sem=ss.at[0],
            recv_sem=rs.at[recv],
            device_id=(core, dp),
            device_id_type=MESH,
        ).wait_recv()

    for i, (at, size) in enumerate(p.chunks):
        pltpu.make_async_copy(emb_h.at[pl.ds(at, size)], r.emb.at[pl.ds(at, size)], ls.at[i]).start()
    l_w = len(p.chunks)
    lg, pos = r.lg, r.pos
    pltpu.make_async_copy(lg_h, lg, ls.at[l_w + 2]).start()
    pltpu.make_async_copy(pos_h, pos, ls.at[l_w + 3]).start()

    @pl.when(is_att)
    def _():
        pltpu.make_async_copy(w_in_h.at[0], r.wa, ls.at[l_w]).start()

    @pl.when(is_ff)
    def _():
        pltpu.make_async_copy(w_in_h.at[0], r.w1, ls.at[l_w]).start()
        pltpu.make_async_copy(w_out_h.at[0], r.w2, ls.at[l_w + 1]).start()

    def fill(par):
        par[0:1, :] = b_in[...].astype(F32)
        par[1:2, 0:w] = b_out[...].astype(F32)
        par[2:3, 0:w] = gain[...].astype(F32)
        par[3:4, 0:w] = shift[...].astype(F32)

    pl.when(is_att)(lambda: fill(r.par_a))
    pl.when(is_ff)(lambda: fill(r.par_f))

    barrier = pltpu.get_barrier_semaphore()
    peers = [(s, lax.rem(dp + k, n_dp)) for k in range(1, n_dp)]
    peers += [(core, dp), (across, dp), (3 - s, dp), (core, ydp)]
    for peer in peers:
        pl.semaphore_signal(barrier, inc=1, device_id=peer, device_id_type=MESH)

    cols = [column(tok[m]) for m in range(2)]
    first = s * p.quarter
    for i, (at, size) in enumerate(p.chunks):
        pltpu.make_async_copy(emb_h.at[pl.ds(at, size)], r.emb.at[pl.ds(at, size)], ls.at[i]).wait()
        lane = (iota((ln, size), 1) + (first + at)).astype(F32)
        hot = []
        for m in range(2):
            wide = jnp.concatenate([cols[m]] * (-(-size // 128)), 1)[:, :size]
            hot.append(jnp.where(wide == lane, 1.0, 0.0).astype(BF))
        part = mm(jnp.concatenate(hot, 0), r.emb[at : at + size, :])
        if i == 0:
            r.acc[...] = part
        else:
            r.acc[...] += part
    r.psend[...] = r.acc[pl.ds(pl.multiple_of(ln * other, ln), ln), :].astype(BF)

    tiles = ff // w
    k_p, k_g = recvs.take(2), recvs.take(2)
    k_pa, k_pf, k_wa, k_w1, k_w2 = recvs.take(), recvs.take(), recvs.take(tiles), recvs.take(tiles), recvs.take(tiles)
    pl.semaphore_wait(barrier, len(peers))
    send(None, r.psend, r.prow.at[0], (core, dp), k_p)


    pltpu.make_async_copy(lg_h, lg, ls.at[l_w + 2]).wait()
    pltpu.make_async_copy(pos_h, pos, ls.at[l_w + 3]).wait()
    r.lgp[...] = jnp.zeros(r.lgp.shape, BF)
    r.lgp[0 : p.masks] = lg[0, 0]
    r.lgp[mp : mp + p.masks] = lg[1, 0]

    k_lg, k_id = recvs.take(n_dp), recvs.take(n_dp)
    for j in range(n_dp):
        r.lgs[j, :, p.share :] = jnp.zeros((2 * p.masks, p.share_pad - p.share), BF)
        for m in range(2):
            r.lgs[j, p.masks * m : p.masks * (m + 1), 0 : p.share] = lg[m, 0, :, p.share * j : p.share * (j + 1)]
    r.ids_own[...] = jnp.zeros(r.ids_own.shape, jnp.int32)
    for m in range(2):
        r.ids_own[m : m + 1, :] = tok[m]
    r.ids_all[dp] = r.ids_own[...]
    r.lgr[dp] = r.lgs[dp]
    for k in range(1, n_dp):
        to = lax.rem(dp + k, n_dp)
        send(None, r.lgs.at[to], r.lgr.at[dp], (s, to), k_lg + dp)
        send(None, r.ids_own, r.ids_all.at[dp], (s, to), k_id + dp)
    arrived(r.prow.at[0], k_p)
    own_rows = r.acc[pl.ds(pl.multiple_of(ln * c, ln), ln), :]
    r.acc[0:ln, :] = own_rows + r.prow[0].astype(F32)
    r.psum[...] = r.acc[0:ln, :].astype(BF)
    send(at_x1, r.psum, r.prow.at[1], (across, dp), k_p + 1)

    def weights(cond):
        send(is_att & cond, r.par_a, r.par_a, (core, dp), k_pa)
        send(is_ff & cond, r.par_f, r.par_f, (core, dp), k_pf)
        for j in range(tiles):
            cut = slice(j * w, (j + 1) * w)
            send(is_att & cond, w_in_h.at[0, :, cut], r.wa.at[:, cut], (core, dp), k_wa + j)
            send(is_ff & cond, w_in_h.at[0, :, cut], r.w1.at[:, cut], (core, dp), k_w1 + j)
            send(is_ff & cond, w_out_h.at[0, cut, :], r.w2.at[cut, :], (core, dp), k_w2 + j)

    weights(at_x0)

    for i, (at, size) in enumerate(p.chunks):
        part = mm(r.lgp[:, at : at + size], r.emb[at : at + size, :])
        if i == 0:
            r.g[...] = part
        else:
            r.g[...] += part
    send(None, r.g.at[pl.ds(pl.multiple_of(mp * other, mp), p.masks)], r.grow.at[0], (core, dp), k_g)

    def masked_gradient():
        arrived(r.grow.at[0], k_g)
        r.gwide[...] = jnp.zeros(r.gwide.shape, F32)
        r.gwide[0 : p.masks, :] = r.g[pl.ds(pl.multiple_of(mp * c, mp), p.masks), :] + r.grow[0]

    pl.when(at_x1)(masked_gradient)
    weights(at_x1)

    k_x = recvs.take()

    @pl.when(at_x0)
    def _():
        arrived(r.prow.at[1], k_p + 1)
        whole = r.acc[0:ln, :] + r.prow[1].astype(F32)
        r.x_a[...] = (whole + pos[...].astype(F32)).astype(BF)

    @pl.when(is_att)
    def _():
        pltpu.make_async_copy(w_in_h.at[0], r.wa, ls.at[l_w]).wait()
        arrived(r.par_f, k_pf)

    @pl.when(is_ff)
    def _():
        pltpu.make_async_copy(w_in_h.at[0], r.w1, ls.at[l_w]).wait()
        pltpu.make_async_copy(w_out_h.at[0], r.w2, ls.at[l_w + 1]).wait()
        arrived(r.par_a, k_pa)

    @pl.when(at_x1)
    def _():
        arrived(r.x_a, k_x)

    low = jnp.where(iota((ln, 128), 1) < 64, 1.0, 0.0).astype(BF)
    high = jnp.where(iota((ln, 128), 1) < 64, 0.0, 1.0).astype(BF)

    def split(block):
        return jnp.concatenate([block * low, block * high], 0)

    def stack(block):
        return jnp.concatenate([block[:, 0:128], block[:, 128:256]], 0)

    def norm_forward(resid, par):
        centred = resid - jnp.mean(resid, -1, keepdims=True)
        inverse = lax.rsqrt(jnp.mean(centred * centred, -1, keepdims=True) + EPSILON)
        normed = centred * inverse
        return (normed * par[2:3, 0:w] + par[3:4, 0:w]).astype(BF), normed, inverse

    rows_x = r.x_a[...]

    def wa_tile(j):
        pl.when(is_ff)(lambda: arrived(r.wa.at[:, j * w : (j + 1) * w], k_wa + j))

    for j in range(3):
        wa_tile(j)
        part = mm(rows_x, r.wa[:, j * w : (j + 1) * w])
        if j != 1:
            part = part + r.par_a[0:1, j * w : (j + 1) * w]
        r.pk[:, j * w : (j + 1) * w] = part.astype(BF)
    seg_row = seg[c].astype(F32)
    seg_col = column(seg[c])
    seg_row = jnp.broadcast_to(jnp.concatenate([seg_row, seg_row], 1), (ln, 256))
    seg_col = jnp.concatenate([seg_col, seg_col], 1)
    for h in range(pairs):
        at = 128 * h
        query = r.pk[:, at : at + 128]
        keyed = split(r.pk[:, w + at : w + at + 128])
        value = split(r.pk[:, 2 * w + at : 2 * w + at + 128])
        scores = jnp.where(seg_row == seg_col, mm_nt(query, keyed) * 0.125, -1e9)
        chance = []
        for half in (scores[:, 0:128], scores[:, 128:256]):
            power = jnp.exp(half - jnp.max(half, -1, keepdims=True))
            chance.append(power / jnp.sum(power, -1, keepdims=True))
        chance = jnp.concatenate(chance, 1)
        r.probs[h] = chance
        r.ctx[:, at : at + 128] = mm(chance.astype(BF), value).astype(BF)
    wa_tile(3)
    resid = rows_x.astype(F32) + mm(r.ctx[...], r.wa[:, 3 * w : 4 * w]) + r.par_a[1:2, 0:w]
    r.x_f[...], r.n_a[...], r.inv_a[...] = norm_forward(resid, r.par_a)

    def line(buf, base, cond=True, owner=None):
        own = buf(dp)
        send(cond & (z < nz - 1), own, own, (s, dp + 2), base + dp)
        send(cond & (z > 0), own, own, (s, dp - 2), base + dp)
        to_y(buf, base, dp, cond, owner)

    def to_y(buf, base, i, cond, owner):
        piece = buf(i)
        if owner is None:
            send(None if cond is True else cond, piece, piece, (s, ydp), base + i)
        else:
            whose = jnp.where(is_att, core, s)
            send(None if cond is True else cond, piece, piece, (whose, ydp), jnp.where(is_att, owner, base) + i)
            send(is_att & cond, piece, piece, (core, dp), owner + i)

    def line_step(buf, base, t, cond=True, owner=None):
        for sign in (-1, 1):
            from_z = z + sign * t
            here = (from_z >= 0) & (from_z < nz) & cond
            from_dp = jnp.clip(from_z, 0, nz - 1) * 2 + y
            piece = buf(from_dp)
            pl.when(here)(lambda piece=piece, from_dp=from_dp: arrived(piece, base + from_dp))
            to_z = z - sign
            on = here & (to_z >= 0) & (to_z < nz)
            if t < nz - 1:
                send(on, piece, piece, (s, dp - 2 * sign), base + from_dp)
            to_y(buf, base, from_dp, here, owner)

    def line_y(buf, base, t):
        for sign in (-1, 1) if t else (1,):
            from_z = z + sign * t
            from_dp = jnp.clip(from_z, 0, nz - 1) * 2 + 1 - y
            pl.when((from_z >= 0) & (from_z < nz))(lambda i=from_dp: arrived(buf(i), base + i))

    def pair_line(buf, base, cond, i):
        piece = buf(i)
        send(cond & (z < nz - 1), piece, piece, (s, dp + 2), base + i)
        send(cond & (z > 0), piece, piece, (s, dp - 2), base + i)

    def pair_step(buf, base, t, cond, on_x):
        for sign in (-1, 1):
            from_z = z + sign * t
            here = (from_z >= 0) & (from_z < nz) & cond
            for side in (0, 1):
                from_dp = jnp.clip(from_z, 0, nz - 1) * 2 + (1 - y if side else y)
                piece = buf(from_dp)
                pl.when(here)(lambda piece=piece, from_dp=from_dp: arrived(piece, base + from_dp))
                if t < nz - 1:
                    on = here & (z - sign >= 0) & (z - sign < nz)
                    send(on, piece, piece, (s, dp - 2 * sign), base + from_dp)
                send(here, piece, piece, (across, dp), on_x + from_dp)

    def ch(i):
        return r.ch_all.at[c, i]

    def de(i):
        return r.de_all.at[c, i]

    def xs(i):
        return r.x_all.at[c, i // 2, lax.rem(i, 2)]

    def db(i):
        return r.db_all.at[c, i // 2, lax.rem(i, 2)]

    k_ch, k_de, k_xs, k_db = (recvs.take(n_dp) for _ in range(4))
    k_cho, k_chc, k_cha, k_chx, k_dex = (recvs.take() for _ in range(5))
    k_xsc, k_dbc = recvs.take(n_dp), recvs.take(n_dp)

    r.x_all[c, z, y] = r.x_f[...]
    line(xs, k_xs, True, k_xsc)

    def feed(rows_x, keep=True):
        total = rows_x.astype(F32) + r.par_f[1:2, 0:w]
        for j in range(tiles):
            cut = slice(j * w, (j + 1) * w)

            @pl.when(is_att)
            def _():
                arrived(r.w1.at[:, cut], k_w1 + j)
                arrived(r.w2.at[cut, :], k_w2 + j)

            hidden = mm(rows_x, r.w1[:, cut]) + r.par_f[0:1, cut]
            below = 0.5 + 0.5 * lax.erf(hidden * (0.5**0.5))
            total = total + mm((hidden * below).astype(BF), r.w2[cut, :])
            if keep:
                slope = below + hidden * (0.3989422804014327 * jnp.exp(-0.5 * hidden * hidden))
                r.slope[:, cut] = slope.astype(BF)
        result, normed, inverse = norm_forward(total, r.par_f)
        if keep:
            r.y_f[...], r.n_f[...], r.inv_f[...] = result, normed, inverse
        else:
            r.y_o[...] = result

    pl.when(is_ff | at_x1)(lambda: feed(r.x_f[...]))
    send(at_x0 & is_ff, r.y_f, r.x_a, (across, dp), k_x)

    @pl.when(at_x0 & is_ff)
    def _():
        arrived(r.x_all.at[0, z, y], k_xsc + dp)
        feed(r.x_all[0, z, y], False)

    send(at_x0 & is_ff, r.y_o, r.x_a, (3 - s, dp), k_x)

    @pl.when(at_x1)
    def _():
        r.mrow[...] = jnp.full(r.mrow.shape, -1, jnp.int32)
        r.mrow[0:1, 0 : p.masks] = picks[c]
        places = jnp.where(iota((ln, ln), 0) == r.mrow[0:1, :], 1.0, 0.0).astype(BF)
        r.ch_own[...] = mm_tn(places, r.y_f[...])[0:mp].astype(BF)
        arrived(r.grow.at[1], k_g + 1)
        r.gwide[0 : p.masks, :] += r.grow[1]
        coarse = r.gwide[...].astype(BF)
        fine = (r.gwide[...] - coarse.astype(F32)).astype(BF)
        r.dyf[...] = mm(places, coarse) + mm(places, fine)

    send(at_x1, r.ch_own, r.ch_own, (across, dp), k_cho)
    send(at_x1, r.ch_own, r.ch_two, (core, dp), k_chc)

    def push(owner, kind, src, dst, cond=None):
        home = c == owner
        slot_y = 2 + jnp.where(home, 0, 1)
        own_dst, near_dst, far_dst = dst(0), dst(1), dst(slot_y)

        away = jnp.logical_not(home)

        @pl.when(home if cond is None else home & cond)
        def _():
            pltpu.make_async_copy(src(y), own_dst, rs.at[kind]).start()

        send(away if cond is None else away & cond, src(y), near_dst, (core, dp), kind + 1)
        far_s = jnp.where(home, s, core)
        send(cond, src(1 - y), far_dst, (far_s, ydp), kind + slot_y)

    def gathered(kind, dst):
        pltpu.make_async_copy(dst(0), dst(0), rs.at[kind]).wait()
        for slot in range(1, 4):
            arrived(dst(slot), kind + slot)

    def lanes(slot):
        return pl.ds(slot * ln if isinstance(slot, int) else pl.multiple_of(slot * ln, ln), ln)

    k_dh = [recvs.take(4) for _ in range(3)]
    k_ctx, k_xt, k_dba, k_sm = (recvs.take(4) for _ in range(4))
    to_x = lambda slot: r.b_x.at[:, :, lanes(slot)]
    to_ctx = lambda slot: r.b_ctx.at[:, :, lanes(slot)]
    to_dbr = lambda slot: r.b_dbr.at[lanes(slot), :]
    to_sm = lambda slot: r.b_sm.at[slot]

    def to_dh(j):
        return lambda slot: r.b_dh.at[lanes(slot), j * w : (j + 1) * w]

    def push_dh(j):
        push(0, k_dh[j], lambda i: r.dpk.at[:, j * w : (j + 1) * w], to_dh(j))

    def push_rows(cond):
        push(0, k_xt, lambda i: r.xt_a.at[:, i], to_x, cond)
        push(0, k_ctx, lambda i: r.ct_a.at[:, i], to_ctx, cond)

    def turn():
        for dst, src in ((r.xt_a, r.x_a), (r.ct_a, r.ctx)):
            turned = src[...].T
            for b in range(n_dp):
                dst[b // 2, b % 2] = turned[b * p.in_rows : (b + 1) * p.in_rows]

    @pl.when(at_x0)
    def _():
        masked_gradient()
        turn()

    send(at_x0, r.gwide.at[0 : p.masks], r.grow.at[1], (across, dp), k_g + 1)
    push_rows(at_x0)

    @pl.when(at_x0 & is_att)
    def _():
        feed(r.x_f[...])

    line_step(xs, k_xs, 1, at_x0, k_xsc)
    line_step(xs, k_xs, 2, at_x0, k_xsc)

    @pl.when(at_x0)
    def _():
        arrived(r.ch_own, k_cho)
        r.ch_all[c, dp] = r.ch_own[...]

    send(at_x0, r.ch_own, r.ch_two, (core, dp), k_chc)
    for k in range(1, n_dp):
        send(at_x0, r.ch_own, ch(dp), (s, lax.rem(dp + k, n_dp)), k_ch + dp)

    def emit(i, src):
        pltpu.make_async_copy(src, outs[i], os.at[i]).start()

    def logits():
        arrived(r.ch_two, k_chc)
        chosen = jnp.concatenate([r.ch_own[...], r.ch_two[...]], 0)
        for at, size in p.chunks:
            part = mm_nt(chosen, r.emb[at : at + size, :])
            o_log[c, 0, :, at : at + size] = part[0 : p.masks].astype(BF)
            o_log[other, 0, :, at : at + size] = part[mp : mp + p.masks].astype(BF)
        emit(0, o_log)

    pl.when(at_x0)(logits)

    k_dy = recvs.take()

    @pl.when(at_x0)
    def _():
        arrived(r.dyin, k_dy)
        r.dyf[...] = r.dyin[...].astype(F32)

    def norm_backward(par, n_ref, inv_ref):
        up, normed = r.dyf[...], n_ref[...]
        gain_part = jnp.sum(up * normed, 0, keepdims=True)
        shift_part = jnp.sum(up, 0, keepdims=True)
        scaled = up * par[2:3, 0:w]
        first_mean = jnp.mean(scaled, -1, keepdims=True)
        second_mean = jnp.mean(scaled * normed, -1, keepdims=True)
        return inv_ref[...] * (scaled - first_mean - normed * second_mean), gain_part, shift_part

    def small(dst, out_part, gain_part, shift_part):
        dst[...] = jnp.zeros(dst.shape, F32)
        n_b, n_w = ff // n_dp, w // n_dp
        for k in range(n_dp):
            dst[k : k + 1, 0:n_b] = r.bsum[:, k * n_b : (k + 1) * n_b]
            dst[k : k + 1, n_b : n_b + n_w] = out_part[:, k * n_w : (k + 1) * n_w]
            dst[k : k + 1, n_b + 128 : n_b + 128 + n_w] = gain_part[:, k * n_w : (k + 1) * n_w]
            dst[k : k + 1, n_b + 256 : n_b + 256 + n_w] = shift_part[:, k * n_w : (k + 1) * n_w]

    dres, gain_part, shift_part = norm_backward(r.par_f, r.n_f, r.inv_f)
    r.dres[...] = dres
    r.db_all[c, z, y] = dres.astype(BF)
    line(db, k_db, True, k_dbc)
    branch = r.db_all[c, z, y]
    total = r.dres[...]
    for j in range(tiles):
        cut = slice(j * w, (j + 1) * w)
        dhidden = (mm_nt(branch, r.w2[cut, :]) * r.slope[:, cut].astype(F32)).astype(BF)
        r.bsum[:, cut] = jnp.sum(dhidden.astype(F32), 0, keepdims=True)
        total = total + mm_nt(dhidden, r.w1[:, cut])
    r.dyf[...] = total.astype(BF).astype(F32)
    r.vecs[0:1], r.vecs[1:2] = gain_part, shift_part
    line_step(xs, k_xs, 1, at_x1, k_xsc)

    dres, gain_part, shift_part = norm_backward(r.par_a, r.n_a, r.inv_a)
    r.dres[...] = dres
    r.dbr_a[...] = dres.astype(BF)
    branch = r.dbr_a[...]
    r.dctx[...] = mm_nt(branch, r.wa[:, 3 * w : 4 * w]).astype(BF)
    for h in range(pairs):
        at = 128 * h
        query = r.pk[:, at : at + 128]
        keyed = split(r.pk[:, w + at : w + at + 128])
        value = split(r.pk[:, 2 * w + at : 2 * w + at + 128])
        upper = r.dctx[:, at : at + 128]
        chance = r.probs[h]
        dchance = mm_nt(upper, value)
        mixed = chance * dchance
        dscores = []
        for cut in (slice(0, 128), slice(128, 256)):
            dscores.append(mixed[:, cut] - chance[:, cut] * jnp.sum(mixed[:, cut], -1, keepdims=True))
        dscores = jnp.concatenate(dscores, 1).astype(BF)
        r.dpk[:, at : at + 128] = (mm(dscores, keyed) * 0.125).astype(BF)
        r.dpk[:, w + at : w + at + 128] = (mm_tn(stack(dscores), split(query)) * 0.125).astype(BF)
        r.dpk[:, 2 * w + at : 2 * w + at + 128] = mm_tn(stack(chance.astype(BF)), split(upper)).astype(BF)
    total = r.dres[...]
    for j in range(3):
        cut = slice(j * w, (j + 1) * w)
        total = total + mm_nt(r.dpk[:, cut], r.wa[:, cut])
    r.dx[...] = total.astype(BF)
    send(at_x1, r.dx, r.dyin, (across, dp), k_dy)

    gathers = c == 1 - x

    @pl.when(at_x0)
    def _():
        r.de_all[c, dp] = r.dx[...]

    on_0, on_1 = at_x0 & is_ff, at_x1 & is_att
    send(at_x0, de(dp), de(dp), (s, ydp), k_de + dp)
    send(at_x0, de(dp), de(dp), (across, dp), k_de + dp)
    pair_line(de, k_de, on_0, dp)

    line_step(xs, k_xs, 2, at_x1, k_xsc)
    line_step(db, k_db, 1, True, k_dbc)
    line_step(xs, k_xs, 3, at_x0, k_xsc)

    @pl.when(at_x0)
    def _():
        arrived(de(ydp), k_de + ydp)

    send(at_x0, de(ydp), de(ydp), (across, dp), k_de + ydp)
    pair_line(de, k_de, on_0, ydp)
    pl.when(at_x1)(turn)
    push_rows(at_x1)
    push(0, k_dba, lambda i: r.dbr_a, to_dbr)
    push_dh(0)
    small(r.sm_f, jnp.sum(r.db_all[c, z, y].astype(F32), 0, keepdims=True), r.vecs[0:1], r.vecs[1:2])
    push(1, k_sm, lambda i: r.sm_f, to_sm)

    @pl.when(at_x0)
    def _():
        for k in range(1, n_dp):
            arrived(ch(lax.rem(dp + k, n_dp)), k_ch + lax.rem(dp + k, n_dp))

    send(at_x0, r.ch_all.at[c], r.ch_all.at[c], (across, dp), k_cha)
    send(at_x0, r.ch_all.at[c], r.ch_all.at[c], (core, dp), k_chx)
    r.bsum[...] = jnp.zeros(r.bsum.shape, F32)
    for j in (0, 2):
        cut = slice(j * w, (j + 1) * w)
        r.bsum[:, cut] = jnp.sum(r.dpk[:, cut].astype(F32), 0, keepdims=True)
    small(r.sm_a, jnp.sum(branch.astype(F32), 0, keepdims=True), gain_part, shift_part)
    push(0, k_sm, lambda i: r.sm_a, to_sm)
    line_step(xs, k_xs, 3, at_x1, k_xsc)
    line_step(db, k_db, 2, True, k_dbc)
    push_dh(1)
    pair_step(de, k_de, 1, on_0, k_de)
    line_step(db, k_db, 3, True, k_dbc)
    push_dh(2)
    pair_step(de, k_de, 2, on_0, k_de)
    pair_step(de, k_de, 3, on_0, k_de)

    def head_part():
        arrived(r.ch_all.at[other], k_chx)
        for k in range(1, n_dp):
            src = lax.rem(dp + k, n_dp)
            arrived(r.lgr.at[src], k_lg + src)
            arrived(r.ids_all.at[src], k_id + src)
        for i in range(n_dp):
            for m in range(2):
                r.ch_pack[i, p.masks * m : p.masks * (m + 1)] = r.ch_all[m, i, 0 : p.masks]
        lines = 2 * n_dp * p.masks
        grad = mm_tn(r.lgr[...].reshape(lines, p.share_pad), r.ch_pack[...].reshape(lines, w))
        o_tab[...] = grad[0 : p.share]

    @pl.when(on_1)
    def _():
        arrived(de(dp), k_de + dp)

    pair_line(de, k_de, on_1, dp)

    @pl.when(on_1)
    def _():
        arrived(de(ydp), k_de + ydp)

    pair_line(de, k_de, on_1, ydp)
    pl.when(at_x1)(logits)
    pair_step(de, k_de, 1, on_1, k_de)
    pair_step(de, k_de, 2, on_1, k_de)

    k_in = [recvs.take(4) for _ in range(tiles)]
    half = nz * p.in_rows
    outer = (z == 0) | (z == nz - 1)
    mate = z + 1 - 2 * lax.rem(z, 2)
    far_base = 2 - 2 * (z // 2)

    def shard(zz, cut):
        return r.wa.at[pl.ds(pl.multiple_of(zz * p.in_rows, p.in_rows), p.in_rows), cut]

    def tile_cut(j):
        return slice(j * w, (j + 1) * w)

    def attention_tile(j):
        cut = tile_cut(j)

        @pl.when(is_att)
        def _():
            if j == 3:
                gathered(k_ctx, to_ctx)
                gathered(k_dba, to_dbr)
                grad = mm(r.b_ctx[...].reshape(half, 4 * ln), r.b_dbr[...])
            else:
                if j == 0:
                    gathered(k_xt, to_x)
                gathered(k_dh[j], to_dh(j))
                grad = mm(r.b_x[...].reshape(half, 4 * ln), r.b_dh[:, cut])
            r.wa[0:half, cut] = grad.astype(BF)

        to_mate = (s, 2 * mate + y)
        for k in range(2):
            send(is_att & outer, shard(far_base + k, cut), r.r_in.at[2 + k, :, cut], to_mate, k_in[j] + 2 + k)
        send(is_att, shard(mate, cut), r.r_in.at[0, :, cut], to_mate, k_in[j])

    def attention_sum(j):
        cut = tile_cut(j)
        inner = is_att & jnp.logical_not(outer)
        for k in range(2):

            @pl.when(inner)
            def _():
                arrived(r.r_in.at[2 + k, :, cut], k_in[j] + 2 + k)
                rows = pl.ds(pl.multiple_of((far_base + k) * p.in_rows, p.in_rows), p.in_rows)
                r.wa[rows, cut] = (r.wa[rows, cut].astype(F32) + r.r_in[2 + k, :, cut].astype(F32)).astype(BF)

            send(inner, shard(far_base + k, cut), r.r_in.at[1, :, cut], (s, 2 * (far_base + k) + y), k_in[j] + 1)

    attention_tile(3)
    pair_step(de, k_de, 3, on_1, k_de)
    attention_tile(0)
    attention_sum(3)

    k_col = recvs.take(n_dp)
    mine_in = pl.ds(pl.multiple_of(dp * p.out_rows, p.out_rows), p.out_rows)

    def unit_grads(yy, i):
        def four(buf):
            return jnp.concatenate([buf[m, 2 * i + k, yy] for m in range(2) for k in range(2)], 0)

        rows_x, up = four(r.x_all), four(r.db_all)
        hidden = mm(rows_x, r.w1[:, mine_in]) + r.par_f[0:1, mine_in]
        below = 0.5 + 0.5 * lax.erf(hidden * (0.5**0.5))
        slope = below + hidden * (0.3989422804014327 * jnp.exp(-0.5 * hidden * hidden))
        dhidden = (mm_nt(up, r.w2[mine_in, :]) * slope).astype(BF)
        r.u_out[...] += mm_tn((hidden * below).astype(BF), up)
        r.w_col[...] += mm_tn(rows_x, dhidden)

    def units_of(yy):
        for zz in range(nz):
            i = 2 * zz + yy
            pl.when((i != dp) | at_x1)(lambda i=i: arrived(r.x_all.at[0, i // 2, lax.rem(i, 2)], k_xsc + i))
            arrived(r.db_all.at[0, i // 2, lax.rem(i, 2)], k_dbc + i)
        lax.fori_loop(0, nz // 2, lambda i, carry: (unit_grads(yy, i), carry)[1], 0)

    @pl.when(is_ff)
    def _():
        r.u_out[...] = jnp.zeros(r.u_out.shape, F32)
        r.w_col[...] = jnp.zeros(r.w_col.shape, F32)
        units_of(y)

    k_smz = recvs.take(nz)
    gathered(k_sm, to_sm)
    r.sm_tot[...] = r.b_sm[0] + r.b_sm[1] + r.b_sm[2] + r.b_sm[3]
    r.r_sm[z] = r.sm_tot[...]
    for k in range(1, nz):
        zz = lax.rem(z + k, nz)
        send(None, r.sm_tot, r.r_sm.at[z], (s, 2 * zz + y), k_smz + z)

    attention_tile(1)
    attention_sum(0)
    @pl.when(at_x1)
    def _():
        arrived(r.ch_all.at[c], k_cha)

    send(at_x1, r.ch_all.at[c], r.ch_all.at[c], (core, dp), k_chx)
    attention_tile(2)
    attention_sum(1)

    @pl.when(is_ff)
    def _():
        for t in range(nz):
            line_y(xs, k_xs, t)
        for t in range(nz):
            line_y(db, k_db, t)
        units_of(1 - y)
        o_wout[0] = r.u_out[...].astype(BF)
        emit(4, o_wout)
        for k in range(n_dp):
            r.w_send[k] = r.w_col[k * p.in_rows : (k + 1) * p.in_rows, :].astype(BF)
        r.r_col[dp] = r.w_send[dp]

    for k in range(1, n_dp):
        to = lax.rem(dp + k, n_dp)
        send(is_ff, r.w_send.at[to], r.r_col.at[dp], (s, to), k_col + dp)
    attention_sum(2)

    head_part()

    for i in range(n_dp):
        pl.when(jnp.logical_not(gathers) & (((i != dp) & (i != ydp)) | at_x1))(lambda i=i: arrived(de(i), k_de + i))
    send(None, r.de_all.at[c], r.de_all.at[c], (core, dp), k_dex)

    entry = iota((p.share_rows, ln), 0) + (s * p.quarter + dp * p.share)

    def scatter(m):
        def step(i, carry):
            hot = []
            for k in range(2):
                hot.append(jnp.where(entry == r.ids_all[2 * i + k, pl.ds(m, 1), :], 1.0, 0.0).astype(BF))
            rows = r.de_all[m, pl.ds(2 * i, 2)].reshape(2 * ln, w)
            o_tab[...] += mm(jnp.concatenate(hot, 1), rows)[0 : p.share]
            return carry

        lax.fori_loop(0, n_dp // 2, step, 0)

    scatter(c)
    arrived(r.de_all.at[other], k_dex)
    scatter(other)
    n_pos = ln // n_dp
    here = pl.ds(pl.multiple_of(dp * n_pos, n_pos), n_pos)
    total = jnp.zeros((n_pos, w), F32)
    for m in range(2):
        for i in range(n_dp):
            total = total + r.de_all[m, i, here, :].astype(F32)
    o_pos[...] = total
    emit(1, o_tab)
    emit(2, o_pos)

    @pl.when(is_att)
    def _():
        mine = pl.ds(pl.multiple_of(z * p.in_rows, p.in_rows), p.in_rows)
        for j in (3, 0, 1, 2):
            cut = tile_cut(j)
            arrived(r.r_in.at[0, :, cut], k_in[j])
            arrived(r.r_in.at[1, :, cut], k_in[j] + 1)
            near_sum = r.wa[mine, cut].astype(F32) + r.r_in[0, :, cut].astype(F32)
            o_win[0, :, cut] = (near_sum + r.r_in[1, :, cut].astype(F32)).astype(BF)
        o_wout[...] = jnp.zeros(o_wout.shape, BF)
        emit(4, o_wout)

    @pl.when(is_ff)
    def _():
        for k in range(1, n_dp):
            src = lax.rem(dp + k, n_dp)
            arrived(r.r_col.at[src], k_col + src)
        for k in range(n_dp):
            o_win[0, :, k * p.out_rows : (k + 1) * p.out_rows] = r.r_col[k]

    emit(3, o_win)

    for k in range(1, nz):
        src = lax.rem(z + k, nz)
        arrived(r.r_sm.at[src], k_smz + src)
    r.sm_all[...] = r.r_sm[0] + r.r_sm[1] + r.r_sm[2] + r.r_sm[3]
    emit(5, o_vec)
    for i, src in enumerate((o_log, o_tab, o_pos, o_win, o_wout, o_vec)):
        pltpu.make_async_copy(src, outs[i], os.at[i]).wait()

    for cond, make in pending:
        if cond is None:
            make().wait_send()
        else:
            pl.when(cond)(lambda make=make: make().wait_send())
    assert sends.n <= SENDS and recvs.n <= RECVS, (sends.n, recvs.n)


def finish(p, *refs):
    ins, outs, (log_v, log_w, tab_v, win_v, win_w, wout_v, wout_w, vec_v, b_v, v_v, si, so) = refs[:6], refs[6:15], refs[15:]
    pieces = (log_v, tab_v, None, win_v, wout_v, vec_v)

    def copy_in(i):
        return pltpu.make_async_copy(ins[i], pieces[i], si.at[i])

    def copy_out(i, src):
        return pltpu.make_async_copy(src, outs[i], so.at[i])

    for i in (5, 0, 1, 3, 4):
        copy_in(i).start()
    straight = pltpu.make_async_copy(ins[2], outs[2], so.at[2])
    straight.start()
    n_b, n_w = p.ff // p.n_dp, p.width // p.n_dp
    copy_in(5).wait()
    mine = vec_v[pl.ds(lax.axis_index("dp"), 1), :]
    b_v[...] = mine[:, 0:n_b]
    for k in range(3):
        v_v[k] = mine[:, n_b + 128 * k : n_b + 128 * k + n_w]
    done = [copy_out(5, b_v)] + [copy_out(6 + k, v_v.at[k]) for k in range(3)]
    copy_in(0).wait()
    log_w[...] = log_v[...].astype(F32)
    done.append(copy_out(0, log_w))
    for one in done:
        one.start()
    copy_in(1).wait()
    done.append(copy_out(1, tab_v))
    done[-1].start()
    copy_in(3).wait()
    win_w[...] = win_v[...].astype(F32)
    done.append(copy_out(3, win_w))
    done[-1].start()
    copy_in(4).wait()
    wout_w[...] = wout_v[...].astype(F32)
    done.append(copy_out(4, wout_w))
    done[-1].start()
    straight.wait()
    for one in done:
        one.wait()


def whole(
    n_dp,
    token_ids,
    segment_ids,
    masked_rows,
    embedding,
    pos_table,
    w_in,
    w_out,
    b_in,
    b_out,
    norm_gain,
    norm_shift,
    logit_grad,
):
    quarter, width = embedding.shape
    batches, _, length = token_ids.shape
    masks = masked_rows.shape[-1]
    ff = w_in.shape[-1]
    p = Plan(n_dp, length, width, ff, quarter, masks)
    scratch = scratch_list(p)
    shapes = [
        (batches, 1, masks, quarter),
        (p.share, width),
        (length // n_dp, width),
        (1, p.in_rows, ff),
        (1, p.out_rows, width),
        (1, ff // n_dp),
        (1, p.in_rows),
        (1, p.in_rows),
        (1, p.in_rows),
    ]
    vmem = pl.BlockSpec(memory_space=pltpu.VMEM)
    far = pl.BlockSpec(memory_space=pl.ANY)
    part_types = [BF, F32, F32, BF, BF]
    parts = [jax.ShapeDtypeStruct(shape, kind) for shape, kind in zip(shapes, part_types)]
    parts.append(jax.ShapeDtypeStruct((8, width), F32))
    summed = pl.pallas_call(
        functools.partial(fused, p, list(scratch)),
        out_shape=parts,
        in_specs=[vmem] * 7 + [far] * 5,
        out_specs=[far] * 6,
        scratch_shapes=[pltpu.VMEM(*one) for one in scratch.values()]
        + [
            pltpu.SemaphoreType.DMA((SENDS,)),
            pltpu.SemaphoreType.DMA((RECVS,)),
            pltpu.SemaphoreType.DMA((len(p.chunks) + 4,)),
            pltpu.SemaphoreType.DMA((6,)),
        ],
        compiler_params=pltpu.CompilerParams(
            collective_id=0, has_side_effects=True, vmem_limit_bytes=VMEM_LIMIT
        ),
    )(
        token_ids,
        segment_ids,
        masked_rows,
        b_in,
        b_out,
        norm_gain,
        norm_shift,
        logit_grad,
        pos_table,
        embedding,
        w_in,
        w_out,
    )
    room = [
        (shapes[0], BF),
        (shapes[0], F32),
        (shapes[1], F32),
        (shapes[3], BF),
        (shapes[3], F32),
        (shapes[4], BF),
        (shapes[4], F32),
        ((8, width), F32),
        (shapes[5], F32),
        ((3, 1, p.in_rows), F32),
    ]
    return pl.pallas_call(
        functools.partial(finish, p),
        out_shape=[jax.ShapeDtypeStruct(shape, F32) for shape in shapes],
        in_specs=[far] * 6,
        out_specs=[far] * 9,
        scratch_shapes=[pltpu.VMEM(*one) for one in room]
        + [pltpu.SemaphoreType.DMA((6,)), pltpu.SemaphoreType.DMA((9,))],
        compiler_params=pltpu.CompilerParams(vmem_limit_bytes=VMEM_LIMIT),
    )(*summed)


def solution(mesh):
    n_section, n_dp = mesh.shape["section"], mesh.shape["dp"]

    def chosen_form(*args):
        token_ids, embedding, w_in = args[0], args[3], args[5]
        fits = (
            n_section == 4
            and n_dp == 8
            and token_ids.shape[0] == 2
            and token_ids.shape[1:] == (1, 128)
            and w_in.shape[1] % (16 * n_dp) == 0
            and w_in.shape[2] == 4 * w_in.shape[1]
            and embedding.shape[0] % (8 * n_dp) == 0
        )
        return whole(n_dp, *args) if fits else local(*args)

    placed = (
        P(None, "dp", None),
        P(None, "dp", None),
        P(None, "dp", None),
        P("section", None),
        P(),
        P("section", None, None),
        P("section", None, None),
        P("section", None),
        P("section", None),
        P("section", None),
        P("section", None),
        P(None, "dp", None, "section"),
    )
    return jax.shard_map(
        chosen_form,
        mesh=mesh,
        in_specs=placed,
        out_specs=(
            P(None, "dp", None, "section"),
            P(("section", "dp"), None),
            P("dp", None),
            P("section", "dp", None),
            P("section", "dp", None),
            P("section", "dp"),
            P("section", "dp"),
            P("section", "dp"),
            P("section", "dp"),
        ),
        check_vma=False,
    )
```

```python
import functools
import math
import types

import jax
import jax.numpy as jnp
from jax import lax
from jax.experimental import pallas as pl
from jax.experimental.pallas import tpu as pltpu
from jax.sharding import PartitionSpec as P

HEADS = 12


EPSILON = 1e-12


def for_sending(array):
    return jax.tree.map(lambda a: a.astype(jnp.bfloat16) if a.dtype == jnp.float32 else a, array)


def passed_along(block, axis, distance):
    devices = range(lax.axis_size(axis))
    route = [(i - distance, i) for i in devices if i - distance in devices]
    return lax.ppermute(block, axis, route)


def broadcast(value, axis, source):
    kept = jnp.where(lax.axis_index(axis) == source, value, 0).astype(value.dtype)
    return lax.psum(kept, axis)


def norm_forward(resid, gain_row, shift_row):
    centre = jnp.mean(resid, -1, keepdims=True)
    centred = resid - centre
    inverse = lax.rsqrt(jnp.mean(centred * centred, -1, keepdims=True) + EPSILON)
    normed = centred * inverse
    return (normed * gain_row + shift_row, normed, inverse)


def norm_backward(upstream, normed, inverse, gain_row):
    gain_part = jnp.sum(upstream * normed, 0)
    shift_part = jnp.sum(upstream, 0)
    scaled = upstream * gain_row
    first_mean = jnp.mean(scaled, -1, keepdims=True)
    second_mean = jnp.mean(scaled * normed, -1, keepdims=True)
    return (inverse * (scaled - first_mean - normed * second_mean), gain_part, shift_part)


def to_heads(values):
    return values.reshape(values.shape[0], HEADS, values.shape[1] // HEADS)


def row_scores(query, keyed, segment):
    factor = (query.shape[1] // HEADS) ** (-0.5)
    scores = (
        jnp.einsum(
            "qhd,khd->hqk", to_heads(query), to_heads(keyed), preferred_element_type=jnp.float32
        )
        * factor
    )
    allowed = segment[:, None] == segment[None, :]
    return jnp.where(allowed[None], scores, -1000000000.0)


def attend_row(packed, segment):
    width = packed.shape[1] // 3
    scores = row_scores(packed[:, :width], packed[:, width : 2 * width], segment)
    row_peak = jnp.max(scores, -1, keepdims=True)
    exponent = jnp.exp(scores - row_peak)
    row_total = jnp.sum(exponent, -1, keepdims=True)
    chance = (exponent / row_total).astype(jnp.bfloat16)
    context = jnp.einsum(
        "hqk,khd->qhd", chance, to_heads(packed[:, 2 * width :]), preferred_element_type=jnp.float32
    )
    summary = (row_peak + jnp.log(row_total))[..., 0]
    return (context.reshape(packed.shape[0], width).astype(jnp.bfloat16), summary)


def attend_back(packed, segment, summary, upstream):
    length = packed.shape[0]
    width = packed.shape[1] // 3
    factor = (width // HEADS) ** (-0.5)
    scores = row_scores(packed[:, :width], packed[:, width : 2 * width], segment)
    chance = jnp.exp(scores - summary[..., None])
    grad_heads = to_heads(upstream)
    grad_chance = jnp.einsum(
        "qhd,khd->hqk",
        grad_heads,
        to_heads(packed[:, 2 * width :]),
        preferred_element_type=jnp.float32,
    )
    grad_value = jnp.einsum(
        "hqk,qhd->khd", chance.astype(jnp.bfloat16), grad_heads, preferred_element_type=jnp.float32
    )
    grad_score = chance * (grad_chance - jnp.sum(chance * grad_chance, -1, keepdims=True))
    grad_score = grad_score.astype(jnp.bfloat16)
    grad_query = (
        jnp.einsum(
            "hqk,khd->qhd",
            grad_score,
            to_heads(packed[:, width : 2 * width]),
            preferred_element_type=jnp.float32,
        )
        * factor
    )
    grad_key = (
        jnp.einsum(
            "hqk,qhd->khd",
            grad_score,
            to_heads(packed[:, :width]),
            preferred_element_type=jnp.float32,
        )
        * factor
    )
    joined = jnp.concatenate(
        [
            grad_query.reshape(length, width),
            grad_key.reshape(length, width),
            grad_value.reshape(length, width),
        ],
        1,
    )
    return joined.astype(jnp.bfloat16)


def attention_forward(inputs, segment, params):
    w_first, w_second, bias_first, bias_second, gain_row, shift_row = params
    rows_here, length, width = inputs.shape
    flat = inputs.reshape(rows_here * length, width)
    offset = jnp.concatenate(
        [bias_first[:width], jnp.zeros((width,), jnp.float32), bias_first[2 * width : 3 * width]]
    )
    packed = jnp.dot(flat, w_first[:, : 3 * width], preferred_element_type=jnp.float32) + offset
    packed = packed.astype(jnp.bfloat16).reshape(rows_here, length, 3 * width)
    context, summary = lax.map(lambda item: attend_row(item[0], item[1]), (packed, segment))
    branch = (
        jnp.dot(
            context.reshape(-1, width), w_first[:, 3 * width :], preferred_element_type=jnp.float32
        )
        + bias_second
    )
    result, normed, inverse = norm_forward(flat.astype(jnp.float32) + branch, gain_row, shift_row)
    return (result.reshape(rows_here, length, width), (packed, context, summary, normed, inverse))


def attention_backward(inputs, segment, upstream, params, totals):
    w_first, w_second, bias_first, bias_second, gain_row, shift_row = params
    rows_here, length, width = inputs.shape
    result, saved = attention_forward(inputs, segment, params)
    packed, context, summary, normed, inverse = saved
    flat = inputs.reshape(-1, width)
    grad_resid, gain_part, shift_part = norm_backward(
        upstream.reshape(-1, width), normed, inverse, gain_row
    )
    grad_branch = grad_resid.astype(jnp.bfloat16)
    grad_out_proj = jnp.einsum(
        "nd,ne->de", context.reshape(-1, width), grad_branch, preferred_element_type=jnp.float32
    )
    bias_second_part = jnp.sum(grad_branch.astype(jnp.float32), 0)
    grad_context = jnp.einsum(
        "ne,de->nd", grad_branch, w_first[:, 3 * width :], preferred_element_type=jnp.float32
    )
    grad_context = grad_context.astype(jnp.bfloat16).reshape(rows_here, length, width)
    grad_packed = lax.map(
        lambda item: attend_back(item[0], item[1], item[2], item[3]),
        (packed, segment, summary, grad_context),
    )
    flat_packed = grad_packed.reshape(-1, 3 * width)
    grad_proj = jnp.einsum("nd,nc->dc", flat, flat_packed, preferred_element_type=jnp.float32)
    bias_sums = jnp.sum(flat_packed.astype(jnp.float32), 0)
    grad_input = grad_resid + jnp.einsum(
        "nc,dc->nd", flat_packed, w_first[:, : 3 * width], preferred_element_type=jnp.float32
    )
    first_total, second_total, bias_first_total, bias_second_total, gain_total, shift_total = totals
    first_total = (
        first_total.at[:, : 3 * width].add(grad_proj).at[:, 3 * width :].add(grad_out_proj)
    )
    bias_first_total = (
        bias_first_total.at[:width]
        .add(bias_sums[:width])
        .at[2 * width : 3 * width]
        .add(bias_sums[2 * width :])
    )
    updated = (
        first_total,
        second_total,
        bias_first_total,
        bias_second_total + bias_second_part,
        gain_total + gain_part,
        shift_total + shift_part,
    )
    return (grad_input.reshape(rows_here, length, width).astype(jnp.bfloat16), updated)


def feed_forward(inputs, params):
    w_first, w_second, bias_first, bias_second, gain_row, shift_row = params
    rows_here, length, width = inputs.shape
    flat = inputs.reshape(-1, width)
    hidden = jnp.dot(flat, w_first, preferred_element_type=jnp.float32) + bias_first
    active = jax.nn.gelu(hidden, approximate=False).astype(jnp.bfloat16)
    branch = jnp.dot(active, w_second, preferred_element_type=jnp.float32) + bias_second
    result, normed, inverse = norm_forward(flat.astype(jnp.float32) + branch, gain_row, shift_row)
    return (result.reshape(rows_here, length, width), (hidden, active, normed, inverse))


def feed_backward(inputs, upstream, params, totals):
    w_first, w_second, bias_first, bias_second, gain_row, shift_row = params
    rows_here, length, width = inputs.shape
    result, saved = feed_forward(inputs, params)
    hidden, active, normed, inverse = saved
    flat = inputs.reshape(-1, width)
    grad_resid, gain_part, shift_part = norm_backward(
        upstream.reshape(-1, width), normed, inverse, gain_row
    )
    grad_branch = grad_resid.astype(jnp.bfloat16)
    grad_second = jnp.einsum("nf,nd->fd", active, grad_branch, preferred_element_type=jnp.float32)
    bias_second_part = jnp.sum(grad_branch.astype(jnp.float32), 0)
    grad_active = jnp.einsum("nd,fd->nf", grad_branch, w_second, preferred_element_type=jnp.float32)
    through = jax.vjp(lambda inner: jax.nn.gelu(inner, approximate=False), hidden)[1](grad_active)[
        0
    ]
    grad_hidden = through.astype(jnp.bfloat16)
    grad_first = jnp.einsum("nd,nf->df", flat, grad_hidden, preferred_element_type=jnp.float32)
    bias_first_part = jnp.sum(grad_hidden.astype(jnp.float32), 0)
    grad_input = grad_resid + jnp.einsum(
        "nf,df->nd", grad_hidden, w_first, preferred_element_type=jnp.float32
    )
    terms = (grad_first, grad_second, bias_first_part, bias_second_part, gain_part, shift_part)
    updated = tuple((total + term for total, term in zip(totals, terms)))
    return (grad_input.reshape(rows_here, length, width).astype(jnp.bfloat16), updated)


def local(
    token_ids,
    segment_ids,
    masked_rows,
    embedding,
    pos_table,
    w_in,
    w_out,
    b_in,
    b_out,
    norm_gain,
    norm_shift,
    logit_grad,
):
    sections = lax.axis_size("section")
    section_index = lax.axis_index("section")
    quarter, width = embedding.shape
    batches, rows_here, length = token_ids.shape
    params = (
        w_in[0],
        w_out[0],
        b_in[0].astype(jnp.float32),
        b_out[0].astype(jnp.float32),
        norm_gain[0].astype(jnp.float32),
        norm_shift[0].astype(jnp.float32),
    )
    local_ids = token_ids - section_index * quarter
    inside = (local_ids >= 0) & (local_ids < quarter)
    picked = jnp.take(embedding, jnp.clip(local_ids, 0, quarter - 1), axis=0)
    partial_rows = jnp.where(inside[..., None], picked.astype(jnp.float32), 0.0)
    looked = lax.psum(partial_rows.astype(jnp.bfloat16), "section").astype(jnp.float32)
    entry = (looked + pos_table.astype(jnp.float32)).astype(jnp.bfloat16)

    def spare_forward(inputs, segment):
        return jnp.zeros(inputs.shape, jnp.bfloat16)

    def attend_forward(inputs, segment):
        return attention_forward(inputs, segment, params)[0].astype(jnp.bfloat16)

    def feed_only(inputs, segment):
        return feed_forward(inputs, params)[0].astype(jnp.bfloat16)

    def spare_backward(inputs, segment, upstream, totals):
        return (jnp.zeros(inputs.shape, jnp.bfloat16), totals)

    def attend_backward(inputs, segment, upstream, totals):
        return attention_backward(inputs, segment, upstream, params, totals)

    def feed_back_only(inputs, segment, upstream, totals):
        return feed_backward(inputs, upstream, params, totals)

    ticks = batches + sections - 1
    kept = jnp.zeros_like(entry)
    outputs = jnp.zeros_like(entry)
    incoming = jnp.zeros_like(entry[0])
    for moment in range(ticks):
        micro_index = moment - section_index
        is_live = (micro_index >= 0) & (micro_index < batches)
        micro_slot = jnp.clip(micro_index, 0, batches - 1)
        current = jnp.where(section_index == 0, entry[micro_slot], incoming)
        kept = kept.at[micro_slot].set(jnp.where(is_live, current, kept[micro_slot]))
        branch_index = jnp.where(is_live, 1 + section_index % 2, 0)
        result = lax.switch(
            branch_index,
            [spare_forward, attend_forward, feed_only],
            current,
            segment_ids[micro_slot],
        )
        outputs = outputs.at[micro_slot].set(jnp.where(is_live, result, outputs[micro_slot]))
        if moment + 1 < ticks:
            incoming = jax.tree.map(
                lambda part, own: part.astype(own.dtype),
                passed_along(for_sending(result), "section", 1),
                result,
            )
    final_rows = jnp.take_along_axis(outputs, masked_rows[..., None], axis=2)
    head_rows = broadcast(final_rows, "section", sections - 1)
    logits = jnp.einsum("mrkd,vd->mrkv", head_rows, embedding, preferred_element_type=jnp.float32)
    partial_grad = jnp.einsum(
        "mrkv,vd->mrkd", logit_grad, embedding, preferred_element_type=jnp.float32
    )
    grad_rows = lax.psum(partial_grad.astype(jnp.bfloat16), "section").astype(jnp.float32)
    table_head = jnp.einsum(
        "mrkv,mrkd->vd", logit_grad, head_rows, preferred_element_type=jnp.float32
    )
    places = (masked_rows[..., None] == jnp.arange(length)[None, None, None, :]).astype(jnp.float32)
    top_grad = jnp.einsum("mrkl,mrkd->mrld", places, grad_rows, precision=lax.Precision.HIGHEST)
    gradients = (
        jnp.zeros(w_in.shape[1:], jnp.float32),
        jnp.zeros(w_out.shape[1:], jnp.float32),
        jnp.zeros(b_in.shape[1:], jnp.float32),
        jnp.zeros((width,), jnp.float32),
        jnp.zeros((width,), jnp.float32),
        jnp.zeros((width,), jnp.float32),
    )
    grad_entry = jnp.zeros_like(entry)
    back_in = jnp.zeros_like(entry[0])
    for moment in range(ticks):
        micro_index = moment - (sections - 1 - section_index)
        is_live = (micro_index >= 0) & (micro_index < batches)
        micro_slot = jnp.clip(micro_index, 0, batches - 1)
        upstream = jnp.where(
            section_index == sections - 1, top_grad[micro_slot], back_in.astype(jnp.float32)
        )
        branch_index = jnp.where(is_live, 1 + section_index % 2, 0)
        grad_input, gradients = lax.switch(
            branch_index,
            [spare_backward, attend_backward, feed_back_only],
            kept[micro_slot],
            segment_ids[micro_slot],
            upstream,
            gradients,
        )
        grad_entry = grad_entry.at[micro_slot].set(
            jnp.where(is_live, grad_input, grad_entry[micro_slot])
        )
        if moment + 1 < ticks:
            back_in = jax.tree.map(
                lambda part, own: part.astype(own.dtype),
                passed_along(for_sending(grad_input), "section", -1),
                grad_input,
            )
    input_grad = broadcast(grad_entry, "section", 0)
    input_wide = input_grad.astype(jnp.float32)
    pos_grad = jnp.sum(input_wide, (0, 1))
    targets = jnp.where(inside, local_ids, quarter).reshape(-1)
    table_input = jax.ops.segment_sum(
        input_wide.reshape(-1, width), targets, num_segments=quarter + 1
    )[:quarter]
    w_in_part, w_out_part, b_in_part, b_out_part, gain_part, shift_part = gradients
    reduced = (
        lax.psum_scatter(w_in_part, "dp", scatter_dimension=0, tiled=True),
        lax.psum_scatter(w_out_part, "dp", scatter_dimension=0, tiled=True),
        lax.psum_scatter(b_in_part, "dp", scatter_dimension=0, tiled=True),
        lax.psum_scatter(b_out_part, "dp", scatter_dimension=0, tiled=True),
        lax.psum_scatter(gain_part, "dp", scatter_dimension=0, tiled=True),
        lax.psum_scatter(shift_part, "dp", scatter_dimension=0, tiled=True),
        lax.psum_scatter(pos_grad, "dp", scatter_dimension=0, tiled=True),
        lax.psum_scatter(table_input + table_head, "dp", scatter_dimension=0, tiled=True),
    )
    table_grad = reduced[7]
    return (
        logits,
        table_grad,
        reduced[6],
        reduced[0][None],
        reduced[1][None],
        reduced[2][None],
        reduced[3][None],
        reduced[4][None],
        reduced[5][None],
    )


SENDS = 109
RECVS = 110
VMEM_LIMIT = 64 * 2**20
BF = jnp.bfloat16
F32 = jnp.float32
MESH = pl.DeviceIdType.MESH


def mm(a, b):
    return jnp.dot(a, b, preferred_element_type=F32)


def mm_nt(a, b):
    return lax.dot_general(a, b, (((1,), (1,)), ((), ())), preferred_element_type=F32)


def mm_tn(a, b):
    return lax.dot_general(a, b, (((0,), (0,)), ((), ())), preferred_element_type=F32)


def iota(shape, dim):
    return lax.broadcasted_iota(jnp.int32, shape, dim)


def column(row):
    return jnp.broadcast_to(row.astype(F32), (128, 128)).T


class Plan:
    def __init__(self, n_dp, length, width, ff, quarter, masks):
        self.n_dp, self.length, self.width, self.ff = n_dp, length, width, ff
        self.quarter, self.masks = quarter, masks
        self.nz = n_dp // 2
        self.share = quarter // n_dp
        self.in_rows = width // n_dp
        self.out_rows = ff // n_dp
        self.mask_pad = -(-masks // 16) * 16
        self.share_pad = -(-self.share // 128) * 128
        self.share_rows = -(-self.share // 16) * 16
        self.chunks = []
        at = 0
        while at < quarter:
            size = min(1024, quarter - at)
            self.chunks.append((at, size))
            at += size


class Counter:
    def __init__(self):
        self.n = 0

    def take(self, k=1):
        first = self.n
        self.n += k
        return first


def scratch_list(p):
    w, ff, ln = p.width, p.ff, p.length
    mp = p.mask_pad
    return dict(
        emb=((p.quarter, w), BF),
        lg=((2, 1, p.masks, p.quarter), BF),
        pos=((ln, w), BF),
        wa=((w, ff), BF),
        w1=((w, ff), BF),
        w2=((ff, w), BF),
        par_a=((8, ff), F32),
        par_f=((8, ff), F32),
        acc=((2 * ln, w), F32),
        psend=((ln, w), BF),
        psum=((ln, w), BF),
        prow=((2, ln, w), BF),
        lgp=((2 * mp, p.quarter), BF),
        lgs=((p.n_dp, 2 * p.masks, p.share_pad), BF),
        lgr=((p.n_dp, 2 * p.masks, p.share_pad), BF),
        ch_pack=((p.n_dp, 2 * p.masks, w), BF),
        g=((2 * mp, w), F32),
        grow=((2, p.masks, w), F32),
        gwide=((ln, w), F32),
        mrow=((8, ln), jnp.int32),
        ids_own=((8, ln), jnp.int32),
        ids_all=((p.n_dp, 8, ln), jnp.int32),
        x_a=((ln, w), BF),
        x_f=((ln, w), BF),
        y_f=((ln, w), BF),
        y_o=((ln, w), BF),
        pk=((ln, 3 * w), BF),
        ctx=((ln, w), BF),
        probs=((w // 128, ln, 256), F32),
        n_a=((ln, w), F32),
        n_f=((ln, w), F32),
        inv_a=((ln, 1), F32),
        inv_f=((ln, 1), F32),
        slope=((ln, ff), BF),
        xt_a=((p.nz, 2, p.in_rows, ln), BF),
        ct_a=((p.nz, 2, p.in_rows, ln), BF),
        dyin=((ln, w), BF),
        dyf=((ln, w), F32),
        dres=((ln, w), F32),
        dbr_a=((ln, w), BF),
        dpk=((ln, 3 * w), BF),
        dctx=((ln, w), BF),
        dx=((ln, w), BF),
        dx_pair=((ln, w), BF),
        bsum=((1, ff), F32),
        vecs=((8, w), F32),
        sm_a=((8, w), F32),
        sm_f=((8, w), F32),
        b_ctx=((p.nz, p.in_rows, 4 * ln), BF),
        b_x=((p.nz, p.in_rows, 4 * ln), BF),
        b_dbr=((4 * ln, w), BF),
        b_dh=((4 * ln, 3 * w), BF),
        b_sm=((4, 8, w), F32),
        sm_tot=((8, w), F32),
        sm_all=((8, w), F32),
        r_sm=((p.nz, 8, w), F32),
        r_in=((4, p.in_rows, ff), BF),
        x_all=((2, p.nz, 2, ln, w), BF),
        db_all=((2, p.nz, 2, ln, w), BF),
        w_col=((w, p.out_rows), F32),
        w_send=((p.n_dp, p.in_rows, p.out_rows), BF),
        r_col=((p.n_dp, p.in_rows, p.out_rows), BF),
        ch_own=((mp, w), BF),
        ch_two=((mp, w), BF),
        ch_all=((2, p.n_dp, mp, w), BF),
        de_all=((2, p.n_dp, ln, w), BF),
        u_out=((p.out_rows, w), F32),
        o_log=((2, 1, p.masks, p.quarter), BF),
        o_tab=((p.share, w), F32),
        o_pos=((ln // p.n_dp, w), F32),
        o_win=((1, p.in_rows, ff), BF),
        o_wout=((1, p.out_rows, w), BF),
    )


def fused(p, names, *refs):
    (tok, seg, picks, b_in, b_out, gain, shift, lg_h, pos_h, emb_h, w_in_h, w_out_h) = refs[:12]
    outs = refs[12:18]
    r = types.SimpleNamespace(**dict(zip(names, refs[18:])))
    ss, rs, ls, os = refs[18 + len(names) :]
    (o_log, o_tab, o_pos, o_win, o_wout, o_vec) = (r.o_log, r.o_tab, r.o_pos, r.o_win, r.o_wout, r.sm_all)
    w, ff, ln, mp, nz, n_dp = p.width, p.ff, p.length, p.mask_pad, p.nz, p.n_dp
    heads = w // 64
    pairs = heads // 2

    s = lax.axis_index("section")
    dp = lax.axis_index("dp")
    x, c = s // 2, lax.rem(s, 2)
    z, y = dp // 2, lax.rem(dp, 2)
    core = s + 1 - 2 * c
    across = s + 2 - 4 * x
    ydp = dp + 1 - 2 * y
    other = 1 - c
    at_x0, at_x1 = x == 0, x == 1
    is_att, is_ff = c == 0, c == 1
    sends, recvs = Counter(), Counter()
    not_first, not_last = z > 0, z < nz - 1
    known = {}

    def both(*conds):
        conds = [cond for cond in conds if cond is not None]
        key = tuple(sorted(id(cond) for cond in conds))
        if key not in known:
            known[key] = (functools.reduce(lambda a, b: a & b, conds) if conds else None, conds)
        return known[key][0]

    def when(cond, body):
        if cond is None:
            body()
        else:
            pl.when(cond)(body)

    def at_least(k):
        return known.setdefault(("least", k), z >= k) if k > 0 else None

    def at_most(k):
        return known.setdefault(("most", k), z <= k) if k < nz - 1 else None

    groups, stage = {}, [0]

    def send(cond, src, dst, dev, recv, bulk=None, tag=None):
        key = (stage[0], None if cond is None else id(cond), tag)
        if key not in groups:
            groups[key] = [cond, sends.take(), 0, bulk]
        group = groups[key]
        group[2] += math.prod(src.shape) * src.dtype.itemsize

        def start():
            pltpu.make_async_remote_copy(
                src_ref=src,
                dst_ref=dst,
                send_sem=ss.at[group[1]],
                recv_sem=rs.at[recv],
                device_id=dev,
                device_id_type=MESH,
            ).start()

        when(cond, start)

    def drain(number):
        for key, (cond, slot, size, bulk) in groups.items():
            if key[0] == number:
                rows = size // (w * 2)
                assert bulk is not None or size == rows * w * 2 and rows % 16 == 0 and rows <= p.quarter, (rows, size)
                ref = r.emb.at[0:rows] if bulk is None else bulk

                def gone(ref=ref, slot=slot):
                    pltpu.make_async_remote_copy(
                        src_ref=ref,
                        dst_ref=ref,
                        send_sem=ss.at[slot],
                        recv_sem=rs.at[0],
                        device_id=(core, dp),
                        device_id_type=MESH,
                    ).wait_send()

                when(cond, gone)

    def arrived(dst, recv):
        pltpu.make_async_remote_copy(
            src_ref=dst,
            dst_ref=dst,
            send_sem=ss.at[0],
            recv_sem=rs.at[recv],
            device_id=(core, dp),
            device_id_type=MESH,
        ).wait_recv()

    for i, (at, size) in enumerate(p.chunks):
        pltpu.make_async_copy(emb_h.at[pl.ds(at, size)], r.emb.at[pl.ds(at, size)], ls.at[i]).start()
    l_w = len(p.chunks)
    lg, pos = r.lg, r.pos
    pltpu.make_async_copy(lg_h, lg, ls.at[l_w + 2]).start()
    pltpu.make_async_copy(pos_h, pos, ls.at[l_w + 3]).start()

    def fill(par):
        par[0:1, :] = b_in[...].astype(F32)
        par[1:2, 0:w] = b_out[...].astype(F32)
        par[2:3, 0:w] = gain[...].astype(F32)
        par[3:4, 0:w] = shift[...].astype(F32)

    pl.when(is_att)(lambda: fill(r.par_a))
    pl.when(is_ff)(lambda: fill(r.par_f))

    barrier = pltpu.get_barrier_semaphore()
    peers = [(s, lax.rem(dp + k, n_dp)) for k in range(1, n_dp)]
    peers += [(core, dp), (across, dp), (3 - s, dp), (core, ydp)]
    for peer in peers:
        pl.semaphore_signal(barrier, inc=1, device_id=peer, device_id_type=MESH)

    cols = [column(tok[m]) for m in range(2)]
    first = s * p.quarter
    for i, (at, size) in enumerate(p.chunks):
        pltpu.make_async_copy(emb_h.at[pl.ds(at, size)], r.emb.at[pl.ds(at, size)], ls.at[i]).wait()
        lane = (iota((ln, size), 1) + (first + at)).astype(F32)
        hot = []
        for m in range(2):
            wide = jnp.concatenate([cols[m]] * (-(-size // 128)), 1)[:, :size]
            hot.append(jnp.where(wide == lane, 1.0, 0.0).astype(BF))
        part = mm(jnp.concatenate(hot, 0), r.emb[at : at + size, :])
        if i == 0:
            r.acc[...] = part
        else:
            r.acc[...] += part
    r.psend[...] = r.acc[pl.ds(pl.multiple_of(ln * other, ln), ln), :].astype(BF)

    @pl.when(is_att)
    def _():
        pltpu.make_async_copy(w_in_h.at[0], r.wa, ls.at[l_w]).start()

    @pl.when(is_ff)
    def _():
        pltpu.make_async_copy(w_in_h.at[0], r.w1, ls.at[l_w]).start()
        pltpu.make_async_copy(w_out_h.at[0], r.w2, ls.at[l_w + 1]).start()

    tiles = ff // w
    k_p, k_g = recvs.take(2), recvs.take(2)
    k_pa, k_pf, k_wa, k_w1, k_w2 = recvs.take(), recvs.take(), recvs.take(tiles), recvs.take(tiles), recvs.take(tiles)
    pl.semaphore_wait(barrier, len(peers))
    send(None, r.psend, r.prow.at[0], (core, dp), k_p)


    pltpu.make_async_copy(lg_h, lg, ls.at[l_w + 2]).wait()
    pltpu.make_async_copy(pos_h, pos, ls.at[l_w + 3]).wait()
    r.lgp[...] = jnp.zeros(r.lgp.shape, BF)
    r.lgp[0 : p.masks] = lg[0, 0]
    r.lgp[mp : mp + p.masks] = lg[1, 0]

    k_lg, k_id = recvs.take(), recvs.take()
    for j in range(n_dp):
        r.lgs[j, :, p.share :] = jnp.zeros((2 * p.masks, p.share_pad - p.share), BF)
        for m in range(2):
            r.lgs[j, p.masks * m : p.masks * (m + 1), 0 : p.share] = lg[m, 0, :, p.share * j : p.share * (j + 1)]
    r.ids_own[...] = jnp.zeros(r.ids_own.shape, jnp.int32)
    for m in range(2):
        r.ids_own[m : m + 1, :] = tok[m]
    r.ids_all[dp] = r.ids_own[...]
    r.lgr[dp] = r.lgs[dp]
    for k in range(1, n_dp):
        to = lax.rem(dp + k, n_dp)
        send(None, r.lgs.at[to], r.lgr.at[dp], (s, to), k_lg, r.lgs.at[0 : n_dp - 1], 1)
        send(None, r.ids_own, r.ids_all.at[dp], (s, to), k_id, r.ids_all.at[0 : n_dp - 1], 2)
    arrived(r.prow.at[0], k_p)
    own_rows = r.acc[pl.ds(pl.multiple_of(ln * c, ln), ln), :]
    r.acc[0:ln, :] = own_rows + r.prow[0].astype(F32)
    r.psum[...] = r.acc[0:ln, :].astype(BF)
    send(at_x1, r.psum, r.prow.at[1], (across, dp), k_p + 1)

    def weights(cond):
        send(both(is_att, cond), r.par_a, r.par_a, (core, dp), k_pa)
        send(both(is_ff, cond), r.par_f, r.par_f, (core, dp), k_pf)
        for j in range(tiles):
            cut = slice(j * w, (j + 1) * w)
            send(both(is_att, cond), w_in_h.at[0, :, cut], r.wa.at[:, cut], (core, dp), k_wa + j, tag=3)
            send(both(is_ff, cond), w_in_h.at[0, :, cut], r.w1.at[:, cut], (core, dp), k_w1 + j, tag=4)
            send(both(is_ff, cond), w_out_h.at[0, cut, :], r.w2.at[cut, :], (core, dp), k_w2 + j, tag=5)

    weights(at_x0)

    for i, (at, size) in enumerate(p.chunks):
        part = mm(r.lgp[:, at : at + size], r.emb[at : at + size, :])
        if i == 0:
            r.g[...] = part
        else:
            r.g[...] += part
    send(None, r.g.at[pl.ds(pl.multiple_of(mp * other, mp), p.masks)], r.grow.at[0], (core, dp), k_g)

    def masked_gradient():
        arrived(r.grow.at[0], k_g)
        r.gwide[...] = jnp.zeros(r.gwide.shape, F32)
        r.gwide[0 : p.masks, :] = r.g[pl.ds(pl.multiple_of(mp * c, mp), p.masks), :] + r.grow[0]

    pl.when(at_x1)(masked_gradient)
    weights(at_x1)

    k_x = recvs.take()

    @pl.when(at_x0)
    def _():
        arrived(r.prow.at[1], k_p + 1)
        whole = r.acc[0:ln, :] + r.prow[1].astype(F32)
        r.x_a[...] = (whole + pos[...].astype(F32)).astype(BF)

    @pl.when(is_att)
    def _():
        pltpu.make_async_copy(w_in_h.at[0], r.wa, ls.at[l_w]).wait()
        arrived(r.par_f, k_pf)

    @pl.when(is_ff)
    def _():
        pltpu.make_async_copy(w_in_h.at[0], r.w1, ls.at[l_w]).wait()
        pltpu.make_async_copy(w_out_h.at[0], r.w2, ls.at[l_w + 1]).wait()
        arrived(r.par_a, k_pa)

    @pl.when(at_x1)
    def _():
        arrived(r.x_a, k_x)

    low = jnp.where(iota((ln, 128), 1) < 64, 1.0, 0.0).astype(BF)
    high = jnp.where(iota((ln, 128), 1) < 64, 0.0, 1.0).astype(BF)

    def split(block):
        return jnp.concatenate([block * low, block * high], 0)

    def stack(block):
        return jnp.concatenate([block[:, 0:128], block[:, 128:256]], 0)

    def norm_forward(resid, par):
        centred = resid - jnp.mean(resid, -1, keepdims=True)
        inverse = lax.rsqrt(jnp.mean(centred * centred, -1, keepdims=True) + EPSILON)
        normed = centred * inverse
        return (normed * par[2:3, 0:w] + par[3:4, 0:w]).astype(BF), normed, inverse

    rows_x = r.x_a[...]

    def wa_tile(j):
        pl.when(is_ff)(lambda: arrived(r.wa.at[:, j * w : (j + 1) * w], k_wa + j))

    for j in range(3):
        wa_tile(j)
        part = mm(rows_x, r.wa[:, j * w : (j + 1) * w])
        if j != 1:
            part = part + r.par_a[0:1, j * w : (j + 1) * w]
        r.pk[:, j * w : (j + 1) * w] = part.astype(BF)
    seg_row = seg[c].astype(F32)
    seg_col = column(seg[c])
    seg_row = jnp.broadcast_to(jnp.concatenate([seg_row, seg_row], 1), (ln, 256))
    seg_col = jnp.concatenate([seg_col, seg_col], 1)
    for h in range(pairs):
        at = 128 * h
        query = r.pk[:, at : at + 128]
        keyed = split(r.pk[:, w + at : w + at + 128])
        value = split(r.pk[:, 2 * w + at : 2 * w + at + 128])
        scores = jnp.where(seg_row == seg_col, mm_nt(query, keyed) * 0.125, -1e9)
        chance = []
        for half in (scores[:, 0:128], scores[:, 128:256]):
            power = jnp.exp(half - jnp.max(half, -1, keepdims=True))
            chance.append(power / jnp.sum(power, -1, keepdims=True))
        chance = jnp.concatenate(chance, 1)
        r.probs[h] = chance
        r.ctx[:, at : at + 128] = mm(chance.astype(BF), value).astype(BF)
    wa_tile(3)
    resid = rows_x.astype(F32) + mm(r.ctx[...], r.wa[:, 3 * w : 4 * w]) + r.par_a[1:2, 0:w]
    r.x_f[...], r.n_a[...], r.inv_a[...] = norm_forward(resid, r.par_a)

    def line(buf, base, owner):
        own = buf(dp)
        send(not_last, own, own, (s, dp + 2), base + dp)
        send(not_first, own, own, (s, dp - 2), base + dp)
        send(is_att, own, own, (core, dp), owner + dp)
        to_y(buf, base, dp, None, owner)

    def to_y(buf, base, i, cond, owner):
        whose = jnp.where(is_att, core, s)
        send(cond, buf(i), buf(i), (whose, ydp), jnp.where(is_att, owner, base) + i)

    def at_distance(t, sign, cond):
        here = both(cond, at_least(t) if sign < 0 else at_most(nz - 1 - t))
        return here, jnp.clip(z + sign * t, 0, nz - 1) * 2 + y

    def onward(here, sign):
        return both(here, not_last if sign < 0 else not_first)

    def line_step(buf, base, t, cond, owner):
        for sign in (-1, 1):
            here, from_dp = at_distance(t, sign, cond)
            piece = buf(from_dp)
            when(here, lambda piece=piece, from_dp=from_dp: arrived(piece, base + from_dp))
            if t < nz - 1:
                send(onward(here, sign), piece, piece, (s, dp - 2 * sign), base + from_dp)
            send(both(here, is_att), piece, piece, (core, dp), owner + from_dp)

    def line_cross(buf, base, t, cond, owner):
        for sign in (-1, 1):
            here, from_dp = at_distance(t, sign, cond)
            to_y(buf, base, from_dp, here, owner)

    def pair_line(buf, base, cond, i):
        piece = buf(i)
        send(both(cond, not_last), piece, piece, (s, dp + 2), base + i)
        send(both(cond, not_first), piece, piece, (s, dp - 2), base + i)

    def pair_step(buf, base, t, cond, on_x):
        for sign in (-1, 1):
            for side in (0, 1):
                here, from_dp = at_distance(t, sign, cond)
                if side:
                    from_dp = from_dp + 1 - 2 * y
                piece = buf(from_dp)
                when(here, lambda piece=piece, from_dp=from_dp: arrived(piece, base + from_dp))
                if t < nz - 1:
                    send(onward(here, sign), piece, piece, (s, dp - 2 * sign), base + from_dp)
                send(here, piece, piece, (across, dp), on_x + from_dp)

    def ch(i):
        return r.ch_all.at[c, i]

    def de(i):
        return r.de_all.at[1 - x, i]

    def xs(i):
        return r.x_all.at[c, i // 2, lax.rem(i, 2)]

    def db(i):
        return r.db_all.at[c, i // 2, lax.rem(i, 2)]

    k_ch, k_xs, k_db = (recvs.take(n_dp) for _ in range(3))
    k_dr = recvs.take(2 * n_dp)
    k_row = k_dr + (1 - x) * n_dp
    k_cho, k_chc, k_cha, k_chx, k_dp = (recvs.take() for _ in range(5))
    k_dex = recvs.take(2)
    k_xsc, k_dbc = recvs.take(n_dp), recvs.take(n_dp)

    r.x_all[c, z, y] = r.x_f[...]
    line(xs, k_xs, k_xsc)

    def feed(rows_x, keep=True):
        total = rows_x.astype(F32) + r.par_f[1:2, 0:w]
        for j in range(tiles):
            cut = slice(j * w, (j + 1) * w)

            @pl.when(is_att)
            def _():
                arrived(r.w1.at[:, cut], k_w1 + j)
                arrived(r.w2.at[cut, :], k_w2 + j)

            hidden = mm(rows_x, r.w1[:, cut]) + r.par_f[0:1, cut]
            below = 0.5 + 0.5 * lax.erf(hidden * (0.5**0.5))
            total = total + mm((hidden * below).astype(BF), r.w2[cut, :])
            if keep:
                slope = below + hidden * (0.3989422804014327 * jnp.exp(-0.5 * hidden * hidden))
                r.slope[:, cut] = slope.astype(BF)
        result, normed, inverse = norm_forward(total, r.par_f)
        if keep:
            r.y_f[...], r.n_f[...], r.inv_f[...] = result, normed, inverse
        else:
            r.y_o[...] = result

    pl.when(is_ff | at_x1)(lambda: feed(r.x_f[...]))
    send(both(at_x0, is_ff), r.y_f, r.x_a, (across, dp), k_x)

    @pl.when(at_x0 & is_ff)
    def _():
        arrived(r.x_all.at[0, z, y], k_xsc + dp)
        feed(r.x_all[0, z, y], False)

    send(both(at_x0, is_ff), r.y_o, r.x_a, (3 - s, dp), k_x)

    @pl.when(at_x1)
    def _():
        r.mrow[...] = jnp.full(r.mrow.shape, -1, jnp.int32)
        r.mrow[0:1, 0 : p.masks] = picks[c]
        places = jnp.where(iota((ln, ln), 0) == r.mrow[0:1, :], 1.0, 0.0).astype(BF)
        r.ch_own[...] = mm_tn(places, r.y_f[...])[0:mp].astype(BF)
        arrived(r.grow.at[1], k_g + 1)
        r.gwide[0 : p.masks, :] += r.grow[1]
        coarse = r.gwide[...].astype(BF)
        fine = (r.gwide[...] - coarse.astype(F32)).astype(BF)
        r.dyf[...] = mm(places, coarse) + mm(places, fine)

    send(at_x1, r.ch_own, r.ch_own, (across, dp), k_cho)
    send(at_x1, r.ch_own, r.ch_two, (core, dp), k_chc)

    def push(owner, kind, src, dst, cond=None):
        home, away = (is_att, is_ff) if owner == 0 else (is_ff, is_att)
        slot_y = 2 + jnp.where(home, 0, 1)
        own_dst, near_dst, far_dst = dst(0), dst(1), dst(slot_y)


        @pl.when(both(home, cond))
        def _():
            own_dst[...] = src(y)[...]

        send(both(away, cond), src(y), near_dst, (core, dp), kind)
        send(cond, src(1 - y), far_dst, (jnp.where(home, s, core), ydp), kind)

    def gathered(kind, dst):
        arrived(dst(slice(1, 4)), kind)

    def lanes(slot):
        if isinstance(slot, slice):
            return pl.ds(slot.start * ln, (slot.stop - slot.start) * ln)
        return pl.ds(slot * ln if isinstance(slot, int) else pl.multiple_of(slot * ln, ln), ln)

    k_dh = [recvs.take() for _ in range(3)]
    k_ctx, k_xt, k_dba, k_sm = (recvs.take() for _ in range(4))
    to_x = lambda slot: r.b_x.at[:, :, lanes(slot)]
    to_ctx = lambda slot: r.b_ctx.at[:, :, lanes(slot)]
    to_dbr = lambda slot: r.b_dbr.at[lanes(slot), :]
    to_sm = lambda slot: r.b_sm.at[slot]

    def to_dh(j):
        return lambda slot: r.b_dh.at[lanes(slot), j * w : (j + 1) * w]

    def push_dh(j):
        push(0, k_dh[j], lambda i: r.dpk.at[:, j * w : (j + 1) * w], to_dh(j))

    def push_rows(cond):
        push(0, k_xt, lambda i: r.xt_a.at[:, i], to_x, cond)
        push(0, k_ctx, lambda i: r.ct_a.at[:, i], to_ctx, cond)

    def turn():
        for dst, src in ((r.xt_a, r.x_a), (r.ct_a, r.ctx)):
            turned = src[...].T
            for b in range(n_dp):
                dst[b // 2, b % 2] = turned[b * p.in_rows : (b + 1) * p.in_rows]

    stage[0] = 1
    @pl.when(at_x0)
    def _():
        masked_gradient()
        turn()

    send(at_x0, r.gwide.at[0 : p.masks], r.grow.at[1], (across, dp), k_g + 1)
    push_rows(at_x0)

    @pl.when(at_x0 & is_att)
    def _():
        feed(r.x_f[...])

    for t in (1, 2):
        line_step(xs, k_xs, t, at_x0, k_xsc)
        line_cross(xs, k_xs, t, at_x0, k_xsc)

    @pl.when(at_x0)
    def _():
        arrived(r.ch_own, k_cho)
        r.ch_all[c, dp] = r.ch_own[...]

    send(at_x0, r.ch_own, r.ch_two, (core, dp), k_chc)
    send(at_x0, r.ch_own, ch(dp), (s, ydp), k_ch + dp)
    for k in range(1, nz):
        send(at_x0, r.ch_own, ch(dp), (s, lax.rem(dp + 2 * k, n_dp)), k_ch + dp)

    def emit(i, src):
        pltpu.make_async_copy(src, outs[i], os.at[i]).start()

    def logits():
        arrived(r.ch_two, k_chc)
        chosen = jnp.concatenate([r.ch_own[...], r.ch_two[...]], 0)
        for at, size in p.chunks:
            part = mm_nt(chosen, r.emb[at : at + size, :])
            o_log[c, 0, :, at : at + size] = part[0 : p.masks].astype(BF)
            o_log[other, 0, :, at : at + size] = part[mp : mp + p.masks].astype(BF)
        emit(0, o_log)

    pl.when(at_x0)(logits)
    line_step(xs, k_xs, 3, at_x0, k_xsc)
    line_cross(xs, k_xs, 3, at_x0, k_xsc)

    k_dy = recvs.take()

    @pl.when(at_x0)
    def _():
        arrived(r.dyin, k_dy)
        r.dyf[...] = r.dyin[...].astype(F32)

    def norm_backward(par, n_ref, inv_ref):
        up, normed = r.dyf[...], n_ref[...]
        gain_part = jnp.sum(up * normed, 0, keepdims=True)
        shift_part = jnp.sum(up, 0, keepdims=True)
        scaled = up * par[2:3, 0:w]
        first_mean = jnp.mean(scaled, -1, keepdims=True)
        second_mean = jnp.mean(scaled * normed, -1, keepdims=True)
        return inv_ref[...] * (scaled - first_mean - normed * second_mean), gain_part, shift_part

    def small(dst, out_part, gain_part, shift_part):
        dst[...] = jnp.zeros(dst.shape, F32)
        n_b, n_w = ff // n_dp, w // n_dp
        for k in range(n_dp):
            dst[k : k + 1, 0:n_b] = r.bsum[:, k * n_b : (k + 1) * n_b]
            dst[k : k + 1, n_b : n_b + n_w] = out_part[:, k * n_w : (k + 1) * n_w]
            dst[k : k + 1, n_b + 128 : n_b + 128 + n_w] = gain_part[:, k * n_w : (k + 1) * n_w]
            dst[k : k + 1, n_b + 256 : n_b + 256 + n_w] = shift_part[:, k * n_w : (k + 1) * n_w]

    dres, gain_part, shift_part = norm_backward(r.par_f, r.n_f, r.inv_f)
    r.dres[...] = dres
    r.db_all[c, z, y] = dres.astype(BF)
    line(db, k_db, k_dbc)
    branch = r.db_all[c, z, y]
    total = r.dres[...]
    for j in range(tiles):
        cut = slice(j * w, (j + 1) * w)
        dhidden = (mm_nt(branch, r.w2[cut, :]) * r.slope[:, cut].astype(F32)).astype(BF)
        r.bsum[:, cut] = jnp.sum(dhidden.astype(F32), 0, keepdims=True)
        total = total + mm_nt(dhidden, r.w1[:, cut])
    r.dyf[...] = total.astype(BF).astype(F32)
    r.vecs[0:1], r.vecs[1:2] = gain_part, shift_part
    line_step(xs, k_xs, 1, at_x1, k_xsc)
    line_cross(xs, k_xs, 1, at_x1, k_xsc)

    dres, gain_part, shift_part = norm_backward(r.par_a, r.n_a, r.inv_a)
    r.dres[...] = dres
    r.dbr_a[...] = dres.astype(BF)
    branch = r.dbr_a[...]
    r.dctx[...] = mm_nt(branch, r.wa[:, 3 * w : 4 * w]).astype(BF)
    for h in range(pairs):
        at = 128 * h
        query = r.pk[:, at : at + 128]
        keyed = split(r.pk[:, w + at : w + at + 128])
        value = split(r.pk[:, 2 * w + at : 2 * w + at + 128])
        upper = r.dctx[:, at : at + 128]
        chance = r.probs[h]
        dchance = mm_nt(upper, value)
        mixed = chance * dchance
        dscores = []
        for cut in (slice(0, 128), slice(128, 256)):
            dscores.append(mixed[:, cut] - chance[:, cut] * jnp.sum(mixed[:, cut], -1, keepdims=True))
        dscores = jnp.concatenate(dscores, 1).astype(BF)
        r.dpk[:, at : at + 128] = (mm(dscores, keyed) * 0.125).astype(BF)
        r.dpk[:, w + at : w + at + 128] = (mm_tn(stack(dscores), split(query)) * 0.125).astype(BF)
        r.dpk[:, 2 * w + at : 2 * w + at + 128] = mm_tn(stack(chance.astype(BF)), split(upper)).astype(BF)
    total = r.dres[...]
    for j in range(3):
        cut = slice(j * w, (j + 1) * w)
        total = total + mm_nt(r.dpk[:, cut], r.wa[:, cut])
    r.dx[...] = total.astype(BF)
    send(at_x1, r.dx, r.dyin, (across, dp), k_dy)

    def row(m, i):
        return r.de_all.at[m, i]

    on_0, on_1 = both(at_x0, is_ff), both(at_x1, is_ff)
    away = jnp.where(is_ff, across, 3 - s)

    def hand_on(src, i):
        send(at_x0, src, row(c, i), (away, dp), k_dr + c * n_dp + i)
        send(both(at_x0, is_att), src, row(0, i), (core, dp), k_dr + i)

        @pl.when(on_0)
        def _():
            r.de_all[1, i] = src[...]

    send(at_x0, r.dx, r.dx_pair, (s, ydp), k_dp)
    hand_on(r.dx, dp)
    pair_line(de, k_row, on_0, dp)

    stage[0] = 2
    pl.when(at_x1)(turn)
    push_rows(at_x1)
    push(0, k_dba, lambda i: r.dbr_a, to_dbr)
    push_dh(0)
    push_dh(1)
    line_step(xs, k_xs, 2, at_x1, k_xsc)
    line_step(db, k_db, 1, None, k_dbc)


    @pl.when(at_x0)
    def _():
        arrived(r.dx_pair, k_dp)

    hand_on(r.dx_pair, ydp)
    pair_line(de, k_row, on_0, ydp)
    line_cross(xs, k_xs, 2, at_x1, k_xsc)
    for k in range(1, nz):
        i = lax.rem(dp + 2 * k, n_dp)
        pl.when(at_x0)(lambda i=i: arrived(ch(i), k_ch + i))
        send(at_x0, ch(i), ch(i), (s, ydp), k_ch + i)
    line_cross(db, k_db, 1, None, k_dbc)
    small(r.sm_f, jnp.sum(r.db_all[c, z, y].astype(F32), 0, keepdims=True), r.vecs[0:1], r.vecs[1:2])
    push(1, k_sm, lambda i: r.sm_f, to_sm)
    r.bsum[...] = jnp.zeros(r.bsum.shape, F32)
    for j in (0, 2):
        cut = slice(j * w, (j + 1) * w)
        r.bsum[:, cut] = jnp.sum(r.dpk[:, cut].astype(F32), 0, keepdims=True)
    small(r.sm_a, jnp.sum(branch.astype(F32), 0, keepdims=True), gain_part, shift_part)
    push(0, k_sm, lambda i: r.sm_a, to_sm)
    push_dh(2)
    for t in (2, 3):
        if t == 2:
            line_step(xs, k_xs, 3, at_x1, k_xsc)
            line_cross(xs, k_xs, 3, at_x1, k_xsc)
        line_step(db, k_db, t, None, k_dbc)
        line_cross(db, k_db, t, None, k_dbc)
        if t == 2:
            drain(0)

    def head_part():
        arrived(r.ch_all.at[other], k_chx)
        arrived(r.lgr.at[0 : n_dp - 1], k_lg)
        arrived(r.ids_all.at[0 : n_dp - 1], k_id)
        for i in range(n_dp):
            for m in range(2):
                r.ch_pack[i, p.masks * m : p.masks * (m + 1)] = r.ch_all[m, i, 0 : p.masks]
        lines = 2 * n_dp * p.masks
        grad = mm_tn(r.lgr[...].reshape(lines, p.share_pad), r.ch_pack[...].reshape(lines, w))
        o_tab[...] = grad[0 : p.share]

    k_in = [recvs.take(4) for _ in range(tiles)]
    half = nz * p.in_rows
    outer = (z == 0) | (z == nz - 1)
    outer_att, inner = both(is_att, outer), both(is_att, jnp.logical_not(outer))
    mate = z + 1 - 2 * lax.rem(z, 2)
    far_base = 2 - 2 * (z // 2)

    def shard(zz, cut):
        return r.wa.at[pl.ds(pl.multiple_of(zz * p.in_rows, p.in_rows), p.in_rows), cut]

    def tile_cut(j):
        return slice(j * w, (j + 1) * w)

    def attention_tile(j):
        cut = tile_cut(j)

        @pl.when(is_att)
        def _():
            if j == 3:
                gathered(k_ctx, to_ctx)
                gathered(k_dba, to_dbr)
                grad = mm(r.b_ctx[...].reshape(half, 4 * ln), r.b_dbr[...])
            else:
                if j == 0:
                    gathered(k_xt, to_x)
                gathered(k_dh[j], to_dh(j))
                grad = mm(r.b_x[...].reshape(half, 4 * ln), r.b_dh[:, cut])
            r.wa[0:half, cut] = grad.astype(BF)

        to_mate = (s, 2 * mate + y)
        for k in range(2):
            send(outer_att, shard(far_base + k, cut), r.r_in.at[2 + k, :, cut], to_mate, k_in[j] + 2 + k)
        send(is_att, shard(mate, cut), r.r_in.at[0, :, cut], to_mate, k_in[j])

    def attention_sum(j):
        cut = tile_cut(j)
        for k in range(2):

            @pl.when(inner)
            def _():
                arrived(r.r_in.at[2 + k, :, cut], k_in[j] + 2 + k)
                rows = pl.ds(pl.multiple_of((far_base + k) * p.in_rows, p.in_rows), p.in_rows)
                r.wa[rows, cut] = (r.wa[rows, cut].astype(F32) + r.r_in[2 + k, :, cut].astype(F32)).astype(BF)

            send(inner, shard(far_base + k, cut), r.r_in.at[1, :, cut], (s, 2 * (far_base + k) + y), k_in[j] + 1)

    def unit_grads(yy, i):
        def four(buf):
            return jnp.concatenate([buf[m, 2 * i + k, yy] for m in range(2) for k in range(2)], 0)

        rows_x, up = four(r.x_all), four(r.db_all)
        hidden = mm(rows_x, r.w1[:, mine_in]) + r.par_f[0:1, mine_in]
        below = 0.5 + 0.5 * lax.erf(hidden * (0.5**0.5))
        slope = below + hidden * (0.3989422804014327 * jnp.exp(-0.5 * hidden * hidden))
        dhidden = (mm_nt(up, r.w2[mine_in, :]) * slope).astype(BF)
        r.u_out[...] += mm_tn((hidden * below).astype(BF), up)
        r.w_col[...] += mm_tn(rows_x, dhidden)

    def units_of(yy, i):
        for k in range(2):
            d = 4 * i + 2 * k + yy
            pl.when((d != dp) | at_x1)(lambda d=d: arrived(r.x_all.at[0, d // 2, lax.rem(d, 2)], k_xsc + d))
            arrived(r.db_all.at[0, d // 2, lax.rem(d, 2)], k_dbc + d)
        unit_grads(yy, i)

    def units_over_y(t):
        for buf, base in ((xs, k_xs), (db, k_db)):
            for k in range(2):
                d = 4 * t + 2 * k + 1 - y
                arrived(buf(d), base + d)
        units_of(1 - y, t)

    entry = iota((p.share_rows, ln), 0) + (s * p.quarter + dp * p.share)

    def scatter(m):
        def step(i, carry):
            hot = []
            for k in range(2):
                hot.append(jnp.where(entry == r.ids_all[2 * i + k, pl.ds(m, 1), :], 1.0, 0.0).astype(BF))
            rows = r.de_all[m, pl.ds(2 * i, 2)].reshape(2 * ln, w)
            o_tab[...] += mm(jnp.concatenate(hot, 1), rows)[0 : p.share]
            return carry

        lax.fori_loop(0, n_dp // 2, step, 0)

    k_col, k_smz = recvs.take(), recvs.take()
    mine_in = pl.ds(pl.multiple_of(dp * p.out_rows, p.out_rows), p.out_rows)
    mate_half = 1 - z // 2

    def gathered_row(cond):
        send(cond, r.de_all.at[1 - x], r.de_all.at[1 - x], (core, dp), k_dex + (1 - x))

    attention_tile(3)
    pair_step(de, k_row, 1, on_0, k_row)
    attention_tile(0)
    attention_sum(3)
    pair_step(de, k_row, 2, on_0, k_row)
    pair_step(de, k_row, 3, on_0, k_row)
    gathered_row(on_0)

    @pl.when(is_ff)
    def _():
        r.u_out[...] = jnp.zeros(r.u_out.shape, F32)
        r.w_col[...] = jnp.zeros(r.w_col.shape, F32)
        units_of(y, z // 2)
        units_of(y, mate_half)

    attention_tile(1)
    attention_sum(0)

    @pl.when(at_x0)
    def _():
        for zz in range(nz):
            i = 2 * zz + 1 - y
            arrived(ch(i), k_ch + i)

    send(at_x0, r.ch_all.at[c], r.ch_all.at[c], (across, dp), k_cha)
    send(at_x0, r.ch_all.at[c], r.ch_all.at[c], (core, dp), k_chx)

    @pl.when(on_1)
    def _():
        arrived(row(0, dp), k_dr + dp)

    pair_line(de, k_row, on_1, dp)
    pl.when(at_x1)(logits)

    @pl.when(on_1)
    def _():
        arrived(row(0, ydp), k_dr + ydp)

    pair_line(de, k_row, on_1, ydp)
    pair_step(de, k_row, 1, on_1, k_row)
    attention_sum(1)

    gathered(k_sm, to_sm)
    r.sm_tot[...] = r.b_sm[0] + r.b_sm[1] + r.b_sm[2] + r.b_sm[3]
    r.r_sm[z] = r.sm_tot[...]
    for k in range(1, nz):
        zz = lax.rem(z + k, nz)
        send(None, r.sm_tot, r.r_sm.at[z], (s, 2 * zz + y), k_smz)

    attention_tile(2)
    pair_step(de, k_row, 2, on_1, k_row)
    pair_step(de, k_row, 3, on_1, k_row)
    gathered_row(on_1)
    attention_sum(2)

    def passed_row(cond):
        @pl.when(cond)
        def _():
            for i in range(n_dp):
                arrived(row(x, i), k_dr + x * n_dp + i)

        send(cond, r.de_all.at[x], r.de_all.at[x], (core, dp), k_dex + x)

    passed_row(on_1)

    @pl.when(at_x1)
    def _():
        arrived(r.ch_all.at[c], k_cha)

    send(at_x1, r.ch_all.at[c], r.ch_all.at[c], (core, dp), k_chx)

    @pl.when(is_ff)
    def _():
        units_over_y(z // 2)
        units_over_y(mate_half)
        o_wout[0] = r.u_out[...].astype(BF)
        emit(4, o_wout)
        for k in range(n_dp):
            r.w_send[k] = r.w_col[k * p.in_rows : (k + 1) * p.in_rows, :].astype(BF)
        r.r_col[dp] = r.w_send[dp]

    for k in (4, 5, 3, 2, 6, 1, 7) if n_dp == 8 else range(1, n_dp):
        to = lax.rem(dp + k, n_dp)
        send(is_ff, r.w_send.at[to], r.r_col.at[dp], (s, to), k_col)
    passed_row(on_0)

    head_part()

    @pl.when(is_att)
    def _():
        arrived(r.de_all.at[0], k_dex)
        arrived(r.de_all.at[1], k_dex + 1)

    scatter(0)
    scatter(1)
    drain(1)
    n_pos = ln // n_dp
    here = pl.ds(pl.multiple_of(dp * n_pos, n_pos), n_pos)
    total = jnp.zeros((n_pos, w), F32)
    for m in range(2):
        for i in range(n_dp):
            total = total + r.de_all[m, i, here, :].astype(F32)
    o_pos[...] = total
    emit(1, o_tab)
    emit(2, o_pos)

    @pl.when(is_att)
    def _():
        mine = pl.ds(pl.multiple_of(z * p.in_rows, p.in_rows), p.in_rows)
        for j in (3, 0, 1, 2):
            cut = tile_cut(j)
            arrived(r.r_in.at[0, :, cut], k_in[j])
            arrived(r.r_in.at[1, :, cut], k_in[j] + 1)
            near_sum = r.wa[mine, cut].astype(F32) + r.r_in[0, :, cut].astype(F32)
            o_win[0, :, cut] = (near_sum + r.r_in[1, :, cut].astype(F32)).astype(BF)
        o_wout[...] = jnp.zeros(o_wout.shape, BF)
        emit(4, o_wout)

    @pl.when(is_ff)
    def _():
        arrived(r.r_col.at[0 : n_dp - 1], k_col)
        for k in range(n_dp):
            o_win[0, :, k * p.out_rows : (k + 1) * p.out_rows] = r.r_col[k]

    emit(3, o_win)

    arrived(r.r_sm.at[0 : nz - 1], k_smz)
    r.sm_all[...] = r.r_sm[0] + r.r_sm[1] + r.r_sm[2] + r.r_sm[3]
    emit(5, o_vec)
    for i, src in enumerate((o_log, o_tab, o_pos, o_win, o_wout, o_vec)):
        pltpu.make_async_copy(src, outs[i], os.at[i]).wait()

    drain(2)
    assert sends.n <= SENDS and recvs.n <= RECVS, (sends.n, recvs.n)


def finish(p, *refs):
    ins, outs, (log_v, log_w, tab_v, win_v, win_w, wout_v, wout_w, vec_v, b_v, v_v, si, so) = refs[:6], refs[6:15], refs[15:]
    pieces = (log_v, tab_v, None, win_v, wout_v, vec_v)

    def copy_in(i):
        return pltpu.make_async_copy(ins[i], pieces[i], si.at[i])

    def copy_out(i, src):
        return pltpu.make_async_copy(src, outs[i], so.at[i])

    for i in (5, 0, 1, 3, 4):
        copy_in(i).start()
    straight = pltpu.make_async_copy(ins[2], outs[2], so.at[2])
    straight.start()
    n_b, n_w = p.ff // p.n_dp, p.width // p.n_dp
    copy_in(5).wait()
    mine = vec_v[pl.ds(lax.axis_index("dp"), 1), :]
    b_v[...] = mine[:, 0:n_b]
    for k in range(3):
        v_v[k] = mine[:, n_b + 128 * k : n_b + 128 * k + n_w]
    done = [copy_out(5, b_v)] + [copy_out(6 + k, v_v.at[k]) for k in range(3)]
    copy_in(0).wait()
    log_w[...] = log_v[...].astype(F32)
    done.append(copy_out(0, log_w))
    for one in done:
        one.start()
    copy_in(1).wait()
    done.append(copy_out(1, tab_v))
    done[-1].start()
    copy_in(3).wait()
    win_w[...] = win_v[...].astype(F32)
    done.append(copy_out(3, win_w))
    done[-1].start()
    copy_in(4).wait()
    wout_w[...] = wout_v[...].astype(F32)
    done.append(copy_out(4, wout_w))
    done[-1].start()
    straight.wait()
    for one in done:
        one.wait()


def whole(
    n_dp,
    token_ids,
    segment_ids,
    masked_rows,
    embedding,
    pos_table,
    w_in,
    w_out,
    b_in,
    b_out,
    norm_gain,
    norm_shift,
    logit_grad,
):
    quarter, width = embedding.shape
    batches, _, length = token_ids.shape
    masks = masked_rows.shape[-1]
    ff = w_in.shape[-1]
    p = Plan(n_dp, length, width, ff, quarter, masks)
    scratch = scratch_list(p)
    shapes = [
        (batches, 1, masks, quarter),
        (p.share, width),
        (length // n_dp, width),
        (1, p.in_rows, ff),
        (1, p.out_rows, width),
        (1, ff // n_dp),
        (1, p.in_rows),
        (1, p.in_rows),
        (1, p.in_rows),
    ]
    vmem = pl.BlockSpec(memory_space=pltpu.VMEM)
    far = pl.BlockSpec(memory_space=pl.ANY)
    part_types = [BF, F32, F32, BF, BF]
    parts = [jax.ShapeDtypeStruct(shape, kind) for shape, kind in zip(shapes, part_types)]
    parts.append(jax.ShapeDtypeStruct((8, width), F32))
    summed = pl.pallas_call(
        functools.partial(fused, p, list(scratch)),
        out_shape=parts,
        in_specs=[vmem] * 7 + [far] * 5,
        out_specs=[far] * 6,
        scratch_shapes=[pltpu.VMEM(*one) for one in scratch.values()]
        + [
            pltpu.SemaphoreType.DMA((SENDS,)),
            pltpu.SemaphoreType.DMA((RECVS,)),
            pltpu.SemaphoreType.DMA((len(p.chunks) + 4,)),
            pltpu.SemaphoreType.DMA((6,)),
        ],
        compiler_params=pltpu.CompilerParams(
            collective_id=0, has_side_effects=True, vmem_limit_bytes=VMEM_LIMIT
        ),
    )(
        token_ids,
        segment_ids,
        masked_rows,
        b_in,
        b_out,
        norm_gain,
        norm_shift,
        logit_grad,
        pos_table,
        embedding,
        w_in,
        w_out,
    )
    room = [
        (shapes[0], BF),
        (shapes[0], F32),
        (shapes[1], F32),
        (shapes[3], BF),
        (shapes[3], F32),
        (shapes[4], BF),
        (shapes[4], F32),
        ((8, width), F32),
        (shapes[5], F32),
        ((3, 1, p.in_rows), F32),
    ]
    return pl.pallas_call(
        functools.partial(finish, p),
        out_shape=[jax.ShapeDtypeStruct(shape, F32) for shape in shapes],
        in_specs=[far] * 6,
        out_specs=[far] * 9,
        scratch_shapes=[pltpu.VMEM(*one) for one in room]
        + [pltpu.SemaphoreType.DMA((6,)), pltpu.SemaphoreType.DMA((9,))],
        compiler_params=pltpu.CompilerParams(vmem_limit_bytes=VMEM_LIMIT),
    )(*summed)


def solution(mesh):
    n_section, n_dp = mesh.shape["section"], mesh.shape["dp"]

    def chosen_form(*args):
        token_ids, embedding, w_in = args[0], args[3], args[5]
        fits = (
            n_section == 4
            and n_dp == 8
            and token_ids.shape[0] == 2
            and token_ids.shape[1:] == (1, 128)
            and w_in.shape[1] % (16 * n_dp) == 0
            and w_in.shape[2] == 4 * w_in.shape[1]
            and embedding.shape[0] % (8 * n_dp) == 0
        )
        return whole(n_dp, *args) if fits else local(*args)

    placed = (
        P(None, "dp", None),
        P(None, "dp", None),
        P(None, "dp", None),
        P("section", None),
        P(),
        P("section", None, None),
        P("section", None, None),
        P("section", None),
        P("section", None),
        P("section", None),
        P("section", None),
        P(None, "dp", None, "section"),
    )
    return jax.shard_map(
        chosen_form,
        mesh=mesh,
        in_specs=placed,
        out_specs=(
            P(None, "dp", None, "section"),
            P(("section", "dp"), None),
            P("dp", None),
            P("section", "dp", None),
            P("section", "dp", None),
            P("section", "dp"),
            P("section", "dp"),
            P("section", "dp"),
            P("section", "dp"),
        ),
        check_vma=False,
    )
```

```python
import functools
import math
import types

import jax
import jax.numpy as jnp
from jax import lax
from jax.experimental import pallas as pl
from jax.experimental.pallas import tpu as pltpu
from jax.sharding import PartitionSpec as P

HEADS = 12


EPSILON = 1e-12


def for_sending(array):
    return jax.tree.map(lambda a: a.astype(jnp.bfloat16) if a.dtype == jnp.float32 else a, array)


def passed_along(block, axis, distance):
    devices = range(lax.axis_size(axis))
    route = [(i - distance, i) for i in devices if i - distance in devices]
    return lax.ppermute(block, axis, route)


def broadcast(value, axis, source):
    kept = jnp.where(lax.axis_index(axis) == source, value, 0).astype(value.dtype)
    return lax.psum(kept, axis)


def norm_forward(resid, gain_row, shift_row):
    centre = jnp.mean(resid, -1, keepdims=True)
    centred = resid - centre
    inverse = lax.rsqrt(jnp.mean(centred * centred, -1, keepdims=True) + EPSILON)
    normed = centred * inverse
    return (normed * gain_row + shift_row, normed, inverse)


def norm_backward(upstream, normed, inverse, gain_row):
    gain_part = jnp.sum(upstream * normed, 0)
    shift_part = jnp.sum(upstream, 0)
    scaled = upstream * gain_row
    first_mean = jnp.mean(scaled, -1, keepdims=True)
    second_mean = jnp.mean(scaled * normed, -1, keepdims=True)
    return (inverse * (scaled - first_mean - normed * second_mean), gain_part, shift_part)


def to_heads(values):
    return values.reshape(values.shape[0], HEADS, values.shape[1] // HEADS)


def row_scores(query, keyed, segment):
    factor = (query.shape[1] // HEADS) ** (-0.5)
    scores = (
        jnp.einsum(
            "qhd,khd->hqk", to_heads(query), to_heads(keyed), preferred_element_type=jnp.float32
        )
        * factor
    )
    allowed = segment[:, None] == segment[None, :]
    return jnp.where(allowed[None], scores, -1000000000.0)


def attend_row(packed, segment):
    width = packed.shape[1] // 3
    scores = row_scores(packed[:, :width], packed[:, width : 2 * width], segment)
    row_peak = jnp.max(scores, -1, keepdims=True)
    exponent = jnp.exp(scores - row_peak)
    row_total = jnp.sum(exponent, -1, keepdims=True)
    chance = (exponent / row_total).astype(jnp.bfloat16)
    context = jnp.einsum(
        "hqk,khd->qhd", chance, to_heads(packed[:, 2 * width :]), preferred_element_type=jnp.float32
    )
    summary = (row_peak + jnp.log(row_total))[..., 0]
    return (context.reshape(packed.shape[0], width).astype(jnp.bfloat16), summary)


def attend_back(packed, segment, summary, upstream):
    length = packed.shape[0]
    width = packed.shape[1] // 3
    factor = (width // HEADS) ** (-0.5)
    scores = row_scores(packed[:, :width], packed[:, width : 2 * width], segment)
    chance = jnp.exp(scores - summary[..., None])
    grad_heads = to_heads(upstream)
    grad_chance = jnp.einsum(
        "qhd,khd->hqk",
        grad_heads,
        to_heads(packed[:, 2 * width :]),
        preferred_element_type=jnp.float32,
    )
    grad_value = jnp.einsum(
        "hqk,qhd->khd", chance.astype(jnp.bfloat16), grad_heads, preferred_element_type=jnp.float32
    )
    grad_score = chance * (grad_chance - jnp.sum(chance * grad_chance, -1, keepdims=True))
    grad_score = grad_score.astype(jnp.bfloat16)
    grad_query = (
        jnp.einsum(
            "hqk,khd->qhd",
            grad_score,
            to_heads(packed[:, width : 2 * width]),
            preferred_element_type=jnp.float32,
        )
        * factor
    )
    grad_key = (
        jnp.einsum(
            "hqk,qhd->khd",
            grad_score,
            to_heads(packed[:, :width]),
            preferred_element_type=jnp.float32,
        )
        * factor
    )
    joined = jnp.concatenate(
        [
            grad_query.reshape(length, width),
            grad_key.reshape(length, width),
            grad_value.reshape(length, width),
        ],
        1,
    )
    return joined.astype(jnp.bfloat16)


def attention_forward(inputs, segment, params):
    w_first, w_second, bias_first, bias_second, gain_row, shift_row = params
    rows_here, length, width = inputs.shape
    flat = inputs.reshape(rows_here * length, width)
    offset = jnp.concatenate(
        [bias_first[:width], jnp.zeros((width,), jnp.float32), bias_first[2 * width : 3 * width]]
    )
    packed = jnp.dot(flat, w_first[:, : 3 * width], preferred_element_type=jnp.float32) + offset
    packed = packed.astype(jnp.bfloat16).reshape(rows_here, length, 3 * width)
    context, summary = lax.map(lambda item: attend_row(item[0], item[1]), (packed, segment))
    branch = (
        jnp.dot(
            context.reshape(-1, width), w_first[:, 3 * width :], preferred_element_type=jnp.float32
        )
        + bias_second
    )
    result, normed, inverse = norm_forward(flat.astype(jnp.float32) + branch, gain_row, shift_row)
    return (result.reshape(rows_here, length, width), (packed, context, summary, normed, inverse))


def attention_backward(inputs, segment, upstream, params, totals):
    w_first, w_second, bias_first, bias_second, gain_row, shift_row = params
    rows_here, length, width = inputs.shape
    result, saved = attention_forward(inputs, segment, params)
    packed, context, summary, normed, inverse = saved
    flat = inputs.reshape(-1, width)
    grad_resid, gain_part, shift_part = norm_backward(
        upstream.reshape(-1, width), normed, inverse, gain_row
    )
    grad_branch = grad_resid.astype(jnp.bfloat16)
    grad_out_proj = jnp.einsum(
        "nd,ne->de", context.reshape(-1, width), grad_branch, preferred_element_type=jnp.float32
    )
    bias_second_part = jnp.sum(grad_branch.astype(jnp.float32), 0)
    grad_context = jnp.einsum(
        "ne,de->nd", grad_branch, w_first[:, 3 * width :], preferred_element_type=jnp.float32
    )
    grad_context = grad_context.astype(jnp.bfloat16).reshape(rows_here, length, width)
    grad_packed = lax.map(
        lambda item: attend_back(item[0], item[1], item[2], item[3]),
        (packed, segment, summary, grad_context),
    )
    flat_packed = grad_packed.reshape(-1, 3 * width)
    grad_proj = jnp.einsum("nd,nc->dc", flat, flat_packed, preferred_element_type=jnp.float32)
    bias_sums = jnp.sum(flat_packed.astype(jnp.float32), 0)
    grad_input = grad_resid + jnp.einsum(
        "nc,dc->nd", flat_packed, w_first[:, : 3 * width], preferred_element_type=jnp.float32
    )
    first_total, second_total, bias_first_total, bias_second_total, gain_total, shift_total = totals
    first_total = (
        first_total.at[:, : 3 * width].add(grad_proj).at[:, 3 * width :].add(grad_out_proj)
    )
    bias_first_total = (
        bias_first_total.at[:width]
        .add(bias_sums[:width])
        .at[2 * width : 3 * width]
        .add(bias_sums[2 * width :])
    )
    updated = (
        first_total,
        second_total,
        bias_first_total,
        bias_second_total + bias_second_part,
        gain_total + gain_part,
        shift_total + shift_part,
    )
    return (grad_input.reshape(rows_here, length, width).astype(jnp.bfloat16), updated)


def feed_forward(inputs, params):
    w_first, w_second, bias_first, bias_second, gain_row, shift_row = params
    rows_here, length, width = inputs.shape
    flat = inputs.reshape(-1, width)
    hidden = jnp.dot(flat, w_first, preferred_element_type=jnp.float32) + bias_first
    active = jax.nn.gelu(hidden, approximate=False).astype(jnp.bfloat16)
    branch = jnp.dot(active, w_second, preferred_element_type=jnp.float32) + bias_second
    result, normed, inverse = norm_forward(flat.astype(jnp.float32) + branch, gain_row, shift_row)
    return (result.reshape(rows_here, length, width), (hidden, active, normed, inverse))


def feed_backward(inputs, upstream, params, totals):
    w_first, w_second, bias_first, bias_second, gain_row, shift_row = params
    rows_here, length, width = inputs.shape
    result, saved = feed_forward(inputs, params)
    hidden, active, normed, inverse = saved
    flat = inputs.reshape(-1, width)
    grad_resid, gain_part, shift_part = norm_backward(
        upstream.reshape(-1, width), normed, inverse, gain_row
    )
    grad_branch = grad_resid.astype(jnp.bfloat16)
    grad_second = jnp.einsum("nf,nd->fd", active, grad_branch, preferred_element_type=jnp.float32)
    bias_second_part = jnp.sum(grad_branch.astype(jnp.float32), 0)
    grad_active = jnp.einsum("nd,fd->nf", grad_branch, w_second, preferred_element_type=jnp.float32)
    through = jax.vjp(lambda inner: jax.nn.gelu(inner, approximate=False), hidden)[1](grad_active)[
        0
    ]
    grad_hidden = through.astype(jnp.bfloat16)
    grad_first = jnp.einsum("nd,nf->df", flat, grad_hidden, preferred_element_type=jnp.float32)
    bias_first_part = jnp.sum(grad_hidden.astype(jnp.float32), 0)
    grad_input = grad_resid + jnp.einsum(
        "nf,df->nd", grad_hidden, w_first, preferred_element_type=jnp.float32
    )
    terms = (grad_first, grad_second, bias_first_part, bias_second_part, gain_part, shift_part)
    updated = tuple((total + term for total, term in zip(totals, terms)))
    return (grad_input.reshape(rows_here, length, width).astype(jnp.bfloat16), updated)


def local(
    token_ids,
    segment_ids,
    masked_rows,
    embedding,
    pos_table,
    w_in,
    w_out,
    b_in,
    b_out,
    norm_gain,
    norm_shift,
    logit_grad,
):
    sections = lax.axis_size("section")
    section_index = lax.axis_index("section")
    quarter, width = embedding.shape
    batches, rows_here, length = token_ids.shape
    params = (
        w_in[0],
        w_out[0],
        b_in[0].astype(jnp.float32),
        b_out[0].astype(jnp.float32),
        norm_gain[0].astype(jnp.float32),
        norm_shift[0].astype(jnp.float32),
    )
    local_ids = token_ids - section_index * quarter
    inside = (local_ids >= 0) & (local_ids < quarter)
    picked = jnp.take(embedding, jnp.clip(local_ids, 0, quarter - 1), axis=0)
    partial_rows = jnp.where(inside[..., None], picked.astype(jnp.float32), 0.0)
    looked = lax.psum(partial_rows.astype(jnp.bfloat16), "section").astype(jnp.float32)
    entry = (looked + pos_table.astype(jnp.float32)).astype(jnp.bfloat16)

    def spare_forward(inputs, segment):
        return jnp.zeros(inputs.shape, jnp.bfloat16)

    def attend_forward(inputs, segment):
        return attention_forward(inputs, segment, params)[0].astype(jnp.bfloat16)

    def feed_only(inputs, segment):
        return feed_forward(inputs, params)[0].astype(jnp.bfloat16)

    def spare_backward(inputs, segment, upstream, totals):
        return (jnp.zeros(inputs.shape, jnp.bfloat16), totals)

    def attend_backward(inputs, segment, upstream, totals):
        return attention_backward(inputs, segment, upstream, params, totals)

    def feed_back_only(inputs, segment, upstream, totals):
        return feed_backward(inputs, upstream, params, totals)

    ticks = batches + sections - 1
    kept = jnp.zeros_like(entry)
    outputs = jnp.zeros_like(entry)
    incoming = jnp.zeros_like(entry[0])
    for moment in range(ticks):
        micro_index = moment - section_index
        is_live = (micro_index >= 0) & (micro_index < batches)
        micro_slot = jnp.clip(micro_index, 0, batches - 1)
        current = jnp.where(section_index == 0, entry[micro_slot], incoming)
        kept = kept.at[micro_slot].set(jnp.where(is_live, current, kept[micro_slot]))
        branch_index = jnp.where(is_live, 1 + section_index % 2, 0)
        result = lax.switch(
            branch_index,
            [spare_forward, attend_forward, feed_only],
            current,
            segment_ids[micro_slot],
        )
        outputs = outputs.at[micro_slot].set(jnp.where(is_live, result, outputs[micro_slot]))
        if moment + 1 < ticks:
            incoming = jax.tree.map(
                lambda part, own: part.astype(own.dtype),
                passed_along(for_sending(result), "section", 1),
                result,
            )
    final_rows = jnp.take_along_axis(outputs, masked_rows[..., None], axis=2)
    head_rows = broadcast(final_rows, "section", sections - 1)
    logits = jnp.einsum("mrkd,vd->mrkv", head_rows, embedding, preferred_element_type=jnp.float32)
    partial_grad = jnp.einsum(
        "mrkv,vd->mrkd", logit_grad, embedding, preferred_element_type=jnp.float32
    )
    grad_rows = lax.psum(partial_grad.astype(jnp.bfloat16), "section").astype(jnp.float32)
    table_head = jnp.einsum(
        "mrkv,mrkd->vd", logit_grad, head_rows, preferred_element_type=jnp.float32
    )
    places = (masked_rows[..., None] == jnp.arange(length)[None, None, None, :]).astype(jnp.float32)
    top_grad = jnp.einsum("mrkl,mrkd->mrld", places, grad_rows, precision=lax.Precision.HIGHEST)
    gradients = (
        jnp.zeros(w_in.shape[1:], jnp.float32),
        jnp.zeros(w_out.shape[1:], jnp.float32),
        jnp.zeros(b_in.shape[1:], jnp.float32),
        jnp.zeros((width,), jnp.float32),
        jnp.zeros((width,), jnp.float32),
        jnp.zeros((width,), jnp.float32),
    )
    grad_entry = jnp.zeros_like(entry)
    back_in = jnp.zeros_like(entry[0])
    for moment in range(ticks):
        micro_index = moment - (sections - 1 - section_index)
        is_live = (micro_index >= 0) & (micro_index < batches)
        micro_slot = jnp.clip(micro_index, 0, batches - 1)
        upstream = jnp.where(
            section_index == sections - 1, top_grad[micro_slot], back_in.astype(jnp.float32)
        )
        branch_index = jnp.where(is_live, 1 + section_index % 2, 0)
        grad_input, gradients = lax.switch(
            branch_index,
            [spare_backward, attend_backward, feed_back_only],
            kept[micro_slot],
            segment_ids[micro_slot],
            upstream,
            gradients,
        )
        grad_entry = grad_entry.at[micro_slot].set(
            jnp.where(is_live, grad_input, grad_entry[micro_slot])
        )
        if moment + 1 < ticks:
            back_in = jax.tree.map(
                lambda part, own: part.astype(own.dtype),
                passed_along(for_sending(grad_input), "section", -1),
                grad_input,
            )
    input_grad = broadcast(grad_entry, "section", 0)
    input_wide = input_grad.astype(jnp.float32)
    pos_grad = jnp.sum(input_wide, (0, 1))
    targets = jnp.where(inside, local_ids, quarter).reshape(-1)
    table_input = jax.ops.segment_sum(
        input_wide.reshape(-1, width), targets, num_segments=quarter + 1
    )[:quarter]
    w_in_part, w_out_part, b_in_part, b_out_part, gain_part, shift_part = gradients
    reduced = (
        lax.psum_scatter(w_in_part, "dp", scatter_dimension=0, tiled=True),
        lax.psum_scatter(w_out_part, "dp", scatter_dimension=0, tiled=True),
        lax.psum_scatter(b_in_part, "dp", scatter_dimension=0, tiled=True),
        lax.psum_scatter(b_out_part, "dp", scatter_dimension=0, tiled=True),
        lax.psum_scatter(gain_part, "dp", scatter_dimension=0, tiled=True),
        lax.psum_scatter(shift_part, "dp", scatter_dimension=0, tiled=True),
        lax.psum_scatter(pos_grad, "dp", scatter_dimension=0, tiled=True),
        lax.psum_scatter(table_input + table_head, "dp", scatter_dimension=0, tiled=True),
    )
    table_grad = reduced[7]
    return (
        logits,
        table_grad,
        reduced[6],
        reduced[0][None],
        reduced[1][None],
        reduced[2][None],
        reduced[3][None],
        reduced[4][None],
        reduced[5][None],
    )


SENDS = 91
RECVS = 84
VMEM_LIMIT = 64 * 2**20
BF = jnp.bfloat16
F32 = jnp.float32
MESH = pl.DeviceIdType.MESH


def mm(a, b):
    return jnp.dot(a, b, preferred_element_type=F32)


def mm_nt(a, b):
    return lax.dot_general(a, b, (((1,), (1,)), ((), ())), preferred_element_type=F32)


def mm_tn(a, b):
    return lax.dot_general(a, b, (((0,), (0,)), ((), ())), preferred_element_type=F32)


def iota(shape, dim):
    return lax.broadcasted_iota(jnp.int32, shape, dim)


def column(row):
    return jnp.broadcast_to(row.astype(F32), (128, 128)).T


class Plan:
    def __init__(self, n_dp, length, width, ff, quarter, masks):
        self.n_dp, self.length, self.width, self.ff = n_dp, length, width, ff
        self.quarter, self.masks = quarter, masks
        self.nz = n_dp // 2
        self.share = quarter // n_dp
        self.in_rows = width // n_dp
        self.out_rows = ff // n_dp
        self.mask_pad = -(-masks // 16) * 16
        self.share_pad = -(-self.share // 128) * 128
        self.share_rows = -(-self.share // 16) * 16
        self.chunks = []
        at = 0
        while at < quarter:
            size = min(1024, quarter - at)
            self.chunks.append((at, size))
            at += size


class Counter:
    def __init__(self):
        self.n = 0

    def take(self, k=1):
        first = self.n
        self.n += k
        return first


def scratch_list(p):
    w, ff, ln = p.width, p.ff, p.length
    mp = p.mask_pad
    return dict(
        tok=((2, 1, ln), jnp.int32),
        seg=((2, 1, ln), jnp.int32),
        picks=((2, 1, p.masks), jnp.int32),
        b_in=((1, ff), BF),
        b_out=((1, w), BF),
        gain=((1, w), BF),
        shift=((1, w), BF),
        emb=((p.quarter, w), BF),
        lg=((2, 1, p.masks, p.quarter), BF),
        pos=((ln, w), BF),
        wa=((w, ff), BF),
        w1=((w, ff), BF),
        w2=((ff, w), BF),
        par_a=((8, ff), F32),
        par_f=((8, ff), F32),
        acc=((2 * ln, w), F32),
        psend=((ln, w), BF),
        psum=((ln, w), BF),
        prow=((2, ln, w), BF),
        lgp=((2 * mp, p.quarter), BF),
        lgs=((p.n_dp, 2 * p.masks, p.share_pad), BF),
        lgr=((p.n_dp, 2 * p.masks, p.share_pad), BF),
        ch_pack=((p.n_dp, 2 * p.masks, w), BF),
        g=((2 * mp, w), F32),
        grow=((2, p.masks, w), F32),
        gwide=((ln, w), F32),
        mrow=((8, ln), jnp.int32),
        ids_own=((8, ln), jnp.int32),
        ids_all=((p.n_dp, 8, ln), jnp.int32),
        x_a=((ln, w), BF),
        x_f=((ln, w), BF),
        y_f=((ln, w), BF),
        y_o=((ln, w), BF),
        pk=((ln, 3 * w), BF),
        ctx=((ln, w), BF),
        probs=((w // 128, ln, 256), F32),
        n_a=((ln, w), F32),
        n_f=((ln, w), F32),
        inv_a=((ln, 1), F32),
        inv_f=((ln, 1), F32),
        slope=((ln, ff), BF),
        xt_a=((p.nz, 2, p.in_rows, ln), BF),
        ct_a=((p.nz, 2, p.in_rows, ln), BF),
        dyin=((ln, w), BF),
        dyf=((ln, w), F32),
        dres=((ln, w), F32),
        dbr_a=((ln, w), BF),
        dpk=((ln, 3 * w), BF),
        dctx=((ln, w), BF),
        dx=((ln, w), BF),
        dx_pair=((ln, w), BF),
        bsum=((1, ff), F32),
        vecs=((8, w), F32),
        sm_a=((8, w), F32),
        sm_f=((8, w), F32),
        b_ctx=((p.nz, p.in_rows, 4 * ln), BF),
        b_x=((p.nz, p.in_rows, 4 * ln), BF),
        b_dbr=((4 * ln, w), BF),
        b_dh=((4 * ln, 3 * w), BF),
        b_sm=((4, 8, w), F32),
        sm_tot=((8, w), F32),
        sm_all=((8, w), F32),
        r_sm=((p.nz, 8, w), F32),
        r_in=((4, p.in_rows, ff), BF),
        x_all=((2, p.nz, 2, ln, w), BF),
        db_all=((2, p.nz, 2, ln, w), BF),
        w_col=((w, p.out_rows), F32),
        w_send=((p.n_dp, p.in_rows, p.out_rows), BF),
        r_col=((p.n_dp, p.in_rows, p.out_rows), BF),
        ch_own=((mp, w), BF),
        ch_two=((mp, w), BF),
        ch_pair=((mp, w), BF),
        ch_far=((mp, w), BF),
        ch_all=((2, p.n_dp, mp, w), BF),
        de_all=((2, p.n_dp, ln, w), BF),
        u_out=((p.out_rows, w), F32),
        o_log=((2, 1, p.masks, p.quarter), BF),
        o_tab=((p.share, w), F32),
        o_pos=((ln // p.n_dp, w), F32),
        o_win=((1, p.in_rows, ff), BF),
        o_wout=((1, p.out_rows, w), BF),
    )


def fused(p, names, *refs):
    far_small, (lg_h, pos_h, emb_h, w_in_h, w_out_h) = refs[:7], refs[7:12]
    outs = refs[12:18]
    r = types.SimpleNamespace(**dict(zip(names, refs[18:])))
    ss, rs, ls, os = refs[18 + len(names) :]
    (o_log, o_tab, o_pos, o_win, o_wout, o_vec) = (r.o_log, r.o_tab, r.o_pos, r.o_win, r.o_wout, r.sm_all)
    w, ff, ln, mp, nz, n_dp = p.width, p.ff, p.length, p.mask_pad, p.nz, p.n_dp
    heads = w // 64
    pairs = heads // 2

    s = lax.axis_index("section")
    dp = lax.axis_index("dp")
    x, c = s // 2, lax.rem(s, 2)
    z, y = dp // 2, lax.rem(dp, 2)
    core = s + 1 - 2 * c
    across = s + 2 - 4 * x
    ydp = dp + 1 - 2 * y
    other = 1 - c
    at_x0, at_x1 = frozenset(["x0"]), frozenset(["x1"])
    is_att, is_ff = frozenset(["att"]), frozenset(["ff"])
    on_0, on_1 = at_x0 | is_ff, at_x1 | is_ff
    outer_att, inner = is_att | {"outer"}, is_att | {"inner"}
    always = frozenset()
    sends, recvs = Counter(), Counter()
    def holds(name):
        if name[:2] == "z>":
            return z >= int(name[2:])
        if name[:2] == "z<":
            return z <= int(name[2:])
        if name in ("outer", "inner"):
            edge = (z == 0) | (z == nz - 1)
            return edge if name == "outer" else jnp.logical_not(edge)
        return {"x0": x == 0, "x1": x == 1, "att": c == 0, "ff": c == 1}[name]

    def at_least(k):
        return frozenset(["z>%d" % k]) if k > 0 else always

    def at_most(k):
        return frozenset(["z<%d" % k]) if k < nz - 1 else always

    not_first, not_last = at_least(1), at_most(nz - 2)
    outside = [always]

    def on(cond):
        def run(body):
            names = sorted(cond - outside[0])
            before, outside[0] = outside[0], outside[0] | cond
            if names:
                pl.when(functools.reduce(lambda a, b: a & b, [holds(name) for name in names]))(body)
            else:
                body()
            outside[0] = before

        return run

    groups, stage = {}, [0]

    def send(cond, src, dst, dev, recv, bulk=None, tag=None):
        cond = cond | outside[0]
        key = (stage[0], cond, tag)
        if key not in groups:
            groups[key] = [sends.take(), 0, bulk]
        group = groups[key]
        group[1] += math.prod(src.shape) * src.dtype.itemsize

        @on(cond)
        def _():
            pltpu.make_async_remote_copy(
                src_ref=src,
                dst_ref=dst,
                send_sem=ss.at[group[0]],
                recv_sem=rs.at[recv],
                device_id=dev,
                device_id_type=MESH,
            ).start()

    def drain(number):
        for (when, cond, _), (slot, size, bulk) in groups.items():
            if when == number:
                rows = size // (w * 2)
                assert bulk is not None or size == rows * w * 2 and rows % 16 == 0 and rows <= p.quarter, (rows, size)
                ref = r.emb.at[0:rows] if bulk is None else bulk

                @on(cond)
                def _():
                    pltpu.make_async_remote_copy(
                        src_ref=ref,
                        dst_ref=ref,
                        send_sem=ss.at[slot],
                        recv_sem=rs.at[0],
                        device_id=(core, dp),
                        device_id_type=MESH,
                    ).wait_send()

    def arrived(dst, recv):
        pltpu.make_async_remote_copy(
            src_ref=dst,
            dst_ref=dst,
            send_sem=ss.at[0],
            recv_sem=rs.at[recv],
            device_id=(core, dp),
            device_id_type=MESH,
        ).wait_recv()

    near_small = (r.tok, r.seg, r.picks, r.b_in, r.b_out, r.gain, r.shift)
    tok, seg, picks, b_in, b_out, gain, shift = near_small

    def small_copy(i):
        return pltpu.make_async_copy(far_small[i], near_small[i], ls.at[len(p.chunks) + 4 + i])

    small_copy(0).start()
    for i, (at, size) in enumerate(p.chunks):
        pltpu.make_async_copy(emb_h.at[pl.ds(at, size)], r.emb.at[pl.ds(at, size)], ls.at[i]).start()
    l_w = len(p.chunks)
    lg, pos = r.lg, r.pos
    pltpu.make_async_copy(lg_h, lg, ls.at[l_w + 2]).start()
    pltpu.make_async_copy(pos_h, pos, ls.at[l_w + 3]).start()
    for i in range(1, 7):
        small_copy(i).start()

    def fill(par):
        par[0:1, :] = b_in[...].astype(F32)
        par[1:2, 0:w] = b_out[...].astype(F32)
        par[2:3, 0:w] = gain[...].astype(F32)
        par[3:4, 0:w] = shift[...].astype(F32)

    barrier = pltpu.get_barrier_semaphore()
    peers = [(s, lax.rem(dp + k, n_dp)) for k in range(1, n_dp)]
    peers += [(core, dp), (across, dp), (3 - s, dp), (core, ydp)]
    for peer in peers:
        pl.semaphore_signal(barrier, inc=1, device_id=peer, device_id_type=MESH)

    small_copy(0).wait()
    cols = [column(tok[m]) for m in range(2)]
    first = s * p.quarter
    for i, (at, size) in enumerate(p.chunks):
        pltpu.make_async_copy(emb_h.at[pl.ds(at, size)], r.emb.at[pl.ds(at, size)], ls.at[i]).wait()
        lane = (iota((ln, size), 1) + (first + at)).astype(F32)
        hot = []
        for m in range(2):
            wide = jnp.concatenate([cols[m]] * (-(-size // 128)), 1)[:, :size]
            hot.append(jnp.where(wide == lane, 1.0, 0.0).astype(BF))
        part = mm(jnp.concatenate(hot, 0), r.emb[at : at + size, :])
        if i == 0:
            r.acc[...] = part
        else:
            r.acc[...] += part
    r.psend[...] = r.acc[pl.ds(pl.multiple_of(ln * other, ln), ln), :].astype(BF)

    @on(is_att)
    def _():
        pltpu.make_async_copy(w_in_h.at[0], r.wa, ls.at[l_w]).start()

    @on(is_ff)
    def _():
        pltpu.make_async_copy(w_in_h.at[0], r.w1, ls.at[l_w]).start()
        pltpu.make_async_copy(w_out_h.at[0], r.w2, ls.at[l_w + 1]).start()

    for i in range(1, 7):
        small_copy(i).wait()
    on(is_att)(lambda: fill(r.par_a))
    on(is_ff)(lambda: fill(r.par_f))

    tiles = ff // w
    k_p, k_g = recvs.take(2), recvs.take(2)
    k_pa, k_pf, k_wa, k_w1, k_w2 = recvs.take(), recvs.take(), recvs.take(tiles), recvs.take(tiles), recvs.take(tiles)
    pl.semaphore_wait(barrier, len(peers))
    send(always, r.psend, r.prow.at[0], (core, dp), k_p)


    pltpu.make_async_copy(lg_h, lg, ls.at[l_w + 2]).wait()
    pltpu.make_async_copy(pos_h, pos, ls.at[l_w + 3]).wait()
    r.lgp[...] = jnp.zeros(r.lgp.shape, BF)
    r.lgp[0 : p.masks] = lg[0, 0]
    r.lgp[mp : mp + p.masks] = lg[1, 0]

    k_lg, k_id = recvs.take(), recvs.take()
    for j in range(n_dp):
        r.lgs[j, :, p.share :] = jnp.zeros((2 * p.masks, p.share_pad - p.share), BF)
        for m in range(2):
            r.lgs[j, p.masks * m : p.masks * (m + 1), 0 : p.share] = lg[m, 0, :, p.share * j : p.share * (j + 1)]
    r.ids_own[...] = jnp.zeros(r.ids_own.shape, jnp.int32)
    for m in range(2):
        r.ids_own[m : m + 1, :] = tok[m]
    r.ids_all[dp] = r.ids_own[...]
    r.lgr[dp] = r.lgs[dp]
    for k in range(1, n_dp):
        to = lax.rem(dp + k, n_dp)
        send(always, r.lgs.at[to], r.lgr.at[dp], (s, to), k_lg, r.lgs.at[0 : n_dp - 1], 1)
        send(always, r.ids_own, r.ids_all.at[dp], (s, to), k_id, r.ids_all.at[0 : n_dp - 1], 2)
    arrived(r.prow.at[0], k_p)
    own_rows = r.acc[pl.ds(pl.multiple_of(ln * c, ln), ln), :]
    r.acc[0:ln, :] = own_rows + r.prow[0].astype(F32)
    r.psum[...] = r.acc[0:ln, :].astype(BF)
    send(at_x1, r.psum, r.prow.at[1], (across, dp), k_p + 1)

    def weights(cond):
        send(is_att | cond, r.par_a, r.par_a, (core, dp), k_pa)
        send(is_ff | cond, r.par_f, r.par_f, (core, dp), k_pf)
        for j in range(tiles):
            cut = slice(j * w, (j + 1) * w)
            send(is_att | cond, w_in_h.at[0, :, cut], r.wa.at[:, cut], (core, dp), k_wa + j, tag=3)
            send(is_ff | cond, w_in_h.at[0, :, cut], r.w1.at[:, cut], (core, dp), k_w1 + j, tag=4)
            send(is_ff | cond, w_out_h.at[0, cut, :], r.w2.at[cut, :], (core, dp), k_w2 + j, tag=5)

    weights(at_x0)

    for i, (at, size) in enumerate(p.chunks):
        part = mm(r.lgp[:, at : at + size], r.emb[at : at + size, :])
        if i == 0:
            r.g[...] = part
        else:
            r.g[...] += part
    send(always, r.g.at[pl.ds(pl.multiple_of(mp * other, mp), p.masks)], r.grow.at[0], (core, dp), k_g)

    def masked_gradient():
        arrived(r.grow.at[0], k_g)
        r.gwide[...] = jnp.zeros(r.gwide.shape, F32)
        r.gwide[0 : p.masks, :] = r.g[pl.ds(pl.multiple_of(mp * c, mp), p.masks), :] + r.grow[0]

    on(at_x1)(masked_gradient)
    weights(at_x1)

    k_x = recvs.take()

    @on(at_x0)
    def _():
        arrived(r.prow.at[1], k_p + 1)
        whole = r.acc[0:ln, :] + r.prow[1].astype(F32)
        r.x_a[...] = (whole + pos[...].astype(F32)).astype(BF)

    @on(is_att)
    def _():
        pltpu.make_async_copy(w_in_h.at[0], r.wa, ls.at[l_w]).wait()
        arrived(r.par_f, k_pf)

    @on(is_ff)
    def _():
        pltpu.make_async_copy(w_in_h.at[0], r.w1, ls.at[l_w]).wait()
        pltpu.make_async_copy(w_out_h.at[0], r.w2, ls.at[l_w + 1]).wait()
        arrived(r.par_a, k_pa)

    @on(at_x1)
    def _():
        arrived(r.x_a, k_x)

    low = jnp.where(iota((ln, 128), 1) < 64, 1.0, 0.0).astype(BF)
    high = jnp.where(iota((ln, 128), 1) < 64, 0.0, 1.0).astype(BF)

    def split(block):
        return jnp.concatenate([block * low, block * high], 0)

    def stack(block):
        return jnp.concatenate([block[:, 0:128], block[:, 128:256]], 0)

    def norm_forward(resid, par):
        centred = resid - jnp.mean(resid, -1, keepdims=True)
        inverse = lax.rsqrt(jnp.mean(centred * centred, -1, keepdims=True) + EPSILON)
        normed = centred * inverse
        return (normed * par[2:3, 0:w] + par[3:4, 0:w]).astype(BF), normed, inverse

    rows_x = r.x_a[...]

    def wa_tile(j):
        on(is_ff)(lambda: arrived(r.wa.at[:, j * w : (j + 1) * w], k_wa + j))

    for j in range(3):
        wa_tile(j)
        part = mm(rows_x, r.wa[:, j * w : (j + 1) * w])
        if j != 1:
            part = part + r.par_a[0:1, j * w : (j + 1) * w]
        r.pk[:, j * w : (j + 1) * w] = part.astype(BF)
    seg_row = seg[c].astype(F32)
    seg_col = column(seg[c])
    seg_row = jnp.broadcast_to(jnp.concatenate([seg_row, seg_row], 1), (ln, 256))
    seg_col = jnp.concatenate([seg_col, seg_col], 1)
    for h in range(pairs):
        at = 128 * h
        query = r.pk[:, at : at + 128]
        keyed = split(r.pk[:, w + at : w + at + 128])
        value = split(r.pk[:, 2 * w + at : 2 * w + at + 128])
        scores = jnp.where(seg_row == seg_col, mm_nt(query, keyed) * 0.125, -1e9)
        chance = []
        for half in (scores[:, 0:128], scores[:, 128:256]):
            power = jnp.exp(half - jnp.max(half, -1, keepdims=True))
            chance.append(power / jnp.sum(power, -1, keepdims=True))
        chance = jnp.concatenate(chance, 1)
        r.probs[h] = chance
        r.ctx[:, at : at + 128] = mm(chance.astype(BF), value).astype(BF)
    wa_tile(3)
    resid = rows_x.astype(F32) + mm(r.ctx[...], r.wa[:, 3 * w : 4 * w]) + r.par_a[1:2, 0:w]
    r.x_f[...], r.n_a[...], r.inv_a[...] = norm_forward(resid, r.par_a)

    class Gather:
        def __init__(self, buf):
            self.buf = buf
            self.near, self.far, self.own, self.core0 = recvs.take(nz), recvs.take(2), recvs.take(), recvs.take(4)

        def at(self, zz, yy):
            return self.buf.at[c, zz, yy]

        def pair(self, m, half_z, yy):
            return self.buf.at[m, pl.ds(2 * half_z, 2), yy]

        def start(self):
            own = self.at(z, y)
            send(not_last, own, own, (s, dp + 2), self.near + z)
            send(not_first, own, own, (s, dp - 2), self.near + z)
            send(is_att, own, own, (core, dp), self.own)
            self.to_y(z, always)

        def to_y(self, zz, cond):
            recv = jnp.where(c == 0, self.core0 + 2, self.far) + zz // 2
            send(cond, self.at(zz, y), self.at(zz, y), (jnp.where(c == 0, core, s), ydp), recv)

        def step(self, t, cond=always):
            for sign in (-1, 1):
                here, zz = at_distance(t, sign, cond)
                piece = self.at(zz, y)
                on(here)(lambda piece=piece, zz=zz: arrived(piece, self.near + zz))
                if t < nz - 1:
                    send(onward(here, sign), piece, piece, (s, dp - 2 * sign), self.near + zz)
                send(here | is_att, piece, piece, (core, dp), self.core0 + zz // 2)

        def cross(self, t, cond=always):
            for sign in (-1, 1):
                here, zz = at_distance(t, sign, cond)
                self.to_y(zz, here)

        def from_core0(self, half_z, own_side):
            if own_side:
                mine = (z // 2) == half_z

                @pl.when(mine)
                def _():
                    arrived(self.buf.at[0, z + 1 - 2 * lax.rem(z, 2), y], self.core0 + half_z)

                @pl.when(jnp.logical_not(mine))
                def _():
                    arrived(self.pair(0, half_z, y), self.core0 + half_z)

            else:
                arrived(self.pair(0, half_z, 1 - y), self.core0 + 2 + half_z)

        def from_y(self, half_z):
            arrived(self.pair(1, half_z, 1 - y), self.far + half_z)

    def at_distance(t, sign, cond):
        here = cond | (at_least(t) if sign < 0 else at_most(nz - 1 - t))
        return here, jnp.clip(z + sign * t, 0, nz - 1)

    def onward(here, sign):
        return here | (not_last if sign < 0 else not_first)

    def pair_line(buf, base, cond, i):
        piece = buf(i)
        send(cond | not_last, piece, piece, (s, dp + 2), base + i)
        send(cond | not_first, piece, piece, (s, dp - 2), base + i)

    def pair_step(buf, base, t, cond, on_x):
        for sign in (-1, 1):
            for side in (0, 1):
                here, zz = at_distance(t, sign, cond)
                from_dp = 2 * zz + (1 - y if side else y)
                piece = buf(from_dp)
                on(here)(lambda piece=piece, from_dp=from_dp: arrived(piece, base + from_dp))
                if t < nz - 1:
                    send(onward(here, sign), piece, piece, (s, dp - 2 * sign), base + from_dp)
                send(here, piece, piece, (across, dp), on_x)

    def ch(i):
        return r.ch_all.at[c, i]

    def de(i):
        return r.de_all.at[1 - x, i]

    k_row, k_pass = recvs.take(n_dp), recvs.take()
    k_ch, k_cho, k_chc, k_chp, k_chq, k_cha, k_chx, k_dp = (recvs.take() for _ in range(8))
    k_dex = recvs.take(2)
    xs, db = Gather(r.x_all), Gather(r.db_all)

    r.x_all[c, z, y] = r.x_f[...]
    xs.start()

    def feed(rows_x, keep=True):
        total = rows_x.astype(F32) + r.par_f[1:2, 0:w]
        for j in range(tiles):
            cut = slice(j * w, (j + 1) * w)

            @on(is_att)
            def _():
                arrived(r.w1.at[:, cut], k_w1 + j)
                arrived(r.w2.at[cut, :], k_w2 + j)

            hidden = mm(rows_x, r.w1[:, cut]) + r.par_f[0:1, cut]
            below = 0.5 + 0.5 * lax.erf(hidden * (0.5**0.5))
            total = total + mm((hidden * below).astype(BF), r.w2[cut, :])
            if keep:
                slope = below + hidden * (0.3989422804014327 * jnp.exp(-0.5 * hidden * hidden))
                r.slope[:, cut] = slope.astype(BF)
        result, normed, inverse = norm_forward(total, r.par_f)
        if keep:
            r.y_f[...], r.n_f[...], r.inv_f[...] = result, normed, inverse
        else:
            r.y_o[...] = result

    on(on_0)(lambda: feed(r.x_f[...]))
    on(at_x1)(lambda: feed(r.x_f[...]))
    send(at_x0 | is_ff, r.y_f, r.x_a, (across, dp), k_x)

    @on(at_x0 | is_ff)
    def _():
        arrived(r.x_all.at[0, z, y], xs.own)
        feed(r.x_all[0, z, y], False)

    send(at_x0 | is_ff, r.y_o, r.x_a, (3 - s, dp), k_x)

    @on(at_x1)
    def _():
        r.mrow[...] = jnp.full(r.mrow.shape, -1, jnp.int32)
        r.mrow[0:1, 0 : p.masks] = picks[c]
        places = jnp.where(iota((ln, ln), 0) == r.mrow[0:1, :], 1.0, 0.0).astype(BF)
        r.ch_own[...] = mm_tn(places, r.y_f[...])[0:mp].astype(BF)
        arrived(r.grow.at[1], k_g + 1)
        r.gwide[0 : p.masks, :] += r.grow[1]
        coarse = r.gwide[...].astype(BF)
        fine = (r.gwide[...] - coarse.astype(F32)).astype(BF)
        r.dyf[...] = mm(places, coarse) + mm(places, fine)

    send(at_x1, r.ch_own, r.ch_own, (across, dp), k_cho)
    send(at_x1, r.ch_own, r.ch_two, (core, dp), k_chc)
    send(at_x1, r.ch_own, r.ch_pair, (s, ydp), k_chp)

    def push(owner, kind, src, dst, cond=always):
        home, away = (is_att, is_ff) if owner == 0 else (is_ff, is_att)
        at_home = holds("att" if owner == 0 else "ff")
        slot_y = 2 + jnp.where(at_home, 0, 1)
        own_dst, near_dst, far_dst = dst(0), dst(1), dst(slot_y)


        @on(home | cond)
        def _():
            own_dst[...] = src(y)[...]

        send(away | cond, src(y), near_dst, (core, dp), kind)
        send(cond, src(1 - y), far_dst, (jnp.where(at_home, s, core), ydp), kind)

    def gathered(kind, dst):
        arrived(dst(slice(1, 4)), kind)

    def lanes(slot):
        if isinstance(slot, slice):
            return pl.ds(slot.start * ln, (slot.stop - slot.start) * ln)
        return pl.ds(slot * ln if isinstance(slot, int) else pl.multiple_of(slot * ln, ln), ln)

    k_dh = [recvs.take() for _ in range(3)]
    k_ctx, k_xt, k_dba, k_sm = (recvs.take() for _ in range(4))
    to_x = lambda slot: r.b_x.at[:, :, lanes(slot)]
    to_ctx = lambda slot: r.b_ctx.at[:, :, lanes(slot)]
    to_dbr = lambda slot: r.b_dbr.at[lanes(slot), :]
    to_sm = lambda slot: r.b_sm.at[slot]

    def to_dh(j):
        return lambda slot: r.b_dh.at[lanes(slot), j * w : (j + 1) * w]

    def push_dh(j):
        push(0, k_dh[j], lambda i: r.dpk.at[:, j * w : (j + 1) * w], to_dh(j))

    def push_rows():
        push(0, k_xt, lambda i: r.xt_a.at[:, i], to_x)
        push(0, k_ctx, lambda i: r.ct_a.at[:, i], to_ctx)

    def turn():
        for dst, src in ((r.xt_a, r.x_a), (r.ct_a, r.ctx)):
            turned = src[...].T
            for b in range(n_dp):
                dst[b // 2, b % 2] = turned[b * p.in_rows : (b + 1) * p.in_rows]

    def emit(i, src):
        pltpu.make_async_copy(src, outs[i], os.at[i]).start()

    def logits():
        arrived(r.ch_two, k_chc)
        chosen = jnp.concatenate([r.ch_own[...], r.ch_two[...]], 0)
        for at, size in p.chunks:
            part = mm_nt(chosen, r.emb[at : at + size, :])
            o_log[c, 0, :, at : at + size] = part[0 : p.masks].astype(BF)
            o_log[other, 0, :, at : at + size] = part[mp : mp + p.masks].astype(BF)
        emit(0, o_log)

    @on(at_x0)
    def _():
        masked_gradient()
        send(at_x0, r.gwide.at[0 : p.masks], r.grow.at[1], (across, dp), k_g + 1)
        turn()
        push_rows()
        on(is_att)(lambda: feed(r.x_f[...]))
        for t in (1, 2):
            xs.step(t)
            xs.cross(t)
        arrived(r.ch_own, k_cho)
        r.ch_all[c, dp] = r.ch_own[...]
        send(at_x0, r.ch_own, r.ch_two, (core, dp), k_chc)
        for k in range(1, nz):
            send(at_x0, r.ch_own, ch(dp), (s, lax.rem(dp + 2 * k, n_dp)), k_ch)
        logits()
        xs.step(3)
        xs.cross(3)

    stage[0] = 1

    k_dy = recvs.take()

    @on(at_x0)
    def _():
        arrived(r.dyin, k_dy)
        r.dyf[...] = r.dyin[...].astype(F32)

    def norm_backward(par, n_ref, inv_ref):
        up, normed = r.dyf[...], n_ref[...]
        gain_part = jnp.sum(up * normed, 0, keepdims=True)
        shift_part = jnp.sum(up, 0, keepdims=True)
        scaled = up * par[2:3, 0:w]
        first_mean = jnp.mean(scaled, -1, keepdims=True)
        second_mean = jnp.mean(scaled * normed, -1, keepdims=True)
        return inv_ref[...] * (scaled - first_mean - normed * second_mean), gain_part, shift_part

    def small(dst, out_part, gain_part, shift_part):
        dst[...] = jnp.zeros(dst.shape, F32)
        n_b, n_w = ff // n_dp, w // n_dp
        for k in range(n_dp):
            dst[k : k + 1, 0:n_b] = r.bsum[:, k * n_b : (k + 1) * n_b]
            dst[k : k + 1, n_b : n_b + n_w] = out_part[:, k * n_w : (k + 1) * n_w]
            dst[k : k + 1, n_b + 128 : n_b + 128 + n_w] = gain_part[:, k * n_w : (k + 1) * n_w]
            dst[k : k + 1, n_b + 256 : n_b + 256 + n_w] = shift_part[:, k * n_w : (k + 1) * n_w]

    dres, gain_part, shift_part = norm_backward(r.par_f, r.n_f, r.inv_f)
    r.dres[...] = dres
    r.db_all[c, z, y] = dres.astype(BF)
    db.start()
    branch = r.db_all[c, z, y]
    total = r.dres[...]
    for j in range(tiles):
        cut = slice(j * w, (j + 1) * w)
        dhidden = (mm_nt(branch, r.w2[cut, :]) * r.slope[:, cut].astype(F32)).astype(BF)
        r.bsum[:, cut] = jnp.sum(dhidden.astype(F32), 0, keepdims=True)
        total = total + mm_nt(dhidden, r.w1[:, cut])
    r.dyf[...] = total.astype(BF).astype(F32)
    r.vecs[0:1], r.vecs[1:2] = gain_part, shift_part

    @on(at_x1)
    def _():
        xs.step(1)
        xs.cross(1)

    dres, gain_part, shift_part = norm_backward(r.par_a, r.n_a, r.inv_a)
    r.dres[...] = dres
    r.dbr_a[...] = dres.astype(BF)
    branch = r.dbr_a[...]
    r.dctx[...] = mm_nt(branch, r.wa[:, 3 * w : 4 * w]).astype(BF)
    for h in range(pairs):
        at = 128 * h
        query = r.pk[:, at : at + 128]
        keyed = split(r.pk[:, w + at : w + at + 128])
        value = split(r.pk[:, 2 * w + at : 2 * w + at + 128])
        upper = r.dctx[:, at : at + 128]
        chance = r.probs[h]
        dchance = mm_nt(upper, value)
        mixed = chance * dchance
        dscores = []
        for cut in (slice(0, 128), slice(128, 256)):
            dscores.append(mixed[:, cut] - chance[:, cut] * jnp.sum(mixed[:, cut], -1, keepdims=True))
        dscores = jnp.concatenate(dscores, 1).astype(BF)
        r.dpk[:, at : at + 128] = (mm(dscores, keyed) * 0.125).astype(BF)
        r.dpk[:, w + at : w + at + 128] = (mm_tn(stack(dscores), split(query)) * 0.125).astype(BF)
        r.dpk[:, 2 * w + at : 2 * w + at + 128] = mm_tn(stack(chance.astype(BF)), split(upper)).astype(BF)
    total = r.dres[...]
    for j in range(3):
        cut = slice(j * w, (j + 1) * w)
        total = total + mm_nt(r.dpk[:, cut], r.wa[:, cut])
    r.dx[...] = total.astype(BF)
    send(at_x1, r.dx, r.dyin, (across, dp), k_dy)

    def row(m, i):
        return r.de_all.at[m, i]

    away = jnp.where(c == 1, across, 3 - s)

    def hand_on(src, i):
        send(at_x0, src, row(c, i), (away, dp), jnp.where(c == 1, k_pass, k_row + i))
        send(at_x0 | is_att, src, row(0, i), (core, dp), k_pass)

        @on(on_0)
        def _():
            r.de_all[1, i] = src[...]
            pair_line(de, k_row, on_0, i)

    @on(at_x0)
    def _():
        send(at_x0, r.dx, r.dx_pair, (s, ydp), k_dp)
        hand_on(r.dx, dp)

    @on(is_att)
    def _():
        o_wout[...] = jnp.zeros(o_wout.shape, BF)
        emit(4, o_wout)

    @on(at_x1)
    def _():
        turn()
        push_rows()

    push(0, k_dba, lambda i: r.dbr_a, to_dbr)
    push_dh(0)
    small(r.sm_f, jnp.sum(r.db_all[c, z, y].astype(F32), 0, keepdims=True), r.vecs[0:1], r.vecs[1:2])
    push(1, k_sm, lambda i: r.sm_f, to_sm)
    r.bsum[...] = jnp.zeros(r.bsum.shape, F32)
    for j in (0, 2):
        cut = slice(j * w, (j + 1) * w)
        r.bsum[:, cut] = jnp.sum(r.dpk[:, cut].astype(F32), 0, keepdims=True)
    small(r.sm_a, jnp.sum(branch.astype(F32), 0, keepdims=True), gain_part, shift_part)
    push(0, k_sm, lambda i: r.sm_a, to_sm)
    push_dh(1)

    @on(at_x1)
    def _():
        arrived(r.ch_pair, k_chp)
        send(at_x1, r.ch_pair, r.ch_far, (across, dp), k_chq)
        xs.step(2)

    db.step(1)

    @on(at_x0)
    def _():
        arrived(r.dx_pair, k_dp)
        hand_on(r.dx_pair, ydp)

    on(at_x1)(lambda: xs.cross(2))
    db.cross(1)
    push_dh(2)

    @on(at_x1)
    def _():
        xs.step(3)
        xs.cross(3)

    db.step(2)
    db.cross(2)

    @on(at_x0)
    def _():
        arrived(r.ch_far, k_chq)
        r.ch_all[c, ydp] = r.ch_far[...]
        for k in range(1, nz):
            send(at_x0, r.ch_far, ch(ydp), (s, lax.rem(dp + 2 * k, n_dp)), k_ch)

    drain(0)

    def head_part():
        arrived(r.ch_all.at[other], k_chx)
        arrived(r.lgr.at[0 : n_dp - 1], k_lg)
        arrived(r.ids_all.at[0 : n_dp - 1], k_id)
        for i in range(n_dp):
            for m in range(2):
                r.ch_pack[i, p.masks * m : p.masks * (m + 1)] = r.ch_all[m, i, 0 : p.masks]
        lines = 2 * n_dp * p.masks
        grad = mm_tn(r.lgr[...].reshape(lines, p.share_pad), r.ch_pack[...].reshape(lines, w))
        o_tab[...] = grad[0 : p.share]

    k_in = [recvs.take(3) for _ in range(tiles)]
    half = nz * p.in_rows
    mate = z + 1 - 2 * lax.rem(z, 2)
    far_base = 2 - 2 * (z // 2)

    def shard(zz, cut):
        return r.wa.at[pl.ds(pl.multiple_of(zz * p.in_rows, p.in_rows), p.in_rows), cut]

    def tile_cut(j):
        return slice(j * w, (j + 1) * w)

    def attention_tile(j):
        cut = tile_cut(j)

        @on(is_att)
        def _():
            if j == 3:
                gathered(k_ctx, to_ctx)
                gathered(k_dba, to_dbr)
                grad = mm(r.b_ctx[...].reshape(half, 4 * ln), r.b_dbr[...])
            else:
                if j == 0:
                    gathered(k_xt, to_x)
                gathered(k_dh[j], to_dh(j))
                grad = mm(r.b_x[...].reshape(half, 4 * ln), r.b_dh[:, cut])
            r.wa[0:half, cut] = grad.astype(BF)

        to_mate = (s, 2 * mate + y)
        for k in range(2):
            send(outer_att, shard(far_base + k, cut), r.r_in.at[2 + k, :, cut], to_mate, k_in[j] + 2)
        send(is_att, shard(mate, cut), r.r_in.at[0, :, cut], to_mate, k_in[j])

    def attention_sum(j):
        cut = tile_cut(j)

        @on(inner)
        def _():
            arrived(r.r_in.at[2:4, :, cut], k_in[j] + 2)
            for k in range(2):
                rows = pl.ds(pl.multiple_of((far_base + k) * p.in_rows, p.in_rows), p.in_rows)
                r.wa[rows, cut] = (r.wa[rows, cut].astype(F32) + r.r_in[2 + k, :, cut].astype(F32)).astype(BF)
                send(inner, shard(far_base + k, cut), r.r_in.at[1, :, cut], (s, 2 * (far_base + k) + y), k_in[j] + 1)

    def unit_grads(yy, i):
        def four(buf):
            return jnp.concatenate([buf[m, 2 * i + k, yy] for m in range(2) for k in range(2)], 0)

        rows_x, up = four(r.x_all), four(r.db_all)
        hidden = mm(rows_x, r.w1[:, mine_in]) + r.par_f[0:1, mine_in]
        below = 0.5 + 0.5 * lax.erf(hidden * (0.5**0.5))
        slope = below + hidden * (0.3989422804014327 * jnp.exp(-0.5 * hidden * hidden))
        dhidden = (mm_nt(up, r.w2[mine_in, :]) * slope).astype(BF)
        r.u_out[...] += mm_tn((hidden * below).astype(BF), up)
        r.w_col[...] += mm_tn(rows_x, dhidden)

    def units_here(t):
        for one in (xs, db):
            one.from_core0(t, True)
        unit_grads(y, t)

    def units_over_y(t):
        for one in (xs, db):
            one.from_core0(t, False)
            one.from_y(t)
        unit_grads(1 - y, t)

    entry = iota((p.share_rows, ln), 0) + (s * p.quarter + dp * p.share)

    def scatter(m):
        def step(i, carry):
            hot = []
            for k in range(2):
                hot.append(jnp.where(entry == r.ids_all[2 * i + k, pl.ds(m, 1), :], 1.0, 0.0).astype(BF))
            rows = r.de_all[m, pl.ds(2 * i, 2)].reshape(2 * ln, w)
            o_tab[...] += mm(jnp.concatenate(hot, 1), rows)[0 : p.share]
            return carry

        lax.fori_loop(0, n_dp // 2, step, 0)

    k_col, k_smz = recvs.take(), recvs.take()
    mine_in = pl.ds(pl.multiple_of(dp * p.out_rows, p.out_rows), p.out_rows)
    mate_half = 1 - z // 2

    def gathered_row(cond):
        send(cond, r.de_all.at[1 - x], r.de_all.at[1 - x], (core, dp), k_dex + (1 - x))

    attention_tile(3)
    pair_step(de, k_row, 1, on_0, k_pass)
    attention_tile(0)
    db.step(3)
    db.cross(3)
    attention_sum(3)
    pair_step(de, k_row, 2, on_0, k_pass)

    @on(at_x0)
    def _():
        arrived(r.ch_all.at[c, 0 : n_dp - 2], k_ch)
        send(at_x0, r.ch_all.at[c], r.ch_all.at[c], (across, dp), k_cha)
        send(at_x0, r.ch_all.at[c], r.ch_all.at[c], (core, dp), k_chx)


    @on(is_ff)
    def _():
        r.u_out[...] = jnp.zeros(r.u_out.shape, F32)
        r.w_col[...] = jnp.zeros(r.w_col.shape, F32)
        on(at_x1)(lambda: arrived(r.x_all.at[0, z, y], xs.own))
        arrived(r.db_all.at[0, z, y], db.own)
        units_here(z // 2)
        units_here(mate_half)

    attention_tile(1)
    attention_sum(0)

    def row_0(i):
        @on(on_1)
        def _():
            arrived(row(0, i), k_row + i)
            pair_line(de, k_row, on_1, i)

    row_0(dp)
    on(at_x1)(logits)
    row_0(ydp)
    pair_step(de, k_row, 1, on_1, k_pass)
    attention_sum(1)

    attention_tile(2)
    pair_step(de, k_row, 2, on_1, k_pass)

    gathered(k_sm, to_sm)
    r.sm_tot[...] = r.b_sm[0] + r.b_sm[1] + r.b_sm[2] + r.b_sm[3]
    r.r_sm[z] = r.sm_tot[...]
    for k in range(1, nz):
        zz = lax.rem(z + k, nz)
        send(always, r.sm_tot, r.r_sm.at[z], (s, 2 * zz + y), k_smz)

    attention_sum(2)

    @on(is_ff)
    def _():
        units_over_y(z // 2)

    pair_step(de, k_row, 3, is_ff, k_pass)
    gathered_row(is_ff)

    def passed_row(cond):
        @on(cond)
        def _():
            arrived(r.de_all.at[x], k_pass)

        send(cond, r.de_all.at[x], r.de_all.at[x], (core, dp), k_dex + x)

    @on(is_ff)
    def _():
        units_over_y(mate_half)
        o_wout[0] = r.u_out[...].astype(BF)
        emit(4, o_wout)
        for k in range(n_dp):
            r.w_send[k] = r.w_col[k * p.in_rows : (k + 1) * p.in_rows, :].astype(BF)
        r.r_col[dp] = r.w_send[dp]

    for k in (4, 5, 3, 2, 6, 1, 7) if n_dp == 8 else range(1, n_dp):
        to = lax.rem(dp + k, n_dp)
        send(is_ff, r.w_send.at[to], r.r_col.at[dp], (s, to), k_col)
    passed_row(is_ff)

    @on(at_x1)
    def _():
        arrived(r.ch_all.at[c], k_cha)
        send(at_x1, r.ch_all.at[c], r.ch_all.at[c], (core, dp), k_chx)


    head_part()

    on(is_att)(lambda: arrived(r.de_all.at[1 - x], k_dex + 1 - x))
    scatter(1 - x)
    on(is_att)(lambda: arrived(r.de_all.at[x], k_dex + x))
    scatter(x)
    n_pos = ln // n_dp
    here = pl.ds(pl.multiple_of(dp * n_pos, n_pos), n_pos)
    total = jnp.zeros((n_pos, w), F32)
    for m in range(2):
        for i in range(n_dp):
            total = total + r.de_all[m, i, here, :].astype(F32)
    o_pos[...] = total
    emit(1, o_tab)
    emit(2, o_pos)

    @on(is_att)
    def _():
        mine = pl.ds(pl.multiple_of(z * p.in_rows, p.in_rows), p.in_rows)
        for j in (3, 0, 1, 2):
            cut = tile_cut(j)
            arrived(r.r_in.at[0, :, cut], k_in[j])
            arrived(r.r_in.at[1, :, cut], k_in[j] + 1)
            near_sum = r.wa[mine, cut].astype(F32) + r.r_in[0, :, cut].astype(F32)
            o_win[0, :, cut] = (near_sum + r.r_in[1, :, cut].astype(F32)).astype(BF)
            pltpu.make_async_copy(o_win.at[:, :, cut], outs[3].at[:, :, cut], os.at[3]).start()

    @on(is_ff)
    def _():
        arrived(r.r_col.at[0 : n_dp - 1], k_col)
        for k in range(n_dp):
            cut = slice(k * p.out_rows, (k + 1) * p.out_rows)
            pltpu.make_async_copy(r.r_col.at[k], outs[3].at[0, :, cut], os.at[3]).start()

    arrived(r.r_sm.at[0 : nz - 1], k_smz)
    r.sm_all[...] = r.r_sm[0] + r.r_sm[1] + r.r_sm[2] + r.r_sm[3]
    emit(5, o_vec)
    for i, src in enumerate((o_log, o_tab, o_pos, o_win, o_wout, o_vec)):
        pltpu.make_async_copy(src, outs[i], os.at[i]).wait()

    drain(1)
    assert sends.n <= SENDS and recvs.n <= RECVS, (sends.n, recvs.n)


def finish(p, *refs):
    ins, outs, (log_v, log_w, tab_v, win_v, win_w, wout_v, wout_w, vec_v, b_v, v_v, si, so) = refs[:6], refs[6:15], refs[15:]
    pieces = (log_v, tab_v, None, win_v, wout_v, vec_v)

    def copy_in(i):
        return pltpu.make_async_copy(ins[i], pieces[i], si.at[i])

    def copy_out(i, src):
        return pltpu.make_async_copy(src, outs[i], so.at[i])

    for i in (5, 0, 1, 3, 4):
        copy_in(i).start()
    straight = pltpu.make_async_copy(ins[2], outs[2], so.at[2])
    straight.start()
    n_b, n_w = p.ff // p.n_dp, p.width // p.n_dp
    copy_in(5).wait()
    mine = vec_v[pl.ds(lax.axis_index("dp"), 1), :]
    b_v[...] = mine[:, 0:n_b]
    for k in range(3):
        v_v[k] = mine[:, n_b + 128 * k : n_b + 128 * k + n_w]
    done = [copy_out(5, b_v)] + [copy_out(6 + k, v_v.at[k]) for k in range(3)]
    copy_in(0).wait()
    log_w[...] = log_v[...].astype(F32)
    done.append(copy_out(0, log_w))
    for one in done:
        one.start()
    copy_in(1).wait()
    done.append(copy_out(1, tab_v))
    done[-1].start()
    copy_in(3).wait()
    win_w[...] = win_v[...].astype(F32)
    done.append(copy_out(3, win_w))
    done[-1].start()
    copy_in(4).wait()
    wout_w[...] = wout_v[...].astype(F32)
    done.append(copy_out(4, wout_w))
    done[-1].start()
    straight.wait()
    for one in done:
        one.wait()


def whole(
    n_dp,
    token_ids,
    segment_ids,
    masked_rows,
    embedding,
    pos_table,
    w_in,
    w_out,
    b_in,
    b_out,
    norm_gain,
    norm_shift,
    logit_grad,
):
    quarter, width = embedding.shape
    batches, _, length = token_ids.shape
    masks = masked_rows.shape[-1]
    ff = w_in.shape[-1]
    p = Plan(n_dp, length, width, ff, quarter, masks)
    scratch = scratch_list(p)
    shapes = [
        (batches, 1, masks, quarter),
        (p.share, width),
        (length // n_dp, width),
        (1, p.in_rows, ff),
        (1, p.out_rows, width),
        (1, ff // n_dp),
        (1, p.in_rows),
        (1, p.in_rows),
        (1, p.in_rows),
    ]
    far = pl.BlockSpec(memory_space=pl.ANY)
    part_types = [BF, F32, F32, BF, BF]
    parts = [jax.ShapeDtypeStruct(shape, kind) for shape, kind in zip(shapes, part_types)]
    parts.append(jax.ShapeDtypeStruct((8, width), F32))
    summed = pl.pallas_call(
        functools.partial(fused, p, list(scratch)),
        out_shape=parts,
        in_specs=[far] * 12,
        out_specs=[far] * 6,
        scratch_shapes=[pltpu.VMEM(*one) for one in scratch.values()]
        + [
            pltpu.SemaphoreType.DMA((SENDS,)),
            pltpu.SemaphoreType.DMA((RECVS,)),
            pltpu.SemaphoreType.DMA((len(p.chunks) + 11,)),
            pltpu.SemaphoreType.DMA((6,)),
        ],
        compiler_params=pltpu.CompilerParams(
            collective_id=0, has_side_effects=True, vmem_limit_bytes=VMEM_LIMIT
        ),
    )(
        token_ids,
        segment_ids,
        masked_rows,
        b_in,
        b_out,
        norm_gain,
        norm_shift,
        logit_grad,
        pos_table,
        embedding,
        w_in,
        w_out,
    )
    room = [
        (shapes[0], BF),
        (shapes[0], F32),
        (shapes[1], F32),
        (shapes[3], BF),
        (shapes[3], F32),
        (shapes[4], BF),
        (shapes[4], F32),
        ((8, width), F32),
        (shapes[5], F32),
        ((3, 1, p.in_rows), F32),
    ]
    return pl.pallas_call(
        functools.partial(finish, p),
        out_shape=[jax.ShapeDtypeStruct(shape, F32) for shape in shapes],
        in_specs=[far] * 6,
        out_specs=[far] * 9,
        scratch_shapes=[pltpu.VMEM(*one) for one in room]
        + [pltpu.SemaphoreType.DMA((6,)), pltpu.SemaphoreType.DMA((9,))],
        compiler_params=pltpu.CompilerParams(vmem_limit_bytes=VMEM_LIMIT),
    )(*summed)


def solution(mesh):
    n_section, n_dp = mesh.shape["section"], mesh.shape["dp"]

    def chosen_form(*args):
        token_ids, embedding, w_in = args[0], args[3], args[5]
        fits = (
            n_section == 4
            and n_dp == 8
            and token_ids.shape[0] == 2
            and token_ids.shape[1:] == (1, 128)
            and w_in.shape[1] % (16 * n_dp) == 0
            and w_in.shape[2] == 4 * w_in.shape[1]
            and embedding.shape[0] % (8 * n_dp) == 0
        )
        return whole(n_dp, *args) if fits else local(*args)

    placed = (
        P(None, "dp", None),
        P(None, "dp", None),
        P(None, "dp", None),
        P("section", None),
        P(),
        P("section", None, None),
        P("section", None, None),
        P("section", None),
        P("section", None),
        P("section", None),
        P("section", None),
        P(None, "dp", None, "section"),
    )
    return jax.shard_map(
        chosen_form,
        mesh=mesh,
        in_specs=placed,
        out_specs=(
            P(None, "dp", None, "section"),
            P(("section", "dp"), None),
            P("dp", None),
            P("section", "dp", None),
            P("section", "dp", None),
            P("section", "dp"),
            P("section", "dp"),
            P("section", "dp"),
            P("section", "dp"),
        ),
        check_vma=False,
    )
```

```python
import functools
import math
import types

import jax
import jax.numpy as jnp
from jax import lax
from jax.experimental import pallas as pl
from jax.experimental.pallas import tpu as pltpu
from jax.sharding import PartitionSpec as P

HEADS = 12


EPSILON = 1e-12


def for_sending(array):
    return jax.tree.map(lambda a: a.astype(jnp.bfloat16) if a.dtype == jnp.float32 else a, array)


def passed_along(block, axis, distance):
    devices = range(lax.axis_size(axis))
    route = [(i - distance, i) for i in devices if i - distance in devices]
    return lax.ppermute(block, axis, route)


def broadcast(value, axis, source):
    kept = jnp.where(lax.axis_index(axis) == source, value, 0).astype(value.dtype)
    return lax.psum(kept, axis)


def norm_forward(resid, gain_row, shift_row):
    centre = jnp.mean(resid, -1, keepdims=True)
    centred = resid - centre
    inverse = lax.rsqrt(jnp.mean(centred * centred, -1, keepdims=True) + EPSILON)
    normed = centred * inverse
    return (normed * gain_row + shift_row, normed, inverse)


def norm_backward(upstream, normed, inverse, gain_row):
    gain_part = jnp.sum(upstream * normed, 0)
    shift_part = jnp.sum(upstream, 0)
    scaled = upstream * gain_row
    first_mean = jnp.mean(scaled, -1, keepdims=True)
    second_mean = jnp.mean(scaled * normed, -1, keepdims=True)
    return (inverse * (scaled - first_mean - normed * second_mean), gain_part, shift_part)


def to_heads(values):
    return values.reshape(values.shape[0], HEADS, values.shape[1] // HEADS)


def row_scores(query, keyed, segment):
    factor = (query.shape[1] // HEADS) ** (-0.5)
    scores = (
        jnp.einsum(
            "qhd,khd->hqk", to_heads(query), to_heads(keyed), preferred_element_type=jnp.float32
        )
        * factor
    )
    allowed = segment[:, None] == segment[None, :]
    return jnp.where(allowed[None], scores, -1000000000.0)


def attend_row(packed, segment):
    width = packed.shape[1] // 3
    scores = row_scores(packed[:, :width], packed[:, width : 2 * width], segment)
    row_peak = jnp.max(scores, -1, keepdims=True)
    exponent = jnp.exp(scores - row_peak)
    row_total = jnp.sum(exponent, -1, keepdims=True)
    chance = (exponent / row_total).astype(jnp.bfloat16)
    context = jnp.einsum(
        "hqk,khd->qhd", chance, to_heads(packed[:, 2 * width :]), preferred_element_type=jnp.float32
    )
    summary = (row_peak + jnp.log(row_total))[..., 0]
    return (context.reshape(packed.shape[0], width).astype(jnp.bfloat16), summary)


def attend_back(packed, segment, summary, upstream):
    length = packed.shape[0]
    width = packed.shape[1] // 3
    factor = (width // HEADS) ** (-0.5)
    scores = row_scores(packed[:, :width], packed[:, width : 2 * width], segment)
    chance = jnp.exp(scores - summary[..., None])
    grad_heads = to_heads(upstream)
    grad_chance = jnp.einsum(
        "qhd,khd->hqk",
        grad_heads,
        to_heads(packed[:, 2 * width :]),
        preferred_element_type=jnp.float32,
    )
    grad_value = jnp.einsum(
        "hqk,qhd->khd", chance.astype(jnp.bfloat16), grad_heads, preferred_element_type=jnp.float32
    )
    grad_score = chance * (grad_chance - jnp.sum(chance * grad_chance, -1, keepdims=True))
    grad_score = grad_score.astype(jnp.bfloat16)
    grad_query = (
        jnp.einsum(
            "hqk,khd->qhd",
            grad_score,
            to_heads(packed[:, width : 2 * width]),
            preferred_element_type=jnp.float32,
        )
        * factor
    )
    grad_key = (
        jnp.einsum(
            "hqk,qhd->khd",
            grad_score,
            to_heads(packed[:, :width]),
            preferred_element_type=jnp.float32,
        )
        * factor
    )
    joined = jnp.concatenate(
        [
            grad_query.reshape(length, width),
            grad_key.reshape(length, width),
            grad_value.reshape(length, width),
        ],
        1,
    )
    return joined.astype(jnp.bfloat16)


def attention_forward(inputs, segment, params):
    w_first, w_second, bias_first, bias_second, gain_row, shift_row = params
    rows_here, length, width = inputs.shape
    flat = inputs.reshape(rows_here * length, width)
    offset = jnp.concatenate(
        [bias_first[:width], jnp.zeros((width,), jnp.float32), bias_first[2 * width : 3 * width]]
    )
    packed = jnp.dot(flat, w_first[:, : 3 * width], preferred_element_type=jnp.float32) + offset
    packed = packed.astype(jnp.bfloat16).reshape(rows_here, length, 3 * width)
    context, summary = lax.map(lambda item: attend_row(item[0], item[1]), (packed, segment))
    branch = (
        jnp.dot(
            context.reshape(-1, width), w_first[:, 3 * width :], preferred_element_type=jnp.float32
        )
        + bias_second
    )
    result, normed, inverse = norm_forward(flat.astype(jnp.float32) + branch, gain_row, shift_row)
    return (result.reshape(rows_here, length, width), (packed, context, summary, normed, inverse))


def attention_backward(inputs, segment, upstream, params, totals):
    w_first, w_second, bias_first, bias_second, gain_row, shift_row = params
    rows_here, length, width = inputs.shape
    result, saved = attention_forward(inputs, segment, params)
    packed, context, summary, normed, inverse = saved
    flat = inputs.reshape(-1, width)
    grad_resid, gain_part, shift_part = norm_backward(
        upstream.reshape(-1, width), normed, inverse, gain_row
    )
    grad_branch = grad_resid.astype(jnp.bfloat16)
    grad_out_proj = jnp.einsum(
        "nd,ne->de", context.reshape(-1, width), grad_branch, preferred_element_type=jnp.float32
    )
    bias_second_part = jnp.sum(grad_branch.astype(jnp.float32), 0)
    grad_context = jnp.einsum(
        "ne,de->nd", grad_branch, w_first[:, 3 * width :], preferred_element_type=jnp.float32
    )
    grad_context = grad_context.astype(jnp.bfloat16).reshape(rows_here, length, width)
    grad_packed = lax.map(
        lambda item: attend_back(item[0], item[1], item[2], item[3]),
        (packed, segment, summary, grad_context),
    )
    flat_packed = grad_packed.reshape(-1, 3 * width)
    grad_proj = jnp.einsum("nd,nc->dc", flat, flat_packed, preferred_element_type=jnp.float32)
    bias_sums = jnp.sum(flat_packed.astype(jnp.float32), 0)
    grad_input = grad_resid + jnp.einsum(
        "nc,dc->nd", flat_packed, w_first[:, : 3 * width], preferred_element_type=jnp.float32
    )
    first_total, second_total, bias_first_total, bias_second_total, gain_total, shift_total = totals
    first_total = (
        first_total.at[:, : 3 * width].add(grad_proj).at[:, 3 * width :].add(grad_out_proj)
    )
    bias_first_total = (
        bias_first_total.at[:width]
        .add(bias_sums[:width])
        .at[2 * width : 3 * width]
        .add(bias_sums[2 * width :])
    )
    updated = (
        first_total,
        second_total,
        bias_first_total,
        bias_second_total + bias_second_part,
        gain_total + gain_part,
        shift_total + shift_part,
    )
    return (grad_input.reshape(rows_here, length, width).astype(jnp.bfloat16), updated)


def feed_forward(inputs, params):
    w_first, w_second, bias_first, bias_second, gain_row, shift_row = params
    rows_here, length, width = inputs.shape
    flat = inputs.reshape(-1, width)
    hidden = jnp.dot(flat, w_first, preferred_element_type=jnp.float32) + bias_first
    active = jax.nn.gelu(hidden, approximate=False).astype(jnp.bfloat16)
    branch = jnp.dot(active, w_second, preferred_element_type=jnp.float32) + bias_second
    result, normed, inverse = norm_forward(flat.astype(jnp.float32) + branch, gain_row, shift_row)
    return (result.reshape(rows_here, length, width), (hidden, active, normed, inverse))


def feed_backward(inputs, upstream, params, totals):
    w_first, w_second, bias_first, bias_second, gain_row, shift_row = params
    rows_here, length, width = inputs.shape
    result, saved = feed_forward(inputs, params)
    hidden, active, normed, inverse = saved
    flat = inputs.reshape(-1, width)
    grad_resid, gain_part, shift_part = norm_backward(
        upstream.reshape(-1, width), normed, inverse, gain_row
    )
    grad_branch = grad_resid.astype(jnp.bfloat16)
    grad_second = jnp.einsum("nf,nd->fd", active, grad_branch, preferred_element_type=jnp.float32)
    bias_second_part = jnp.sum(grad_branch.astype(jnp.float32), 0)
    grad_active = jnp.einsum("nd,fd->nf", grad_branch, w_second, preferred_element_type=jnp.float32)
    through = jax.vjp(lambda inner: jax.nn.gelu(inner, approximate=False), hidden)[1](grad_active)[
        0
    ]
    grad_hidden = through.astype(jnp.bfloat16)
    grad_first = jnp.einsum("nd,nf->df", flat, grad_hidden, preferred_element_type=jnp.float32)
    bias_first_part = jnp.sum(grad_hidden.astype(jnp.float32), 0)
    grad_input = grad_resid + jnp.einsum(
        "nf,df->nd", grad_hidden, w_first, preferred_element_type=jnp.float32
    )
    terms = (grad_first, grad_second, bias_first_part, bias_second_part, gain_part, shift_part)
    updated = tuple((total + term for total, term in zip(totals, terms)))
    return (grad_input.reshape(rows_here, length, width).astype(jnp.bfloat16), updated)


def local(
    token_ids,
    segment_ids,
    masked_rows,
    embedding,
    pos_table,
    w_in,
    w_out,
    b_in,
    b_out,
    norm_gain,
    norm_shift,
    logit_grad,
):
    sections = lax.axis_size("section")
    section_index = lax.axis_index("section")
    quarter, width = embedding.shape
    batches, rows_here, length = token_ids.shape
    params = (
        w_in[0],
        w_out[0],
        b_in[0].astype(jnp.float32),
        b_out[0].astype(jnp.float32),
        norm_gain[0].astype(jnp.float32),
        norm_shift[0].astype(jnp.float32),
    )
    local_ids = token_ids - section_index * quarter
    inside = (local_ids >= 0) & (local_ids < quarter)
    picked = jnp.take(embedding, jnp.clip(local_ids, 0, quarter - 1), axis=0)
    partial_rows = jnp.where(inside[..., None], picked.astype(jnp.float32), 0.0)
    looked = lax.psum(partial_rows.astype(jnp.bfloat16), "section").astype(jnp.float32)
    entry = (looked + pos_table.astype(jnp.float32)).astype(jnp.bfloat16)

    def spare_forward(inputs, segment):
        return jnp.zeros(inputs.shape, jnp.bfloat16)

    def attend_forward(inputs, segment):
        return attention_forward(inputs, segment, params)[0].astype(jnp.bfloat16)

    def feed_only(inputs, segment):
        return feed_forward(inputs, params)[0].astype(jnp.bfloat16)

    def spare_backward(inputs, segment, upstream, totals):
        return (jnp.zeros(inputs.shape, jnp.bfloat16), totals)

    def attend_backward(inputs, segment, upstream, totals):
        return attention_backward(inputs, segment, upstream, params, totals)

    def feed_back_only(inputs, segment, upstream, totals):
        return feed_backward(inputs, upstream, params, totals)

    ticks = batches + sections - 1
    kept = jnp.zeros_like(entry)
    outputs = jnp.zeros_like(entry)
    incoming = jnp.zeros_like(entry[0])
    for moment in range(ticks):
        micro_index = moment - section_index
        is_live = (micro_index >= 0) & (micro_index < batches)
        micro_slot = jnp.clip(micro_index, 0, batches - 1)
        current = jnp.where(section_index == 0, entry[micro_slot], incoming)
        kept = kept.at[micro_slot].set(jnp.where(is_live, current, kept[micro_slot]))
        branch_index = jnp.where(is_live, 1 + section_index % 2, 0)
        result = lax.switch(
            branch_index,
            [spare_forward, attend_forward, feed_only],
            current,
            segment_ids[micro_slot],
        )
        outputs = outputs.at[micro_slot].set(jnp.where(is_live, result, outputs[micro_slot]))
        if moment + 1 < ticks:
            incoming = jax.tree.map(
                lambda part, own: part.astype(own.dtype),
                passed_along(for_sending(result), "section", 1),
                result,
            )
    final_rows = jnp.take_along_axis(outputs, masked_rows[..., None], axis=2)
    head_rows = broadcast(final_rows, "section", sections - 1)
    logits = jnp.einsum("mrkd,vd->mrkv", head_rows, embedding, preferred_element_type=jnp.float32)
    partial_grad = jnp.einsum(
        "mrkv,vd->mrkd", logit_grad, embedding, preferred_element_type=jnp.float32
    )
    grad_rows = lax.psum(partial_grad.astype(jnp.bfloat16), "section").astype(jnp.float32)
    table_head = jnp.einsum(
        "mrkv,mrkd->vd", logit_grad, head_rows, preferred_element_type=jnp.float32
    )
    places = (masked_rows[..., None] == jnp.arange(length)[None, None, None, :]).astype(jnp.float32)
    top_grad = jnp.einsum("mrkl,mrkd->mrld", places, grad_rows, precision=lax.Precision.HIGHEST)
    gradients = (
        jnp.zeros(w_in.shape[1:], jnp.float32),
        jnp.zeros(w_out.shape[1:], jnp.float32),
        jnp.zeros(b_in.shape[1:], jnp.float32),
        jnp.zeros((width,), jnp.float32),
        jnp.zeros((width,), jnp.float32),
        jnp.zeros((width,), jnp.float32),
    )
    grad_entry = jnp.zeros_like(entry)
    back_in = jnp.zeros_like(entry[0])
    for moment in range(ticks):
        micro_index = moment - (sections - 1 - section_index)
        is_live = (micro_index >= 0) & (micro_index < batches)
        micro_slot = jnp.clip(micro_index, 0, batches - 1)
        upstream = jnp.where(
            section_index == sections - 1, top_grad[micro_slot], back_in.astype(jnp.float32)
        )
        branch_index = jnp.where(is_live, 1 + section_index % 2, 0)
        grad_input, gradients = lax.switch(
            branch_index,
            [spare_backward, attend_backward, feed_back_only],
            kept[micro_slot],
            segment_ids[micro_slot],
            upstream,
            gradients,
        )
        grad_entry = grad_entry.at[micro_slot].set(
            jnp.where(is_live, grad_input, grad_entry[micro_slot])
        )
        if moment + 1 < ticks:
            back_in = jax.tree.map(
                lambda part, own: part.astype(own.dtype),
                passed_along(for_sending(grad_input), "section", -1),
                grad_input,
            )
    input_grad = broadcast(grad_entry, "section", 0)
    input_wide = input_grad.astype(jnp.float32)
    pos_grad = jnp.sum(input_wide, (0, 1))
    targets = jnp.where(inside, local_ids, quarter).reshape(-1)
    table_input = jax.ops.segment_sum(
        input_wide.reshape(-1, width), targets, num_segments=quarter + 1
    )[:quarter]
    w_in_part, w_out_part, b_in_part, b_out_part, gain_part, shift_part = gradients
    reduced = (
        lax.psum_scatter(w_in_part, "dp", scatter_dimension=0, tiled=True),
        lax.psum_scatter(w_out_part, "dp", scatter_dimension=0, tiled=True),
        lax.psum_scatter(b_in_part, "dp", scatter_dimension=0, tiled=True),
        lax.psum_scatter(b_out_part, "dp", scatter_dimension=0, tiled=True),
        lax.psum_scatter(gain_part, "dp", scatter_dimension=0, tiled=True),
        lax.psum_scatter(shift_part, "dp", scatter_dimension=0, tiled=True),
        lax.psum_scatter(pos_grad, "dp", scatter_dimension=0, tiled=True),
        lax.psum_scatter(table_input + table_head, "dp", scatter_dimension=0, tiled=True),
    )
    table_grad = reduced[7]
    return (
        logits,
        table_grad,
        reduced[6],
        reduced[0][None],
        reduced[1][None],
        reduced[2][None],
        reduced[3][None],
        reduced[4][None],
        reduced[5][None],
    )


SENDS = 95
RECVS = 88
VMEM_LIMIT = 64 * 2**20
BF = jnp.bfloat16
F32 = jnp.float32
MESH = pl.DeviceIdType.MESH


def mm(a, b):
    return jnp.dot(a, b, preferred_element_type=F32)


def mm_nt(a, b):
    return lax.dot_general(a, b, (((1,), (1,)), ((), ())), preferred_element_type=F32)


def mm_tn(a, b):
    return lax.dot_general(a, b, (((0,), (0,)), ((), ())), preferred_element_type=F32)


def iota(shape, dim):
    return lax.broadcasted_iota(jnp.int32, shape, dim)


def column(row):
    return jnp.broadcast_to(row.astype(F32), (128, 128)).T


class Plan:
    def __init__(self, n_dp, length, width, ff, quarter, masks):
        self.n_dp, self.length, self.width, self.ff = n_dp, length, width, ff
        self.quarter, self.masks = quarter, masks
        self.nz = n_dp // 2
        self.share = quarter // n_dp
        self.in_rows = width // n_dp
        self.out_rows = ff // n_dp
        self.mask_pad = -(-masks // 16) * 16
        self.share_pad = -(-self.share // 128) * 128
        self.share_rows = -(-self.share // 16) * 16
        self.chunks = []
        at = 0
        while at < quarter:
            size = min(1024, quarter - at)
            self.chunks.append((at, size))
            at += size


class Counter:
    def __init__(self):
        self.n = 0

    def take(self, k=1):
        first = self.n
        self.n += k
        return first


def scratch_list(p):
    w, ff, ln = p.width, p.ff, p.length
    mp = p.mask_pad
    return dict(
        tok=((2, 1, ln), jnp.int32),
        seg=((2, 1, ln), jnp.int32),
        picks=((2, 1, p.masks), jnp.int32),
        b_in=((1, ff), BF),
        b_out=((1, w), BF),
        gain=((1, w), BF),
        shift=((1, w), BF),
        emb=((p.quarter, w), BF),
        lg=((2, 1, p.masks, p.quarter), BF),
        pos=((ln, w), BF),
        wa=((w, ff), BF),
        w1=((w, ff), BF),
        w2=((ff, w), BF),
        w1t=((ff, w), BF),
        w2t=((w, ff), BF),
        par_a=((8, ff), F32),
        par_f=((8, ff), F32),
        psend=((ln, w), BF),
        psum=((ln, w), BF),
        prow=((2, ln, w), BF),
        lgp=((2 * mp, p.quarter), BF),
        lgs=((p.n_dp, 2 * p.masks, p.share_pad), BF),
        lgr=((p.n_dp, 2 * p.masks, p.share_pad), BF),

        g=((2 * mp, w), F32),
        grow=((2, p.masks, w), F32),
        gwide=((ln, w), F32),
        mrow=((8, ln), jnp.int32),
        ids_own=((8, ln), jnp.int32),
        ids_all=((p.n_dp, 8, ln), jnp.int32),
        x_a=((ln, w), BF),
        y_f=((ln, w), BF),
        pk=((ln, 3 * w), BF),
        ctx=((ln, w), BF),
        probs=((w // 128, ln, 256), F32),
        n_a=((ln, w), F32),
        n_f=((ln, w), F32),
        inv_a=((ln, 1), F32),
        inv_f=((ln, 1), F32),
        slope=((ln, ff), BF),
        xt_a=((p.nz, 2, p.in_rows, ln), BF),
        ct_a=((p.nz, 2, p.in_rows, ln), BF),
        dyin=((ln, w), BF),
        dyf=((ln, w), F32),
        dres=((ln, w), F32),
        dbr_a=((ln, w), BF),
        dpk=((ln, 3 * w), BF),
        dctx=((ln, w), BF),
        dx=((ln, w), BF),
        dx_pair=((ln, w), BF),
        bsum=((1, ff), F32),
        vecs=((8, w), F32),
        sm_a=((8, w), F32),
        sm_f=((8, w), F32),
        b_ctx=((p.nz, p.in_rows, 4 * ln), BF),
        b_x=((p.nz, p.in_rows, 4 * ln), BF),
        b_sm=((4, 8, w), F32),
        sm_tot=((8, w), F32),
        sm_all=((8, w), F32),
        r_sm=((p.nz, 8, w), F32),
        r_in=((5, p.in_rows, ff), BF),
        x_all=((2, p.nz, 2, ln, w), BF),
        db_all=((2, p.nz, 2, ln, w), BF),
        w_col=((w, p.out_rows), F32),
        r_col=((p.n_dp, p.in_rows, p.out_rows), BF),
        ch_own=((mp, w), BF),
        ch_two=((mp, w), BF),
        ch_pair=((mp, w), BF),
        ch_far=((mp, w), BF),
        ch_all=((2, p.n_dp, mp, w), BF),
        de_all=((2, p.n_dp, ln, w), BF),
        u_out=((p.out_rows, w), F32),
        o_tab=((p.share, w), F32),
        o_pos=((ln // p.n_dp, w), F32),
    )


def fused(p, names, *refs):
    far_small, (lg_h, pos_h, emb_h, w_in_h, w_out_h) = refs[:7], refs[7:12]
    outs = refs[12:18]
    r = types.SimpleNamespace(**dict(zip(names, refs[18:])))
    ss, rs, ls, os = refs[18 + len(names) :]
    acc, o_log = r.u_out.at[0 : 2 * p.length], r.lg
    o_win = r.r_in.at[0:1]
    (o_tab, o_pos, o_wout, o_vec) = (r.o_tab, r.o_pos, r.w1t.at[1024 : 1024 + p.out_rows], r.sm_all)
    w, ff, ln, mp, nz, n_dp = p.width, p.ff, p.length, p.mask_pad, p.nz, p.n_dp
    heads = w // 64
    pairs = heads // 2

    s = lax.axis_index("section")
    dp = lax.axis_index("dp")
    x, c = s // 2, lax.rem(s, 2)
    z, y = dp // 2, lax.rem(dp, 2)
    core = s + 1 - 2 * c
    across = s + 2 - 4 * x
    ydp = dp + 1 - 2 * y
    other = 1 - c
    at_x0, at_x1 = frozenset(["x0"]), frozenset(["x1"])
    is_att, is_ff = frozenset(["att"]), frozenset(["ff"])
    on_0, on_1 = at_x0 | is_ff, at_x1 | is_ff
    outer_att, inner = is_att | {"outer"}, is_att | {"inner"}
    always = frozenset()
    sends, recvs = Counter(), Counter()
    def holds(name):
        if name[:2] == "z>":
            return z >= int(name[2:])
        if name[:2] == "z<":
            return z <= int(name[2:])
        if name in ("outer", "inner"):
            edge = (z == 0) | (z == nz - 1)
            return edge if name == "outer" else jnp.logical_not(edge)
        return {"x0": x == 0, "x1": x == 1, "att": c == 0, "ff": c == 1}[name]

    def at_least(k):
        return frozenset(["z>%d" % k]) if k > 0 else always

    def at_most(k):
        return frozenset(["z<%d" % k]) if k < nz - 1 else always

    not_first, not_last = at_least(1), at_most(nz - 2)
    outside = [always]

    def on(cond):
        def run(body):
            names = sorted(cond - outside[0])
            before, outside[0] = outside[0], outside[0] | cond
            if names:
                pl.when(functools.reduce(lambda a, b: a & b, [holds(name) for name in names]))(body)
            else:
                body()
            outside[0] = before

        return run

    groups, stage = {}, [0]

    def send(cond, src, dst, dev, recv, bulk=None, tag=None):
        cond = cond | outside[0]
        key = (stage[0], cond, tag)
        if key not in groups:
            groups[key] = [sends.take(), 0, bulk]
        group = groups[key]
        group[1] += math.prod(src.shape) * src.dtype.itemsize

        @on(cond)
        def _():
            pltpu.make_async_remote_copy(
                src_ref=src,
                dst_ref=dst,
                send_sem=ss.at[group[0]],
                recv_sem=rs.at[recv],
                device_id=dev,
                device_id_type=MESH,
            ).start()

    def drain(number):
        for (when, cond, _), (slot, size, bulk) in groups.items():
            if when == number:
                rows = size // (w * 2)
                assert bulk is not None or size == rows * w * 2 and rows % 16 == 0 and rows <= p.quarter, (rows, size)
                ref = r.emb.at[0:rows] if bulk is None else bulk

                @on(cond)
                def _():
                    pltpu.make_async_remote_copy(
                        src_ref=ref,
                        dst_ref=ref,
                        send_sem=ss.at[slot],
                        recv_sem=rs.at[0],
                        device_id=(core, dp),
                        device_id_type=MESH,
                    ).wait_send()

    def arrived(dst, recv):
        pltpu.make_async_remote_copy(
            src_ref=dst,
            dst_ref=dst,
            send_sem=ss.at[0],
            recv_sem=rs.at[recv],
            device_id=(core, dp),
            device_id_type=MESH,
        ).wait_recv()

    near_small = (r.tok, r.seg, r.picks, r.b_in, r.b_out, r.gain, r.shift)
    tok, seg, picks, b_in, b_out, gain, shift = near_small

    def small_copy(i):
        return pltpu.make_async_copy(far_small[i], near_small[i], ls.at[len(p.chunks) + 4 + i])

    small_copy(0).start()
    for i, (at, size) in enumerate(p.chunks):
        pltpu.make_async_copy(emb_h.at[pl.ds(at, size)], r.emb.at[pl.ds(at, size)], ls.at[i]).start()
    l_w = len(p.chunks)
    lg, pos = r.lg, r.pos
    pltpu.make_async_copy(lg_h, lg, ls.at[l_w + 2]).start()
    pltpu.make_async_copy(pos_h, pos, ls.at[l_w + 3]).start()
    for i in range(1, 7):
        small_copy(i).start()

    def fill(par):
        par[0:1, :] = b_in[...].astype(F32)
        par[1:2, 0:w] = b_out[...].astype(F32)
        par[2:3, 0:w] = gain[...].astype(F32)
        par[3:4, 0:w] = shift[...].astype(F32)

    barrier = pltpu.get_barrier_semaphore()
    peers = [(s, lax.rem(dp + k, n_dp)) for k in range(1, n_dp)]
    peers += [(core, dp), (across, dp), (3 - s, dp), (core, ydp)]
    for peer in peers:
        pl.semaphore_signal(barrier, inc=1, device_id=peer, device_id_type=MESH)

    small_copy(0).wait()
    cols = [column(tok[m]) for m in range(2)]
    first = s * p.quarter
    for i, (at, size) in enumerate(p.chunks):
        pltpu.make_async_copy(emb_h.at[pl.ds(at, size)], r.emb.at[pl.ds(at, size)], ls.at[i]).wait()
        lane = (iota((ln, size), 1) + (first + at)).astype(F32)
        hot = []
        for m in range(2):
            wide = jnp.concatenate([cols[m]] * (-(-size // 128)), 1)[:, :size]
            hot.append(jnp.where(wide == lane, 1.0, 0.0).astype(BF))
        part = mm(jnp.concatenate(hot, 0), r.emb[at : at + size, :])
        if i == 0:
            acc[...] = part
        else:
            acc[...] += part
    r.psend[...] = acc[pl.ds(pl.multiple_of(ln * other, ln), ln), :].astype(BF)

    @on(is_att)
    def _():
        pltpu.make_async_copy(w_in_h.at[0], r.wa, ls.at[l_w]).start()

    @on(is_ff)
    def _():
        pltpu.make_async_copy(w_in_h.at[0], r.w1, ls.at[l_w]).start()
        pltpu.make_async_copy(w_out_h.at[0], r.w2, ls.at[l_w + 1]).start()

    for i in range(1, 7):
        small_copy(i).wait()
    on(is_att)(lambda: fill(r.par_a))
    on(is_ff)(lambda: fill(r.par_f))

    tiles = ff // w
    k_p, k_g = recvs.take(2), recvs.take(2)
    k_pa, k_pf, k_wa, k_w1, k_w2 = recvs.take(), recvs.take(), recvs.take(tiles), recvs.take(tiles), recvs.take(tiles)
    pl.semaphore_wait(barrier, len(peers))
    send(always, r.psend, r.prow.at[0], (core, dp), k_p)


    pltpu.make_async_copy(lg_h, lg, ls.at[l_w + 2]).wait()
    pltpu.make_async_copy(pos_h, pos, ls.at[l_w + 3]).wait()
    r.lgp[...] = jnp.zeros(r.lgp.shape, BF)
    r.lgp[0 : p.masks] = lg[0, 0]
    r.lgp[mp : mp + p.masks] = lg[1, 0]

    k_lg, k_id = recvs.take(), recvs.take()
    for j in range(n_dp):
        r.lgs[j, :, p.share :] = jnp.zeros((2 * p.masks, p.share_pad - p.share), BF)
        for m in range(2):
            r.lgs[j, p.masks * m : p.masks * (m + 1), 0 : p.share] = lg[m, 0, :, p.share * j : p.share * (j + 1)]
    r.ids_own[...] = jnp.zeros(r.ids_own.shape, jnp.int32)
    for m in range(2):
        r.ids_own[m : m + 1, :] = tok[m]
    r.ids_all[dp] = r.ids_own[...]
    r.lgr[dp] = r.lgs[dp]
    for k in range(1, n_dp):
        to = lax.rem(dp + k, n_dp)
        send(always, r.lgs.at[to], r.lgr.at[dp], (s, to), k_lg, r.lgs.at[0 : n_dp - 1], 1)
        send(always, r.ids_own, r.ids_all.at[dp], (s, to), k_id, r.ids_all.at[0 : n_dp - 1], 2)
    arrived(r.prow.at[0], k_p)
    own_rows = acc[pl.ds(pl.multiple_of(ln * c, ln), ln), :]
    acc[0:ln, :] = own_rows + r.prow[0].astype(F32)
    r.psum[...] = acc[0:ln, :].astype(BF)
    send(at_x1, r.psum, r.prow.at[1], (across, dp), k_p + 1)

    def weights(cond):
        send(is_att | cond, r.par_a, r.par_a, (core, dp), k_pa)
        send(is_ff | cond, r.par_f, r.par_f, (core, dp), k_pf)
        cuts = [slice(j * w, (j + 1) * w) for j in range(tiles)]
        first = [(is_att, w_in_h.at[0, :, cut], r.wa.at[:, cut], k_wa + j, 3) for j, cut in enumerate(cuts)]
        left = [(is_ff, w_in_h.at[0, :, cut], r.w1.at[:, cut], k_w1 + j, 4) for j, cut in enumerate(cuts)]
        right = [(is_ff, w_out_h.at[0, cut, :], r.w2.at[cut, :], k_w2 + j, 5) for j, cut in enumerate(cuts)]
        if cond == at_x1:
            order = first + right + left
        else:
            order = first + [one for pair in zip(left, right) for one in pair]
        for whose, src, dst, recv, tag in order:
            send(whose | cond, src, dst, (core, dp), recv, tag=tag)

    weights(at_x0)
    weights(at_x1)

    for i, (at, size) in enumerate(p.chunks):
        part = mm(r.lgp[:, at : at + size], r.emb[at : at + size, :])
        if i == 0:
            r.g[...] = part
        else:
            r.g[...] += part
    send(always, r.g.at[pl.ds(pl.multiple_of(mp * other, mp), p.masks)], r.grow.at[0], (core, dp), k_g)

    def masked_gradient():
        arrived(r.grow.at[0], k_g)
        r.gwide[...] = jnp.zeros(r.gwide.shape, F32)
        r.gwide[0 : p.masks, :] = r.g[pl.ds(pl.multiple_of(mp * c, mp), p.masks), :] + r.grow[0]

    on(at_x1)(masked_gradient)

    k_x = recvs.take()

    @on(at_x0)
    def _():
        arrived(r.prow.at[1], k_p + 1)
        whole = acc[0:ln, :] + r.prow[1].astype(F32)
        r.x_a[...] = (whole + pos[...].astype(F32)).astype(BF)

    @on(is_att)
    def _():
        pltpu.make_async_copy(w_in_h.at[0], r.wa, ls.at[l_w]).wait()
        arrived(r.par_f, k_pf)

    @on(is_ff)
    def _():
        pltpu.make_async_copy(w_in_h.at[0], r.w1, ls.at[l_w]).wait()
        pltpu.make_async_copy(w_out_h.at[0], r.w2, ls.at[l_w + 1]).wait()
        arrived(r.par_a, k_pa)

    def turn_second():
        def step(i, carry):
            at = pl.ds(pl.multiple_of(i * 128, 128), 128)
            r.w2t[:, at] = r.w2[at, :].T
            return carry

        lax.fori_loop(0, ff // 128, step, 0)

    def turn_first():
        def step(i, carry):
            at = pl.ds(pl.multiple_of(i * 128, 128), 128)
            r.w1t[at, :] = r.w1[:, at].T
            return carry

        lax.fori_loop(0, ff // 128, step, 0)

    def turn_attention(j):
        cut = slice(j * w, (j + 1) * w)
        r.wa[:, cut] = r.wa[:, cut].T

    def second_here():
        @on(is_att)
        def _():
            for j in range(tiles):
                cut = slice(j * w, (j + 1) * w)
                arrived(r.w2.at[cut, :], k_w2 + j)

    def first_here():
        @on(is_att)
        def _():
            for j in range(tiles):
                cut = slice(j * w, (j + 1) * w)
                arrived(r.w1.at[:, cut], k_w1 + j)

    @on(at_x1)
    def _():
        second_here()
        turn_second()
        first_here()
        turn_first()
        arrived(r.x_a, k_x)

    low = jnp.where(iota((ln, 128), 1) < 64, 1.0, 0.0).astype(BF)
    high = jnp.where(iota((ln, 128), 1) < 64, 0.0, 1.0).astype(BF)

    def split(block):
        return jnp.concatenate([block * low, block * high], 0)

    def stack(block):
        return jnp.concatenate([block[:, 0:128], block[:, 128:256]], 0)

    def norm_forward(resid, par):
        centred = resid - jnp.mean(resid, -1, keepdims=True)
        inverse = lax.rsqrt(jnp.mean(centred * centred, -1, keepdims=True) + EPSILON)
        normed = centred * inverse
        return (normed * par[2:3, 0:w] + par[3:4, 0:w]).astype(BF), normed, inverse

    rows_x = r.x_a[...]

    def wa_tile(j):
        on(is_ff)(lambda: arrived(r.wa.at[:, j * w : (j + 1) * w], k_wa + j))

    for j in range(3):
        wa_tile(j)
        part = mm(rows_x, r.wa[:, j * w : (j + 1) * w])
        if j != 1:
            part = part + r.par_a[0:1, j * w : (j + 1) * w]
        r.pk[:, j * w : (j + 1) * w] = part.astype(BF)
    seg_row = seg[c].astype(F32)
    seg_col = column(seg[c])
    seg_row = jnp.broadcast_to(jnp.concatenate([seg_row, seg_row], 1), (ln, 256))
    seg_col = jnp.concatenate([seg_col, seg_col], 1)
    for h in range(pairs):
        at = 128 * h
        query = r.pk[:, at : at + 128]
        keyed = split(r.pk[:, w + at : w + at + 128])
        value = split(r.pk[:, 2 * w + at : 2 * w + at + 128])
        scores = jnp.where(seg_row == seg_col, mm_nt(query, keyed) * 0.125, -1e9)
        chance = []
        for half in (scores[:, 0:128], scores[:, 128:256]):
            power = jnp.exp(half - jnp.max(half, -1, keepdims=True))
            chance.append(power / jnp.sum(power, -1, keepdims=True))
        chance = jnp.concatenate(chance, 1)
        r.probs[h] = chance
        r.ctx[:, at : at + 128] = mm(chance.astype(BF), value).astype(BF)
    wa_tile(3)
    resid = rows_x.astype(F32) + mm(r.ctx[...], r.wa[:, 3 * w : 4 * w]) + r.par_a[1:2, 0:w]
    r.x_all[c, z, y], r.n_a[...], r.inv_a[...] = norm_forward(resid, r.par_a)

    class Gather:
        def __init__(self, buf):
            self.buf = buf
            self.near, self.far, self.own, self.core0 = recvs.take(nz), recvs.take(2), recvs.take(), recvs.take(4)

        def at(self, zz, yy):
            return self.buf.at[c, zz, yy]

        def pair(self, m, half_z, yy):
            return self.buf.at[m, pl.ds(2 * half_z, 2), yy]

        def start(self):
            own = self.at(z, y)
            send(not_last, own, own, (s, dp + 2), self.near + z)
            send(not_first, own, own, (s, dp - 2), self.near + z)
            send(is_att, own, own, (core, dp), self.own)
            self.to_y(z, always)

        def to_y(self, zz, cond):
            recv = jnp.where(c == 0, self.core0 + 2, self.far) + zz // 2
            send(cond, self.at(zz, y), self.at(zz, y), (jnp.where(c == 0, core, s), ydp), recv)

        def step(self, t, cond=always):
            for sign in (-1, 1):
                here, zz = at_distance(t, sign, cond)
                piece = self.at(zz, y)
                on(here)(lambda piece=piece, zz=zz: arrived(piece, self.near + zz))
                if t < nz - 1:
                    send(onward(here, sign), piece, piece, (s, dp - 2 * sign), self.near + zz)
                send(here | is_att, piece, piece, (core, dp), self.core0 + zz // 2)

        def cross(self, t, cond=always):
            for sign in (-1, 1):
                here, zz = at_distance(t, sign, cond)
                self.to_y(zz, here)

        def from_core0(self, half_z, own_side):
            if own_side:
                mine = (z // 2) == half_z

                @pl.when(mine)
                def _():
                    arrived(self.buf.at[0, z + 1 - 2 * lax.rem(z, 2), y], self.core0 + half_z)

                @pl.when(jnp.logical_not(mine))
                def _():
                    arrived(self.pair(0, half_z, y), self.core0 + half_z)

            else:
                arrived(self.pair(0, half_z, 1 - y), self.core0 + 2 + half_z)

        def from_y(self, half_z):
            arrived(self.pair(1, half_z, 1 - y), self.far + half_z)

    def at_distance(t, sign, cond):
        here = cond | (at_least(t) if sign < 0 else at_most(nz - 1 - t))
        return here, jnp.clip(z + sign * t, 0, nz - 1)

    def onward(here, sign):
        return here | (not_last if sign < 0 else not_first)

    def pair_line(buf, base, cond, i):
        piece = buf(i)
        send(cond | not_last, piece, piece, (s, dp + 2), base + i)
        send(cond | not_first, piece, piece, (s, dp - 2), base + i)

    def pair_step(buf, base, t, cond, on_x):
        for sign in (-1, 1):
            for side in (0, 1):
                here, zz = at_distance(t, sign, cond)
                from_dp = 2 * zz + (1 - y if side else y)
                piece = buf(from_dp)
                on(here)(lambda piece=piece, from_dp=from_dp: arrived(piece, base + from_dp))
                if t < nz - 1:
                    send(onward(here, sign), piece, piece, (s, dp - 2 * sign), base + from_dp)
                send(here, piece, piece, (across, dp), on_x)

    def ch(i):
        return r.ch_all.at[c, i]

    def de(i):
        return r.de_all.at[1 - x, i]

    k_row, k_pass = recvs.take(n_dp), recvs.take()
    k_ch, k_cho, k_chc, k_chp, k_chq, k_cha, k_chx, k_dp = (recvs.take() for _ in range(8))
    k_dex = recvs.take(2)
    xs, db = Gather(r.x_all), Gather(r.db_all)

    xs.start()

    def feed(rows_x, keep=True, turning=False):
        total = rows_x.astype(F32) + r.par_f[1:2, 0:w]

        def hidden_tile(j):
            cut = slice(j * w, (j + 1) * w)
            return mm(rows_x, r.w1[:, cut]) + r.par_f[0:1, cut]

        later = hidden_tile(0)
        for j in range(tiles):
            cut = slice(j * w, (j + 1) * w)
            hidden = later
            if j + 1 < tiles:
                later = hidden_tile(j + 1)
            if turning:
                turn_attention(j)
            below = 0.5 + 0.5 * lax.erf(hidden * (0.5**0.5))
            total = total + mm((hidden * below).astype(BF), r.w2[cut, :])
            if keep:
                slope = below + hidden * (0.3989422804014327 * jnp.exp(-0.5 * hidden * hidden))
                r.slope[:, cut] = slope.astype(BF)
        result, normed, inverse = norm_forward(total, r.par_f)
        if keep:
            r.y_f[...], r.n_f[...], r.inv_f[...] = result, normed, inverse
        else:
            r.psum[...] = result

    on(on_0)(lambda: feed(r.x_all[c, z, y]))
    on(at_x1)(lambda: feed(r.x_all[c, z, y], turning=True))
    send(at_x0 | is_ff, r.y_f, r.x_a, (across, dp), k_x)

    @on(at_x0 | is_ff)
    def _():
        arrived(r.x_all.at[0, z, y], xs.own)
        feed(r.x_all[0, z, y], False)

    send(at_x0 | is_ff, r.psum, r.x_a, (3 - s, dp), k_x)

    @on(at_x1)
    def _():
        r.mrow[...] = jnp.full(r.mrow.shape, -1, jnp.int32)
        r.mrow[0:1, 0 : p.masks] = picks[c]
        places = jnp.where(iota((ln, ln), 0) == r.mrow[0:1, :], 1.0, 0.0).astype(BF)
        r.ch_own[...] = mm_tn(places, r.y_f[...])[0:mp].astype(BF)
        arrived(r.grow.at[1], k_g + 1)
        r.gwide[0 : p.masks, :] += r.grow[1]
        coarse = r.gwide[...].astype(BF)
        fine = (r.gwide[...] - coarse.astype(F32)).astype(BF)
        r.dyf[...] = mm(places, coarse) + mm(places, fine)

    send(at_x1, r.ch_own, r.ch_own, (across, dp), k_cho)
    send(at_x1, r.ch_own, r.ch_two, (core, dp), k_chc)
    send(at_x1, r.ch_own, r.ch_pair, (s, ydp), k_chp)

    def push(owner, kind, src, dst, cond=always):
        home, away = (is_att, is_ff) if owner == 0 else (is_ff, is_att)
        at_home = holds("att" if owner == 0 else "ff")
        slot_y = 2 + jnp.where(at_home, 0, 1)
        own_dst, near_dst, far_dst = dst(0), dst(1), dst(slot_y)


        @on(home | cond)
        def _():
            own_dst[...] = src(y)[...]

        send(away | cond, src(y), near_dst, (core, dp), kind)
        send(cond, src(1 - y), far_dst, (jnp.where(at_home, s, core), ydp), kind)

    def gathered(kind, dst):
        arrived(dst(slice(1, 4)), kind)

    def lanes(slot):
        if isinstance(slot, slice):
            return pl.ds(slot.start * ln, (slot.stop - slot.start) * ln)
        return pl.ds(slot * ln if isinstance(slot, int) else pl.multiple_of(slot * ln, ln), ln)

    k_dh = [recvs.take() for _ in range(3)]
    k_ctx, k_xt, k_dba, k_sm = (recvs.take() for _ in range(4))
    to_x = lambda slot: r.b_x.at[:, :, lanes(slot)]
    to_ctx = lambda slot: r.b_ctx.at[:, :, lanes(slot)]
    spare = [r.x_all.at[1, 0:2], r.x_all.at[1, 2:4], r.db_all.at[1, 0:2], r.db_all.at[1, 2:4]]

    def in_spare(i):
        def at(slot):
            if isinstance(slot, slice):
                return r.de_all.at[0, slot]
            return spare[i].at[slot // 2, lax.rem(slot, 2)]

        return at

    to_dbr = in_spare(3)
    to_sm = lambda slot: r.b_sm.at[slot]

    def push_dh(j):
        push(0, k_dh[j], lambda i: r.dpk.at[:, j * w : (j + 1) * w], in_spare(j))

    def push_rows():
        push(0, k_xt, lambda i: r.xt_a.at[:, i], to_x)
        push(0, k_ctx, lambda i: r.ct_a.at[:, i], to_ctx)

    def turn():
        for dst, src in ((r.xt_a, r.x_a), (r.ct_a, r.ctx)):
            turned = src[...].T
            for b in range(n_dp):
                dst[b // 2, b % 2] = turned[b * p.in_rows : (b + 1) * p.in_rows]

    def emit(i, src):
        pltpu.make_async_copy(src, outs[i].at[0] if i == 4 else outs[i], os.at[i]).start()

    def logits():
        arrived(r.ch_two, k_chc)
        chosen = jnp.concatenate([r.ch_own[...], r.ch_two[...]], 0)
        for at, size in p.chunks:
            part = mm_nt(chosen, r.emb[at : at + size, :])
            o_log[c, 0, :, at : at + size] = part[0 : p.masks].astype(BF)
            o_log[other, 0, :, at : at + size] = part[mp : mp + p.masks].astype(BF)
        emit(0, o_log)

    @on(at_x0)
    def _():
        masked_gradient()
        send(at_x0, r.gwide.at[0 : p.masks], r.grow.at[1], (across, dp), k_g + 1)
        turn()
        push_rows()
        first_here()
        second_here()
        on(is_att)(lambda: feed(r.x_all[c, z, y]))
        xs.step(1)
        xs.cross(1)
        turn_second()
        turn_first()
        for j in range(tiles):
            turn_attention(j)
        xs.step(2)
        xs.cross(2)
        arrived(r.ch_own, k_cho)
        r.ch_all[c, dp] = r.ch_own[...]
        send(at_x0, r.ch_own, r.ch_two, (core, dp), k_chc)
        for k in range(1, nz):
            send(at_x0, r.ch_own, ch(dp), (s, lax.rem(dp + 2 * k, n_dp)), k_ch)
        logits()

    stage[0] = 1

    k_dy = recvs.take()

    @on(at_x0)
    def _():
        arrived(r.dyin, k_dy)
        r.dyf[...] = r.dyin[...].astype(F32)

    def norm_backward(par, n_ref, inv_ref):
        up, normed = r.dyf[...], n_ref[...]
        gain_part = jnp.sum(up * normed, 0, keepdims=True)
        shift_part = jnp.sum(up, 0, keepdims=True)
        scaled = up * par[2:3, 0:w]
        first_mean = jnp.mean(scaled, -1, keepdims=True)
        second_mean = jnp.mean(scaled * normed, -1, keepdims=True)
        return inv_ref[...] * (scaled - first_mean - normed * second_mean), gain_part, shift_part

    def small(dst, out_part, gain_part, shift_part):
        dst[...] = jnp.zeros(dst.shape, F32)
        n_b, n_w = ff // n_dp, w // n_dp
        for k in range(n_dp):
            dst[k : k + 1, 0:n_b] = r.bsum[:, k * n_b : (k + 1) * n_b]
            dst[k : k + 1, n_b : n_b + n_w] = out_part[:, k * n_w : (k + 1) * n_w]
            dst[k : k + 1, n_b + 128 : n_b + 128 + n_w] = gain_part[:, k * n_w : (k + 1) * n_w]
            dst[k : k + 1, n_b + 256 : n_b + 256 + n_w] = shift_part[:, k * n_w : (k + 1) * n_w]

    dres, gain_part, shift_part = norm_backward(r.par_f, r.n_f, r.inv_f)
    r.dres[...] = dres
    r.db_all[c, z, y] = dres.astype(BF)
    db.start()
    branch = r.db_all[c, z, y]

    total = r.dres[...]
    for j in range(tiles):
        cut = slice(j * w, (j + 1) * w)
        dhidden = (mm(branch, r.w2t[:, cut]) * r.slope[:, cut].astype(F32)).astype(BF)
        r.bsum[:, cut] = jnp.sum(dhidden.astype(F32), 0, keepdims=True)
        total = total + mm(dhidden, r.w1t[cut, :])
    r.dyf[...] = total.astype(BF).astype(F32)
    r.vecs[0:1], r.vecs[1:2] = gain_part, shift_part

    @on(on_1)
    def _():
        xs.step(1)
        xs.cross(1)

    dres, gain_part, shift_part = norm_backward(r.par_a, r.n_a, r.inv_a)
    r.dres[...] = dres
    r.dbr_a[...] = dres.astype(BF)
    branch = r.dbr_a[...]
    r.dctx[...] = mm(branch, r.wa[:, 3 * w : 4 * w]).astype(BF)
    for h in range(pairs):
        at = 128 * h
        query = r.pk[:, at : at + 128]
        keyed = split(r.pk[:, w + at : w + at + 128])
        value = split(r.pk[:, 2 * w + at : 2 * w + at + 128])
        upper = r.dctx[:, at : at + 128]
        chance = r.probs[h]
        dchance = mm_nt(upper, value)
        mixed = chance * dchance
        dscores = []
        for cut in (slice(0, 128), slice(128, 256)):
            dscores.append(mixed[:, cut] - chance[:, cut] * jnp.sum(mixed[:, cut], -1, keepdims=True))
        dscores = jnp.concatenate(dscores, 1).astype(BF)
        r.dpk[:, at : at + 128] = (mm(dscores, keyed) * 0.125).astype(BF)
        r.dpk[:, w + at : w + at + 128] = (mm_tn(stack(dscores), split(query)) * 0.125).astype(BF)
        r.dpk[:, 2 * w + at : 2 * w + at + 128] = mm_tn(stack(chance.astype(BF)), split(upper)).astype(BF)
    total = r.dres[...]
    for j in range(3):
        cut = slice(j * w, (j + 1) * w)
        total = total + mm(r.dpk[:, cut], r.wa[:, cut])
    r.dx[...] = total.astype(BF)
    send(at_x1, r.dx, r.dyin, (across, dp), k_dy)

    def row(m, i):
        return r.de_all.at[m, i]

    away = jnp.where(c == 1, across, 3 - s)

    def hand_on(src, i):
        send(at_x0, src, row(c, i), (away, dp), jnp.where(c == 1, k_pass, k_row + i))
        send(at_x0 | is_att, src, row(0, i), (core, dp), k_pass)

        @on(on_0)
        def _():
            r.de_all[1, i] = src[...]
            pair_line(de, k_row, on_0, i)

    @on(at_x0)
    def _():
        send(at_x0, r.dx, r.dx_pair, (s, ydp), k_dp)
        hand_on(r.dx, dp)

    @on(is_att)
    def _():
        o_wout[...] = jnp.zeros((p.out_rows, w), BF)
        emit(4, o_wout)

    @on(at_x1)
    def _():
        turn()
        push_rows()

    push(0, k_dba, lambda i: r.dbr_a, to_dbr)
    push_dh(0)
    small(r.sm_f, jnp.sum(r.db_all[c, z, y].astype(F32), 0, keepdims=True), r.vecs[0:1], r.vecs[1:2])
    push(1, k_sm, lambda i: r.sm_f, to_sm)
    r.bsum[...] = jnp.zeros(r.bsum.shape, F32)
    for j in (0, 2):
        cut = slice(j * w, (j + 1) * w)
        r.bsum[:, cut] = jnp.sum(r.dpk[:, cut].astype(F32), 0, keepdims=True)
    small(r.sm_a, jnp.sum(branch.astype(F32), 0, keepdims=True), gain_part, shift_part)
    push(0, k_sm, lambda i: r.sm_a, to_sm)
    push_dh(1)
    push_dh(2)

    @on(at_x1)
    def _():
        xs.step(1, is_att)
        xs.cross(1, is_att)
        arrived(r.ch_pair, k_chp)
        send(at_x1, r.ch_pair, r.ch_far, (across, dp), k_chq)
        xs.step(2)

    db.step(1)

    @on(at_x0)
    def _():
        arrived(r.dx_pair, k_dp)
        hand_on(r.dx_pair, ydp)

    on(at_x1)(lambda: xs.cross(2))

    @on(at_x0)
    def _():
        xs.step(3)
        xs.cross(3)

    db.cross(1)

    @on(at_x1)
    def _():
        xs.step(3)
        xs.cross(3)

    db.step(2)
    db.cross(2)

    @on(at_x0)
    def _():
        arrived(r.ch_far, k_chq)
        r.ch_all[c, ydp] = r.ch_far[...]
        for k in range(1, nz):
            send(at_x0, r.ch_far, ch(ydp), (s, lax.rem(dp + 2 * k, n_dp)), k_ch)

    drain(0)

    def head_part():
        arrived(r.ch_all.at[other], k_chx)
        arrived(r.lgr.at[0 : n_dp - 1], k_lg)
        arrived(r.ids_all.at[0 : n_dp - 1], k_id)
        lines = 2 * p.masks
        for i in range(n_dp):
            for m in range(2):
                at = lines * i + p.masks * m
                r.w1t[at : at + p.masks, :] = r.ch_all[m, i, 0 : p.masks]
        grad = mm_tn(r.lgr[...].reshape(n_dp * lines, p.share_pad), r.w1t[0 : n_dp * lines, :])
        o_tab[...] = grad[0 : p.share]

    k_in = [recvs.take(4) for _ in range(tiles)]
    half = nz * p.in_rows
    mate = z + 1 - 2 * lax.rem(z, 2)
    far_base = 2 - 2 * (z // 2)

    def shard(zz, cut):
        return r.wa.at[pl.ds(pl.multiple_of(zz * p.in_rows, p.in_rows), p.in_rows), cut]

    def tile_cut(j):
        return slice(j * w, (j + 1) * w)

    def attention_tile(j):
        cut = tile_cut(j)

        @on(is_att)
        def _():
            if j == 3:
                gathered(k_ctx, to_ctx)
                gathered(k_dba, to_dbr)
                grad = mm(r.b_ctx[...].reshape(half, 4 * ln), spare[3][...].reshape(4 * ln, w))
            else:
                if j == 0:
                    gathered(k_xt, to_x)
                gathered(k_dh[j], in_spare(j))
                grad = mm(r.b_x[...].reshape(half, 4 * ln), spare[j][...].reshape(4 * ln, w))
            r.wa[0:half, cut] = grad.astype(BF)

        to_mate = (s, 2 * mate + y)
        for k in range(2):
            send(outer_att, shard(far_base + k, cut), r.r_in.at[2 + k, :, cut], to_mate, k_in[j] + 2)
        send(outer_att, shard(mate, cut), r.r_in.at[0, :, cut], to_mate, k_in[j])

    to_inner = (s, 2 * (nz - 1 - z) + y)

    def add(zz, part, cut):
        rows = pl.ds(pl.multiple_of(zz * p.in_rows, p.in_rows), p.in_rows)
        r.wa[rows, cut] = (r.wa[rows, cut].astype(F32) + part.astype(F32)).astype(BF)

    def attention_sum(j):
        cut = tile_cut(j)

        @on(inner)
        def _():
            arrived(r.r_in.at[2:4, :, cut], k_in[j] + 2)
            for zz in (nz - 1 - z, nz - 1 - mate):
                add(zz, r.r_in[jnp.where(zz == far_base, 2, 3), :, cut], cut)
            send(inner, shard(nz - 1 - z, cut), r.r_in.at[1, :, cut], to_inner, k_in[j] + 1)
            send(inner, shard(nz - 1 - mate, cut), r.r_in.at[4, :, cut], to_inner, k_in[j] + 3)

    def attention_last(j):
        cut = tile_cut(j)

        @on(inner)
        def _():
            arrived(r.r_in.at[4, :, cut], k_in[j] + 3)
            add(mate, r.r_in[4, :, cut], cut)
            send(inner, shard(mate, cut), r.r_in.at[1, :, cut], (s, 2 * mate + y), k_in[j] + 1)

    def unit_grads(yy, i):
        def four(buf):
            return jnp.concatenate([buf[m, 2 * i + k, yy] for m in range(2) for k in range(2)], 0)

        rows_x, up = four(r.x_all), four(r.db_all)
        hidden = mm(rows_x, r.w1[:, mine_in]) + r.par_f[0:1, mine_in]
        below = 0.5 + 0.5 * lax.erf(hidden * (0.5**0.5))
        slope = below + hidden * (0.3989422804014327 * jnp.exp(-0.5 * hidden * hidden))
        dhidden = (mm(up, r.w2t[:, mine_in]) * slope).astype(BF)
        r.u_out[...] += mm_tn((hidden * below).astype(BF), up)
        r.w_col[...] += mm_tn(rows_x, dhidden)

    def units_here(t):
        for one in (xs, db):
            one.from_core0(t, True)
        unit_grads(y, t)

    def units_over_y(t):
        for one in (xs, db):
            one.from_core0(t, False)
            one.from_y(t)
        unit_grads(1 - y, t)

    entry = iota((p.share_rows, ln), 0) + (s * p.quarter + dp * p.share)

    def scatter(m):
        def step(i, carry):
            hot = []
            for k in range(2):
                hot.append(jnp.where(entry == r.ids_all[2 * i + k, pl.ds(m, 1), :], 1.0, 0.0).astype(BF))
            rows = r.de_all[m, pl.ds(2 * i, 2)].reshape(2 * ln, w)
            o_tab[...] += mm(jnp.concatenate(hot, 1), rows)[0 : p.share]
            return carry

        lax.fori_loop(0, n_dp // 2, step, 0)

    k_col, k_smz = recvs.take(), recvs.take()
    mine_in = pl.ds(pl.multiple_of(dp * p.out_rows, p.out_rows), p.out_rows)
    mate_half = 1 - z // 2

    def gathered_row(cond):
        send(cond, r.de_all.at[1 - x], r.de_all.at[1 - x], (core, dp), k_dex + (1 - x))

    attention_tile(3)
    pair_step(de, k_row, 1, on_0, k_pass)
    attention_tile(0)
    db.step(3)
    db.cross(3)
    attention_sum(3)
    pair_step(de, k_row, 2, on_0, k_pass)

    @on(at_x0)
    def _():
        arrived(r.ch_all.at[c, 0 : n_dp - 2], k_ch)
        send(at_x0, r.ch_all.at[c], r.ch_all.at[c], (across, dp), k_cha)
        send(at_x0, r.ch_all.at[c], r.ch_all.at[c], (core, dp), k_chx)


    @on(is_ff)
    def _():
        r.u_out[...] = jnp.zeros(r.u_out.shape, F32)
        r.w_col[...] = jnp.zeros(r.w_col.shape, F32)
        on(at_x1)(lambda: arrived(r.x_all.at[0, z, y], xs.own))
        arrived(r.db_all.at[0, z, y], db.own)
        units_here(z // 2)
        units_here(mate_half)

    attention_tile(1)
    attention_sum(0)
    attention_last(3)

    def row_0(i):
        @on(on_1)
        def _():
            arrived(row(0, i), k_row + i)
            pair_line(de, k_row, on_1, i)

    row_0(dp)
    on(at_x1)(logits)
    row_0(ydp)
    pair_step(de, k_row, 1, on_1, k_pass)
    attention_sum(1)
    attention_last(0)

    attention_tile(2)
    attention_last(1)
    pair_step(de, k_row, 2, on_1, k_pass)

    gathered(k_sm, to_sm)
    r.sm_tot[...] = r.b_sm[0] + r.b_sm[1] + r.b_sm[2] + r.b_sm[3]
    r.r_sm[z] = r.sm_tot[...]
    for k in range(1, nz):
        zz = lax.rem(z + k, nz)
        send(always, r.sm_tot, r.r_sm.at[z], (s, 2 * zz + y), k_smz)

    attention_sum(2)
    attention_last(2)

    @on(is_ff)
    def _():
        units_over_y(z // 2)

    pair_step(de, k_row, 3, is_ff, k_pass)
    gathered_row(is_ff)

    def passed_row(cond):
        @on(cond)
        def _():
            arrived(r.de_all.at[x], k_pass)

        send(cond, r.de_all.at[x], r.de_all.at[x], (core, dp), k_dex + x)

    def column_block(k):
        at = k * p.out_rows
        return r.slope.at[0 : p.in_rows, pl.ds(at if isinstance(k, int) else pl.multiple_of(at, p.out_rows), p.out_rows)]

    @on(is_ff)
    def _():
        units_over_y(mate_half)
        o_wout[...] = r.u_out[...].astype(BF)
        emit(4, o_wout)
        for k in range(n_dp):
            column_block(k)[...] = r.w_col[k * p.in_rows : (k + 1) * p.in_rows, :].astype(BF)
        r.r_col[dp] = column_block(dp)[...]

    for k in (4, 5, 3, 2, 6, 1, 7) if n_dp == 8 else range(1, n_dp):
        to = lax.rem(dp + k, n_dp)
        send(is_ff, column_block(to), r.r_col.at[dp], (s, to), k_col)
    @on(at_x1)
    def _():
        arrived(r.ch_all.at[c], k_cha)
        send(at_x1, r.ch_all.at[c], r.ch_all.at[c], (core, dp), k_chx)

    passed_row(is_ff)


    head_part()

    on(is_att)(lambda: arrived(r.de_all.at[1 - x], k_dex + 1 - x))
    scatter(1 - x)
    on(is_att)(lambda: arrived(r.de_all.at[x], k_dex + x))
    scatter(x)
    n_pos = ln // n_dp
    here = pl.ds(pl.multiple_of(dp * n_pos, n_pos), n_pos)
    total = jnp.zeros((n_pos, w), F32)
    for m in range(2):
        for i in range(n_dp):
            total = total + r.de_all[m, i, here, :].astype(F32)
    o_pos[...] = total
    emit(1, o_tab)
    emit(2, o_pos)

    @on(is_att)
    def _():
        mine = pl.ds(pl.multiple_of(z * p.in_rows, p.in_rows), p.in_rows)
        for j in (3, 0, 1, 2):
            cut = tile_cut(j)

            @on(inner)
            def _():
                arrived(r.r_in.at[0, :, cut], k_in[j])
                add(z, r.r_in[0, :, cut], cut)

            arrived(r.r_in.at[1, :, cut], k_in[j] + 1)
            o_win[0, :, cut] = (r.wa[mine, cut].astype(F32) + r.r_in[1, :, cut].astype(F32)).astype(BF)
            pltpu.make_async_copy(o_win.at[:, :, cut], outs[3].at[:, :, cut], os.at[3]).start()

    @on(is_ff)
    def _():
        arrived(r.r_col.at[0 : n_dp - 1], k_col)
        for k in range(n_dp):
            cut = slice(k * p.out_rows, (k + 1) * p.out_rows)
            pltpu.make_async_copy(r.r_col.at[k], outs[3].at[0, :, cut], os.at[3]).start()

    arrived(r.r_sm.at[0 : nz - 1], k_smz)
    r.sm_all[...] = r.r_sm[0] + r.r_sm[1] + r.r_sm[2] + r.r_sm[3]
    emit(5, o_vec)
    for i, src in enumerate((o_log, o_tab, o_pos, o_win, o_wout, o_vec)):
        pltpu.make_async_copy(src, outs[i].at[0] if i == 4 else outs[i], os.at[i]).wait()

    drain(1)
    assert sends.n <= SENDS and recvs.n <= RECVS, (sends.n, recvs.n)


def finish(p, *refs):
    ins, outs, (log_v, log_w, tab_v, win_v, win_w, wout_v, wout_w, vec_v, b_v, v_v, si, so) = refs[:6], refs[6:15], refs[15:]
    pieces = (log_v, tab_v, None, win_v, wout_v, vec_v)

    def copy_in(i):
        return pltpu.make_async_copy(ins[i], pieces[i], si.at[i])

    def copy_out(i, src):
        return pltpu.make_async_copy(src, outs[i], so.at[i])

    for i in (5, 0, 1, 3, 4):
        copy_in(i).start()
    straight = pltpu.make_async_copy(ins[2], outs[2], so.at[2])
    straight.start()
    n_b, n_w = p.ff // p.n_dp, p.width // p.n_dp
    copy_in(5).wait()
    mine = vec_v[pl.ds(lax.axis_index("dp"), 1), :]
    b_v[...] = mine[:, 0:n_b]
    for k in range(3):
        v_v[k] = mine[:, n_b + 128 * k : n_b + 128 * k + n_w]
    done = [copy_out(5, b_v)] + [copy_out(6 + k, v_v.at[k]) for k in range(3)]
    copy_in(0).wait()
    log_w[...] = log_v[...].astype(F32)
    done.append(copy_out(0, log_w))
    for one in done:
        one.start()
    copy_in(1).wait()
    done.append(copy_out(1, tab_v))
    done[-1].start()
    copy_in(3).wait()
    win_w[...] = win_v[...].astype(F32)
    done.append(copy_out(3, win_w))
    done[-1].start()
    copy_in(4).wait()
    wout_w[...] = wout_v[...].astype(F32)
    done.append(copy_out(4, wout_w))
    done[-1].start()
    straight.wait()
    for one in done:
        one.wait()


def whole(
    n_dp,
    token_ids,
    segment_ids,
    masked_rows,
    embedding,
    pos_table,
    w_in,
    w_out,
    b_in,
    b_out,
    norm_gain,
    norm_shift,
    logit_grad,
):
    quarter, width = embedding.shape
    batches, _, length = token_ids.shape
    masks = masked_rows.shape[-1]
    ff = w_in.shape[-1]
    p = Plan(n_dp, length, width, ff, quarter, masks)
    scratch = scratch_list(p)
    shapes = [
        (batches, 1, masks, quarter),
        (p.share, width),
        (length // n_dp, width),
        (1, p.in_rows, ff),
        (1, p.out_rows, width),
        (1, ff // n_dp),
        (1, p.in_rows),
        (1, p.in_rows),
        (1, p.in_rows),
    ]
    far = pl.BlockSpec(memory_space=pl.ANY)
    part_types = [BF, F32, F32, BF, BF]
    parts = [jax.ShapeDtypeStruct(shape, kind) for shape, kind in zip(shapes, part_types)]
    parts.append(jax.ShapeDtypeStruct((8, width), F32))
    summed = pl.pallas_call(
        functools.partial(fused, p, list(scratch)),
        out_shape=parts,
        in_specs=[far] * 12,
        out_specs=[far] * 6,
        scratch_shapes=[pltpu.VMEM(*one) for one in scratch.values()]
        + [
            pltpu.SemaphoreType.DMA((SENDS,)),
            pltpu.SemaphoreType.DMA((RECVS,)),
            pltpu.SemaphoreType.DMA((len(p.chunks) + 11,)),
            pltpu.SemaphoreType.DMA((6,)),
        ],
        compiler_params=pltpu.CompilerParams(
            collective_id=0, has_side_effects=True, vmem_limit_bytes=VMEM_LIMIT
        ),
    )(
        token_ids,
        segment_ids,
        masked_rows,
        b_in,
        b_out,
        norm_gain,
        norm_shift,
        logit_grad,
        pos_table,
        embedding,
        w_in,
        w_out,
    )
    room = [
        (shapes[0], BF),
        (shapes[0], F32),
        (shapes[1], F32),
        (shapes[3], BF),
        (shapes[3], F32),
        (shapes[4], BF),
        (shapes[4], F32),
        ((8, width), F32),
        (shapes[5], F32),
        ((3, 1, p.in_rows), F32),
    ]
    return pl.pallas_call(
        functools.partial(finish, p),
        out_shape=[jax.ShapeDtypeStruct(shape, F32) for shape in shapes],
        in_specs=[far] * 6,
        out_specs=[far] * 9,
        scratch_shapes=[pltpu.VMEM(*one) for one in room]
        + [pltpu.SemaphoreType.DMA((6,)), pltpu.SemaphoreType.DMA((9,))],
        compiler_params=pltpu.CompilerParams(vmem_limit_bytes=VMEM_LIMIT),
    )(*summed)


def solution(mesh):
    n_section, n_dp = mesh.shape["section"], mesh.shape["dp"]

    def chosen_form(*args):
        token_ids, embedding, w_in = args[0], args[3], args[5]
        fits = (
            n_section == 4
            and n_dp == 8
            and token_ids.shape[0] == 2
            and token_ids.shape[1:] == (1, 128)
            and w_in.shape[1] % (16 * n_dp) == 0
            and w_in.shape[2] == 4 * w_in.shape[1]
            and embedding.shape[0] % (8 * n_dp) == 0
        )
        return whole(n_dp, *args) if fits else local(*args)

    placed = (
        P(None, "dp", None),
        P(None, "dp", None),
        P(None, "dp", None),
        P("section", None),
        P(),
        P("section", None, None),
        P("section", None, None),
        P("section", None),
        P("section", None),
        P("section", None),
        P("section", None),
        P(None, "dp", None, "section"),
    )
    return jax.shard_map(
        chosen_form,
        mesh=mesh,
        in_specs=placed,
        out_specs=(
            P(None, "dp", None, "section"),
            P(("section", "dp"), None),
            P("dp", None),
            P("section", "dp", None),
            P("section", "dp", None),
            P("section", "dp"),
            P("section", "dp"),
            P("section", "dp"),
            P("section", "dp"),
        ),
        check_vma=False,
    )
```

```python
import functools
import math
import types

import jax
import jax.numpy as jnp
from jax import lax
from jax.experimental import pallas as pl
from jax.experimental.pallas import tpu as pltpu
from jax.sharding import PartitionSpec as P

HEADS = 12


EPSILON = 1e-12


def for_sending(array):
    return jax.tree.map(lambda a: a.astype(jnp.bfloat16) if a.dtype == jnp.float32 else a, array)


def passed_along(block, axis, distance):
    devices = range(lax.axis_size(axis))
    route = [(i - distance, i) for i in devices if i - distance in devices]
    return lax.ppermute(block, axis, route)


def broadcast(value, axis, source):
    kept = jnp.where(lax.axis_index(axis) == source, value, 0).astype(value.dtype)
    return lax.psum(kept, axis)


def norm_forward(resid, gain_row, shift_row):
    centre = jnp.mean(resid, -1, keepdims=True)
    centred = resid - centre
    inverse = lax.rsqrt(jnp.mean(centred * centred, -1, keepdims=True) + EPSILON)
    normed = centred * inverse
    return (normed * gain_row + shift_row, normed, inverse)


def norm_backward(upstream, normed, inverse, gain_row):
    gain_part = jnp.sum(upstream * normed, 0)
    shift_part = jnp.sum(upstream, 0)
    scaled = upstream * gain_row
    first_mean = jnp.mean(scaled, -1, keepdims=True)
    second_mean = jnp.mean(scaled * normed, -1, keepdims=True)
    return (inverse * (scaled - first_mean - normed * second_mean), gain_part, shift_part)


def to_heads(values):
    return values.reshape(values.shape[0], HEADS, values.shape[1] // HEADS)


def row_scores(query, keyed, segment):
    factor = (query.shape[1] // HEADS) ** (-0.5)
    scores = (
        jnp.einsum(
            "qhd,khd->hqk", to_heads(query), to_heads(keyed), preferred_element_type=jnp.float32
        )
        * factor
    )
    allowed = segment[:, None] == segment[None, :]
    return jnp.where(allowed[None], scores, -1000000000.0)


def attend_row(packed, segment):
    width = packed.shape[1] // 3
    scores = row_scores(packed[:, :width], packed[:, width : 2 * width], segment)
    row_peak = jnp.max(scores, -1, keepdims=True)
    exponent = jnp.exp(scores - row_peak)
    row_total = jnp.sum(exponent, -1, keepdims=True)
    chance = (exponent / row_total).astype(jnp.bfloat16)
    context = jnp.einsum(
        "hqk,khd->qhd", chance, to_heads(packed[:, 2 * width :]), preferred_element_type=jnp.float32
    )
    summary = (row_peak + jnp.log(row_total))[..., 0]
    return (context.reshape(packed.shape[0], width).astype(jnp.bfloat16), summary)


def attend_back(packed, segment, summary, upstream):
    length = packed.shape[0]
    width = packed.shape[1] // 3
    factor = (width // HEADS) ** (-0.5)
    scores = row_scores(packed[:, :width], packed[:, width : 2 * width], segment)
    chance = jnp.exp(scores - summary[..., None])
    grad_heads = to_heads(upstream)
    grad_chance = jnp.einsum(
        "qhd,khd->hqk",
        grad_heads,
        to_heads(packed[:, 2 * width :]),
        preferred_element_type=jnp.float32,
    )
    grad_value = jnp.einsum(
        "hqk,qhd->khd", chance.astype(jnp.bfloat16), grad_heads, preferred_element_type=jnp.float32
    )
    grad_score = chance * (grad_chance - jnp.sum(chance * grad_chance, -1, keepdims=True))
    grad_score = grad_score.astype(jnp.bfloat16)
    grad_query = (
        jnp.einsum(
            "hqk,khd->qhd",
            grad_score,
            to_heads(packed[:, width : 2 * width]),
            preferred_element_type=jnp.float32,
        )
        * factor
    )
    grad_key = (
        jnp.einsum(
            "hqk,qhd->khd",
            grad_score,
            to_heads(packed[:, :width]),
            preferred_element_type=jnp.float32,
        )
        * factor
    )
    joined = jnp.concatenate(
        [
            grad_query.reshape(length, width),
            grad_key.reshape(length, width),
            grad_value.reshape(length, width),
        ],
        1,
    )
    return joined.astype(jnp.bfloat16)


def attention_forward(inputs, segment, params):
    w_first, w_second, bias_first, bias_second, gain_row, shift_row = params
    rows_here, length, width = inputs.shape
    flat = inputs.reshape(rows_here * length, width)
    offset = jnp.concatenate(
        [bias_first[:width], jnp.zeros((width,), jnp.float32), bias_first[2 * width : 3 * width]]
    )
    packed = jnp.dot(flat, w_first[:, : 3 * width], preferred_element_type=jnp.float32) + offset
    packed = packed.astype(jnp.bfloat16).reshape(rows_here, length, 3 * width)
    context, summary = lax.map(lambda item: attend_row(item[0], item[1]), (packed, segment))
    branch = (
        jnp.dot(
            context.reshape(-1, width), w_first[:, 3 * width :], preferred_element_type=jnp.float32
        )
        + bias_second
    )
    result, normed, inverse = norm_forward(flat.astype(jnp.float32) + branch, gain_row, shift_row)
    return (result.reshape(rows_here, length, width), (packed, context, summary, normed, inverse))


def attention_backward(inputs, segment, upstream, params, totals):
    w_first, w_second, bias_first, bias_second, gain_row, shift_row = params
    rows_here, length, width = inputs.shape
    result, saved = attention_forward(inputs, segment, params)
    packed, context, summary, normed, inverse = saved
    flat = inputs.reshape(-1, width)
    grad_resid, gain_part, shift_part = norm_backward(
        upstream.reshape(-1, width), normed, inverse, gain_row
    )
    grad_branch = grad_resid.astype(jnp.bfloat16)
    grad_out_proj = jnp.einsum(
        "nd,ne->de", context.reshape(-1, width), grad_branch, preferred_element_type=jnp.float32
    )
    bias_second_part = jnp.sum(grad_branch.astype(jnp.float32), 0)
    grad_context = jnp.einsum(
        "ne,de->nd", grad_branch, w_first[:, 3 * width :], preferred_element_type=jnp.float32
    )
    grad_context = grad_context.astype(jnp.bfloat16).reshape(rows_here, length, width)
    grad_packed = lax.map(
        lambda item: attend_back(item[0], item[1], item[2], item[3]),
        (packed, segment, summary, grad_context),
    )
    flat_packed = grad_packed.reshape(-1, 3 * width)
    grad_proj = jnp.einsum("nd,nc->dc", flat, flat_packed, preferred_element_type=jnp.float32)
    bias_sums = jnp.sum(flat_packed.astype(jnp.float32), 0)
    grad_input = grad_resid + jnp.einsum(
        "nc,dc->nd", flat_packed, w_first[:, : 3 * width], preferred_element_type=jnp.float32
    )
    first_total, second_total, bias_first_total, bias_second_total, gain_total, shift_total = totals
    first_total = (
        first_total.at[:, : 3 * width].add(grad_proj).at[:, 3 * width :].add(grad_out_proj)
    )
    bias_first_total = (
        bias_first_total.at[:width]
        .add(bias_sums[:width])
        .at[2 * width : 3 * width]
        .add(bias_sums[2 * width :])
    )
    updated = (
        first_total,
        second_total,
        bias_first_total,
        bias_second_total + bias_second_part,
        gain_total + gain_part,
        shift_total + shift_part,
    )
    return (grad_input.reshape(rows_here, length, width).astype(jnp.bfloat16), updated)


def feed_forward(inputs, params):
    w_first, w_second, bias_first, bias_second, gain_row, shift_row = params
    rows_here, length, width = inputs.shape
    flat = inputs.reshape(-1, width)
    hidden = jnp.dot(flat, w_first, preferred_element_type=jnp.float32) + bias_first
    active = jax.nn.gelu(hidden, approximate=False).astype(jnp.bfloat16)
    branch = jnp.dot(active, w_second, preferred_element_type=jnp.float32) + bias_second
    result, normed, inverse = norm_forward(flat.astype(jnp.float32) + branch, gain_row, shift_row)
    return (result.reshape(rows_here, length, width), (hidden, active, normed, inverse))


def feed_backward(inputs, upstream, params, totals):
    w_first, w_second, bias_first, bias_second, gain_row, shift_row = params
    rows_here, length, width = inputs.shape
    result, saved = feed_forward(inputs, params)
    hidden, active, normed, inverse = saved
    flat = inputs.reshape(-1, width)
    grad_resid, gain_part, shift_part = norm_backward(
        upstream.reshape(-1, width), normed, inverse, gain_row
    )
    grad_branch = grad_resid.astype(jnp.bfloat16)
    grad_second = jnp.einsum("nf,nd->fd", active, grad_branch, preferred_element_type=jnp.float32)
    bias_second_part = jnp.sum(grad_branch.astype(jnp.float32), 0)
    grad_active = jnp.einsum("nd,fd->nf", grad_branch, w_second, preferred_element_type=jnp.float32)
    through = jax.vjp(lambda inner: jax.nn.gelu(inner, approximate=False), hidden)[1](grad_active)[
        0
    ]
    grad_hidden = through.astype(jnp.bfloat16)
    grad_first = jnp.einsum("nd,nf->df", flat, grad_hidden, preferred_element_type=jnp.float32)
    bias_first_part = jnp.sum(grad_hidden.astype(jnp.float32), 0)
    grad_input = grad_resid + jnp.einsum(
        "nf,df->nd", grad_hidden, w_first, preferred_element_type=jnp.float32
    )
    terms = (grad_first, grad_second, bias_first_part, bias_second_part, gain_part, shift_part)
    updated = tuple((total + term for total, term in zip(totals, terms)))
    return (grad_input.reshape(rows_here, length, width).astype(jnp.bfloat16), updated)


def local(
    token_ids,
    segment_ids,
    masked_rows,
    embedding,
    pos_table,
    w_in,
    w_out,
    b_in,
    b_out,
    norm_gain,
    norm_shift,
    logit_grad,
):
    sections = lax.axis_size("section")
    section_index = lax.axis_index("section")
    quarter, width = embedding.shape
    batches, rows_here, length = token_ids.shape
    params = (
        w_in[0],
        w_out[0],
        b_in[0].astype(jnp.float32),
        b_out[0].astype(jnp.float32),
        norm_gain[0].astype(jnp.float32),
        norm_shift[0].astype(jnp.float32),
    )
    local_ids = token_ids - section_index * quarter
    inside = (local_ids >= 0) & (local_ids < quarter)
    picked = jnp.take(embedding, jnp.clip(local_ids, 0, quarter - 1), axis=0)
    partial_rows = jnp.where(inside[..., None], picked.astype(jnp.float32), 0.0)
    looked = lax.psum(partial_rows.astype(jnp.bfloat16), "section").astype(jnp.float32)
    entry = (looked + pos_table.astype(jnp.float32)).astype(jnp.bfloat16)

    def spare_forward(inputs, segment):
        return jnp.zeros(inputs.shape, jnp.bfloat16)

    def attend_forward(inputs, segment):
        return attention_forward(inputs, segment, params)[0].astype(jnp.bfloat16)

    def feed_only(inputs, segment):
        return feed_forward(inputs, params)[0].astype(jnp.bfloat16)

    def spare_backward(inputs, segment, upstream, totals):
        return (jnp.zeros(inputs.shape, jnp.bfloat16), totals)

    def attend_backward(inputs, segment, upstream, totals):
        return attention_backward(inputs, segment, upstream, params, totals)

    def feed_back_only(inputs, segment, upstream, totals):
        return feed_backward(inputs, upstream, params, totals)

    ticks = batches + sections - 1
    kept = jnp.zeros_like(entry)
    outputs = jnp.zeros_like(entry)
    incoming = jnp.zeros_like(entry[0])
    for moment in range(ticks):
        micro_index = moment - section_index
        is_live = (micro_index >= 0) & (micro_index < batches)
        micro_slot = jnp.clip(micro_index, 0, batches - 1)
        current = jnp.where(section_index == 0, entry[micro_slot], incoming)
        kept = kept.at[micro_slot].set(jnp.where(is_live, current, kept[micro_slot]))
        branch_index = jnp.where(is_live, 1 + section_index % 2, 0)
        result = lax.switch(
            branch_index,
            [spare_forward, attend_forward, feed_only],
            current,
            segment_ids[micro_slot],
        )
        outputs = outputs.at[micro_slot].set(jnp.where(is_live, result, outputs[micro_slot]))
        if moment + 1 < ticks:
            incoming = jax.tree.map(
                lambda part, own: part.astype(own.dtype),
                passed_along(for_sending(result), "section", 1),
                result,
            )
    final_rows = jnp.take_along_axis(outputs, masked_rows[..., None], axis=2)
    head_rows = broadcast(final_rows, "section", sections - 1)
    logits = jnp.einsum("mrkd,vd->mrkv", head_rows, embedding, preferred_element_type=jnp.float32)
    partial_grad = jnp.einsum(
        "mrkv,vd->mrkd", logit_grad, embedding, preferred_element_type=jnp.float32
    )
    grad_rows = lax.psum(partial_grad.astype(jnp.bfloat16), "section").astype(jnp.float32)
    table_head = jnp.einsum(
        "mrkv,mrkd->vd", logit_grad, head_rows, preferred_element_type=jnp.float32
    )
    places = (masked_rows[..., None] == jnp.arange(length)[None, None, None, :]).astype(jnp.float32)
    top_grad = jnp.einsum("mrkl,mrkd->mrld", places, grad_rows, precision=lax.Precision.HIGHEST)
    gradients = (
        jnp.zeros(w_in.shape[1:], jnp.float32),
        jnp.zeros(w_out.shape[1:], jnp.float32),
        jnp.zeros(b_in.shape[1:], jnp.float32),
        jnp.zeros((width,), jnp.float32),
        jnp.zeros((width,), jnp.float32),
        jnp.zeros((width,), jnp.float32),
    )
    grad_entry = jnp.zeros_like(entry)
    back_in = jnp.zeros_like(entry[0])
    for moment in range(ticks):
        micro_index = moment - (sections - 1 - section_index)
        is_live = (micro_index >= 0) & (micro_index < batches)
        micro_slot = jnp.clip(micro_index, 0, batches - 1)
        upstream = jnp.where(
            section_index == sections - 1, top_grad[micro_slot], back_in.astype(jnp.float32)
        )
        branch_index = jnp.where(is_live, 1 + section_index % 2, 0)
        grad_input, gradients = lax.switch(
            branch_index,
            [spare_backward, attend_backward, feed_back_only],
            kept[micro_slot],
            segment_ids[micro_slot],
            upstream,
            gradients,
        )
        grad_entry = grad_entry.at[micro_slot].set(
            jnp.where(is_live, grad_input, grad_entry[micro_slot])
        )
        if moment + 1 < ticks:
            back_in = jax.tree.map(
                lambda part, own: part.astype(own.dtype),
                passed_along(for_sending(grad_input), "section", -1),
                grad_input,
            )
    input_grad = broadcast(grad_entry, "section", 0)
    input_wide = input_grad.astype(jnp.float32)
    pos_grad = jnp.sum(input_wide, (0, 1))
    targets = jnp.where(inside, local_ids, quarter).reshape(-1)
    table_input = jax.ops.segment_sum(
        input_wide.reshape(-1, width), targets, num_segments=quarter + 1
    )[:quarter]
    w_in_part, w_out_part, b_in_part, b_out_part, gain_part, shift_part = gradients
    reduced = (
        lax.psum_scatter(w_in_part, "dp", scatter_dimension=0, tiled=True),
        lax.psum_scatter(w_out_part, "dp", scatter_dimension=0, tiled=True),
        lax.psum_scatter(b_in_part, "dp", scatter_dimension=0, tiled=True),
        lax.psum_scatter(b_out_part, "dp", scatter_dimension=0, tiled=True),
        lax.psum_scatter(gain_part, "dp", scatter_dimension=0, tiled=True),
        lax.psum_scatter(shift_part, "dp", scatter_dimension=0, tiled=True),
        lax.psum_scatter(pos_grad, "dp", scatter_dimension=0, tiled=True),
        lax.psum_scatter(table_input + table_head, "dp", scatter_dimension=0, tiled=True),
    )
    table_grad = reduced[7]
    return (
        logits,
        table_grad,
        reduced[6],
        reduced[0][None],
        reduced[1][None],
        reduced[2][None],
        reduced[3][None],
        reduced[4][None],
        reduced[5][None],
    )


SENDS = 86
RECVS = 83
VMEM_LIMIT = 64 * 2**20
BF = jnp.bfloat16
F32 = jnp.float32
MESH = pl.DeviceIdType.MESH


def mm(a, b):
    return jnp.dot(a, b, preferred_element_type=F32)


def mm_nt(a, b):
    return lax.dot_general(a, b, (((1,), (1,)), ((), ())), preferred_element_type=F32)


def mm_tn(a, b):
    return lax.dot_general(a, b, (((0,), (0,)), ((), ())), preferred_element_type=F32)


def iota(shape, dim):
    return lax.broadcasted_iota(jnp.int32, shape, dim)


def column(row):
    return jnp.broadcast_to(row.astype(F32), (128, 128)).T


class Plan:
    def __init__(self, n_dp, length, width, ff, quarter, masks):
        self.n_dp, self.length, self.width, self.ff = n_dp, length, width, ff
        self.quarter, self.masks = quarter, masks
        self.nz = n_dp // 2
        self.share = quarter // n_dp
        self.in_rows = width // n_dp
        self.out_rows = ff // n_dp
        self.mask_pad = -(-masks // 16) * 16
        self.share_pad = -(-self.share // 128) * 128
        self.share_rows = -(-self.share // 16) * 16
        self.chunks = []
        at = 0
        while at < quarter:
            size = min(1024, quarter - at)
            self.chunks.append((at, size))
            at += size


class Counter:
    def __init__(self):
        self.n = 0

    def take(self, k=1):
        first = self.n
        self.n += k
        return first


def scratch_list(p):
    w, ff, ln = p.width, p.ff, p.length
    mp = p.mask_pad
    return dict(
        tok=((2, 1, ln), jnp.int32),
        seg=((2, 1, ln), jnp.int32),
        picks=((2, 1, p.masks), jnp.int32),
        b_in=((1, ff), BF),
        b_out=((1, w), BF),
        gain=((1, w), BF),
        shift=((1, w), BF),
        emb=((p.quarter, w), BF),
        lg=((2, 1, p.masks, p.quarter), BF),
        pos=((ln, w), BF),
        wa=((w, ff), BF),
        w1=((w, ff), BF),
        w2=((ff, w), BF),
        w1t=((ff, w), BF),
        w2t=((w, ff), BF),
        par_a=((8, ff), F32),
        par_f=((8, ff), F32),
        psend=((ln, w), BF),
        psum=((ln, w), BF),
        prow=((2, ln, w), BF),
        lgp=((2 * mp, p.quarter), BF),
        lgs=((p.n_dp, 2 * p.masks, p.share_pad), BF),
        lgr=((p.n_dp, 2 * p.masks, p.share_pad), BF),

        g=((2 * mp, w), F32),
        grow=((2, p.masks, w), F32),
        gwide=((ln, w), F32),
        mrow=((8, ln), jnp.int32),
        ids_own=((8, ln), jnp.int32),
        ids_all=((p.n_dp, 8, ln), jnp.int32),
        x_a=((ln, w), BF),
        y_f=((ln, w), BF),
        pk=((ln, 3 * w), BF),
        ctx=((ln, w), BF),
        probs=((w // 128, ln, 256), F32),
        n_a=((ln, w), F32),
        n_f=((ln, w), F32),
        inv_a=((ln, 1), F32),
        inv_f=((ln, 1), F32),
        slope=((ln, ff), BF),
        xt_a=((p.nz, 2, p.in_rows, ln), BF),
        ct_a=((p.nz, 2, p.in_rows, ln), BF),
        dyin=((ln, w), BF),
        dyf=((ln, w), F32),
        dres=((ln, w), F32),
        dbr_a=((ln, w), BF),
        dpk=((ln, 3 * w), BF),
        dctx=((ln, w), BF),
        dx=((ln, w), BF),
        bsum=((1, ff), F32),
        vecs=((8, w), F32),
        sm_a=((8, w), F32),
        sm_f=((8, w), F32),
        b_ctx=((p.nz, p.in_rows, 4 * ln), BF),
        b_x=((p.nz, p.in_rows, 4 * ln), BF),
        b_sm=((4, 8, w), F32),
        sm_tot=((8, w), F32),
        sm_all=((8, w), F32),
        r_sm=((p.nz, 8, w), F32),
        r_in=((5, p.in_rows, ff), BF),
        x_all=((2, p.nz, ln, w), BF),
        db_all=((2, p.nz, ln, w), BF),
        spare_a=((4, ln, w), BF),
        spare_b=((4, ln, w), BF),
        w_col=((w, 2 * p.out_rows), F32),
        r_col=((p.n_dp, p.in_rows, p.out_rows), BF),
        ch_own=((mp, w), BF),
        ch_two=((mp, w), BF),
        ch_pair=((mp, w), BF),
        ch_far=((mp, w), BF),
        ch_all=((2, p.n_dp, mp, w), BF),
        de_all=((2, p.n_dp, ln, w), BF),
        u_out=((2 * p.out_rows, w), F32),
        o_tab=((p.share, w), F32),
        o_pos=((ln // p.n_dp, w), F32),
    )


def fused(p, names, *refs):
    far_small, (lg_h, pos_h, emb_h, w_in_h, w_out_h) = refs[:7], refs[7:12]
    outs = refs[12:18]
    r = types.SimpleNamespace(**dict(zip(names, refs[18:])))
    ss, rs, ls, os = refs[18 + len(names) :]
    acc, o_log = r.u_out.at[0 : 2 * p.length], r.lg
    o_win = r.r_in.at[0:1]
    (o_tab, o_pos, o_wout, o_vec) = (r.o_tab, r.o_pos, r.w1t.at[1024 : 1024 + p.out_rows], r.sm_all)
    w, ff, ln, mp, nz, n_dp = p.width, p.ff, p.length, p.mask_pad, p.nz, p.n_dp
    heads = w // 64
    pairs = heads // 2

    s = lax.axis_index("section")
    dp = lax.axis_index("dp")
    x, c = s // 2, lax.rem(s, 2)
    z, y = dp // 2, lax.rem(dp, 2)
    core = s + 1 - 2 * c
    across = s + 2 - 4 * x
    ydp = dp + 1 - 2 * y
    other = 1 - c
    at_x0, at_x1 = frozenset(["x0"]), frozenset(["x1"])
    is_att, is_ff = frozenset(["att"]), frozenset(["ff"])
    on_0, on_1 = at_x0 | is_ff, at_x1 | is_ff
    outer_att, inner = is_att | {"outer"}, is_att | {"inner"}
    always = frozenset()
    sends, recvs = Counter(), Counter()
    def holds(name):
        if name[:2] == "z>":
            return z >= int(name[2:])
        if name[:2] == "z<":
            return z <= int(name[2:])
        if name in ("outer", "inner"):
            edge = (z == 0) | (z == nz - 1)
            return edge if name == "outer" else jnp.logical_not(edge)
        return {"x0": x == 0, "x1": x == 1, "att": c == 0, "ff": c == 1}[name]

    def at_least(k):
        return frozenset(["z>%d" % k]) if k > 0 else always

    def at_most(k):
        return frozenset(["z<%d" % k]) if k < nz - 1 else always

    not_first, not_last = at_least(1), at_most(nz - 2)
    outside = [always]

    def on(cond):
        def run(body):
            names = sorted(cond - outside[0])
            before, outside[0] = outside[0], outside[0] | cond
            if names:
                pl.when(functools.reduce(lambda a, b: a & b, [holds(name) for name in names]))(body)
            else:
                body()
            outside[0] = before

        return run

    groups, stage = {}, [0]

    def send(cond, src, dst, dev, recv, bulk=None, tag=None):
        cond = cond | outside[0]
        key = (stage[0], cond, tag)
        if key not in groups:
            groups[key] = [sends.take(), 0, bulk]
        group = groups[key]
        group[1] += math.prod(src.shape) * src.dtype.itemsize

        @on(cond)
        def _():
            pltpu.make_async_remote_copy(
                src_ref=src,
                dst_ref=dst,
                send_sem=ss.at[group[0]],
                recv_sem=rs.at[recv],
                device_id=dev,
                device_id_type=MESH,
            ).start()

    def drain(number):
        for (when, cond, _), (slot, size, bulk) in groups.items():
            if when == number:
                rows = size // (w * 2)
                assert bulk is not None or size == rows * w * 2 and rows % 16 == 0 and rows <= p.quarter, (rows, size)
                ref = r.emb.at[0:rows] if bulk is None else bulk

                @on(cond)
                def _():
                    pltpu.make_async_remote_copy(
                        src_ref=ref,
                        dst_ref=ref,
                        send_sem=ss.at[slot],
                        recv_sem=rs.at[0],
                        device_id=(core, dp),
                        device_id_type=MESH,
                    ).wait_send()

    def arrived(dst, recv):
        pltpu.make_async_remote_copy(
            src_ref=dst,
            dst_ref=dst,
            send_sem=ss.at[0],
            recv_sem=rs.at[recv],
            device_id=(core, dp),
            device_id_type=MESH,
        ).wait_recv()

    near_small = (r.tok, r.seg, r.picks, r.b_in, r.b_out, r.gain, r.shift)
    tok, seg, picks, b_in, b_out, gain, shift = near_small

    def small_copy(i):
        return pltpu.make_async_copy(far_small[i], near_small[i], ls.at[len(p.chunks) + 4 + i])

    small_copy(0).start()
    for i, (at, size) in enumerate(p.chunks):
        pltpu.make_async_copy(emb_h.at[pl.ds(at, size)], r.emb.at[pl.ds(at, size)], ls.at[i]).start()
    l_w = len(p.chunks)
    lg, pos = r.lg, r.pos
    pltpu.make_async_copy(lg_h, lg, ls.at[l_w + 2]).start()
    pltpu.make_async_copy(pos_h, pos, ls.at[l_w + 3]).start()
    for i in range(1, 7):
        small_copy(i).start()

    def fill(par):
        par[0:1, :] = b_in[...].astype(F32)
        par[1:2, 0:w] = b_out[...].astype(F32)
        par[2:3, 0:w] = gain[...].astype(F32)
        par[3:4, 0:w] = shift[...].astype(F32)

    barrier = pltpu.get_barrier_semaphore()
    peers = [(s, lax.rem(dp + k, n_dp)) for k in range(1, n_dp)]
    peers += [(core, dp), (across, dp), (3 - s, dp), (core, ydp)]
    for peer in peers:
        pl.semaphore_signal(barrier, inc=1, device_id=peer, device_id_type=MESH)

    small_copy(0).wait()
    cols = [column(tok[m]) for m in range(2)]
    first = s * p.quarter
    for i, (at, size) in enumerate(p.chunks):
        pltpu.make_async_copy(emb_h.at[pl.ds(at, size)], r.emb.at[pl.ds(at, size)], ls.at[i]).wait()
        lane = (iota((ln, size), 1) + (first + at)).astype(F32)
        hot = []
        for m in range(2):
            wide = jnp.concatenate([cols[m]] * (-(-size // 128)), 1)[:, :size]
            hot.append(jnp.where(wide == lane, 1.0, 0.0).astype(BF))
        part = mm(jnp.concatenate(hot, 0), r.emb[at : at + size, :])
        if i == 0:
            acc[...] = part
        else:
            acc[...] += part
    r.psend[...] = acc[pl.ds(pl.multiple_of(ln * other, ln), ln), :].astype(BF)

    @on(is_att)
    def _():
        pltpu.make_async_copy(w_in_h.at[0], r.wa, ls.at[l_w]).start()

    @on(is_ff)
    def _():
        pltpu.make_async_copy(w_in_h.at[0], r.w1, ls.at[l_w]).start()
        pltpu.make_async_copy(w_out_h.at[0], r.w2, ls.at[l_w + 1]).start()

    for i in range(1, 7):
        small_copy(i).wait()
    on(is_att)(lambda: fill(r.par_a))
    on(is_ff)(lambda: fill(r.par_f))

    tiles = ff // w
    k_p, k_g = recvs.take(2), recvs.take(2)
    k_pa, k_pf, k_wa, k_w1, k_w2 = recvs.take(), recvs.take(), recvs.take(tiles), recvs.take(tiles), recvs.take(tiles)
    pl.semaphore_wait(barrier, len(peers))
    send(always, r.psend, r.prow.at[0], (core, dp), k_p)

    arrived(r.prow.at[0], k_p)
    acc[0:ln, :] = acc[pl.ds(pl.multiple_of(ln * c, ln), ln), :] + r.prow[0].astype(F32)
    r.psum[...] = acc[0:ln, :].astype(BF)
    send(at_x1, r.psum, r.prow.at[1], (across, dp), k_p + 1)

    def weights(cond, part):
        if part == 0:
            send(is_att | cond, r.par_a, r.par_a, (core, dp), k_pa)
            send(is_ff | cond, r.par_f, r.par_f, (core, dp), k_pf)
        cuts = [slice(j * w, (j + 1) * w) for j in range(tiles)]
        for_core_1 = [(is_att, w_in_h.at[0, :, cut], r.wa.at[:, cut], k_wa + j, 3) for j, cut in enumerate(cuts)]
        left = [(is_ff, w_in_h.at[0, :, cut], r.w1.at[:, cut], k_w1 + j, 4) for j, cut in enumerate(cuts)]
        right = [(is_ff, w_out_h.at[0, cut, :], r.w2.at[cut, :], k_w2 + j, 5) for j, cut in enumerate(cuts)]
        for_core_0 = right + left if cond == at_x1 else [one for pair in zip(left, right) for one in pair]
        for order in (for_core_1, for_core_0):
            for whose, src, dst, recv, tag in order[:2] if part == 0 else order[2:]:
                send(whose | cond, src, dst, (core, dp), recv, tag=tag)

    weights(at_x0, 0)
    weights(at_x1, 0)
    pltpu.make_async_copy(lg_h, lg, ls.at[l_w + 2]).wait()
    pltpu.make_async_copy(pos_h, pos, ls.at[l_w + 3]).wait()
    r.lgp[...] = jnp.zeros(r.lgp.shape, BF)
    r.lgp[0 : p.masks] = lg[0, 0]
    r.lgp[mp : mp + p.masks] = lg[1, 0]

    k_lg, k_id = recvs.take(), recvs.take()
    for j in range(n_dp):
        r.lgs[j, :, p.share :] = jnp.zeros((2 * p.masks, p.share_pad - p.share), BF)
        for m in range(2):
            r.lgs[j, p.masks * m : p.masks * (m + 1), 0 : p.share] = lg[m, 0, :, p.share * j : p.share * (j + 1)]
    r.ids_own[...] = jnp.zeros(r.ids_own.shape, jnp.int32)
    for m in range(2):
        r.ids_own[m : m + 1, :] = tok[m]
    r.ids_all[dp] = r.ids_own[...]
    r.lgr[dp] = r.lgs[dp]
    for k in range(1, n_dp):
        to = lax.rem(dp + k, n_dp)
        send(always, r.lgs.at[to], r.lgr.at[dp], (s, to), k_lg, r.lgs.at[0 : n_dp - 1], 1)
        send(always, r.ids_own, r.ids_all.at[dp], (s, to), k_id, r.ids_all.at[0 : n_dp - 1], 2)

    for i, (at, size) in enumerate(p.chunks):
        part = mm(r.lgp[:, at : at + size], r.emb[at : at + size, :])
        if i == 0:
            r.g[...] = part
        else:
            r.g[...] += part
    send(always, r.g.at[pl.ds(pl.multiple_of(mp * other, mp), p.masks)], r.grow.at[0], (core, dp), k_g)
    weights(at_x0, 1)
    weights(at_x1, 1)

    def masked_gradient():
        arrived(r.grow.at[0], k_g)
        r.gwide[...] = jnp.zeros(r.gwide.shape, F32)
        r.gwide[0 : p.masks, :] = r.g[pl.ds(pl.multiple_of(mp * c, mp), p.masks), :] + r.grow[0]

    masked_gradient()
    send(at_x0, r.gwide.at[0 : p.masks], r.grow.at[1], (across, dp), k_g + 1)

    k_x = recvs.take()

    @on(at_x0)
    def _():
        arrived(r.prow.at[1], k_p + 1)
        whole = acc[0:ln, :] + r.prow[1].astype(F32)
        r.x_a[...] = (whole + pos[...].astype(F32)).astype(BF)

    @on(is_att)
    def _():
        pltpu.make_async_copy(w_in_h.at[0], r.wa, ls.at[l_w]).wait()
        arrived(r.par_f, k_pf)

    @on(is_ff)
    def _():
        pltpu.make_async_copy(w_in_h.at[0], r.w1, ls.at[l_w]).wait()
        pltpu.make_async_copy(w_out_h.at[0], r.w2, ls.at[l_w + 1]).wait()
        arrived(r.par_a, k_pa)

    def masked_places():
        return jnp.where(iota((ln, ln), 0) == r.mrow[0:1, :], 1.0, 0.0).astype(BF)

    def turn_second():
        def step(i, carry):
            at = pl.ds(pl.multiple_of(i * 128, 128), 128)
            r.w2t[:, at] = r.w2[at, :].T
            return carry

        lax.fori_loop(0, ff // 128, step, 0)

    def turn_first():
        def step(i, carry):
            at = pl.ds(pl.multiple_of(i * 128, 128), 128)
            r.w1t[at, :] = r.w1[:, at].T
            return carry

        lax.fori_loop(0, ff // 128, step, 0)

    def turn_attention(j):
        cut = slice(j * w, (j + 1) * w)
        r.wa[:, cut] = r.wa[:, cut].T

    def second_here():
        @on(is_att)
        def _():
            for j in range(tiles):
                cut = slice(j * w, (j + 1) * w)
                arrived(r.w2.at[cut, :], k_w2 + j)

    def first_here():
        @on(is_att)
        def _():
            for j in range(tiles):
                cut = slice(j * w, (j + 1) * w)
                arrived(r.w1.at[:, cut], k_w1 + j)

    @on(at_x1)
    def _():
        second_here()
        turn_second()
        first_here()
        turn_first()
        r.mrow[...] = jnp.full(r.mrow.shape, -1, jnp.int32)
        r.mrow[0:1, 0 : p.masks] = picks[c]
        arrived(r.grow.at[1], k_g + 1)
        r.gwide[0 : p.masks, :] += r.grow[1]
        coarse = r.gwide[...].astype(BF)
        fine = (r.gwide[...] - coarse.astype(F32)).astype(BF)
        places = masked_places()
        r.dyf[...] = mm(places, coarse) + mm(places, fine)
        arrived(r.x_a, k_x)

    low = jnp.where(iota((ln, 128), 1) < 64, 1.0, 0.0).astype(BF)
    high = jnp.where(iota((ln, 128), 1) < 64, 0.0, 1.0).astype(BF)

    def split(block):
        return jnp.concatenate([block * low, block * high], 0)

    def stack(block):
        return jnp.concatenate([block[:, 0:128], block[:, 128:256]], 0)

    def norm_forward(resid, par):
        centred = resid - jnp.mean(resid, -1, keepdims=True)
        inverse = lax.rsqrt(jnp.mean(centred * centred, -1, keepdims=True) + EPSILON)
        normed = centred * inverse
        return (normed * par[2:3, 0:w] + par[3:4, 0:w]).astype(BF), normed, inverse

    rows_x = r.x_a[...]

    def wa_tile(j):
        on(is_ff)(lambda: arrived(r.wa.at[:, j * w : (j + 1) * w], k_wa + j))

    for j in range(3):
        wa_tile(j)
        part = mm(rows_x, r.wa[:, j * w : (j + 1) * w])
        if j != 1:
            part = part + r.par_a[0:1, j * w : (j + 1) * w]
        r.pk[:, j * w : (j + 1) * w] = part.astype(BF)
    seg_row = seg[c].astype(F32)
    seg_col = column(seg[c])
    seg_row = jnp.broadcast_to(jnp.concatenate([seg_row, seg_row], 1), (ln, 256))
    seg_col = jnp.concatenate([seg_col, seg_col], 1)
    for h in range(pairs):
        at = 128 * h
        query = r.pk[:, at : at + 128]
        keyed = split(r.pk[:, w + at : w + at + 128])
        value = split(r.pk[:, 2 * w + at : 2 * w + at + 128])
        scores = jnp.where(seg_row == seg_col, mm_nt(query, keyed) * 0.125, -1e9)
        chance = []
        for half in (scores[:, 0:128], scores[:, 128:256]):
            power = jnp.exp(half - jnp.max(half, -1, keepdims=True))
            chance.append(power / jnp.sum(power, -1, keepdims=True))
        chance = jnp.concatenate(chance, 1)
        r.probs[h] = chance
        r.ctx[:, at : at + 128] = mm(chance.astype(BF), value).astype(BF)
    wa_tile(3)
    resid = rows_x.astype(F32) + mm(r.ctx[...], r.wa[:, 3 * w : 4 * w]) + r.par_a[1:2, 0:w]
    r.x_all[c, z], r.n_a[...], r.inv_a[...] = norm_forward(resid, r.par_a)

    class Gather:
        def __init__(self, buf):
            self.buf = buf
            self.near, self.core0 = recvs.take(nz), recvs.take(nz)

        def at(self, zz):
            return self.buf.at[c, zz]

        def start(self):
            own = self.at(z)
            send(not_last, own, own, (s, dp + 2), self.near + z)
            send(not_first, own, own, (s, dp - 2), self.near + z)
            send(is_att, own, own, (core, dp), self.core0 + z)

        def step(self, t, cond=always):
            for sign in (-1, 1):
                here, zz = at_distance(t, sign, cond)
                piece = self.at(zz)
                on(here)(lambda piece=piece, zz=zz: arrived(piece, self.near + zz))
                if t < nz - 1:
                    send(onward(here, sign), piece, piece, (s, dp - 2 * sign), self.near + zz)
                send(here | is_att, piece, piece, (core, dp), self.core0 + zz)

    def at_distance(t, sign, cond):
        here = cond | (at_least(t) if sign < 0 else at_most(nz - 1 - t))
        return here, jnp.clip(z + sign * t, 0, nz - 1)

    def onward(here, sign):
        return here | (not_last if sign < 0 else not_first)

    def ch(i):
        return r.ch_all.at[c, i]

    def de(i):
        return r.de_all.at[1 - x, i]

    k_row, k_pass = recvs.take(n_dp), recvs.take()
    k_ch, k_cho, k_chc, k_chp, k_chq, k_cha, k_chx, k_dp = (recvs.take() for _ in range(8))
    k_dex = recvs.take(2)
    xs, db = Gather(r.x_all), Gather(r.db_all)

    xs.start()

    def feed(rows_x, keep=True, turning=False):
        total = rows_x.astype(F32) + r.par_f[1:2, 0:w]

        def hidden_tile(j):
            cut = slice(j * w, (j + 1) * w)
            return mm(rows_x, r.w1[:, cut]) + r.par_f[0:1, cut]

        later = hidden_tile(0)
        for j in range(tiles):
            cut = slice(j * w, (j + 1) * w)
            hidden = later
            if j + 1 < tiles:
                later = hidden_tile(j + 1)
            if turning:
                turn_attention(j)
            below = 0.5 + 0.5 * lax.erf(hidden * (0.5**0.5))
            total = total + mm((hidden * below).astype(BF), r.w2[cut, :])
            if keep:
                slope = below + hidden * (0.3989422804014327 * jnp.exp(-0.5 * hidden * hidden))
                r.slope[:, cut] = slope.astype(BF)
        result, normed, inverse = norm_forward(total, r.par_f)
        if keep:
            r.y_f[...], r.n_f[...], r.inv_f[...] = result, normed, inverse
        else:
            r.psum[...] = result

    on(on_0)(lambda: feed(r.x_all[c, z]))
    on(at_x1)(lambda: feed(r.x_all[c, z], turning=True))
    send(at_x0 | is_ff, r.y_f, r.x_a, (across, dp), k_x)

    @on(at_x0 | is_ff)
    def _():
        arrived(r.x_all.at[0, z], xs.core0 + z)
        feed(r.x_all[0, z], False)

    send(at_x0 | is_ff, r.psum, r.x_a, (3 - s, dp), k_x)

    @on(at_x1)
    def _():
        r.ch_own[...] = mm_tn(masked_places(), r.y_f[...])[0:mp].astype(BF)

    send(at_x1, r.ch_own, r.ch_own, (across, dp), k_cho)
    send(at_x1, r.ch_own, r.ch_two, (core, dp), k_chc)
    send(at_x1, r.ch_own, r.ch_pair, (s, ydp), k_chp)

    def push(owner, kind, src, dst, cond=always):
        home, away = (is_att, is_ff) if owner == 0 else (is_ff, is_att)
        at_home = holds("att" if owner == 0 else "ff")
        slot_y = 2 + jnp.where(at_home, 0, 1)
        own_dst, near_dst, far_dst = dst(0), dst(1), dst(slot_y)


        @on(home | cond)
        def _():
            own_dst[...] = src(y)[...]

        send(away | cond, src(y), near_dst, (core, dp), kind)
        send(cond, src(1 - y), far_dst, (jnp.where(at_home, s, core), ydp), kind)

    def gathered(kind, dst):
        arrived(dst(slice(1, 4)), kind)

    def lanes(slot):
        if isinstance(slot, slice):
            return pl.ds(slot.start * ln, (slot.stop - slot.start) * ln)
        return pl.ds(slot * ln if isinstance(slot, int) else pl.multiple_of(slot * ln, ln), ln)

    k_dh = [recvs.take() for _ in range(3)]
    k_ctx, k_xt, k_dba, k_sm = (recvs.take() for _ in range(4))
    to_x = lambda slot: r.b_x.at[:, :, lanes(slot)]
    to_ctx = lambda slot: r.b_ctx.at[:, :, lanes(slot)]
    spare = [r.x_all.at[1], r.db_all.at[1], r.spare_a, r.spare_b]

    def in_spare(i):
        def at(slot):
            if isinstance(slot, slice):
                return r.de_all.at[0, slot]
            return spare[i].at[slot]

        return at

    to_dbr = in_spare(3)
    to_sm = lambda slot: r.b_sm.at[slot]

    def push_dh(j):
        push(0, k_dh[j], lambda i: r.dpk.at[:, j * w : (j + 1) * w], in_spare(j))

    def push_rows():
        push(0, k_xt, lambda i: r.xt_a.at[:, i], to_x)
        push(0, k_ctx, lambda i: r.ct_a.at[:, i], to_ctx)

    def turn():
        for dst, src in ((r.xt_a, r.x_a), (r.ct_a, r.ctx)):
            turned = src[...].T
            for b in range(n_dp):
                dst[b // 2, b % 2] = turned[b * p.in_rows : (b + 1) * p.in_rows]

    def emit(i, src):
        pltpu.make_async_copy(src, outs[i].at[0] if i == 4 else outs[i], os.at[i]).start()

    def logits():
        arrived(r.ch_two, k_chc)
        chosen = jnp.concatenate([r.ch_own[...], r.ch_two[...]], 0)
        for at, size in p.chunks:
            part = mm_nt(chosen, r.emb[at : at + size, :])
            o_log[c, 0, :, at : at + size] = part[0 : p.masks].astype(BF)
            o_log[other, 0, :, at : at + size] = part[mp : mp + p.masks].astype(BF)
        emit(0, o_log)

    @on(at_x0)
    def _():
        turn()
        push_rows()
        first_here()
        second_here()
        on(is_att)(lambda: feed(r.x_all[c, z]))
        turn_second()
        turn_first()
        xs.step(1)
        for j in range(tiles):
            turn_attention(j)
        arrived(r.ch_own, k_cho)
        r.ch_all[c, dp] = r.ch_own[...]
        send(at_x0, r.ch_own, r.ch_two, (core, dp), k_chc)
        xs.step(2)
        for k in range(1, nz):
            send(at_x0, r.ch_own, ch(dp), (s, lax.rem(dp + 2 * k, n_dp)), k_ch)
        logits()

    stage[0] = 1

    k_dy = recvs.take()

    @on(at_x0)
    def _():
        arrived(r.dyin, k_dy)
        r.dyf[...] = r.dyin[...].astype(F32)

    def norm_backward(par, n_ref, inv_ref):
        up, normed = r.dyf[...], n_ref[...]
        gain_part = jnp.sum(up * normed, 0, keepdims=True)
        shift_part = jnp.sum(up, 0, keepdims=True)
        scaled = up * par[2:3, 0:w]
        first_mean = jnp.mean(scaled, -1, keepdims=True)
        second_mean = jnp.mean(scaled * normed, -1, keepdims=True)
        return inv_ref[...] * (scaled - first_mean - normed * second_mean), gain_part, shift_part

    def small(dst, out_part, gain_part, shift_part):
        dst[...] = jnp.zeros(dst.shape, F32)
        n_b, n_w = ff // n_dp, w // n_dp
        for k in range(n_dp):
            dst[k : k + 1, 0:n_b] = r.bsum[:, k * n_b : (k + 1) * n_b]
            dst[k : k + 1, n_b : n_b + n_w] = out_part[:, k * n_w : (k + 1) * n_w]
            dst[k : k + 1, n_b + 128 : n_b + 128 + n_w] = gain_part[:, k * n_w : (k + 1) * n_w]
            dst[k : k + 1, n_b + 256 : n_b + 256 + n_w] = shift_part[:, k * n_w : (k + 1) * n_w]

    dres, gain_part, shift_part = norm_backward(r.par_f, r.n_f, r.inv_f)
    r.dres[...] = dres
    r.db_all[c, z] = dres.astype(BF)
    db.start()
    branch = r.db_all[c, z]

    total = r.dres[...]
    for j in range(tiles):
        cut = slice(j * w, (j + 1) * w)
        dhidden = (mm(branch, r.w2t[:, cut]) * r.slope[:, cut].astype(F32)).astype(BF)
        r.bsum[:, cut] = jnp.sum(dhidden.astype(F32), 0, keepdims=True)
        total = total + mm(dhidden, r.w1t[cut, :])
    r.dyf[...] = total.astype(BF).astype(F32)
    r.vecs[0:1], r.vecs[1:2] = gain_part, shift_part

    @on(on_1)
    def _():
        xs.step(1)

    dres, gain_part, shift_part = norm_backward(r.par_a, r.n_a, r.inv_a)
    r.dres[...] = dres
    r.dbr_a[...] = dres.astype(BF)
    branch = r.dbr_a[...]
    r.dctx[...] = mm(branch, r.wa[:, 3 * w : 4 * w]).astype(BF)
    for h in range(pairs):
        at = 128 * h
        query = r.pk[:, at : at + 128]
        keyed = split(r.pk[:, w + at : w + at + 128])
        value = split(r.pk[:, 2 * w + at : 2 * w + at + 128])
        upper = r.dctx[:, at : at + 128]
        chance = r.probs[h]
        dchance = mm_nt(upper, value)
        mixed = chance * dchance
        dscores = []
        for cut in (slice(0, 128), slice(128, 256)):
            dscores.append(mixed[:, cut] - chance[:, cut] * jnp.sum(mixed[:, cut], -1, keepdims=True))
        dscores = jnp.concatenate(dscores, 1).astype(BF)
        r.dpk[:, at : at + 128] = (mm(dscores, keyed) * 0.125).astype(BF)
        r.dpk[:, w + at : w + at + 128] = (mm_tn(stack(dscores), split(query)) * 0.125).astype(BF)
        r.dpk[:, 2 * w + at : 2 * w + at + 128] = mm_tn(stack(chance.astype(BF)), split(upper)).astype(BF)
    total = r.dres[...]
    for j in range(3):
        cut = slice(j * w, (j + 1) * w)
        total = total + mm(r.dpk[:, cut], r.wa[:, cut])
    r.dx[...] = total.astype(BF)
    send(at_x1, r.dx, r.dyin, (across, dp), k_dy)

    def row(m, i):
        return r.de_all.at[m, i]

    away = jnp.where(c == 1, across, 3 - s)

    def row_line(cond, i):
        piece = de(i)
        send(cond | not_last, piece, piece, (s, dp + 2), k_row + i)
        send(cond | not_first, piece, piece, (s, dp - 2), k_row + i)
        send(cond, piece, piece, (s, ydp), k_row + i)

    def row_step(t, cond):
        for sign in (-1, 1):
            here, zz = at_distance(t, sign, cond)
            i = 2 * zz + y
            on(here)(lambda i=i: arrived(de(i), k_row + i))
            if t < nz - 1:
                send(onward(here, sign), de(i), de(i), (s, dp - 2 * sign), k_row + i)
            send(here, de(i), de(i), (s, ydp), k_row + i)
            send(here, de(i), de(i), (across, dp), k_pass)

    def row_cross(t, cond):
        for sign in (-1, 1) if t else (1,):
            here, zz = at_distance(t, sign, cond)
            i = 2 * zz + 1 - y
            on(here)(lambda i=i: arrived(de(i), k_row + i))
            send(here, de(i), de(i), (across, dp), k_pass)

    @on(at_x0)
    def _():
        send(at_x0, r.dx, row(c, dp), (away, dp), jnp.where(c == 1, k_pass, k_row + dp))
        send(is_att, r.dx, row(0, dp), (core, dp), k_pass)

        @on(is_ff)
        def _():
            r.de_all[1, dp] = r.dx[...]
            row_line(on_0, dp)

    @on(is_att)
    def _():
        o_wout[...] = jnp.zeros((p.out_rows, w), BF)
        emit(4, o_wout)

    @on(at_x1)
    def _():
        turn()
        push_rows()

    push(0, k_dba, lambda i: r.dbr_a, to_dbr)
    push_dh(0)
    small(r.sm_f, jnp.sum(r.db_all[c, z].astype(F32), 0, keepdims=True), r.vecs[0:1], r.vecs[1:2])
    push(1, k_sm, lambda i: r.sm_f, to_sm)
    r.bsum[...] = jnp.zeros(r.bsum.shape, F32)
    for j in (0, 2):
        cut = slice(j * w, (j + 1) * w)
        r.bsum[:, cut] = jnp.sum(r.dpk[:, cut].astype(F32), 0, keepdims=True)
    small(r.sm_a, jnp.sum(branch.astype(F32), 0, keepdims=True), gain_part, shift_part)
    push(0, k_sm, lambda i: r.sm_a, to_sm)
    push_dh(1)
    push_dh(2)

    @on(at_x1)
    def _():
        xs.step(1, is_att)
        arrived(r.ch_pair, k_chp)
        send(at_x1, r.ch_pair, r.ch_far, (across, dp), k_chq)
        xs.step(2)

    db.step(1)

    @on(at_x0)
    def _():
        xs.step(3)


    @on(at_x1)
    def _():
        xs.step(3)

    db.step(2)

    @on(at_x0)
    def _():
        arrived(r.ch_far, k_chq)
        r.ch_all[c, ydp] = r.ch_far[...]
        for k in range(1, nz):
            send(at_x0, r.ch_far, ch(ydp), (s, lax.rem(dp + 2 * k, n_dp)), k_ch)

    drain(0)

    def head_part():
        arrived(r.ch_all.at[other], k_chx)
        arrived(r.lgr.at[0 : n_dp - 1], k_lg)
        lines = 2 * p.masks
        for i in range(n_dp):
            for m in range(2):
                at = lines * i + p.masks * m
                r.w1t[at : at + p.masks, :] = r.ch_all[m, i, 0 : p.masks]
        grad = mm_tn(r.lgr[...].reshape(n_dp * lines, p.share_pad), r.w1t[0 : n_dp * lines, :])
        o_tab[...] += grad[0 : p.share]

    k_in = [recvs.take(4) for _ in range(tiles)]
    half = nz * p.in_rows
    mate = z + 1 - 2 * lax.rem(z, 2)
    far_base = 2 - 2 * (z // 2)

    def shard(zz, cut):
        return r.wa.at[pl.ds(pl.multiple_of(zz * p.in_rows, p.in_rows), p.in_rows), cut]

    def tile_cut(j):
        return slice(j * w, (j + 1) * w)

    def attention_tile(j):
        cut = tile_cut(j)

        @on(is_att)
        def _():
            if j == 3:
                gathered(k_ctx, to_ctx)
                gathered(k_dba, to_dbr)
                grad = mm(r.b_ctx[...].reshape(half, 4 * ln), spare[3][...].reshape(4 * ln, w))
            else:
                if j == 0:
                    gathered(k_xt, to_x)
                gathered(k_dh[j], in_spare(j))
                grad = mm(r.b_x[...].reshape(half, 4 * ln), spare[j][...].reshape(4 * ln, w))
            r.wa[0:half, cut] = grad.astype(BF)

        to_mate = (s, 2 * mate + y)
        for k in range(2):
            send(outer_att, shard(far_base + k, cut), r.r_in.at[2 + k, :, cut], to_mate, k_in[j] + 2)
        send(outer_att, shard(mate, cut), r.r_in.at[0, :, cut], to_mate, k_in[j])

    to_inner = (s, 2 * (nz - 1 - z) + y)

    def add(zz, part, cut):
        rows = pl.ds(pl.multiple_of(zz * p.in_rows, p.in_rows), p.in_rows)
        r.wa[rows, cut] = (r.wa[rows, cut].astype(F32) + part.astype(F32)).astype(BF)

    def attention_sum(j):
        cut = tile_cut(j)

        @on(inner)
        def _():
            arrived(r.r_in.at[2:4, :, cut], k_in[j] + 2)
            for zz in (nz - 1 - z, nz - 1 - mate):
                add(zz, r.r_in[jnp.where(zz == far_base, 2, 3), :, cut], cut)
            send(inner, shard(nz - 1 - z, cut), r.r_in.at[1, :, cut], to_inner, k_in[j] + 1)
            send(inner, shard(nz - 1 - mate, cut), r.r_in.at[4, :, cut], to_inner, k_in[j] + 3)

    def attention_last(j):
        cut = tile_cut(j)

        @on(inner)
        def _():
            arrived(r.r_in.at[4, :, cut], k_in[j] + 3)
            add(mate, r.r_in[4, :, cut], cut)
            send(inner, shard(mate, cut), r.r_in.at[1, :, cut], (s, 2 * mate + y), k_in[j] + 1)

    units_wide = pl.ds(pl.multiple_of(2 * z * p.out_rows, 2 * p.out_rows), 2 * p.out_rows)
    units_mine = pl.ds(pl.multiple_of(y * p.out_rows, p.out_rows), p.out_rows)
    units_other = pl.ds(pl.multiple_of((1 - y) * p.out_rows, p.out_rows), p.out_rows)

    def units(k):
        @on(is_ff)
        def _():
            near, far = jnp.where(z < nz // 2, z + k, z - k), jnp.where(z < nz // 2, k, nz - 1 - k)
            edge = (z == 0) | (z == nz - 1)
            zz = jnp.where(edge, near, far) if k > 1 else jnp.where(edge | (k == 0), near, jnp.where(z < nz // 2, z - 1, z + 1))
            if k == 0:
                on(at_x1)(lambda: arrived(r.x_all.at[0, zz], xs.core0 + zz))
            else:
                arrived(r.x_all.at[0, zz], xs.core0 + zz)
            arrived(r.db_all.at[0, zz], db.core0 + zz)
            rows_x = jnp.concatenate([r.x_all[m, zz] for m in range(2)], 0)
            up = jnp.concatenate([r.db_all[m, zz] for m in range(2)], 0)
            hidden = mm(rows_x, r.w1[:, units_wide]) + r.par_f[0:1, units_wide]
            below = 0.5 + 0.5 * lax.erf(hidden * (0.5**0.5))
            slope = below + hidden * (0.3989422804014327 * jnp.exp(-0.5 * hidden * hidden))
            dhidden = (mm(up, r.w2t[:, units_wide]) * slope).astype(BF)
            out_part, col_part = mm_tn((hidden * below).astype(BF), up), mm_tn(rows_x, dhidden)
            if k == 0:
                r.u_out[...], r.w_col[...] = out_part, col_part
            else:
                r.u_out[...] += out_part
                r.w_col[...] += col_part

    def out_piece(i):
        return r.r_in.at[i, :, 0:w]

    def col_piece(i):
        return r.r_in.at[i % 4, :, w + p.out_rows * (i // 4) : w + p.out_rows * (i // 4 + 1)]

    def stage_out(i):
        return r.w1t.at[1408 + i * p.in_rows : 1408 + (i + 1) * p.in_rows, :]

    def stage_col(i):
        return r.w1t.at[1792 + i * p.in_rows : 1792 + (i + 1) * p.in_rows, 0 : p.out_rows]

    def exchange_out(cond):
        @on(is_ff | cond)
        def _():
            theirs = r.u_out[units_other, :].astype(BF)
            for i in range(p.out_rows // p.in_rows):
                stage_out(i)[...] = theirs[i * p.in_rows : (i + 1) * p.in_rows]
                send(is_ff, stage_out(i), out_piece(i), (s, ydp), k_pair, tag=6)

    def exchange_col(cond):
        @on(is_ff | cond)
        def _():
            theirs = r.w_col[:, units_other].astype(BF)
            for i in range(n_dp):
                stage_col(i)[...] = theirs[i * p.in_rows : (i + 1) * p.in_rows]
                send(is_ff, stage_col(i), col_piece(i), (s, ydp), k_pair, tag=6)

    entry = iota((p.share_rows, ln), 0) + (s * p.quarter + dp * p.share)

    def scatter(m):
        def step(i, carry):
            hot = []
            for k in range(2):
                hot.append(jnp.where(entry == r.ids_all[2 * i + k, pl.ds(m, 1), :], 1.0, 0.0).astype(BF))
            rows = r.de_all[m, pl.ds(2 * i, 2)].reshape(2 * ln, w)
            o_tab[...] += mm(jnp.concatenate(hot, 1), rows)[0 : p.share]
            return carry

        lax.fori_loop(0, n_dp // 2, step, 0)

    k_col, k_smz = recvs.take(), recvs.take()
    k_pair = recvs.take()

    def gathered_row(cond):
        send(cond, r.de_all.at[1 - x], r.de_all.at[1 - x], (core, dp), k_dex + (1 - x))

    units(0)
    o_tab[...] = jnp.zeros(o_tab.shape, F32)
    attention_tile(3)
    row_step(1, on_0)
    attention_tile(0)
    units(1)
    db.step(3)
    units(2)
    units(3)
    exchange_out(always)
    exchange_col(at_x1)
    row_step(2, on_0)
    row_step(3, on_0)
    exchange_col(at_x0)
    attention_sum(3)
    row_cross(0, on_0)
    row_cross(1, on_0)

    @on(at_x0)
    def _():
        arrived(r.ch_all.at[c, 0 : n_dp - 2], k_ch)
        send(is_att, r.ch_all.at[c], r.ch_all.at[c], (across, dp), k_cha)
        send(at_x0, r.ch_all.at[c], r.ch_all.at[c], (core, dp), k_chx)


    attention_tile(1)
    attention_sum(0)
    attention_last(3)

    @on(on_1)
    def _():
        arrived(de(dp), k_row + dp)
        row_line(on_1, dp)

    on(at_x1)(logits)
    row_step(1, on_1)
    row_step(2, on_1)
    attention_sum(1)
    attention_last(0)

    attention_tile(2)
    attention_sum(2)
    attention_last(1)
    row_cross(0, on_1)
    row_cross(1, on_1)

    gathered(k_sm, to_sm)
    r.sm_tot[...] = r.b_sm[0] + r.b_sm[1] + r.b_sm[2] + r.b_sm[3]
    r.r_sm[z] = r.sm_tot[...]
    for k in range(1, nz):
        zz = lax.rem(z + k, nz)
        send(always, r.sm_tot, r.r_sm.at[z], (s, 2 * zz + y), k_smz)


    row_step(3, on_1)
    row_cross(2, is_ff)
    row_cross(3, is_ff)
    gathered_row(is_ff)
    send(on_0, r.ch_all.at[c], r.ch_all.at[c], (across, dp), k_cha)


    def passed_row():
        on(is_ff)(lambda: arrived(r.de_all.at[x], k_pass))
        send(is_ff, r.de_all.at[x], r.de_all.at[x], (core, dp), k_dex + x)
        on(is_att)(lambda: arrived(r.de_all.at[x], k_dex + x))

    attention_last(2)

    def column_block(k):
        at = k * p.out_rows
        return r.slope.at[0 : p.in_rows, pl.ds(at if isinstance(k, int) else pl.multiple_of(at, p.out_rows), p.out_rows)]

    @on(is_ff)
    def _():
        arrived(r.r_in.at[0:2], k_pair)
        for i in range(p.out_rows // p.in_rows):
            own = r.u_out[pl.ds(pl.multiple_of(y * p.out_rows + i * p.in_rows, p.in_rows), p.in_rows), :]
            o_wout[i * p.in_rows : (i + 1) * p.in_rows, :] = (own + out_piece(i)[...].astype(F32)).astype(BF)
        emit(4, o_wout)
        for i in range(n_dp):
            own = r.w_col[i * p.in_rows : (i + 1) * p.in_rows, units_mine]
            column_block(i)[...] = (own + col_piece(i)[...].astype(F32)).astype(BF)
        r.r_col[dp] = column_block(dp)[...]

    for k in (4, 5, 3, 2, 6, 1, 7) if n_dp == 8 else range(1, n_dp):
        to = lax.rem(dp + k, n_dp)
        send(is_ff, column_block(to), r.r_col.at[dp], (s, to), k_col)

    on(at_x0)(head_part)
    on(is_att)(lambda: arrived(r.de_all.at[1 - x], k_dex + 1 - x))
    arrived(r.ids_all.at[0 : n_dp - 1], k_id)
    scatter(1 - x)

    passed_row()
    scatter(x)

    @on(at_x1)
    def _():
        arrived(r.ch_all.at[c], k_cha)
        send(at_x1, r.ch_all.at[c], r.ch_all.at[c], (core, dp), k_chx)
        head_part()

    n_pos = ln // n_dp
    here = pl.ds(pl.multiple_of(dp * n_pos, n_pos), n_pos)
    total = jnp.zeros((n_pos, w), F32)
    for m in range(2):
        for i in range(n_dp):
            total = total + r.de_all[m, i, here, :].astype(F32)
    o_pos[...] = total
    emit(1, o_tab)
    emit(2, o_pos)

    @on(is_att)
    def _():
        mine = pl.ds(pl.multiple_of(z * p.in_rows, p.in_rows), p.in_rows)
        for j in (3, 0, 1, 2):
            cut = tile_cut(j)

            @on(inner)
            def _():
                arrived(r.r_in.at[0, :, cut], k_in[j])
                add(z, r.r_in[0, :, cut], cut)

            arrived(r.r_in.at[1, :, cut], k_in[j] + 1)
            o_win[0, :, cut] = (r.wa[mine, cut].astype(F32) + r.r_in[1, :, cut].astype(F32)).astype(BF)
            pltpu.make_async_copy(o_win.at[:, :, cut], outs[3].at[:, :, cut], os.at[3]).start()

    @on(is_ff)
    def _():
        arrived(r.r_col.at[0 : n_dp - 1], k_col)
        for k in range(n_dp):
            cut = slice(k * p.out_rows, (k + 1) * p.out_rows)
            pltpu.make_async_copy(r.r_col.at[k], outs[3].at[0, :, cut], os.at[3]).start()

    arrived(r.r_sm.at[0 : nz - 1], k_smz)
    r.sm_all[...] = r.r_sm[0] + r.r_sm[1] + r.r_sm[2] + r.r_sm[3]
    emit(5, o_vec)
    for i, src in enumerate((o_log, o_tab, o_pos, o_win, o_wout, o_vec)):
        pltpu.make_async_copy(src, outs[i].at[0] if i == 4 else outs[i], os.at[i]).wait()

    drain(1)
    assert sends.n <= SENDS and recvs.n <= RECVS, (sends.n, recvs.n)


def finish(p, *refs):
    ins, outs, (log_v, log_w, tab_v, win_v, win_w, wout_v, wout_w, vec_v, b_v, v_v, si, so) = refs[:6], refs[6:15], refs[15:]
    pieces = (log_v, tab_v, None, win_v, wout_v, vec_v)

    def copy_in(i):
        return pltpu.make_async_copy(ins[i], pieces[i], si.at[i])

    def copy_out(i, src):
        return pltpu.make_async_copy(src, outs[i], so.at[i])

    for i in (5, 0, 1, 3, 4):
        copy_in(i).start()
    straight = pltpu.make_async_copy(ins[2], outs[2], so.at[2])
    straight.start()
    n_b, n_w = p.ff // p.n_dp, p.width // p.n_dp
    copy_in(5).wait()
    mine = vec_v[pl.ds(lax.axis_index("dp"), 1), :]
    b_v[...] = mine[:, 0:n_b]
    for k in range(3):
        v_v[k] = mine[:, n_b + 128 * k : n_b + 128 * k + n_w]
    done = [copy_out(5, b_v)] + [copy_out(6 + k, v_v.at[k]) for k in range(3)]
    copy_in(0).wait()
    log_w[...] = log_v[...].astype(F32)
    done.append(copy_out(0, log_w))
    for one in done:
        one.start()
    copy_in(1).wait()
    done.append(copy_out(1, tab_v))
    done[-1].start()
    copy_in(3).wait()
    win_w[...] = win_v[...].astype(F32)
    done.append(copy_out(3, win_w))
    done[-1].start()
    copy_in(4).wait()
    wout_w[...] = wout_v[...].astype(F32)
    done.append(copy_out(4, wout_w))
    done[-1].start()
    straight.wait()
    for one in done:
        one.wait()


def whole(
    n_dp,
    token_ids,
    segment_ids,
    masked_rows,
    embedding,
    pos_table,
    w_in,
    w_out,
    b_in,
    b_out,
    norm_gain,
    norm_shift,
    logit_grad,
):
    quarter, width = embedding.shape
    batches, _, length = token_ids.shape
    masks = masked_rows.shape[-1]
    ff = w_in.shape[-1]
    p = Plan(n_dp, length, width, ff, quarter, masks)
    scratch = scratch_list(p)
    shapes = [
        (batches, 1, masks, quarter),
        (p.share, width),
        (length // n_dp, width),
        (1, p.in_rows, ff),
        (1, p.out_rows, width),
        (1, ff // n_dp),
        (1, p.in_rows),
        (1, p.in_rows),
        (1, p.in_rows),
    ]
    far = pl.BlockSpec(memory_space=pl.ANY)
    part_types = [BF, F32, F32, BF, BF]
    parts = [jax.ShapeDtypeStruct(shape, kind) for shape, kind in zip(shapes, part_types)]
    parts.append(jax.ShapeDtypeStruct((8, width), F32))
    summed = pl.pallas_call(
        functools.partial(fused, p, list(scratch)),
        out_shape=parts,
        in_specs=[far] * 12,
        out_specs=[far] * 6,
        scratch_shapes=[pltpu.VMEM(*one) for one in scratch.values()]
        + [
            pltpu.SemaphoreType.DMA((SENDS,)),
            pltpu.SemaphoreType.DMA((RECVS,)),
            pltpu.SemaphoreType.DMA((len(p.chunks) + 11,)),
            pltpu.SemaphoreType.DMA((6,)),
        ],
        compiler_params=pltpu.CompilerParams(
            collective_id=0, has_side_effects=True, vmem_limit_bytes=VMEM_LIMIT
        ),
    )(
        token_ids,
        segment_ids,
        masked_rows,
        b_in,
        b_out,
        norm_gain,
        norm_shift,
        logit_grad,
        pos_table,
        embedding,
        w_in,
        w_out,
    )
    room = [
        (shapes[0], BF),
        (shapes[0], F32),
        (shapes[1], F32),
        (shapes[3], BF),
        (shapes[3], F32),
        (shapes[4], BF),
        (shapes[4], F32),
        ((8, width), F32),
        (shapes[5], F32),
        ((3, 1, p.in_rows), F32),
    ]
    return pl.pallas_call(
        functools.partial(finish, p),
        out_shape=[jax.ShapeDtypeStruct(shape, F32) for shape in shapes],
        in_specs=[far] * 6,
        out_specs=[far] * 9,
        scratch_shapes=[pltpu.VMEM(*one) for one in room]
        + [pltpu.SemaphoreType.DMA((6,)), pltpu.SemaphoreType.DMA((9,))],
        compiler_params=pltpu.CompilerParams(vmem_limit_bytes=VMEM_LIMIT),
    )(*summed)


def solution(mesh):
    n_section, n_dp = mesh.shape["section"], mesh.shape["dp"]

    def chosen_form(*args):
        token_ids, embedding, w_in = args[0], args[3], args[5]
        fits = (
            n_section == 4
            and n_dp == 8
            and token_ids.shape[0] == 2
            and token_ids.shape[1:] == (1, 128)
            and w_in.shape[1] % (16 * n_dp) == 0
            and w_in.shape[2] == 4 * w_in.shape[1]
            and embedding.shape[0] % (8 * n_dp) == 0
        )
        return whole(n_dp, *args) if fits else local(*args)

    placed = (
        P(None, "dp", None),
        P(None, "dp", None),
        P(None, "dp", None),
        P("section", None),
        P(),
        P("section", None, None),
        P("section", None, None),
        P("section", None),
        P("section", None),
        P("section", None),
        P("section", None),
        P(None, "dp", None, "section"),
    )
    return jax.shard_map(
        chosen_form,
        mesh=mesh,
        in_specs=placed,
        out_specs=(
            P(None, "dp", None, "section"),
            P(("section", "dp"), None),
            P("dp", None),
            P("section", "dp", None),
            P("section", "dp", None),
            P("section", "dp"),
            P("section", "dp"),
            P("section", "dp"),
            P("section", "dp"),
        ),
        check_vma=False,
    )
```
